32 devices in a mesh: dp: 4 (over x, core), seq: 8 (over z, y).
Axes of the slice: x: 2, y: 2, z: 4, core: 2. Of those that a mesh axis runs over, the one named last changes fastest.
Arguments:
- tokens: bfloat16 [4, 4096, 1280], P('dp', 'seq'), may hold values from -6 to 6
- bounds: int32 [2, 4, 4096], P(None, 'dp', 'seq'), may hold values from 0 to 4095, as said below
- w_in: bfloat16 [2, 1280, 640], replicated, may hold values from -0.15625 to 0.15625
- w_mid: bfloat16 [2, 5, 640, 640], replicated, may hold values from -0.109375 to 0.109375
- w_out: bfloat16 [2, 640, 1280], replicated, may hold values from -0.25 to 0.25
- gain_wide: float32 [2, 1280], replicated, may hold values from 0.25 to 1.75
- shift_wide: float32 [2, 1280], replicated, may hold values from -1.5 to 1.5
- gain_narrow: float32 [2, 2, 640], replicated, may hold values from 0.25 to 1.75
- shift_narrow: float32 [2, 2, 640], replicated, may hold values from -1.5 to 1.5
- bias_narrow: float32 [2, 2, 640], replicated, may hold values from -1.5 to 1.5
- bias_wide: float32 [2, 1280], replicated, may hold values from -1.5 to 1.5
- cotangent: bfloat16 [4, 4096, 1280], P('dp', 'seq'), may hold values from -6 to 6
Outputs:
- out: float32 [4, 4096, 1280], P('dp', 'seq')
- grad_tokens: float32 [4, 4096, 1280], P('dp', 'seq')
- grad_w_in: float32 [2, 1280, 640], P(None, 'seq')
- grad_w_mid: float32 [2, 5, 640, 640], P(None, None, None, 'seq')
- grad_w_out: float32 [2, 640, 1280], P(None, None, 'seq')
- grad_gain_wide: float32 [2, 1280], replicated
- grad_shift_wide: float32 [2, 1280], replicated
- grad_gain_narrow: float32 [2, 2, 640], replicated
- grad_shift_narrow: float32 [2, 2, 640], replicated
- grad_bias_narrow: float32 [2, 2, 640], replicated
- grad_bias_wide: float32 [2, 1280], replicated
The draws below stay inside these ranges and needn't reach their ends.
Inputs may be any that keep to these rules, and one draw needn't show every extreme that they name: bounds[0] and bounds[1] give, for each token, the first position and one past the last position of its protein in its row. Proteins are contiguous and follow one another from position 0; each run of 512 positions starting at a multiple of 512 holds exactly one protein end, at least 128 and less than 384 into the run; after the last protein end the row is padding, where both entries equal the token's own position (an empty protein).
All inputs are finite; a program needn't handle non-finite values.
Results may differ from the reference program's by a relative error of at most 0.015.
Values may be sent and summed in bfloat16 or wider, within the bound.
No kernel may reach another device: no remote copies, remote signals or barrier semaphores. Data moves between devices by JAX's collectives and lax.ppermute only.
A program may use at most 256 MiB of HBM per device.

```python
import jax
import jax.numpy as jnp
from jax import lax

D = 1280
INNER = 640
KERNEL = 5
DILATION_CLOSE = 4
DILATION_BROAD = 128
BLOCKS = 2
TOK_DEV = 512
SEQ_LEN = 4096
ROWS = 4


def draw_bounds(key, part):
    key = jax.random.fold_in(key, 7)
    pieces = SEQ_LEN // TOK_DEV
    offsets = jax.random.randint(key, (ROWS, pieces), TOK_DEV // 4, 3 * TOK_DEV // 4)
    cut_points = jnp.arange(pieces, dtype=jnp.int32)[None, :] * TOK_DEV + offsets.astype(jnp.int32)
    position = jnp.arange(SEQ_LEN, dtype=jnp.int32)
    passed = jnp.sum((cut_points[:, None, :] <= position[None, :, None]).astype(jnp.int32), axis=-1)
    first_cuts = jnp.concatenate([jnp.zeros((ROWS, 1), jnp.int32), cut_points], axis=1)
    starts = jnp.take_along_axis(first_cuts, passed, axis=1)
    next_cuts = jnp.take_along_axis(cut_points, jnp.minimum(passed, pieces - 1), axis=1)
    in_tail = passed == pieces
    own_place = jnp.broadcast_to(position[None, :], (ROWS, SEQ_LEN))
    starts = jnp.where(in_tail, own_place, starts)
    end_points = jnp.where(in_tail, own_place, next_cuts)
    return jnp.stack([starts, end_points]).astype(jnp.int32)


def with_spikes(array, rng, source, target, shards_of, factor):
    owner, partner = [(jnp.arange(array.shape[dim]) // (array.shape[dim] // shards_of)).reshape([-1 if axis == dim else 1 for axis in range(array.ndim)]) for dim in (source, target)]
    chosen = jax.random.permutation(rng, shards_of)[partner]
    strong = (owner == chosen) | (owner == (partner + shards_of // 2) % shards_of)
    return jnp.where(strong, factor * array, array)


def shard_levels(rng, shape, split, least, top_value):
    level = 1.0
    for dim, blocks in split:
        steps = jax.random.uniform(jax.random.fold_in(jax.random.fold_in(rng, 6), dim), (blocks,), jnp.float32, least / len(split), top_value / len(split))
        level = level * jnp.repeat(jnp.exp(steps), shape[dim] // blocks).reshape((-1,) + (1,) * (len(shape) - 1 - dim))
    return level


def gaussian(key, shape, width, most, shards=(), held_as=jnp.bfloat16):
    array = jax.random.normal(key, shape, jnp.float32) * width
    if len(shards) > 0:
        array = shard_levels(key, shape, shards, -0.22, 0.18) * array
    return jnp.clip(array, min=-most, max=most).astype(held_as)


def noise_with(own_key, extent, deviation, bound, cuts, heavy, kind=jnp.bfloat16):
    values = deviation * jax.random.normal(own_key, extent, jnp.float32)
    if cuts:
        values = values * shard_levels(own_key, extent, cuts, -0.22, 0.18)
    return jnp.clip(with_spikes(values, jax.random.fold_in(own_key, 3), *heavy), -bound, bound).astype(kind)


def setup_inputs(seed: int = 0) -> dict:
    keys = jax.random.split(jax.random.key(seed), 13)
    return {
        "tokens": noise_with(keys[0], (ROWS, SEQ_LEN, D), 1.0, 6.0, ((0, 4), (1, 8)), (1, 2, 8, 2.0)),
        "bounds": draw_bounds(jax.random.fold_in(keys[12], 71), 0),
        "w_in": gaussian(keys[2], (BLOCKS, D, INNER), D ** -0.5, 0.15625),
        "w_mid": gaussian(keys[3], (BLOCKS, KERNEL, INNER, INNER), (KERNEL * INNER) ** -0.5, 0.109375),
        "w_out": gaussian(keys[4], (BLOCKS, INNER, D), INNER ** -0.5, 0.25),
        "gain_wide": jnp.clip(1.0 + 0.15 * jax.random.normal(keys[5], (BLOCKS, D), jnp.float32), 0.25, 1.75),
        "shift_wide": gaussian(keys[6], (BLOCKS, D), 0.3, 1.5, (), jnp.float32),
        "gain_narrow": jnp.clip(1.0 + 0.15 * jax.random.normal(keys[7], (BLOCKS, 2, INNER), jnp.float32), 0.25, 1.75),
        "shift_narrow": gaussian(keys[8], (BLOCKS, 2, INNER), 0.3, 1.5, (), jnp.float32),
        "bias_narrow": gaussian(keys[9], (BLOCKS, 2, INNER), 0.3, 1.5, (), jnp.float32),
        "bias_wide": gaussian(keys[10], (BLOCKS, D), 0.3, 1.5, (), jnp.float32),
        "cotangent": noise_with(keys[11], (ROWS, SEQ_LEN, D), 1.0, 6.0, ((0, 4), (1, 8)), (1, 2, 8, 2.0)),
    }


@jax.custom_vjp
def low(v):
    return lax.optimization_barrier(v.astype(jnp.bfloat16)).astype(jnp.float32)

@jax.custom_vjp
def low_back(v):
    return v

def low_keep(v):
    return (low(v), None)

def low_pass(kept, grad):
    return (grad,)

def back_keep(v):
    return (v, None)

def back_low(kept, grad):
    return (low(grad),)
low.defvjp(low_keep, low_pass)
low_back.defvjp(back_keep, back_low)

def norm_act(values, gain_row, shift_row):
    average = lax.optimization_barrier(jnp.mean(values, axis=-1, keepdims=True))
    centred = values - average
    inverse = lax.rsqrt(lax.optimization_barrier(jnp.mean(centred * centred, axis=-1, keepdims=True)) + 1e-05)
    return jax.nn.gelu(centred * inverse * gain_row + shift_row, approximate=False)

def make_masks(starts, end_points, position, dilation_step, tap_count):
    offsets = (jnp.arange(tap_count, dtype=jnp.int32) - tap_count // 2) * dilation_step
    target = position[None, :] + offsets[:, None]
    inside = (starts[None, :] <= target) & (target < end_points[None, :])
    return inside.astype(jnp.float32)

def matmul(left, right):
    return jnp.dot(left, right, precision=lax.Precision.HIGHEST, preferred_element_type=jnp.float32)

def bytenet_block(current, layer_params, tap_masks, dilation_step):
    wide_in, wide_mid, wide_out, gain_row, shift_row, gain_pair, shift_pair, bias_pair, bias_row = layer_params
    seq_length = current.shape[0]
    act_one = low(norm_act(current, gain_row, shift_row))
    inner_one = low_back(matmul(act_one, wide_in) + bias_pair[0])
    second_activation = low(norm_act(inner_one, gain_pair[0], shift_pair[0]))
    rim_width = 2 * dilation_step
    padded = jnp.pad(second_activation, ((rim_width, rim_width), (0, 0)))
    mixed = bias_pair[1]
    for tap_index in range(wide_mid.shape[0]):
        window = padded[tap_index * dilation_step:tap_index * dilation_step + seq_length] * tap_masks[tap_index][:, None]
        mixed = mixed + matmul(window, wide_mid[tap_index])
    inner_two = low_back(mixed)
    third_activation = low(norm_act(inner_two, gain_pair[1], shift_pair[1]))
    return current + low_back(matmul(third_activation, wide_out) + bias_row)

def reference(tokens, bounds, w_in, w_mid, w_out, gain_wide, shift_wide, gain_narrow, shift_narrow, bias_narrow, bias_wide, cotangent):
    params = (w_in.astype(jnp.float32), w_mid.astype(jnp.float32), w_out.astype(jnp.float32), gain_wide, shift_wide, gain_narrow, shift_narrow, bias_narrow, bias_wide)
    position = jnp.arange(SEQ_LEN, dtype=jnp.int32)
    dilation_steps = (DILATION_CLOSE, DILATION_BROAD)
    checked_block = jax.checkpoint(bytenet_block, static_argnums=(3,))

    def forward(row_tokens, weights, row_masks):
        current = row_tokens
        for index_of_block in range(2):
            layer_params = tuple((item[index_of_block] for item in weights))
            current = checked_block(current, layer_params, row_masks[index_of_block], dilation_steps[index_of_block])
        return current

    def row_step(totals, inputs):
        row_tokens, starts, end_points, row_cotangent = inputs
        row_masks = [make_masks(starts, end_points, position, dilation_step, KERNEL) for dilation_step in dilation_steps]
        result, pullback = jax.vjp(lambda values, weights: forward(values, weights, row_masks), row_tokens.astype(jnp.float32), params)
        grad_row, grad_params = pullback(row_cotangent.astype(jnp.float32))
        totals = jax.tree.map(jnp.add, totals, grad_params)
        return (totals, (result, grad_row))
    initial = jax.tree.map(jnp.zeros_like, params)
    totals, outputs = lax.scan(row_step, initial, (tokens, bounds[0], bounds[1], cotangent))
    return (outputs[0], outputs[1], totals[0], totals[1], totals[2], totals[3], totals[4], totals[5], totals[6], totals[7], totals[8])
```

```python
import functools

import jax
import jax.numpy as jnp
from jax import lax
from jax.experimental import pallas as pl
from jax.experimental.pallas import tpu as pltpu
from jax.sharding import PartitionSpec as P

DILATION_CLOSE = 4
DILATION_BROAD = 128
EPS = 1e-05
F32 = jnp.float32
BF16 = jnp.bfloat16
VMEM_LIMIT = 56 * 1024 * 1024

C0 = 0.3275911 * 0.7071067811865476
POLY = tuple(0.5 * c for c in (0.254829592, -0.284496736, 1.421413741, -1.453152027, 1.061405429))
ROOT_2PI = 0.3989422804014327


def normal_parts(q):
    bell = jnp.exp(-0.5 * q * q)
    den = 1.0 + C0 * jnp.abs(q)
    t = pl.reciprocal(den, approx=True)
    t = t * (2.0 - den * t)
    h = POLY[4]
    for c in POLY[3::-1]:
        h = h * t + c
    tail = h * t * bell
    return jnp.where(q >= 0, 1.0 - tail, tail), q * bell * ROOT_2PI


def act_forward(v, gain, shift):
    c = v.shape[-1]
    centred = v - jnp.sum(v, axis=-1, keepdims=True) * (1.0 / c)
    r = lax.rsqrt(jnp.sum(centred * centred, axis=-1, keepdims=True) * (1.0 / c) + EPS)
    n = centred * r
    q = n * gain + shift
    below, slope = normal_parts(q)
    return n, r, q * below, below + slope


def act_backward(f, n, r, d, gain):
    c = f.shape[-1]
    p = f * d
    gp = gain * p
    first = jnp.sum(gp, axis=-1, keepdims=True) * (1.0 / c)
    second = jnp.sum(gp * n, axis=-1, keepdims=True) * (1.0 / c)
    return p, r * (gp - first - n * second)


def fold(v):
    return jnp.sum(v.reshape(v.shape[0] // 8, 8, v.shape[1]), axis=0)


def total(acc):
    return jnp.sum(acc, axis=0, keepdims=True)


def strips(rows, height, step, carry=()):
    def body(i, c):
        return step(pl.ds(pl.multiple_of(i * height, height), height), c)

    return lax.fori_loop(0, rows // height, body, carry)


def dot(a, b):
    return jnp.dot(a, b, preferred_element_type=F32)


def dot_nt(a, b):
    return lax.dot_general(a, b, (((1,), (1,)), ((), ())), preferred_element_type=F32)


def dot_tn(a, b):
    return lax.dot_general(a, b, (((0,), (0,)), ((), ())), preferred_element_type=F32)


def call(kernel, outs, args, scratch=(), flops=0, name=None):
    nbytes = sum(a.size * a.dtype.itemsize for a in args)
    out_shape = [jax.ShapeDtypeStruct(s, t) for s, t in outs]
    nbytes += sum(a.size * a.dtype.itemsize for a in out_shape)
    return pl.pallas_call(
        kernel,
        out_shape=out_shape,
        in_specs=[pl.BlockSpec(memory_space=pltpu.VMEM)] * len(args),
        out_specs=[pl.BlockSpec(memory_space=pltpu.VMEM)] * len(outs),
        scratch_shapes=list(scratch),
        compiler_params=pltpu.CompilerParams(vmem_limit_bytes=VMEM_LIMIT),
        cost_estimate=pl.CostEstimate(flops=flops, bytes_accessed=nbytes, transcendentals=0),
        name=name,
    )(*args)


def first_half(x_ref, w_in, vecw, vecn, a1, n1, d1, r1, a2, n2, d2, r2, z):
    rows = x_ref.shape[0]

    def wide(at, c):
        n, r, a, d = act_forward(x_ref[at].astype(F32), vecw[0:1], vecw[1:2])
        n1[at], d1[at], a1[at] = n, d, a.astype(BF16)
        r1[at] = jnp.broadcast_to(r, (r.shape[0], 128))
        return c

    strips(rows, 16, wide)
    z[...] = dot(a1[...], w_in[...]) + vecn[2:3]

    def narrow(at, c):
        n, r, a, d = act_forward(z[at], vecn[0:1], vecn[1:2])
        n2[at], d2[at], a2[at] = n, d, a.astype(BF16)
        r2[at] = jnp.broadcast_to(r, (r.shape[0], 128))
        return c

    strips(rows, 32, narrow)


def windows(before, own, after, masks, win, pad, step):
    rows, width = own.shape
    rim = before.shape[0]
    taps = masks.shape[0]
    pad[0:rim] = before[...].astype(pad.dtype)
    pad[rim : rim + rows] = own[...].astype(pad.dtype)
    pad[rim + rows : rim + rows + rim] = after[...].astype(pad.dtype)
    for k in range(taps):
        start = rim + (k - taps // 2) * step
        for i in range(0, rows, 64):
            m = masks[k, i : i + 64].astype(pad.dtype)
            m = jnp.concatenate([m] * (width // 128), axis=1)
            v = pad[start + i : start + i + 64] * m
            win[i : i + 64, k * width : (k + 1) * width] = v.astype(BF16)


def k_in(x_ref, w_in, vecw, vecn, *rest):
    first_half(x_ref, w_in, vecw, vecn, *rest)


def k_mid(
    x_ref, before, own, after, masks, w_mid, w_out, w_in, vecn, vecw_out, vecw, vecn2,
    win, a3, n3, d3, r3, y, a1, n1, d1, r1, a2, n2, d2, r2, pad, z, *, step,
):
    rows = x_ref.shape[0]
    windows(before, own, after, masks, win, pad, step)
    z[...] = dot(win[...], w_mid[...]) + vecn[2:3]

    def narrow(at, c):
        n, r, a, d = act_forward(z[at], vecn[0:1], vecn[1:2])
        n3[at], d3[at], a3[at] = n, d, a.astype(BF16)
        r3[at] = jnp.broadcast_to(r, (r.shape[0], 128))
        return c

    strips(rows, 32, narrow)
    y[...] = x_ref[...].astype(F32) + dot(a3[...], w_out[...]) + vecw_out[0:1]
    first_half(y, w_in, vecw, vecn2, a1, n1, d1, r1, a2, n2, d2, r2, z)


def k_flow(e, w_out, f, sums):
    f[...] = dot_nt(e[...], w_out[...])

    def step(at, acc):
        return acc + fold(e[at].astype(F32))

    sums[...] = total(strips(e.shape[0], 32, step, jnp.zeros((8, e.shape[1]), F32)))


def k_conv(before, own, after, masks, w_mid, vecn, f, win, a3, e2, sums, pad, z, *, step):
    rows, width = own.shape
    windows(before, own, after, masks, win, pad, step)
    z[...] = dot(win[...], w_mid[...]) + vecn[2:3]

    def narrow(at, c):
        n, r, a, d = act_forward(z[at], vecn[0:1], vecn[1:2])
        a3[at] = a.astype(BF16)
        p, v = act_backward(f[at], n, r, d, vecn[0:1])
        e = v.astype(BF16)
        e2[at] = e
        return c[0] + fold(p * n), c[1] + fold(p), c[2] + fold(e.astype(F32))

    zero = jnp.zeros((8, width), F32)
    for i, acc in enumerate(strips(rows, 32, narrow, (zero,) * 3)):
        sums[i : i + 1] = total(acc)


def k_out(x, a3, w_out, bias, y):
    y[...] = x[...] + dot(a3[...], w_out[...]) + bias[0:1]


def k_weights(*refs, shapes):
    pairs, outs = refs[: 2 * len(shapes)], refs[2 * len(shapes) :]
    for i, taps in enumerate(shapes):
        left, right = pairs[2 * i], pairs[2 * i + 1]
        left_t = left[...].T
        if taps == 1:
            outs[i][...] = dot(left_t, right[...]).astype(BF16)
        else:
            width = right.shape[1] // taps
            for k in range(taps):
                outs[i][k] = dot(left_t, right[:, k * width : (k + 1) * width]).astype(BF16)


def back_narrow(f, n, d, r, gain, e_out, sums):
    rows, width = f.shape

    def step(at, c):
        nn = n[at]
        p, v = act_backward(f[at], nn, r[at][:, 0:1], d[at], gain[0:1])
        e = v.astype(BF16)
        e_out[at] = e
        return c[0] + fold(p * nn), c[1] + fold(p), c[2] + fold(e.astype(F32))

    zero = jnp.zeros((8, width), F32)
    for i, acc in enumerate(strips(rows, 32, step, (zero,) * 3)):
        sums[i : i + 1] = total(acc)


def back_wide(f, n, d, r, gain, dy, dx, sums):
    rows, width = f.shape

    def step(at, c):
        nn = n[at]
        p, v = act_backward(f[at], nn, r[at][:, 0:1], d[at], gain[0:1])
        dx[at] = dy[at].astype(F32) + v
        return c[0] + fold(p * nn), c[1] + fold(p)

    zero = jnp.zeros((8, width), F32)
    for i, acc in enumerate(strips(rows, 16, step, (zero,) * 2)):
        sums[i : i + 1] = total(acc)


def flow_two(win, w_mid, z):
    taps = w_mid.shape[0]
    width = w_mid.shape[1]
    for j in range(taps):
        part = dot_nt(win[:, j * width : (j + 1) * width], w_mid[taps - 1 - j])
        if j == 0:
            z[...] = part
        else:
            z[...] += part


def k_back1(
    before, own, after, masks, w_mid, w_in, n2, d2, r2, vecn, n1, d1, r1, vecw, dy,
    w_out0, n3, d3, r3, vecn0,
    e1, sums1, sums_w, dx, e3, sums_e3, e2, sums2, win, pad, z, f1, *, step,
):
    windows(before, own, after, masks, win, pad, step)
    flow_two(win, w_mid, z)
    back_narrow(z, n2, d2, r2, vecn, e1, sums1)
    f1[...] = dot_nt(e1[...], w_in[...])
    back_wide(f1, n1, d1, r1, vecw, dy, dx, sums_w)

    def cast(at, acc):
        e = dx[at].astype(BF16)
        e3[at] = e
        return acc + fold(e.astype(F32))

    sums_e3[...] = total(strips(dx.shape[0], 32, cast, jnp.zeros((8, dx.shape[1]), F32)))
    z[...] = dot_nt(e3[...], w_out0[...])
    back_narrow(z, n3, d3, r3, vecn0, e2, sums2)


def k_back0(
    before, own, after, masks, w_mid, w_in, n2, d2, r2, vecn, n1, d1, r1, vecw, dy,
    e1, sums1, sums_w, dx, win, pad, z, f1, *, step,
):
    windows(before, own, after, masks, win, pad, step)
    flow_two(win, w_mid, z)
    back_narrow(z, n2, d2, r2, vecn, e1, sums1)
    f1[...] = dot_nt(e1[...], w_in[...])
    back_wide(f1, n1, d1, r1, vecw, dy, dx, sums_w)


def halos(v, rim):
    count = lax.axis_size("seq")
    up = [(i, i + 1) for i in range(count - 1)]
    down = [(i + 1, i) for i in range(count - 1)]
    before = lax.ppermute(v[v.shape[0] - rim :], "seq", up)
    after = lax.ppermute(v[:rim], "seq", down)
    return before, after


def swap(v, axis, bit):
    count = lax.axis_size(axis)
    return lax.ppermute(v, axis, [(i, i ^ (1 << bit)) for i in range(count)])


def my_bit(axis, bit):
    return (lax.axis_index(axis) >> bit) & 1


def bits_of(count):
    return count.bit_length() - 1


def halve(v, axis, bit, dim):
    mine = my_bit(axis, bit)
    send = lax.dynamic_index_in_dim(v, 1 - mine, dim, keepdims=False)
    keep = lax.dynamic_index_in_dim(v, mine, dim, keepdims=False)
    got = swap(send, axis, bit)
    return (keep.astype(F32) + got.astype(F32)).astype(BF16)


def widen(v, axis, bit):
    got = swap(v, axis, bit)
    mine = my_bit(axis, bit) == 0
    return jnp.stack([jnp.where(mine, v, got), jnp.where(mine, got, v)])


def reduce_chunk(v, seq_first):
    shards, units, u, width = v.shape
    n = bits_of(shards)
    v = v.reshape((2,) * n + (units, 2, u // 2, width))
    v = halve(v, "dp", 0, n + 1)
    split = units % 2 == 0 and not seq_first

    def along_seq(v, n):
        for bit in range(n):
            v = halve(v, "seq", bit, n - 1 - bit)
        return v

    if split:
        v = v.reshape((2,) * n + (2, units // 2, u // 2, width))
        v = halve(v, "dp", 1, n)
        v = along_seq(v, n)
        v = widen(v, "dp", 1).reshape(units, u // 2, width)
    else:
        v = along_seq(v, n)
        v = (v.astype(F32) + swap(v, "dp", 1).astype(F32)).astype(BF16)
    v = widen(v, "dp", 0)
    return jnp.moveaxis(v, 0, 1).reshape(units, u, width).astype(F32)


def sum_everywhere(v):
    for axis in ("dp", "seq"):
        for bit in range(bits_of(lax.axis_size(axis))):
            v = v + swap(v, axis, bit)
    return v


def make_masks(bounds, taps, step):
    rows = bounds.shape[2]
    position = lax.axis_index("seq") * rows + jnp.arange(rows, dtype=jnp.int32)
    offsets = (jnp.arange(taps, dtype=jnp.int32) - taps // 2) * step
    target = position[None, :] + offsets[:, None]
    inside = (bounds[0, 0][None, :] <= target) & (target < bounds[1, 0][None, :])
    return jnp.broadcast_to(inside.astype(BF16)[:, :, None], (taps, rows, 128))


def body(
    tokens, bounds, w_in, w_mid, w_out, gain_wide, shift_wide, gain_narrow, shift_narrow,
    bias_narrow, bias_wide, cotangent,
):
    x0 = tokens[0]
    cot = cotangent[0]
    rows, width = x0.shape
    taps, inner = w_mid.shape[1], w_mid.shape[2]
    shards = lax.axis_size("seq")
    u = inner // shards
    steps = (DILATION_CLOSE, DILATION_BROAD)
    masks = [make_masks(bounds, taps, step) for step in steps]
    flat_mid = [w_mid[b].reshape(taps * inner, inner) for b in range(2)]
    vecw = [jnp.stack([gain_wide[b], shift_wide[b]]) for b in range(2)]
    vecn = [
        [jnp.stack([gain_narrow[b, i], shift_narrow[b, i], bias_narrow[b, i]]) for i in range(2)]
        for b in range(2)
    ]
    wide_bias = [bias_wide[b][None] for b in range(2)]

    f_wide, f_narrow = (rows, width), (rows, inner)
    mm = 2 * rows * width * inner
    mid = 2 * rows * taps * inner * inner
    saved_in = [
        (f_wide, BF16), (f_wide, F32), (f_wide, F32), ((rows, 128), F32),
        (f_narrow, BF16), (f_narrow, F32), (f_narrow, F32), ((rows, 128), F32),
    ]
    z_scratch = pltpu.VMEM(f_narrow, F32)
    pads = [
        pltpu.VMEM((rows + 4 * steps[0], inner), F32),
        pltpu.VMEM((rows + 4 * steps[1], inner), BF16),
    ]
    win_shape = (rows, taps * inner)

    a1_0, n1_0, d1_0, r1_0, a2_0, n2_0, d2_0, r2_0 = call(
        k_in, saved_in, (x0, w_in[0], vecw[0], vecn[0][0]), [z_scratch], mm, "k_in"
    )
    before, after = halos(a2_0, 2 * steps[0])
    (
        win_0, a3_0, n3_0, d3_0, r3_0, y0, a1_1, n1_1, d1_1, r1_1, a2_1, n2_1, d2_1, r2_1,
    ) = call(
        functools.partial(k_mid, step=steps[0]),
        [(win_shape, BF16), (f_narrow, BF16), (f_narrow, F32), (f_narrow, F32),
         ((rows, 128), F32), (f_wide, F32)] + saved_in,
        (x0, before, a2_0, after, masks[0], flat_mid[0], w_out[0], w_in[1], vecn[0][1],
         wide_bias[0], vecw[1], vecn[1][0]),
        [pads[0], z_scratch], mid + 2 * mm, "k_mid",
    )
    before, after = halos(a2_1, 2 * steps[1])
    f3_1, sum_e3_1 = call(
        k_flow, [(f_narrow, F32), ((1, width), F32)], (cot, w_out[1]), (), mm, "k_flow"
    )
    win_1, a3_1, e2_1, sums2_1 = call(
        functools.partial(k_conv, step=steps[1]),
        [(win_shape, BF16), (f_narrow, BF16), (f_narrow, BF16), ((3, inner), F32)],
        (before, a2_1, after, masks[1], flat_mid[1], vecn[1][1], f3_1),
        [pads[1], z_scratch], mid, "k_conv",
    )
    before, after = halos(e2_1, 2 * steps[1])
    (y1,) = call(k_out, [(f_wide, F32)], (y0, a3_1, w_out[1], wide_bias[1]), (), mm, "k_out")
    g_out_1, g_mid_1 = call(
        functools.partial(k_weights, shapes=(1, taps)),
        [((width, inner), BF16), ((taps, inner, inner), BF16)],
        (cot, a3_1, e2_1, win_1), (), mm + mid, "k_weights1",
    )
    e1_1, sums1_1, sums_w_1, dx_1, e3_0, sum_e3_0, e2_0, sums2_0 = call(
        functools.partial(k_back1, step=steps[1]),
        [(f_narrow, BF16), ((3, inner), F32), ((2, width), F32), (f_wide, F32), (f_wide, BF16),
         ((1, width), F32), (f_narrow, BF16), ((3, inner), F32)],
        (before, e2_1, after, masks[1], w_mid[1], w_in[1], n2_1, d2_1, r2_1, vecn[1][0],
         n1_1, d1_1, r1_1, vecw[1], cot, w_out[0], n3_0, d3_0, r3_0, vecn[0][1]),
        [pltpu.VMEM(win_shape, BF16), pads[1], z_scratch, pltpu.VMEM(f_wide, F32)],
        mid + 2 * mm, "k_back1",
    )
    before, after = halos(e2_0, 2 * steps[0])
    g_in_1, g_out_0, g_mid_0 = call(
        functools.partial(k_weights, shapes=(1, 1, taps)),
        [((width, inner), BF16), ((width, inner), BF16), ((taps, inner, inner), BF16)],
        (a1_1, e1_1, e3_0, a3_0, e2_0, win_0), (), 2 * mm + mid, "k_weights2",
    )
    e1_0, sums1_0, sums_w_0, dx_0 = call(
        functools.partial(k_back0, step=steps[0]),
        [(f_narrow, BF16), ((3, inner), F32), ((2, width), F32), (f_wide, F32)],
        (before, e2_0, after, masks[0], w_mid[0], w_in[0], n2_0, d2_0, r2_0, vecn[0][0],
         n1_0, d1_0, r1_0, vecw[0], dx_1),
        [pltpu.VMEM(win_shape, BF16), pads[0], z_scratch, pltpu.VMEM(f_wide, F32)],
        mid + mm, "k_back0",
    )
    (g_in_0,) = call(
        functools.partial(k_weights, shapes=(1,)),
        [((width, inner), BF16)], (a1_0, e1_0), (), mm, "k_weights3",
    )

    def pair(v):
        return v.reshape(shards, 2, u, inner)

    def by_shard(v):
        return jnp.swapaxes(v.reshape(v.shape[0], shards, u, inner), 0, 1)

    s_mid_1a = reduce_chunk(by_shard(g_mid_1[:4]), False)
    s_1b = reduce_chunk(jnp.concatenate([pair(g_out_1), by_shard(g_mid_1[4:])], axis=1), True)
    s_mid_0a = reduce_chunk(by_shard(g_mid_0[:4]), False)
    s_2b = reduce_chunk(
        jnp.concatenate([pair(g_out_0), by_shard(g_mid_0[4:]), pair(g_in_1)], axis=1), True
    )
    s_3 = reduce_chunk(pair(g_in_0), False)

    vec = jnp.concatenate(
        [sums2_0, sums2_1, sums1_0, sums1_1,
         sums_w_0.reshape(-1, inner), sums_w_1.reshape(-1, inner),
         sum_e3_0.reshape(-1, inner), sum_e3_1.reshape(-1, inner)]
    )
    vec = sum_everywhere(vec)
    two = width // inner
    s2_0, s2_1, s1_0, s1_1 = vec[0:3], vec[3:6], vec[6:9], vec[9:12]
    wide = vec[12:].reshape(6, two * inner)

    def shard_of(v):
        return v.reshape(-1, inner)

    grad_w_in = jnp.stack([shard_of(s_3), shard_of(s_2b[3:5])])
    grad_w_mid = jnp.stack(
        [jnp.concatenate([s_mid_0a, s_2b[2:3]]), jnp.concatenate([s_mid_1a, s_1b[2:3]])]
    ).swapaxes(2, 3)
    grad_w_out = jnp.stack([shard_of(s_2b[0:2]), shard_of(s_1b[0:2])]).swapaxes(1, 2)
    narrow = [jnp.stack([jnp.stack([s1_0[i], s2_0[i]]), jnp.stack([s1_1[i], s2_1[i]])]) for i in range(3)]
    return (
        y1[None],
        dx_0[None],
        grad_w_in,
        grad_w_mid,
        grad_w_out,
        jnp.stack([wide[0], wide[2]]),
        jnp.stack([wide[1], wide[3]]),
        narrow[0],
        narrow[1],
        narrow[2],
        jnp.stack([wide[4], wide[5]]),
    )


def solution(mesh):
    row = P("dp", "seq", None)
    return jax.shard_map(
        body,
        mesh=mesh,
        in_specs=(row, P(None, "dp", "seq")) + (P(),) * 9 + (row,),
        out_specs=(
            row,
            row,
            P(None, "seq", None),
            P(None, None, None, "seq"),
            P(None, None, "seq"),
        )
        + (P(),) * 6,
        check_vma=False,
    )
```

```python
import functools

import jax
import jax.numpy as jnp
from jax import lax
from jax.experimental import pallas as pl
from jax.experimental.pallas import tpu as pltpu
from jax.sharding import PartitionSpec as P

DILATION_CLOSE = 4
DILATION_BROAD = 128
EPS = 1e-05
F32 = jnp.float32
BF16 = jnp.bfloat16
VMEM_LIMIT = 28 * 1024 * 1024
EXP2 = -0.7213475204444817

C0 = 0.3275911 * 0.7071067811865476
POLY = tuple(0.5 * c for c in (0.254829592, -0.284496736, 1.421413741, -1.453152027, 1.061405429))
ROOT_2PI = 0.3989422804014327


def normal_parts(q):
    bell = jnp.exp2((q * EXP2) * q)
    t = pltpu.reciprocal(1.0 + C0 * jnp.abs(q), approx=True)
    h = POLY[4]
    for c in POLY[3::-1]:
        h = h * t + c
    tail = h * t * bell
    return jnp.where(q >= 0, 1.0 - tail, tail), q * bell * ROOT_2PI


def act_forward(v, gain, shift):
    c = v.shape[-1]
    mean = jnp.sum(v, axis=-1, keepdims=True) * (1.0 / c)
    centred = v - mean
    r = lax.rsqrt(jnp.sum(centred * centred, axis=-1, keepdims=True) * (1.0 / c) + EPS)
    n = centred * r
    q = n * gain + shift
    below, slope = normal_parts(q)
    return mean, r, n, q * below, below + slope


def act_backward(f, n, r, d, gain):
    c = f.shape[-1]
    p = f * d
    gp = gain * p
    first = jnp.sum(gp, axis=-1, keepdims=True) * (1.0 / c)
    second = jnp.sum(gp * n, axis=-1, keepdims=True) * (1.0 / c)
    return p, r * (gp - first - n * second)


def fold(v):
    return jnp.sum(v.reshape(v.shape[0] // 8, 8, v.shape[1]), axis=0)


def total(acc):
    return jnp.sum(acc, axis=0, keepdims=True)


def lanes(column):
    return jnp.broadcast_to(column, (column.shape[0], 128))


def strips(rows, height, step, carry=(), unroll=4):
    turns = rows // (height * unroll)

    def body(i, c):
        for j in range(unroll):
            c = step(pl.ds(pl.multiple_of((i * unroll + j) * height, height), height), c)
        return c

    return lax.fori_loop(0, turns, body, carry)


def at_base(at, base):
    return pl.ds(pl.multiple_of(at.start + base, at.size), at.size)


def dot(a, b):
    return jnp.dot(a, b, preferred_element_type=F32)


def dot_nt(a, b):
    return lax.dot_general(a, b, (((1,), (1,)), ((), ())), preferred_element_type=F32)


class Loads:
    def __init__(self, sources, targets, sems):
        self.targets = targets
        self.copies = [
            pltpu.make_async_copy(src if b is None else src.at[b], dst, sems.at[i])
            for i, ((src, b), dst) in enumerate(zip(sources, targets))
        ]
        self.waiting = set(range(len(targets)))
        for copy in self.copies:
            copy.start()

    def get(self, i):
        if i in self.waiting:
            self.waiting.remove(i)
            self.copies[i].wait()
        return self.targets[i]

    def finish(self):
        for i in sorted(self.waiting):
            self.get(i)


class Stores:
    def __init__(self, held, targets, sems):
        self.held = held
        self.copies = [
            pltpu.make_async_copy(src, dst, sems.at[i]) for i, (src, dst) in enumerate(zip(held, targets))
        ]

    def put(self, *which):
        for i in which:
            self.copies[i].start()

    def finish(self):
        for copy in self.copies:
            copy.wait()


def call(
    kernel, outs, args, scratch=(), name=None, deps=(), loads=(), stores=(), free=(), limit=VMEM_LIMIT
):
    n_args, n_loads, n_deps = len(args), len(loads), len(deps)
    n_outs, n_stores = len(outs), len(stores)
    loaded = [(a.shape if b is None else a.shape[1:], a.dtype) for a, b, _ in loads]
    kept = [i for i, (_, _, keep) in enumerate(loads) if keep]
    brief = [i for i in range(n_loads) if i not in kept]
    out_shape = [
        (jax.ShapeDtypeStruct if i in free else pltpu.VMEM)(s, t) for i, (s, t) in enumerate(outs)
    ]
    out_shape += [pltpu.HBM(s, t) for s, t in stores] + [pltpu.VMEM(*loaded[i]) for i in kept]

    def run(*refs):
        ins, rest = refs[:n_args], refs[n_args + n_loads + n_deps :]
        results, rest = rest[:n_outs], rest[n_outs:]
        stored, rest = rest[:n_stores], rest[n_stores:]
        targets = dict(zip(kept, rest[: len(kept)]))
        scr = list(rest[len(kept) :])
        more = {}
        if n_loads:
            sems = scr.pop()
            for i in reversed(brief):
                targets[i] = scr.pop()
            sources = [(r, b) for r, (_, b, _) in zip(refs[n_args : n_args + n_loads], loads)]
            more["coming"] = Loads(sources, [targets[i] for i in range(n_loads)], sems)
        if n_stores:
            sems = scr.pop()
            held = [scr.pop() for _ in stores][::-1]
            more["keeping"] = Stores(held, stored, sems)
        kernel(*ins, *results, *scr, **more)
        for part in more.values():
            part.finish()

    hbm, vmem = pl.BlockSpec(memory_space=pltpu.HBM), pl.BlockSpec(memory_space=pltpu.VMEM)
    specs = [vmem] * n_args + [hbm] * n_loads + [pl.BlockSpec(memory_space=pl.ANY)] * n_deps
    out_specs = [vmem] * n_outs + [hbm] * n_stores + [vmem] * len(kept)
    scratch = list(scratch)
    if n_stores:
        scratch += [pltpu.VMEM(s, t) for s, t in stores] + [pltpu.SemaphoreType.DMA((n_stores,))]
    if n_loads:
        scratch += [pltpu.VMEM(*loaded[i]) for i in brief] + [pltpu.SemaphoreType.DMA((n_loads,))]
    return pl.pallas_call(
        run,
        out_shape=out_shape,
        in_specs=specs,
        out_specs=out_specs,
        scratch_shapes=scratch,
        compiler_params=pltpu.CompilerParams(vmem_limit_bytes=limit),
        cost_estimate=pl.CostEstimate(flops=10**8, bytes_accessed=10**6, transcendentals=0),
        name=name,
    )(
        *[pltpu.with_memory_space_constraint(a, pltpu.VMEM) for a in args],
        *[pltpu.with_memory_space_constraint(a, pltpu.HBM) for a, _, _ in loads],
        *deps,
    )


NEAR, CUT, LOW_0, LOW_1, HIGH_1, CORE, BIT_X, BIT_Y = range(8)


def find_place(bounds, place, rows):
    seq, dp = lax.axis_index("seq"), lax.axis_index("dp")
    first = seq * rows
    marks = (bounds[1, 0:1, 0:1], bounds[0, 0:1, 0:1], bounds[0, 0:1, rows - 1 :], bounds[1, 0:1, rows - 1 :])
    for row, v in zip((CUT, LOW_0, LOW_1, HIGH_1), marks):
        place[row : row + 1] = jnp.broadcast_to(v - first, (1, 128))
    for row, v in ((NEAR, seq & 1), (CORE, dp & 1), (BIT_X, dp >> 1), (BIT_Y, seq & 1)):
        place[row : row + 1] = jnp.full((1, 128), v, jnp.int32)


def base_of(place, near, rows):
    odd = place[NEAR, 0]
    return rows * (1 - odd) if near else rows * odd


def wide_act(x, base, gain, shift, a1, d1, stat):
    def wide(at, c):
        mean, r, n, a, d = act_forward(x[at_base(at, base)].astype(F32), gain, shift)
        a1[at], d1[at] = a.astype(BF16), d.astype(BF16)
        stat[0, at], stat[1, at] = lanes(mean), lanes(r)
        return c

    strips(a1.shape[0], 32, wide)


def narrow_act(z, gain, shift, a, n, d, stat):
    def narrow(at, c):
        _, r, nn, aa, dd = act_forward(z[at], gain, shift)
        n[at], d[at], a[at] = nn.astype(BF16), dd.astype(BF16), aa.astype(BF16)
        stat[at] = lanes(r)
        return c

    strips(z.shape[0], 32, narrow)


def windows(place, near, own, other, halo, win, pad, step):
    rows, width = own.shape
    taps = win.shape[1] // width
    rim = (pad.shape[0] - rows) // 2
    pad[rim : rim + rows] = own[...].astype(pad.dtype)
    lower = place[NEAR, 0] == (1 if near else 0)

    @pl.when(lower)
    def _():
        pad[0:rim] = halo[halo.shape[0] - rim :].astype(pad.dtype)
        pad[rim + rows :] = other[0:rim].astype(pad.dtype)

    @pl.when(jnp.logical_not(lower))
    def _():
        pad[0:rim] = other[rows - rim :].astype(pad.dtype)
        pad[rim + rows :] = halo[0:rim].astype(pad.dtype)

    base = base_of(place, near, rows)
    cut, low_0, low_1, high_1 = (place[i : i + 1] for i in (CUT, LOW_0, LOW_1, HIGH_1))
    height = 64
    for i in range(0, rows, height):
        t = lax.broadcasted_iota(jnp.int32, (height, 128), 0) + (base + i)
        first = t < cut
        low = jnp.where(first, low_0, low_1)
        high = jnp.where(first, cut, high_1)
        for k in range(taps):
            offset = (k - taps // 2) * step
            m = jnp.where((t + offset >= low) & (t + offset < high), 1.0, 0.0).astype(pad.dtype)
            m = jnp.concatenate([m] * (width // 128), axis=1)
            start = rim + offset + i
            win[i : i + height, k * width : (k + 1) * width] = (
                pad[start : start + height] * m
            ).astype(BF16)


def put_edge(edge, v, place, near):
    n = edge.shape[0]
    lower = place[NEAR, 0] == (1 if near else 0)

    @pl.when(lower)
    def _():
        edge[...] = v[0:n]

    @pl.when(jnp.logical_not(lower))
    def _():
        edge[...] = v[v.shape[0] - n :]


def k_in_near(bounds, place, a2, n2, d2, r2, edge, z, *, coming, keeping):
    a1, d1, stat1 = keeping.held
    find_place(bounds, place, bounds.shape[2])
    x, gw, sw = coming.get(0), coming.get(1), coming.get(2)
    wide_act(x, base_of(place, True, a1.shape[0]), gw[0:1], sw[0:1], a1, d1, stat1)
    keeping.put(0, 1, 2)
    w_in, gn, sn, bn = (coming.get(i) for i in (3, 4, 5, 6))
    z[...] = dot(a1[...], w_in[...]) + bn[0, 0:1]
    narrow_act(z, gn[0, 0:1], sn[0, 0:1], a2, n2, d2, r2)
    put_edge(edge, a2, place, True)


def k_in_far(place, x, gw, sw, gn, sn, bn, a2, n2, d2, r2, edge, z, *, coming, keeping):
    a1, d1, stat1 = keeping.held
    wide_act(x, base_of(place, False, a1.shape[0]), gw[0:1], sw[0:1], a1, d1, stat1)
    keeping.put(0, 1, 2)
    z[...] = dot(a1[...], coming.get(0)[...]) + bn[0, 0:1]
    narrow_act(z, gn[0, 0:1], sn[0, 0:1], a2, n2, d2, r2)
    put_edge(edge, a2, place, False)


def k_mid(
    place, x, own, other, halo, w_mid, gw, sw, bw, gn, sn, bn,
    a3, r3, a2, n2, d2, r2, pad, z, *, near, step, coming, keeping,
):
    rows, width = own.shape
    win, n3, d3, y, a1, d1, stat1 = keeping.held
    windows(place, near, own, other, halo, win, pad, step)
    keeping.put(0)
    z[...] = dot(win[...], w_mid[...].reshape(win.shape[1], width)) + bn[0, 1:2]
    narrow_act(z, gn[0, 1:2], sn[0, 1:2], a3, n3, d3, r3)
    keeping.put(1, 2)
    base = base_of(place, near, rows)
    old = x[pl.ds(pl.multiple_of(base, rows), rows)].astype(F32)
    y[...] = old + dot(a3[...], coming.get(0)[...]) + bw[0:1]
    keeping.put(3)
    wide_act(y, 0, gw[1:2], sw[1:2], a1, d1, stat1)
    keeping.put(4, 5, 6)
    z[...] = dot(a1[...], coming.get(1)[...]) + bn[1, 0:1]
    narrow_act(z, gn[1, 0:1], sn[1, 0:1], a2, n2, d2, r2)


def put_wide(vec, row, acc):
    inner = vec.shape[1]
    for i in range(acc.shape[1] // inner):
        vec[row + i : row + i + 1] += total(acc[:, i * inner : (i + 1) * inner])


def k_flow(e, w_out, f, vec, *, row):
    f[...] = dot_nt(e[...], w_out[...])
    vec[...] = jnp.zeros_like(vec)

    def step(at, acc):
        return acc + fold(e[at].astype(F32))

    put_wide(vec, row, strips(e.shape[0], 32, step, jnp.zeros((8, e.shape[1]), F32)))


def k_conv(
    place, vec_in, own, other, halo, w_mid, gn, sn, bn, f, win, a3, e2, vec, pad, z, *, near, step, row
):
    rows, width = own.shape
    windows(place, near, own, other, halo, win, pad, step)
    z[...] = dot(win[...], w_mid[...].reshape(win.shape[1], width)) + bn[1, 1:2]
    gain = gn[1, 1:2]
    base = base_of(place, near, rows)

    def narrow(at, c):
        _, r, n, a, d = act_forward(z[at], gain, sn[1, 1:2])
        a3[at] = a.astype(BF16)
        p, v = act_backward(f[at_base(at, base)], n, r, d, gain)
        e = v.astype(BF16)
        e2[at] = e
        return c[0] + fold(p * n), c[1] + fold(p), c[2] + fold(e.astype(F32))

    vec[...] = vec_in[...]
    zero = jnp.zeros((8, width), F32)
    for i, acc in enumerate(strips(rows, 32, narrow, (zero,) * 3)):
        vec[row + i : row + i + 1] += total(acc)


def k_out(place, a_n, a_f, w_out, bw, y, *, coming):
    half = a_n.shape[0]
    for near, a in ((True, a_n), (False, a_f)):
        at = pl.ds(pl.multiple_of(base_of(place, near, half), half), half)
        y[at] = dot(a[...], w_out[...]) + bw[1:2]
        y[at] += coming.get(0 if near else 1)[...]


def back_narrow(f, n, d, r, gain, e_out, vec, row):
    rows, width = f.shape

    def step(at, c):
        nn = n[at].astype(F32)
        p, v = act_backward(f[at], nn, r[at][:, 0:1], d[at].astype(F32), gain)
        e = v.astype(BF16)
        e_out[at] = e
        return c[0] + fold(p * nn), c[1] + fold(p), c[2] + fold(e.astype(F32))

    zero = jnp.zeros((8, width), F32)
    for i, acc in enumerate(strips(rows, 32, step, (zero,) * 3)):
        vec[row + i : row + i + 1] += total(acc)


def back_wide(f, x, x_base, stat, d, gain, dy, dy_base, out, out_base, cast, vec, row, cast_row):
    rows, width = f.shape

    def step(at, c):
        r = stat[1, at][:, 0:1]
        n = (x[at_base(at, x_base)].astype(F32) - stat[0, at][:, 0:1]) * r
        p, v = act_backward(f[at], n, r, d[at].astype(F32), gain)
        dx = dy[at_base(at, dy_base)].astype(F32) + v
        out[at_base(at, out_base)] = dx
        sums = (c[0] + fold(p * n), c[1] + fold(p))
        if cast is not None:
            e = dx.astype(BF16)
            cast[at] = e
            sums += (c[2] + fold(e.astype(F32)),)
        return sums

    zero = jnp.zeros((8, width), F32)
    sums = strips(rows, 32, step, (zero,) * (2 if cast is None else 3), 2)
    put_wide(vec, row, sums[0])
    put_wide(vec, row + width // vec.shape[1], sums[1])
    if cast is not None:
        put_wide(vec, cast_row, sums[2])


def flow_two(win, w_mid, z):
    taps, width = w_mid.shape[0], w_mid.shape[1]
    for j in range(taps):
        part = dot_nt(win[:, j * width : (j + 1) * width], w_mid[taps - 1 - j])
        if j == 0:
            z[...] = part
        else:
            z[...] += part


def k_back1(
    place, vec_in, own, other, halo, w_mid, gw, gn, n2, d2, r2, dy, r3,
    e1, e3, e2, edge, vec, win, pad, z, f1, *, near, step, rows_of, coming, keeping,
):
    vec[...] = vec_in[...]
    windows(place, near, own, other, halo, win, pad, step)
    flow_two(win, w_mid, z)
    back_narrow(z, n2, d2, r2, gn[1, 0:1], e1, vec, rows_of[0])
    f1[...] = dot_nt(e1[...], coming.get(0)[...])
    base = base_of(place, near, own.shape[0])
    (dx,) = keeping.held
    x, d1, stat1 = (coming.get(i) for i in (1, 2, 3))
    back_wide(f1, x, 0, stat1, d1, gw[1:2], dy, base, dx, 0, e3, vec, rows_of[1], rows_of[3])
    keeping.put(0)
    z[...] = dot_nt(e3[...], coming.get(4)[...])
    back_narrow(z, coming.get(5), coming.get(6), r3, gn[0, 1:2], e2, vec, rows_of[2])
    put_edge(edge, e2, place, near)


def k_back0(
    place, vec_in, own, other, halo, w_mid, gn, n2, d2, r2, e1, vec, win, pad, z, *, near, step, row, coming
):
    vec[...] = vec_in[...]
    windows(place, near, own, other, halo, win, pad, step)
    flow_two(win, w_mid, z)
    back_narrow(z, n2, d2, r2, gn[0, 0:1], e1, vec, row)


def k_dx(place, vec_in, x, gw, e1_n, e1_f, out, vec, f1, *, row, coming):
    vec[...] = vec_in[...]
    half = e1_n.shape[0]
    for near, e1 in ((True, e1_n), (False, e1_f)):
        f1[...] = dot_nt(e1[...], coming.get(0)[...])
        d, stat, dy = (coming.get(i + (0 if near else 3)) for i in (1, 2, 3))
        base = base_of(place, near, half)
        back_wide(f1, x, base, stat, d, gw[0:1], dy, 0, out, base, None, vec, row, None)


def k_weights(place, *refs, jobs, n_outs, shards, regroup, coming=None):
    refs, outs = list(refs[:-n_outs]), refs[-n_outs:]
    inner = outs[0].shape[-1]

    def ref(i):
        return refs[i] if i < len(refs) else coming.get(i - len(refs))

    kept = {}
    for left, right, tap, places in jobs:
        if right is None:
            o, place = places[0]
            outs[o][place] = ref(left[0])[...]
            continue
        if left not in kept:
            parts = [ref(i)[...] for i in left]
            if len(left) == 1:
                half = parts[0].shape[0] // 2
                bases = [base_of(place, near, half) for near in (True, False)]
                parts = [ref(left[0])[pl.ds(pl.multiple_of(b, half), half)] for b in bases]
            kept[left] = jnp.concatenate(parts, axis=0).T
        at = slice(None) if tap is None else slice(tap * inner, (tap + 1) * inner)
        b = jnp.concatenate([ref(i)[:, at] for i in right], axis=0)
        left_t = kept[left]
        if len(places) == 1:
            o, place = places[0]
            outs[o][place] = dot(left_t, b).astype(BF16)
            continue
        if regroup:
            left_t = left_t.reshape(shards, 2, inner // shards, left_t.shape[1])
        for j, (o, place) in enumerate(places):
            if regroup:
                part = left_t[:, j].reshape(inner, left_t.shape[3])
            else:
                part = left_t[j * inner : (j + 1) * inner]
            outs[o][place] = dot(part, b).astype(BF16)


def swap(v, axis, bits):
    count = lax.axis_size(axis)
    return lax.ppermute(v, axis, [(i, i ^ bits) for i in range(count)])


def to_near(v):
    return swap(v, "seq", 1)


def to_far(v):
    count = lax.axis_size("seq")
    pairs = [(i, i + 1) for i in range(1, count - 1, 2)]
    return lax.ppermute(v, "seq", pairs + [(j, i) for i, j in pairs])


def my_bit(axis, bit):
    return (lax.axis_index(axis) >> bit) & 1


def pick(v, index, dim):
    return lax.dynamic_index_in_dim(v, index, dim, keepdims=False)


def halve(v, axis, bit, dim):
    mine = my_bit(axis, bit)
    got = swap(pick(v, 1 - mine, dim), axis, 1 << bit)
    return (pick(v, mine, dim).astype(F32) + got.astype(F32)).astype(BF16)


def quarter(v, axis, bit, dim):
    lower, upper = my_bit(axis, bit), my_bit(axis, bit + 1)

    def part(d):
        return pick(pick(v, upper ^ (d >> 1), dim), lower ^ (d & 1), dim)

    sums = part(0).astype(F32)
    for got in [swap(part(d), axis, d << bit) for d in (1, 2, 3)]:
        sums = sums + got.astype(F32)
    return sums.astype(BF16)


def widen(v, axis, bit):
    got = swap(v, axis, 1 << bit)
    mine = my_bit(axis, bit) == 0
    return jnp.stack([jnp.where(mine, v, got), jnp.where(mine, got, v)])


def plane_first(h):
    units, shards, u, width = h.shape
    n = shards.bit_length() - 1
    h = h.reshape((units,) + (2,) * n + (2, u // 2, width))
    return halve(h[:, 0], "dp", 1, n), halve(h[:, 1], "seq", 0, n - 1)


def plane_second(a, b):
    n = a.ndim - 3
    return jnp.stack([halve(a, "seq", 0, n), halve(b, "dp", 1, n)], axis=1)


def reduce_line(v):
    n = v.ndim - 3
    bit = 1
    while n >= 2:
        v = quarter(v, "seq", bit, n - 1)
        bit, n = bit + 2, n - 2
    if n == 1:
        v = halve(v, "seq", bit, 1)
    return v


def gather_rows(v):
    v = jnp.moveaxis(widen(v, "dp", 1), 0, 1).reshape(v.shape[0], -1, v.shape[2])
    return widen(v, "dp", 0).astype(F32)


def sum_everywhere(v):
    for axis in ("dp", "seq"):
        count = lax.axis_size(axis)
        for bit in range(count.bit_length() - 1):
            v = v + swap(v, axis, 1 << bit)
    return v


def body(
    tokens, bounds, w_in, w_mid, w_out, gain_wide, shift_wide, gain_narrow, shift_narrow,
    bias_narrow, bias_wide, cotangent,
):
    x0 = tokens[0]
    cot = cotangent[0]
    rows, width = x0.shape
    taps, inner = w_mid.shape[1], w_mid.shape[2]
    shards = lax.axis_size("seq")
    u = inner // shards
    two = width // inner
    half = rows // 2
    close, broad = DILATION_CLOSE, DILATION_BROAD

    wide_h, narrow_h, column = (half, width), (half, inner), ((half, 128), F32)
    win_h = ((half, taps * inner), BF16)
    act_wide = [(wide_h, BF16), (wide_h, BF16), ((2, half, 128), F32)]
    act_narrow = [(narrow_h, BF16), (narrow_h, BF16), (narrow_h, BF16), column]
    edge = ((16, inner), BF16)
    z = pltpu.VMEM(narrow_h, F32)
    f1 = pltpu.VMEM(wide_h, F32)
    win_scratch = pltpu.VMEM(*win_h)
    pad_0 = pltpu.VMEM((half + 32, inner), F32)
    pad_1 = pltpu.VMEM((half + 4 * broad, inner), BF16)
    n_narrow = 12
    vec_shape = ((n_narrow + 6 * two, inner), F32)

    def row_narrow(b, i):
        return 3 * (2 * b + i)

    def row_wide(b, i):
        return n_narrow + (3 * b + i) * two

    place, *in_n, edge_n, a1_n, d1_n, stat_n, x, gw, sw, gn, sn, bn, bw, w_mid_0 = call(
        k_in_near, [((8, 128), jnp.int32)] + act_narrow + [edge], (bounds,), [z], "k_in",
        loads=((x0, None, True), (gain_wide, None, True), (shift_wide, None, True), (w_in, 0, False),
               (gain_narrow, None, True), (shift_narrow, None, True), (bias_narrow, None, True),
               (bias_wide, None, True), (w_mid, 0, True)),
        stores=act_wide,
    )
    halo_n = to_near(edge_n)
    *in_f, edge_f, a1_f, d1_f, stat_f = call(
        k_in_far, act_narrow + [edge], (place, x, gw, sw, gn, sn, bn), [z], "k_in", (edge_n,),
        loads=((w_in, 0, False),), stores=act_wide,
    )
    halo_f = to_far(edge_f)

    def mid_call(near, own, other, halo, deps, loads):
        return call(
            functools.partial(k_mid, near=near, step=close),
            [(narrow_h, BF16), column] + act_narrow,
            (place, x, own, other, halo, w_mid_0, gw, sw, bw, gn, sn, bn),
            [pad_0, z], "k_mid", deps, ((w_out, 0, False), (w_in, 1, False)) + loads,
            stores=[win_h, (narrow_h, BF16), (narrow_h, BF16), (wide_h, F32)] + act_wide,
        )

    *mid_n, w_mid_1 = mid_call(True, in_n[0], in_f[0], halo_n, (), ((w_mid, 1, True),))
    halo_n = to_near(mid_n[2])
    *mid_f, w_out_1, cot = mid_call(
        False, in_f[0], in_n[0], halo_f, (mid_n[2],), ((w_out, 1, True), (cot, None, True))
    )
    halo_f = to_far(mid_f[2])
    f3, vec = call(
        functools.partial(k_flow, row=row_wide(1, 2)),
        [((rows, inner), F32), vec_shape], (cot, w_out_1), (), "k_flow",
    )

    def conv_call(near, vec, own, other, halo):
        return call(
            functools.partial(k_conv, near=near, step=broad, row=row_narrow(1, 1)),
            [win_h, (narrow_h, BF16), (narrow_h, BF16), vec_shape],
            (place, vec, own, other, halo, w_mid_1, gn, sn, bn, f3),
            [pad_1, z], "k_conv",
        )

    win_n, a3_n, e2_n, vec = conv_call(True, vec, mid_n[2], mid_f[2], halo_n)
    halo_n = to_near(e2_n)
    win_f, a3_f, e2_f, vec = conv_call(False, vec, mid_f[2], mid_n[2], halo_f)
    halo_f = to_far(e2_f)

    regroup = u % 16 == 0

    def grads(args, jobs, units, name, more=(), deps=(), loads=()):
        g, *rest = call(
            functools.partial(
                k_weights, jobs=jobs, n_outs=1 + len(more), shards=shards, regroup=regroup
            ),
            [((2, units, inner, inner), BF16)] + list(more), (place,) + args, (), name, deps, loads,
            free=(0,),
        )
        if not regroup:
            for _, _, tap, places in jobs:
                if len(places) == 2:
                    unit = places[0][1][1]
                    v = jnp.swapaxes(g[:, unit].reshape(shards, 2, u, inner), 0, 1)
                    g = g.at[:, unit].set(v.reshape(2, inner, inner))
        return (g.reshape(2, units, shards, u, inner), *rest)

    def at(core, unit, out=0):
        return (out, (core, unit))

    g_1, t_1 = grads(
        (cot, a3_n, a3_f, e2_n, e2_f, win_n, win_f),
        [((0,), (1, 2), None, (at(0, 0), at(1, 0)))]
        + [((3, 4), (5, 6), k, (at(k // 2, 1 + k % 2),)) for k in range(4)]
        + [((3, 4), (5, 6), 4, ((1, slice(None)),))],
        3, "k_weights1", [((inner, inner), BF16)],
    )
    h_1 = halve(g_1, "dp", 0, 0)
    (y1,) = call(
        k_out, [((rows, width), F32)], (place, a3_n, a3_f, w_out_1, bw), (), "k_out", (g_1,),
        loads=((mid_n[9], None, False), (mid_f[9], None, False)), free=(0,),
    )

    def back1_call(near, vec, own, other, halo, mid, deps):
        return call(
            functools.partial(
                k_back1, near=near, step=broad,
                rows_of=(row_narrow(1, 0), row_wide(1, 0), row_narrow(0, 1), row_wide(0, 2)),
            ),
            [(narrow_h, BF16), (wide_h, BF16), (narrow_h, BF16), edge, vec_shape],
            (place, vec, own, other, halo, w_mid_1, gw, gn, mid[3], mid[4], mid[5], cot, mid[1]),
            [win_scratch, pad_1, z, f1], "k_back1", deps, stores=[(wide_h, F32)],
            loads=((w_in, 1, False), (mid[9], None, False), (mid[11], None, False),
                   (mid[12], None, False), (w_out, 0, False), (mid[7], None, False),
                   (mid[8], None, False)),
        )

    e1_n, e3_n, e2_n0, edge_n, vec, dx_n = back1_call(True, vec, e2_n, e2_f, halo_n, mid_n, (y1, h_1))
    halo_n = to_near(edge_n)
    pa_1, pb_1 = plane_first(h_1)
    e1_f, e3_f, e2_f0, edge_f, vec, dx_f = back1_call(False, vec, e2_f, e2_n, halo_f, mid_f, ())
    halo_f = to_far(edge_f)

    g_2, w_mid_0 = grads(
        (mid_n[0], mid_f[0], e1_n, e1_f, e3_n, e3_f, e2_n0, e2_f0, t_1),
        [((4, 5), (0, 1), None, (at(0, 1), at(1, 1))), ((9, 10), (2, 3), None, (at(0, 0), at(1, 0)))]
        + [((6, 7), (11, 12), k, (at(k // 2, 2 + k % 2),)) for k in range(4)]
        + [((6, 7), (11, 12), 4, (at(1, 4),)), ((8,), None, None, (at(0, 4),))],
        5, "k_weights2", deps=(pa_1, pb_1),
        loads=((mid_n[10], None, False), (mid_f[10], None, False), (mid_n[6], None, False),
               (mid_f[6], None, False), (w_mid, 0, True)),
    )
    h_2 = halve(g_2, "dp", 0, 0)
    q_1 = plane_second(pa_1, pb_1)

    def back0_call(near, vec, own, other, halo, saved, deps, load):
        return call(
            functools.partial(k_back0, near=near, step=close, row=row_narrow(0, 0)),
            [(narrow_h, BF16), vec_shape],
            (place, vec, own, other, halo, w_mid_0, gn, saved[1], saved[2], saved[3]),
            [win_scratch, pad_0, z], "k_back0", deps, loads=((load, None, True),),
        )

    e1_n0, vec, a1_n = back0_call(True, vec, e2_n0, e2_f0, halo_n, in_n, (g_2,), a1_n)
    e1_f0, vec, a1_f = back0_call(False, vec, e2_f0, e2_n0, halo_f, in_f, (h_2, q_1), a1_f)
    pa_2, pb_2 = plane_first(h_2)
    (g_3,) = grads(
        (a1_n, a1_f, e1_n0, e1_f0),
        [((0, 1), (2, 3), None, (at(0, 0), at(1, 0)))], 1, "k_weights3",
    )
    h_3 = halve(g_3, "dp", 0, 0)
    dx, vec = call(
        functools.partial(k_dx, row=row_wide(0, 0)), [((rows, width), F32), vec_shape],
        (place, vec, x, gw, e1_n0, e1_f0), [f1], "k_dx", (g_3,), free=(0, 1),
        loads=((w_in, 0, False), (d1_n, None, False), (stat_n, None, False), (dx_n, None, False),
               (d1_f, None, False), (stat_f, None, False), (dx_f, None, False)),
    )
    vec = sum_everywhere(vec)

    p_1 = reduce_line(q_1)
    p_2 = reduce_line(plane_second(pa_2, pb_2))
    p_3 = reduce_line(plane_second(*plane_first(h_3)))
    s_1, s_2, s_3 = gather_rows(p_1), gather_rows(p_2), gather_rows(p_3)

    def rows_of(v):
        return v.reshape(2 * u, inner)

    grad_w_in = jnp.stack([rows_of(s_3[:, 0]), rows_of(s_2[:, 0])])
    grad_w_mid = jnp.stack(
        [
            jnp.concatenate([s_2[0, 2:4], s_2[1, 2:5]]),
            jnp.concatenate([s_1[0, 1:3], s_1[1, 1:3], s_2[0, 4:5]]),
        ]
    ).swapaxes(2, 3)
    grad_w_out = jnp.stack([rows_of(s_2[:, 1]), rows_of(s_1[:, 0])]).swapaxes(1, 2)
    narrow = vec[:n_narrow].reshape(2, 2, 3, inner)
    wide = vec[n_narrow:].reshape(2, 3, width)
    return (
        y1[None],
        dx[None],
        grad_w_in,
        grad_w_mid,
        grad_w_out,
        wide[:, 0],
        wide[:, 1],
        narrow[:, :, 0],
        narrow[:, :, 1],
        narrow[:, :, 2],
        wide[:, 2],
    )


def solution(mesh):
    row = P("dp", "seq", None)
    return jax.shard_map(
        body,
        mesh=mesh,
        in_specs=(row, P(None, "dp", "seq")) + (P(),) * 9 + (row,),
        out_specs=(
            row,
            row,
            P(None, "seq", None),
            P(None, None, None, "seq"),
            P(None, None, "seq"),
        )
        + (P(),) * 6,
        check_vma=False,
    )
```

```python
import functools

import jax
import jax.numpy as jnp
from jax import lax
from jax.experimental import pallas as pl
from jax.experimental.pallas import tpu as pltpu
from jax.sharding import PartitionSpec as P

DILATION_CLOSE = 4
DILATION_BROAD = 128
EPS = 1e-05
F32 = jnp.float32
BF16 = jnp.bfloat16
VMEM_LIMIT = 16 * 1024 * 1024
EXP2 = -0.7213475204444817

C0 = 0.3275911 * 0.7071067811865476
POLY = tuple(0.5 * c for c in (0.254829592, -0.284496736, 1.421413741, -1.453152027, 1.061405429))
ROOT_2PI = 0.3989422804014327


def normal_parts(q):
    bell = jnp.exp2((q * EXP2) * q)
    t = pltpu.reciprocal(1.0 + C0 * jnp.abs(q), approx=True)
    h = POLY[4]
    for c in POLY[3::-1]:
        h = h * t + c
    tail = h * t * bell
    return jnp.where(q >= 0, 1.0 - tail, tail), q * bell * ROOT_2PI


def act_forward(v, gain, shift):
    c = v.shape[-1]
    mean = jnp.sum(v, axis=-1, keepdims=True) * (1.0 / c)
    centred = v - mean
    r = lax.rsqrt(jnp.sum(centred * centred, axis=-1, keepdims=True) * (1.0 / c) + EPS)
    n = centred * r
    q = n * gain + shift
    below, slope = normal_parts(q)
    return mean, r, n, q * below, below + slope


def act_backward(f, n, r, d, gain):
    c = f.shape[-1]
    p = f * d
    gp = gain * p
    first = jnp.sum(gp, axis=-1, keepdims=True) * (1.0 / c)
    second = jnp.sum(gp * n, axis=-1, keepdims=True) * (1.0 / c)
    return p, r * (gp - first - n * second)


def fold(v):
    return jnp.sum(v.reshape(v.shape[0] // 8, 8, v.shape[1]), axis=0)


def total(acc):
    return jnp.sum(acc, axis=0, keepdims=True)


def lanes(column):
    return jnp.broadcast_to(column, (column.shape[0], 128))


def strips(rows, height, step, carry=(), unroll=4):
    turns = rows // (height * unroll)

    def body(i, c):
        for j in range(unroll):
            c = step(pl.ds(pl.multiple_of((i * unroll + j) * height, height), height), c)
        return c

    return lax.fori_loop(0, turns, body, carry)


def at_base(at, base):
    return pl.ds(pl.multiple_of(at.start + base, at.size), at.size)


def dot(a, b):
    return jnp.dot(a, b, preferred_element_type=F32)


def dot_nt(a, b):
    return lax.dot_general(a, b, (((1,), (1,)), ((), ())), preferred_element_type=F32)


class Loads:
    def __init__(self, sources, targets, sems):
        self.targets = targets
        self.copies = [
            pltpu.make_async_copy(src if b is None else src.at[b], dst, sems.at[i])
            for i, ((src, b), dst) in enumerate(zip(sources, targets))
        ]
        self.waiting = set(range(len(targets)))
        for copy in self.copies:
            copy.start()

    def get(self, i):
        if i in self.waiting:
            self.waiting.remove(i)
            self.copies[i].wait()
        return self.targets[i]

    def finish(self):
        for i in sorted(self.waiting):
            self.get(i)


class Stores:
    def __init__(self, held, targets, sems):
        self.held, self.targets, self.sems = held, targets, sems
        self.copies = []

    def put(self, *which, at=None):
        for i in which:
            src, dst = self.held[i], self.targets[i]
            if at is not None:
                src, dst = src.at[at], dst.at[at]
            copy = pltpu.make_async_copy(src, dst, self.sems.at[len(self.copies)])
            copy.start()
            self.copies.append(copy)

    def finish(self):
        for copy in self.copies:
            copy.wait()


def call(
    kernel, outs, args, scratch=(), name=None, deps=(), loads=(), stores=(), offloads=(), parts=1,
    limit=VMEM_LIMIT, cost=0,
):
    n_args, n_loads, n_deps, n_off = len(args), len(loads), len(deps), len(offloads)
    n_outs, n_stores = len(outs), len(stores)
    loaded = [(a.shape if b is None else a.shape[1:], a.dtype) for a, b, _ in loads]
    kept = [i for i, (_, _, keep) in enumerate(loads) if keep]
    brief = [i for i in range(n_loads) if i not in kept]
    out_shape = [pltpu.VMEM(s, t) for s, t in outs] + [pltpu.HBM(s, t) for s, t in stores]
    out_shape += [pltpu.VMEM(*loaded[i]) for i in kept]
    out_shape += [pltpu.HBM(a.shape, a.dtype) for a in offloads]

    def run(*refs):
        def take(n):
            nonlocal refs
            first, refs = refs[:n], refs[n:]
            return first

        ins, going, sources, _ = take(n_args), take(n_off), take(n_loads), take(n_deps)
        results, stored, held, gone = take(n_outs), take(n_stores), take(len(kept)), take(n_off)
        targets = dict(zip(kept, held))
        scr = list(refs)
        more = {}
        if n_loads:
            sems = scr.pop()
            for i in reversed(brief):
                targets[i] = scr.pop()
            sources = [(r, b) for r, (_, b, _) in zip(sources, loads)]
            more["coming"] = Loads(sources, [targets[i] for i in range(n_loads)], sems)
        if n_off:
            leaving = Stores(going, gone, scr.pop())
            leaving.put(*range(n_off))
        if n_stores:
            sems = scr.pop()
            held = [scr.pop() for _ in stores][::-1]
            more["keeping"] = Stores(held, stored, sems)
        kernel(*ins, *results, *scr, **more)
        for part in more.values():
            part.finish()
        if n_off:
            leaving.finish()

    hbm, vmem = pl.BlockSpec(memory_space=pltpu.HBM), pl.BlockSpec(memory_space=pltpu.VMEM)
    specs = [vmem] * (n_args + n_off) + [hbm] * n_loads
    specs += [pl.BlockSpec(memory_space=pl.ANY)] * n_deps
    out_specs = [vmem] * n_outs + [hbm] * n_stores + [vmem] * len(kept) + [hbm] * n_off
    scratch = list(scratch)
    if n_stores:
        scratch += [pltpu.VMEM(s, t) for s, t in stores]
        scratch += [pltpu.SemaphoreType.DMA((n_stores * parts,))]
    if n_off:
        scratch += [pltpu.SemaphoreType.DMA((n_off,))]
    if n_loads:
        scratch += [pltpu.VMEM(*loaded[i]) for i in brief] + [pltpu.SemaphoreType.DMA((n_loads,))]
    return pl.pallas_call(
        run,
        out_shape=out_shape,
        in_specs=specs,
        out_specs=out_specs,
        scratch_shapes=scratch,
        compiler_params=pltpu.CompilerParams(vmem_limit_bytes=limit),
        cost_estimate=pl.CostEstimate(flops=1 + int(cost * 1.15e9), bytes_accessed=1, transcendentals=0),
        name=name,
    )(
        *[pltpu.with_memory_space_constraint(a, pltpu.VMEM) for a in (*args, *offloads)],
        *[pltpu.with_memory_space_constraint(a, pltpu.HBM) for a, _, _ in loads],
        *deps,
    )


NEAR, CUT, LOW_0, LOW_1, HIGH_1, CORE, BIT_X, LINE = range(8)


def find_place(bounds, place, rows):
    seq, dp = lax.axis_index("seq"), lax.axis_index("dp")
    first = seq * rows
    marks = (bounds[1, 0:1, 0:1], bounds[0, 0:1, 0:1], bounds[0, 0:1, rows - 1 :], bounds[1, 0:1, rows - 1 :])
    for row, v in zip((CUT, LOW_0, LOW_1, HIGH_1), marks):
        place[row : row + 1] = jnp.broadcast_to(v - first, (1, 128))
    for row, v in ((NEAR, seq & 1), (CORE, dp & 1), (BIT_X, dp >> 1), (LINE, seq >> 1)):
        place[row : row + 1] = jnp.full((1, 128), v, jnp.int32)


def base_of(place, near, rows):
    odd = place[NEAR, 0]
    return rows * (1 - odd) if near else rows * odd


def wide_act(x, base, gain, shift, a1, d1, stat):
    def wide(at, c):
        mean, r, n, a, d = act_forward(x[at_base(at, base)].astype(F32), gain, shift)
        a1[at], d1[at] = a.astype(BF16), d.astype(BF16)
        stat[0, at], stat[1, at] = lanes(mean), lanes(r)
        return c

    strips(a1.shape[0], 32, wide)


def narrow_act(z, gain, shift, a, n, d, stat):
    def narrow(at, c):
        _, r, nn, aa, dd = act_forward(z[at], gain, shift)
        n[at], d[at], a[at] = nn.astype(BF16), dd.astype(BF16), aa.astype(BF16)
        stat[at] = lanes(r)
        return c

    strips(z.shape[0], 32, narrow)


def windows(place, near, own, other, halo, win, pad, step):
    rows, width = own.shape
    taps = win.shape[1] // width
    rim = (pad.shape[0] - rows) // 2
    pad[rim : rim + rows] = own[...].astype(pad.dtype)
    lower = place[NEAR, 0] == (1 if near else 0)

    @pl.when(lower)
    def _():
        pad[0:rim] = halo[halo.shape[0] - rim :].astype(pad.dtype)
        pad[rim + rows :] = other[0:rim].astype(pad.dtype)

    @pl.when(jnp.logical_not(lower))
    def _():
        pad[0:rim] = other[rows - rim :].astype(pad.dtype)
        pad[rim + rows :] = halo[0:rim].astype(pad.dtype)

    base = base_of(place, near, rows)
    cut, low_0, low_1, high_1 = (place[i : i + 1] for i in (CUT, LOW_0, LOW_1, HIGH_1))
    height = 64
    for i in range(0, rows, height):
        t = lax.broadcasted_iota(jnp.int32, (height, 128), 0) + (base + i)
        first = t < cut
        low = jnp.where(first, low_0, low_1)
        high = jnp.where(first, cut, high_1)
        for k in range(taps):
            offset = (k - taps // 2) * step
            m = jnp.where((t + offset >= low) & (t + offset < high), 1.0, 0.0).astype(pad.dtype)
            m = jnp.concatenate([m] * (width // 128), axis=1)
            start = rim + offset + i
            win[i : i + height, k * width : (k + 1) * width] = (
                pad[start : start + height] * m
            ).astype(BF16)


def put_edge(edge, v, place, near):
    n = edge.shape[0]
    lower = place[NEAR, 0] == (1 if near else 0)

    @pl.when(lower)
    def _():
        edge[...] = v[0:n]

    @pl.when(jnp.logical_not(lower))
    def _():
        edge[...] = v[v.shape[0] - n :]


def k_in_near(bounds, place, a2, n2, d2, r2, edge, z, *, coming, keeping):
    a1, d1, stat1 = keeping.held
    find_place(bounds, place, bounds.shape[2])
    x, gw, sw = coming.get(0), coming.get(1), coming.get(2)
    wide_act(x, base_of(place, True, a1.shape[0]), gw[0:1], sw[0:1], a1, d1, stat1)
    keeping.put(0, 1, 2)
    w_in, gn, sn, bn = (coming.get(i) for i in (3, 4, 5, 6))
    z[...] = dot(a1[...], w_in[...]) + bn[0, 0:1]
    narrow_act(z, gn[0, 0:1], sn[0, 0:1], a2, n2, d2, r2)
    put_edge(edge, a2, place, True)


def k_in_far(place, x, gw, sw, gn, sn, bn, a2, n2, d2, r2, edge, z, *, coming, keeping):
    a1, d1, stat1 = keeping.held
    wide_act(x, base_of(place, False, a1.shape[0]), gw[0:1], sw[0:1], a1, d1, stat1)
    keeping.put(0, 1, 2)
    z[...] = dot(a1[...], coming.get(0)[...]) + bn[0, 0:1]
    narrow_act(z, gn[0, 0:1], sn[0, 0:1], a2, n2, d2, r2)
    put_edge(edge, a2, place, False)


def k_mid(
    place, x, own, other, halo, w_mid, gw, sw, bw, gn, sn, bn,
    a3, r3, a2, n2, d2, r2, pad, z, *, near, step, coming, keeping,
):
    rows, width = own.shape
    win, n3, d3, y, a1, d1, stat1 = keeping.held
    windows(place, near, own, other, halo, win, pad, step)
    keeping.put(0)
    z[...] = dot(win[...], w_mid[...].reshape(win.shape[1], width)) + bn[0, 1:2]
    narrow_act(z, gn[0, 1:2], sn[0, 1:2], a3, n3, d3, r3)
    keeping.put(1, 2)
    base = base_of(place, near, rows)
    old = x[pl.ds(pl.multiple_of(base, rows), rows)].astype(F32)
    y[...] = old + dot(a3[...], coming.get(0)[...]) + bw[0:1]
    keeping.put(3)
    wide_act(y, 0, gw[1:2], sw[1:2], a1, d1, stat1)
    keeping.put(4, 5, 6)
    z[...] = dot(a1[...], coming.get(1)[...]) + bn[1, 0:1]
    narrow_act(z, gn[1, 0:1], sn[1, 0:1], a2, n2, d2, r2)


def put_wide(vec, row, acc):
    inner = vec.shape[1]
    for i in range(acc.shape[1] // inner):
        vec[row + i : row + i + 1] += total(acc[:, i * inner : (i + 1) * inner])


def k_flow(e, w_out, f, vec, *, row, coming):
    f[...] = dot_nt(e[...], w_out[...])
    vec[...] = jnp.zeros_like(vec)

    def step(at, acc):
        return acc + fold(e[at].astype(F32))

    put_wide(vec, row, strips(e.shape[0], 32, step, jnp.zeros((8, e.shape[1]), F32)))


def k_conv(
    place, vec_in, own, other, halo, w_mid, gn, sn, bn, f, a3, e2, vec, pad, z, *, near, step, row, keeping
):
    rows, width = own.shape
    (win,) = keeping.held
    windows(place, near, own, other, halo, win, pad, step)
    keeping.put(0)
    z[...] = dot(win[...], w_mid[...].reshape(win.shape[1], width)) + bn[1, 1:2]
    gain = gn[1, 1:2]
    base = base_of(place, near, rows)

    def narrow(at, c):
        _, r, n, a, d = act_forward(z[at], gain, sn[1, 1:2])
        a3[at] = a.astype(BF16)
        p, v = act_backward(f[at_base(at, base)], n, r, d, gain)
        e = v.astype(BF16)
        e2[at] = e
        return c[0] + fold(p * n), c[1] + fold(p), c[2] + fold(e.astype(F32))

    vec[...] = vec_in[...]
    zero = jnp.zeros((8, width), F32)
    for i, acc in enumerate(strips(rows, 32, narrow, (zero,) * 3)):
        vec[row + i : row + i + 1] += total(acc)


def k_out(place, a_n, a_f, bw, *, coming, keeping):
    half = a_n.shape[0]
    (y,) = keeping.held
    w_out = coming.get(0)
    for near, a in ((True, a_n), (False, a_f)):
        at = pl.ds(pl.multiple_of(base_of(place, near, half), half), half)
        y[at] = dot(a[...], w_out[...]) + bw[1:2] + coming.get(1 if near else 2)[...]
        keeping.put(0, at=at)


def back_narrow(f, n, d, r, gain, e_out, vec, row):
    rows, width = f.shape

    def step(at, c):
        nn = n[at].astype(F32)
        p, v = act_backward(f[at], nn, r[at][:, 0:1], d[at].astype(F32), gain)
        e = v.astype(BF16)
        e_out[at] = e
        return c[0] + fold(p * nn), c[1] + fold(p), c[2] + fold(e.astype(F32))

    zero = jnp.zeros((8, width), F32)
    for i, acc in enumerate(strips(rows, 32, step, (zero,) * 3)):
        vec[row + i : row + i + 1] += total(acc)


def back_wide(f, x, x_base, stat, d, gain, dy, dy_base, out, out_base, cast, vec, row, cast_row):
    rows, width = f.shape

    def step(at, c):
        r = stat[1, at][:, 0:1]
        n = (x[at_base(at, x_base)].astype(F32) - stat[0, at][:, 0:1]) * r
        p, v = act_backward(f[at], n, r, d[at].astype(F32), gain)
        dx = dy[at_base(at, dy_base)].astype(F32) + v
        out[at_base(at, out_base)] = dx
        sums = (c[0] + fold(p * n), c[1] + fold(p))
        if cast is not None:
            e = dx.astype(BF16)
            cast[at] = e
            sums += (c[2] + fold(e.astype(F32)),)
        return sums

    zero = jnp.zeros((8, width), F32)
    sums = strips(rows, 32, step, (zero,) * (2 if cast is None else 3), 2)
    put_wide(vec, row, sums[0])
    put_wide(vec, row + width // vec.shape[1], sums[1])
    if cast is not None:
        put_wide(vec, cast_row, sums[2])


def flow_two(win, w_mid, z):
    taps, width = w_mid.shape[0], w_mid.shape[1]
    for j in range(taps):
        part = dot_nt(win[:, j * width : (j + 1) * width], w_mid[taps - 1 - j])
        if j == 0:
            z[...] = part
        else:
            z[...] += part


def k_back1(
    place, vec_in, own, other, halo, w_mid, gw, gn,
    e1, e3, e2, edge, vec, win, pad, z, f1, *, near, step, rows_of, coming, keeping,
):
    vec[...] = vec_in[...]
    windows(place, near, own, other, halo, win, pad, step)
    flow_two(win, w_mid, z)
    n2, d2, r2, w_in = (coming.get(i) for i in range(4))
    back_narrow(z, n2, d2, r2, gn[1, 0:1], e1, vec, rows_of[0])
    f1[...] = dot_nt(e1[...], w_in[...])
    base = base_of(place, near, own.shape[0])
    (dx,) = keeping.held
    x, d1, stat1, dy = (coming.get(i) for i in range(4, 8))
    back_wide(f1, x, 0, stat1, d1, gw[1:2], dy, base, dx, 0, e3, vec, rows_of[1], rows_of[3])
    keeping.put(0)
    w_out, n3, d3, r3 = (coming.get(i) for i in range(8, 12))
    z[...] = dot_nt(e3[...], w_out[...])
    back_narrow(z, n3, d3, r3, gn[0, 1:2], e2, vec, rows_of[2])
    put_edge(edge, e2, place, near)


def k_back0(
    place, vec_in, own, other, halo, gn, *rest, near, step, row, coming
):
    *w_mid, e1, vec, win, pad, z = rest
    vec[...] = vec_in[...]
    windows(place, near, own, other, halo, win, pad, step)
    flow_two(win, w_mid[0] if w_mid else coming.get(3), z)
    n2, d2, r2 = (coming.get(i) for i in range(3))
    back_narrow(z, n2, d2, r2, gn[0, 0:1], e1, vec, row)


def k_dx(place, vec_in, gw, e1_n, e1_f, vec, f1, *, row, coming, keeping):
    vec[...] = vec_in[...]
    half = e1_n.shape[0]
    (out,) = keeping.held
    w_in, x = coming.get(0), coming.get(1)
    for near, e1 in ((True, e1_n), (False, e1_f)):
        f1[...] = dot_nt(e1[...], w_in[...])
        d, stat, dy = (coming.get(i + (0 if near else 3)) for i in (2, 3, 4))
        base = base_of(place, near, half)
        back_wide(f1, x, base, stat, d, gw[0:1], dy, 0, out, base, None, vec, row, None)
        keeping.put(0, at=pl.ds(pl.multiple_of(base, half), half))


def k_split(place, *refs, jobs, side, coming=None):
    outs, turned = refs[-1 - len(jobs) : -1], refs[-1]
    refs = refs[: -1 - len(jobs)]
    _, shards, _, u, rows = turned.shape
    inner = outs[0].shape[-1]

    def ref(i):
        return refs[i] if i < len(refs) else coming.get(i - len(refs))

    def whole(places, at=slice(None)):
        if len(places) == 1:
            half = rows // 2
            bases = [base_of(place, near, half) for near in (True, False)]
            parts = [ref(places[0])[pl.ds(pl.multiple_of(b, half), half)] for b in bases]
        else:
            parts = [ref(i)[:, at] for i in places]
        return jnp.concatenate(parts, axis=0)

    core = place[CORE, 0] ^ side
    kept = {}
    halves = 0
    for out, (kind, left, right, j) in zip(outs, jobs):
        if kind == "half":
            turned[halves] = whole(left).T.reshape(turned.shape[1:])
            part = turned[halves, :, core].reshape(shards * u, rows)
            out[...] = dot(part, whole(right)).astype(BF16)
            halves += 1
            continue
        if left not in kept:
            kept[left] = whole(left).T
        if kind == "taps":
            at = pl.ds(pl.multiple_of((j + 2 * core) * inner, 128), inner)
            out[...] = dot(kept[left], whole(right, at)).astype(BF16)
            continue
        tap, before = j

        @pl.when(core == 0)
        def _():
            out[...] = ref(before)[...]

        @pl.when(core != 0)
        def _():
            at = slice(tap * inner, (tap + 1) * inner)
            out[...] = dot(kept[left], whole(right, at)).astype(BF16)


def k_tap(e_n, e_f, win_n, win_f, out, *, tap):
    inner = out.shape[-1]
    at = slice(tap * inner, (tap + 1) * inner)
    left = jnp.concatenate([e_n[...], e_f[...]], axis=0).T
    right = jnp.concatenate([win_n[:, at], win_f[:, at]], axis=0)
    out[...] = dot(left, right).astype(BF16)


def added(*parts):
    first, *rest = [p.astype(F32) for p in parts]
    for p in rest:
        first = first + p
    return first


def k_first(place, *refs, n_pairs, n_units):
    ins, outs = list(refs[: 4 * n_pairs + 2 * n_units]), list(refs[4 * n_pairs + 2 * n_units :])
    x, y = place[BIT_X, 0], place[NEAR, 0]

    def add_rows(a, b, out):
        def step(k, c):
            at = pl.ds(pl.multiple_of(k * 80, 80), 80)
            out[at] = added(a[at], b[at]).astype(BF16)
            return c

        lax.fori_loop(0, a.shape[0] // 80, step, 0)

    for _ in range(n_pairs):
        (a0, b0, a1, b1), (send, stay) = ins[:4], outs[:2]
        ins, outs = ins[4:], outs[2:]

        @pl.when(x == 0)
        def _():
            add_rows(a1, b1, send)
            add_rows(a0, b0, stay)

        @pl.when(x != 0)
        def _():
            add_rows(a0, b0, send)
            add_rows(a1, b1, stay)

    for _ in range(n_units):
        (a, b), (send, stay) = ins[:2], outs[:2]
        ins, outs = ins[2:], outs[2:]
        for out, side in ((send, 1 - y), (stay, y)):

            def step(k, c):
                out[k] = added(a[k, side], b[k, side]).astype(BF16)
                return c

            lax.fori_loop(0, 4, step, 0)


def k_second(place, a, b, send, stay):
    mine = place[NEAR, 0]
    for out, side in ((send, 1 - mine), (stay, mine)):

        def step(k, c):
            out[k] = added(a[k, side], b[k, side]).astype(BF16)
            return c

        lax.fori_loop(0, 4, step, 0)


def k_line(place, *refs, count):
    line = place[LINE, 0]
    for d in range(4):
        for i in range(count):
            a, b = refs[2 * i], refs[2 * i + 1]
            refs[2 * count + d][i] = added(a[line ^ d], b[line ^ d]).astype(BF16)


def k_sum(place, *refs, count):
    out = refs[-1]
    at = 0
    for i in range(count):
        parts = refs[4 * i : 4 * i + 4]
        for k in range(parts[0].shape[0]):
            out[at] = added(*[p[k] for p in parts]).astype(BF16)
            at += 1


def k_rows(place, mine, got, out, *, split):
    x = place[BIT_X, 0]
    at = 0
    for k in range(mine.shape[0]):
        if k in split:
            out[at + x], out[at + 1 - x] = mine[k], got[k]
            at += 2
        else:
            out[at] = added(mine[k], got[k]).astype(BF16)
            at += 1


def k_cores(place, mine, got, out):
    core = place[CORE, 0]
    out[core], out[1 - core] = mine[...].astype(F32), got[...].astype(F32)


def k_add(a, b, out):
    out[...] = a[...] + b[...]


def swap(v, axis, bits):
    count = lax.axis_size(axis)
    return lax.ppermute(v, axis, [(i, i ^ bits) for i in range(count)])


def to_near(v):
    return swap(v, "seq", 1)


def to_far(v):
    count = lax.axis_size("seq")
    pairs = [(i, i + 1) for i in range(1, count - 1, 2)]
    return lax.ppermute(v, "seq", pairs + [(j, i) for i, j in pairs])


def dot_tn(a, b):
    return lax.dot_general(a, b, (((0,), (0,)), ((), ())), preferred_element_type=F32)


def plain_weights(a1, e1, win, e2, a3, e3):
    taps = win.shape[1] // e2.shape[1]
    grad_mid = dot_tn(win, e2).reshape(taps, e2.shape[1], e2.shape[1])
    shares = (
        lax.psum_scatter(dot_tn(a1, e1), "seq", scatter_dimension=0, tiled=True),
        lax.psum_scatter(grad_mid, "seq", scatter_dimension=2, tiled=True),
        lax.psum_scatter(dot_tn(a3, e3), "seq", scatter_dimension=1, tiled=True),
    )
    return [lax.psum(v.astype(BF16), "dp").astype(F32) for v in shares]


def body(
    tokens, bounds, w_in, w_mid, w_out, gain_wide, shift_wide, gain_narrow, shift_narrow,
    bias_narrow, bias_wide, cotangent,
):
    x0 = tokens[0]
    cot = cotangent[0]
    rows, width = x0.shape
    taps, inner = w_mid.shape[1], w_mid.shape[2]
    shards = lax.axis_size("seq")
    u = inner // shards
    two = width // inner
    half = rows // 2
    close, broad = DILATION_CLOSE, DILATION_BROAD

    wide_h, narrow_h, column = (half, width), (half, inner), ((half, 128), F32)
    win_h = ((half, taps * inner), BF16)
    act_wide = [(wide_h, BF16), (wide_h, BF16), ((2, half, 128), F32)]
    act_narrow = [(narrow_h, BF16), (narrow_h, BF16), (narrow_h, BF16), column]
    edge = ((16, inner), BF16)
    z = pltpu.VMEM(narrow_h, F32)
    f1 = pltpu.VMEM(wide_h, F32)
    win_scratch = pltpu.VMEM(*win_h)
    pad_0 = pltpu.VMEM((half + 32, inner), F32)
    pad_1 = pltpu.VMEM((half + 4 * broad, inner), BF16)
    n_narrow = 12
    vec_shape = ((n_narrow + 6 * two, inner), F32)

    def row_narrow(b, i):
        return 3 * (2 * b + i)

    def row_wide(b, i):
        return n_narrow + (3 * b + i) * two

    def brief(*arrays):
        return tuple((a, None, False) for a in arrays)

    place, a2_n, *p_n, edge_n, a1_n, d1_n, stat_n, x, gw, sw, gn, sn, bn, bw, w_mid_0 = call(
        k_in_near, [((8, 128), jnp.int32)] + act_narrow + [edge], (bounds,), [z], "k_in",
        loads=((x0, None, True), (gain_wide, None, True), (shift_wide, None, True), (w_in, 0, False),
               (gain_narrow, None, True), (shift_narrow, None, True), (bias_narrow, None, True),
               (bias_wide, None, True), (w_mid, 0, True)),
        stores=act_wide,
    )
    halo_n = to_near(edge_n)
    a2_f, *p_f, edge_f, a1_f, d1_f, stat_f, p1, p2, p3 = call(
        k_in_far, act_narrow + [edge], (place, x, gw, sw, gn, sn, bn), [z], "k_in", (edge_n,),
        loads=((w_in, 0, False),), stores=act_wide, offloads=p_n,
    )
    p_n = (p1, p2, p3)
    halo_f = to_far(edge_f)

    def mid_call(near, own, other, halo, deps, loads, offloads):
        return call(
            functools.partial(k_mid, near=near, step=close),
            [(narrow_h, BF16), column] + act_narrow,
            (place, x, own, other, halo, w_mid_0, gw, sw, bw, gn, sn, bn),
            [pad_0, z], "k_mid", deps, ((w_out, 0, False), (w_in, 1, False)) + loads,
            [win_h, (narrow_h, BF16), (narrow_h, BF16), (wide_h, F32)] + act_wide, offloads,
        )

    a3_n, r3_n, b2_n, *q_n = mid_call(True, a2_n, a2_f, halo_n, (), (), p_f)
    s_n, p_f = q_n[3:10], q_n[10:]
    halo_n = to_near(b2_n)
    a3_f, r3_f, b2_f, *q_f = mid_call(
        False, a2_f, a2_n, halo_f, (b2_n,), ((w_out, 1, True), (cot, None, True)),
        (a3_n, r3_n, *q_n[:3]),
    )
    s_f, (w_out_1, cot_v), q_n = q_f[3:10], q_f[10:12], q_f[12:]
    halo_f = to_far(b2_f)
    f3, vec, w_mid_1, *q_f = call(
        functools.partial(k_flow, row=row_wide(1, 2)),
        [((rows, inner), F32), vec_shape], (cot_v, w_out_1), (), "k_flow",
        loads=((w_mid, 1, True),), offloads=(a3_f, r3_f, *q_f[:3]),
    )

    def conv_call(near, vec, own, other, halo):
        return call(
            functools.partial(k_conv, near=near, step=broad, row=row_narrow(1, 1)),
            [(narrow_h, BF16), (narrow_h, BF16), vec_shape],
            (place, vec, own, other, halo, w_mid_1, gn, sn, bn, f3),
            [pad_1, z], "k_conv", stores=[win_h],
        )

    c3_n, e2_n, vec, win_n = conv_call(True, vec, b2_n, b2_f, halo_n)
    halo_n = to_near(e2_n)
    c3_f, e2_f, vec, win_f = conv_call(False, vec, b2_f, b2_n, halo_f)
    halo_f = to_far(e2_f)

    fast = shards == 8 and u % 16 == 0
    unit = (inner, inner)
    part = (u, inner)

    def split_call(jobs, args, loads, side, name, deps):
        halves = sum(kind == "half" for kind, *_ in jobs)
        turned = pltpu.VMEM((halves, shards, 2, u, rows), BF16)
        return call(
            functools.partial(k_split, jobs=jobs, side=side), [(unit, BF16)] * len(jobs),
            (place, *args), [turned], name, deps, loads,
        )

    def swap_cores(units):
        return [swap(v, "dp", 1) for v in units]

    def first_sum(keep, got, pairs, singles, name, deps):
        args = []
        for i in pairs:
            args += [keep[i], got[i], keep[i + 1], got[i + 1]]
        for i in singles:
            args += [keep[i].reshape(4, 2, u, inner), got[i].reshape(4, 2, u, inner)]
        outs = [(unit, BF16)] * (2 * len(pairs)) + [((4, *part), BF16)] * (2 * len(singles))
        kernel = functools.partial(k_first, n_pairs=len(pairs), n_units=len(singles))
        return call(kernel, outs, (place, *args), (), name, deps)

    def second_sum(stay, got, name, deps):
        views = [v.reshape(4, 2, u, inner) for v in (stay, got)]
        return call(k_second, [((4, *part), BF16)] * 2, (place, *views), (), name, deps)

    def line_parts(pairs, name, deps):
        own, *others = call(
            functools.partial(k_line, count=len(pairs)), [((len(pairs), *part), BF16)] * 4,
            (place, *[v for pair in pairs for v in pair]), (), name, deps,
        )
        return (own, *[swap(v, "seq", 2 * d) for d, v in zip((1, 2, 3), others)])

    def line_sums(groups, name, deps):
        n = sum(g[0].shape[0] for g in groups)
        kernel = functools.partial(k_sum, count=len(groups))
        args = [v for g in groups for v in g]
        return call(kernel, [((n, *part), BF16)], (place, *args), (), name, deps)[0]

    def row_sums(mine, got, split, name, deps):
        n = mine.shape[0] + len(split)
        kernel = functools.partial(k_rows, split=split)
        return call(kernel, [((n, *part), BF16)], (place, mine, got), (), name, deps)[0]

    def both_cores(mine, got, name, deps):
        return call(k_cores, [((2, *mine.shape), F32)], (place, mine, got), (), name, deps)[0]

    def add_vec(a, deps, axis, bit):
        return call(k_add, [vec_shape], (a, swap(a, axis, bit)), (), "k_add", deps)[0]

    def back1_call(near, vec, own, other, halo, q, s, deps):
        return call(
            functools.partial(
                k_back1, near=near, step=broad,
                rows_of=(row_narrow(1, 0), row_wide(1, 0), row_narrow(0, 1), row_wide(0, 2)),
            ),
            [(narrow_h, BF16), (wide_h, BF16), (narrow_h, BF16), edge, vec_shape],
            (place, vec, own, other, halo, w_mid_1, gw, gn),
            [win_scratch, pad_1, z, f1], "k_back1", deps, stores=[(wide_h, F32)], cost=6,
            loads=(*brief(*q[2:5]), (w_in, 1, False), *brief(s[3], s[5], s[6], cot),
                   (w_out, 0, False), *brief(s[1], s[2], q[1])),
        )

    def back0_call(near, vec, own, other, halo, p, deps, loads):
        return call(
            functools.partial(k_back0, near=near, step=close, row=row_narrow(0, 0)),
            [(narrow_h, BF16), vec_shape], (place, vec, own, other, halo, gn) + (() if near else (w_mid_0,)),
            [win_scratch, pad_0, z], "k_back0", deps, loads=brief(*p) + loads,
        )

    def out_call(deps):
        return call(
            k_out, [], (place, c3_n, c3_f, bw), (), "k_out", deps,
            loads=((w_out, 1, False), *brief(s_n[3], s_f[3])), stores=[((rows, width), F32)], parts=2,
        )[0]

    def dx_call(vec, deps):
        return call(
            functools.partial(k_dx, row=row_wide(0, 0)), [vec_shape],
            (place, vec, gw, e1_n0, e1_f0), [f1], "k_dx", deps,
            loads=((w_in, 0, False), *brief(x0, d1_n, stat_n, dx_n, d1_f, stat_f, dx_f)),
            stores=[((rows, width), F32)], parts=2,
        )

    if fast:
        jobs = (("taps", (0, 1), (5, 6), 0), ("taps", (0, 1), (5, 6), 1), ("half", (2,), (3, 4), None))
        args = (e2_n, e2_f, cot_v, c3_n, c3_f)
        loads = ((win_n, None, True), (win_f, None, True))
        *send_1, win_n, win_f = split_call(jobs, args, loads, 1, "k_weights1", (vec,))
        got_1 = swap_cores(send_1)
        keep_1 = split_call(jobs, (*args, win_n, win_f), (), 0, "k_weights1", (send_1[0],))
        (tap_1,) = call(
            functools.partial(k_tap, tap=4), [(unit, BF16)], (e2_n, e2_f, win_n, win_f), (), "k_tap",
            (keep_1[0],),
        )
        last = tap_1
    else:
        last = vec
    e1_n, e3_n, e2_n0, edge_n, vec, dx_n = back1_call(
        True, vec, e2_n, e2_f, halo_n, q_n, s_n, (last,)
    )
    halo_n = to_near(edge_n)
    if fast:
        xs, x1, ys, y1b = first_sum(keep_1, got_1, (0,), (2,), "k_first1", (vec,))
        x_got, y_got = swap(xs, "dp", 2), swap(ys, "seq", 1)
        last = x1
    e1_f, e3_f, e2_f0, edge_f, vec, dx_f = back1_call(
        False, vec, e2_f, e2_n, halo_f, q_f, s_f, (last,)
    )
    halo_f = to_far(edge_f)

    if not fast:
        e1_n0, vec, w_mid_0 = back0_call(True, vec, e2_n0, e2_f0, halo_n, p_n, (), ((w_mid, 0, True),))
        e1_f0, vec = back0_call(False, vec, e2_f0, e2_n0, halo_f, p_f, (), ())
        y1 = out_call((vec,))
        vec, dx = dx_call(vec, (y1,))

        def both(n, f):
            return jnp.concatenate([n, f])

        at = half * (1 - (lax.axis_index("seq") & 1))
        e3_1 = jnp.roll(cot, -at, axis=0)
        w_1 = plain_weights(
            both(s_n[4], s_f[4]), both(e1_n, e1_f), both(win_n, win_f), both(e2_n, e2_f),
            both(c3_n, c3_f), e3_1,
        )
        w_0 = plain_weights(
            both(a1_n, a1_f), both(e1_n0, e1_f0), both(s_n[0], s_f[0]), both(e2_n0, e2_f0),
            both(q_n[0], q_f[0]), both(e3_n, e3_f),
        )
        grad_w_in, grad_w_mid, grad_w_out = (jnp.stack(pair) for pair in zip(w_0, w_1))
        vec = lax.psum(vec, ("dp", "seq"))
    else:
        jobs = (
            ("taps", (4, 5), (7, 8), 0), ("taps", (4, 5), (7, 8), 1), ("half", (9, 10), (0, 1), None),
            ("half", (2, 3), (11, 12), None), ("odd", (4, 5), (7, 8), (4, 6)),
        )
        args = (e1_n, e1_f, e3_n, e3_f, e2_n0, e2_f0, tap_1)
        loads = brief(s_n[0], s_f[0], s_n[4], s_f[4], q_n[0], q_f[0])
        loads = tuple((v, None, True) for v in (s_n[0], s_f[0], s_n[4], s_f[4], q_n[0], q_f[0]))
        results = split_call(jobs, args, loads, 1, "k_weights2", (vec,))
        send_2, held = results[:5], results[5:]
        got_2 = swap_cores(send_2)
        keep_2 = split_call(jobs, (*args, *held), (), 0, "k_weights2", (send_2[0],))
        e1_n0, vec, w_mid_0 = back0_call(
            True, vec, e2_n0, e2_f0, halo_n, p_n, (keep_2[0],), ((w_mid, 0, True),)
        )
        e1_f0, vec, a1_n, a1_f = back0_call(
            False, vec, e2_f0, e2_n0, halo_f, p_f, (e1_n0,), ((a1_n, None, True), (a1_f, None, True))
        )
        as_, a1, bs, b1 = first_sum(keep_2, got_2, (0,), (4,), "k_first2", (e1_f0,))
        a_got, b_got = swap(as_, "dp", 2), swap(bs, "seq", 1)
        jobs = (("half", (0, 1), (2, 3), None),)
        args = (a1_n, a1_f, e1_n0, e1_f0)
        send_3 = split_call(jobs, args, (), 1, "k_weights3", (a1,))
        got_3 = swap_cores(send_3)
        keep_3 = split_call(jobs, args, (), 0, "k_weights3", (send_3[0],))
        xys, xy = second_sum(x1, x_got, "k_second1", (keep_3[0],))
        xy_got = swap(xys, "seq", 1)
        y1 = out_call((xy,))
        line_2 = line_parts([(b1, b_got)], "k_line2", (y1,))
        cs, c1 = first_sum(keep_3, got_3, (), (0,), "k_first3", (line_2[0],))
        c_got = swap(cs, "seq", 1)
        vec, dx = dx_call(vec, (c1,))
        line_1 = line_parts([(xy, xy_got), (y1b, y_got)], "k_line1", (vec,))
        vec = add_vec(vec, (line_1[0],), "dp", 1)
        ays, ay = second_sum(a1, a_got, "k_second2", (vec,))
        ay_got = swap(ays, "seq", 1)
        ds, d1 = first_sum(keep_2, got_2, (2,), (), "k_first4", (ay, a_got))
        d_got = swap(ds, "dp", 2)
        vec = add_vec(vec, (d1,), "dp", 2)
        line_3 = line_parts([(c1, c_got)], "k_line3", (vec,))
        vec = add_vec(vec, (line_3[0],), "seq", 1)
        line_4 = line_parts([(ay, ay_got)], "k_line4", (vec,))
        vec = add_vec(vec, (line_4[0],), "seq", 2)
        dys, dy = second_sum(d1, d_got, "k_second3", (vec,))
        dy_got = swap(dys, "seq", 1)
        sums = line_sums([line_1, line_4, line_2, line_3], "k_sum1", (dy,))
        sums_got = swap(sums, "dp", 2)
        vec = add_vec(vec, (sums,), "seq", 4)
        line_5 = line_parts([(dy, dy_got)], "k_line5", (vec,))
        whole = row_sums(sums, sums_got, (0, 2), "k_rows1", (line_5[0],))
        whole_got = swap(whole, "dp", 1)
        sums = line_sums([line_5], "k_sum2", (whole,))
        sums_got = swap(sums, "dp", 2)
        first = both_cores(whole, whole_got, "k_cores1", (sums,))
        whole = row_sums(sums, sums_got, (0,), "k_rows2", (first,))
        then = both_cores(whole, swap(whole, "dp", 1), "k_cores2", ())

        def rows_of(v):
            return v.reshape(2 * u, inner)

        grad_w_in = jnp.stack([rows_of(first[:, 6]), rows_of(then[:, 0])])
        grad_w_mid = jnp.stack(
            [
                jnp.concatenate([first[0, 3:5], first[1, 3:6]]),
                jnp.concatenate([first[0, 0:2], first[1, 0:2], first[0, 5:6]]),
            ]
        ).swapaxes(2, 3)
        grad_w_out = jnp.stack([rows_of(then[:, 1]), rows_of(first[:, 2])]).swapaxes(1, 2)

    narrow = vec[:n_narrow].reshape(2, 2, 3, inner)
    wide = vec[n_narrow:].reshape(2, 3, width)
    return (
        y1[None],
        dx[None],
        grad_w_in,
        grad_w_mid,
        grad_w_out,
        wide[:, 0],
        wide[:, 1],
        narrow[:, :, 0],
        narrow[:, :, 1],
        narrow[:, :, 2],
        wide[:, 2],
    )


def solution(mesh):
    row = P("dp", "seq", None)
    return jax.shard_map(
        body,
        mesh=mesh,
        in_specs=(row, P(None, "dp", "seq")) + (P(),) * 9 + (row,),
        out_specs=(
            row,
            row,
            P(None, "seq", None),
            P(None, None, None, "seq"),
            P(None, None, "seq"),
        )
        + (P(),) * 6,
        check_vma=False,
    )
```

```python
import functools

import jax
import jax.numpy as jnp
from jax import lax
from jax.experimental import pallas as pl
from jax.experimental.pallas import tpu as pltpu
from jax.sharding import PartitionSpec as P

DILATION_CLOSE = 4
DILATION_BROAD = 128
EPS = 1e-05
F32 = jnp.float32
BF16 = jnp.bfloat16
VMEM_LIMIT = 18 * 1024 * 1024
EXP2 = -0.7213475204444817

C0 = 0.3275911 * 0.7071067811865476
POLY = tuple(0.5 * c for c in (0.254829592, -0.284496736, 1.421413741, -1.453152027, 1.061405429))
ROOT_2PI = 0.3989422804014327


def normal_parts(q):
    bell = jnp.exp2((q * EXP2) * q)
    t = pltpu.reciprocal(1.0 + C0 * jnp.abs(q), approx=True)
    h = POLY[4]
    for c in POLY[3::-1]:
        h = h * t + c
    tail = h * t * bell
    return jnp.where(q >= 0, 1.0 - tail, tail), q * bell * ROOT_2PI


def act_forward(v, gain, shift):
    c = v.shape[-1]
    mean = jnp.sum(v, axis=-1, keepdims=True) * (1.0 / c)
    centred = v - mean
    r = lax.rsqrt(jnp.sum(centred * centred, axis=-1, keepdims=True) * (1.0 / c) + EPS)
    n = centred * r
    q = n * gain + shift
    below, slope = normal_parts(q)
    return mean, r, n, q * below, below + slope


def act_backward(f, n, r, d, gain):
    c = f.shape[-1]
    p = f * d
    gp = gain * p
    first = jnp.sum(gp, axis=-1, keepdims=True) * (1.0 / c)
    second = jnp.sum(gp * n, axis=-1, keepdims=True) * (1.0 / c)
    return p, r * (gp - first - n * second)


def fold(v):
    return jnp.sum(v.reshape(v.shape[0] // 8, 8, v.shape[1]), axis=0)


def total(acc):
    return jnp.sum(acc, axis=0, keepdims=True)


def lanes(column):
    return jnp.broadcast_to(column, (column.shape[0], 128))


def strips(rows, height, step, carry=(), unroll=4):
    turns = rows // (height * unroll)

    def body(i, c):
        for j in range(unroll):
            c = step(pl.ds(pl.multiple_of((i * unroll + j) * height, height), height), c)
        return c

    return lax.fori_loop(0, turns, body, carry)


def at_base(at, base):
    return pl.ds(pl.multiple_of(at.start + base, at.size), at.size)


def dot(a, b):
    return jnp.dot(a, b, preferred_element_type=F32)


def dot_nt(a, b):
    return lax.dot_general(a, b, (((1,), (1,)), ((), ())), preferred_element_type=F32)


class Loads:
    def __init__(self, sources, targets, sems):
        self.targets = targets
        self.copies = [
            pltpu.make_async_copy(src if b is None else src.at[b], dst, sems.at[i])
            for i, ((src, b), dst) in enumerate(zip(sources, targets))
        ]
        self.waiting = set(range(len(targets)))
        for copy in self.copies:
            copy.start()

    def get(self, i):
        if i in self.waiting:
            self.waiting.remove(i)
            self.copies[i].wait()
        return self.targets[i]

    def finish(self):
        for i in sorted(self.waiting):
            self.get(i)


class Stores:
    def __init__(self, held, targets, sems):
        self.held, self.targets, self.sems = held, targets, sems
        self.copies = []

    def put(self, *which, at=None):
        for i in which:
            src, dst = self.held[i], self.targets[i]
            if at is not None:
                src, dst = src.at[at], dst.at[at]
            copy = pltpu.make_async_copy(src, dst, self.sems.at[len(self.copies)])
            copy.start()
            self.copies.append(copy)

    def finish(self):
        for copy in self.copies:
            copy.wait()


def call(
    kernel, outs, args, scratch=(), name=None, deps=(), loads=(), stores=(), offloads=(), parts=1,
    limit=VMEM_LIMIT, cost=0,
):
    n_args, n_loads, n_deps, n_off = len(args), len(loads), len(deps), len(offloads)
    n_outs, n_stores = len(outs), len(stores)
    loaded = [(a.shape if b is None else a.shape[1:], a.dtype) for a, b, _ in loads]
    kept = [i for i, (_, _, keep) in enumerate(loads) if keep]
    brief = [i for i in range(n_loads) if i not in kept]
    out_shape = [pltpu.VMEM(s, t) for s, t in outs] + [pltpu.HBM(s, t) for s, t in stores]
    out_shape += [pltpu.VMEM(*loaded[i]) for i in kept]
    out_shape += [pltpu.HBM(a.shape, a.dtype) for a in offloads]

    def run(*refs):
        def take(n):
            nonlocal refs
            first, refs = refs[:n], refs[n:]
            return first

        ins, going, sources, _ = take(n_args), take(n_off), take(n_loads), take(n_deps)
        results, stored, held, gone = take(n_outs), take(n_stores), take(len(kept)), take(n_off)
        targets = dict(zip(kept, held))
        scr = list(refs)
        more = {}
        if n_loads:
            sems = scr.pop()
            for i in reversed(brief):
                targets[i] = scr.pop()
            sources = [(r, b) for r, (_, b, _) in zip(sources, loads)]
            more["coming"] = Loads(sources, [targets[i] for i in range(n_loads)], sems)
        if n_off:
            leaving = Stores(going, gone, scr.pop())
            leaving.put(*range(n_off))
        if n_stores:
            sems = scr.pop()
            held = [scr.pop() for _ in stores][::-1]
            more["keeping"] = Stores(held, stored, sems)
        kernel(*ins, *results, *scr, **more)
        for part in more.values():
            part.finish()
        if n_off:
            leaving.finish()

    hbm, vmem = pl.BlockSpec(memory_space=pltpu.HBM), pl.BlockSpec(memory_space=pltpu.VMEM)
    specs = [vmem] * (n_args + n_off) + [hbm] * n_loads
    specs += [pl.BlockSpec(memory_space=pl.ANY)] * n_deps
    out_specs = [vmem] * n_outs + [hbm] * n_stores + [vmem] * len(kept) + [hbm] * n_off
    scratch = list(scratch)
    if n_stores:
        scratch += [pltpu.VMEM(s, t) for s, t in stores]
        scratch += [pltpu.SemaphoreType.DMA((n_stores * parts,))]
    if n_off:
        scratch += [pltpu.SemaphoreType.DMA((n_off,))]
    if n_loads:
        scratch += [pltpu.VMEM(*loaded[i]) for i in brief] + [pltpu.SemaphoreType.DMA((n_loads,))]
    return pl.pallas_call(
        run,
        out_shape=out_shape,
        in_specs=specs,
        out_specs=out_specs,
        scratch_shapes=scratch,
        compiler_params=pltpu.CompilerParams(vmem_limit_bytes=limit),
        cost_estimate=pl.CostEstimate(flops=1 + int(cost * 1.15e9), bytes_accessed=1, transcendentals=0),
        name=name,
    )(
        *[pltpu.with_memory_space_constraint(a, pltpu.VMEM) for a in (*args, *offloads)],
        *[pltpu.with_memory_space_constraint(a, pltpu.HBM) for a, _, _ in loads],
        *deps,
    )


NEAR, CUT, LOW_0, LOW_1, HIGH_1, CORE, BIT_X, LINE = range(8)


def find_marks(bounds, place):
    rows = bounds.shape[2]
    first = lax.axis_index("seq") * rows
    marks = (bounds[1, 0:1, 0:1], bounds[0, 0:1, 0:1], bounds[0, 0:1, rows - 1 :], bounds[1, 0:1, rows - 1 :])
    for row, v in zip((CUT, LOW_0, LOW_1, HIGH_1), marks):
        place[row : row + 1] = jnp.broadcast_to(v - first, (1, 128))


def find_place(place):
    seq, dp = lax.axis_index("seq"), lax.axis_index("dp")
    for row, v in ((NEAR, seq & 1), (CORE, dp & 1), (BIT_X, dp >> 1), (LINE, seq >> 1)):
        place[row : row + 1] = jnp.full((1, 128), v, jnp.int32)


def base_of(place, near, rows):
    odd = place[NEAR, 0]
    return rows * (1 - odd) if near else rows * odd


def wide_act(x, base, gain, shift, a1, d1, stat):
    def wide(at, c):
        mean, r, n, a, d = act_forward(x[at_base(at, base)].astype(F32), gain, shift)
        a1[at], d1[at] = a.astype(BF16), d.astype(BF16)
        stat[0, at], stat[1, at] = lanes(mean), lanes(r)
        return c

    strips(a1.shape[0], 32, wide)


def narrow_act(z, gain, shift, a, n, d, stat):
    def narrow(at, c):
        _, r, nn, aa, dd = act_forward(z[at], gain, shift)
        n[at], d[at], a[at] = nn.astype(BF16), dd.astype(BF16), aa.astype(BF16)
        stat[at] = lanes(r)
        return c

    strips(z.shape[0], 32, narrow)


def windows(place, near, own, other, halo, win, pad, step):
    rows, width = own.shape
    taps = win.shape[1] // width
    rim = (pad.shape[0] - rows) // 2
    pad[rim : rim + rows] = own[...].astype(pad.dtype)
    lower = place[NEAR, 0] == (1 if near else 0)

    @pl.when(lower)
    def _():
        pad[0:rim] = halo[halo.shape[0] - rim :].astype(pad.dtype)
        pad[rim + rows :] = other[0:rim].astype(pad.dtype)

    @pl.when(jnp.logical_not(lower))
    def _():
        pad[0:rim] = other[rows - rim :].astype(pad.dtype)
        pad[rim + rows :] = halo[0:rim].astype(pad.dtype)

    base = base_of(place, near, rows)
    cut, low_0, low_1, high_1 = (place[i : i + 1] for i in (CUT, LOW_0, LOW_1, HIGH_1))
    height = 64
    for i in range(0, rows, height):
        t = lax.broadcasted_iota(jnp.int32, (height, 128), 0) + (base + i)
        first = t < cut
        low = jnp.where(first, low_0, low_1)
        high = jnp.where(first, cut, high_1)
        for k in range(taps):
            offset = (k - taps // 2) * step
            m = jnp.where((t + offset >= low) & (t + offset < high), 1.0, 0.0).astype(pad.dtype)
            m = jnp.concatenate([m] * (width // 128), axis=1)
            start = rim + offset + i
            win[i : i + height, k * width : (k + 1) * width] = (
                pad[start : start + height] * m
            ).astype(BF16)


def put_edge(edge, v, place, near):
    n = edge.shape[0]
    lower = place[NEAR, 0] == (1 if near else 0)

    @pl.when(lower)
    def _():
        edge[...] = v[0:n]

    @pl.when(jnp.logical_not(lower))
    def _():
        edge[...] = v[v.shape[0] - n :]


def k_in_near(place, a2, n2, d2, r2, edge, z, *, coming, keeping):
    a1, d1, stat1 = keeping.held
    find_place(place)
    x, gw, sw = coming.get(0), coming.get(1), coming.get(2)
    wide_act(x, base_of(place, True, a1.shape[0]), gw[0:1], sw[0:1], a1, d1, stat1)
    keeping.put(0, 1, 2)
    w_in, gn, sn, bn = (coming.get(i) for i in (3, 4, 5, 6))
    z[...] = dot(a1[...], w_in[...]) + bn[0, 0:1]
    narrow_act(z, gn[0, 0:1], sn[0, 0:1], a2, n2, d2, r2)
    put_edge(edge, a2, place, True)
    find_marks(coming.get(9), place)


def k_in_far(place, x, gw, sw, gn, sn, bn, a2, n2, d2, r2, edge, z, *, coming, keeping):
    a1, d1, stat1 = keeping.held
    wide_act(x, base_of(place, False, a1.shape[0]), gw[0:1], sw[0:1], a1, d1, stat1)
    keeping.put(0, 1, 2)
    z[...] = dot(a1[...], coming.get(0)[...]) + bn[0, 0:1]
    narrow_act(z, gn[0, 0:1], sn[0, 0:1], a2, n2, d2, r2)
    put_edge(edge, a2, place, False)


def k_mid(
    place, x, own, other, halo, w_mid, gw, sw, bw, gn, sn, bn,
    a3, r3, a2, n2, d2, r2, pad, z, *, near, step, coming, keeping,
):
    rows, width = own.shape
    win, n3, d3, y, a1, d1, stat1 = keeping.held
    windows(place, near, own, other, halo, win, pad, step)
    keeping.put(0)
    z[...] = dot(win[...], w_mid[...].reshape(win.shape[1], width)) + bn[0, 1:2]
    narrow_act(z, gn[0, 1:2], sn[0, 1:2], a3, n3, d3, r3)
    keeping.put(1, 2)
    base = base_of(place, near, rows)
    old = x[pl.ds(pl.multiple_of(base, rows), rows)].astype(F32)
    y[...] = old + dot(a3[...], coming.get(0)[...]) + bw[0:1]
    keeping.put(3)
    wide_act(y, 0, gw[1:2], sw[1:2], a1, d1, stat1)
    keeping.put(4, 5, 6)
    z[...] = dot(a1[...], coming.get(1)[...]) + bn[1, 0:1]
    narrow_act(z, gn[1, 0:1], sn[1, 0:1], a2, n2, d2, r2)


def put_wide(vec, row, acc):
    inner = vec.shape[1]
    for i in range(acc.shape[1] // inner):
        vec[row + i : row + i + 1] += total(acc[:, i * inner : (i + 1) * inner])


def k_flow(e, w_out, f, vec, *, row, coming):
    f[...] = dot_nt(e[...], w_out[...])
    vec[...] = jnp.zeros_like(vec)

    def step(at, acc):
        return acc + fold(e[at].astype(F32))

    put_wide(vec, row, strips(e.shape[0], 32, step, jnp.zeros((8, e.shape[1]), F32)))


def k_conv(
    place, vec_in, own, other, halo, w_mid, gn, sn, bn, f, a3, e2, vec, win, pad, z, *, near, step, row
):
    rows, width = own.shape
    windows(place, near, own, other, halo, win, pad, step)
    z[...] = dot(win[...], w_mid[...].reshape(win.shape[1], width)) + bn[1, 1:2]
    gain = gn[1, 1:2]
    base = base_of(place, near, rows)

    def narrow(at, c):
        _, r, n, a, d = act_forward(z[at], gain, sn[1, 1:2])
        a3[at] = a.astype(BF16)
        p, v = act_backward(f[at_base(at, base)], n, r, d, gain)
        e = v.astype(BF16)
        e2[at] = e
        return c[0] + fold(p * n), c[1] + fold(p), c[2] + fold(e.astype(F32))

    vec[...] = vec_in[...]
    zero = jnp.zeros((8, width), F32)
    for i, acc in enumerate(strips(rows, 32, narrow, (zero,) * 3)):
        vec[row + i : row + i + 1] += total(acc)


def k_out(place, a_n, a_f, bw, *, coming, keeping):
    half = a_n.shape[0]
    (y,) = keeping.held
    w_out = coming.get(0)
    for near, a in ((True, a_n), (False, a_f)):
        at = pl.ds(pl.multiple_of(base_of(place, near, half), half), half)
        y[at] = dot(a[...], w_out[...]) + bw[1:2] + coming.get(1 if near else 2)[...]
        keeping.put(0, at=at)


def back_narrow(f, n, d, r, gain, e_out, vec, row):
    rows, width = f.shape

    def step(at, c):
        nn = n[at].astype(F32)
        p, v = act_backward(f[at], nn, r[at][:, 0:1], d[at].astype(F32), gain)
        e = v.astype(BF16)
        e_out[at] = e
        return c[0] + fold(p * nn), c[1] + fold(p), c[2] + fold(e.astype(F32))

    zero = jnp.zeros((8, width), F32)
    for i, acc in enumerate(strips(rows, 32, step, (zero,) * 3)):
        vec[row + i : row + i + 1] += total(acc)


def back_wide(f, x, x_base, stat, d, gain, dy, dy_base, out, out_base, cast, vec, row, cast_row):
    rows, width = f.shape

    def step(at, c):
        r = stat[1, at][:, 0:1]
        n = (x[at_base(at, x_base)].astype(F32) - stat[0, at][:, 0:1]) * r
        p, v = act_backward(f[at], n, r, d[at].astype(F32), gain)
        dx = dy[at_base(at, dy_base)].astype(F32) + v
        out[at_base(at, out_base)] = dx
        sums = (c[0] + fold(p * n), c[1] + fold(p))
        if cast is not None:
            e = dx.astype(BF16)
            cast[at] = e
            sums += (c[2] + fold(e.astype(F32)),)
        return sums

    zero = jnp.zeros((8, width), F32)
    sums = strips(rows, 32, step, (zero,) * (2 if cast is None else 3), 2)
    put_wide(vec, row, sums[0])
    put_wide(vec, row + width // vec.shape[1], sums[1])
    if cast is not None:
        put_wide(vec, cast_row, sums[2])


def flow_two(win, w_mid, z):
    taps, width = w_mid.shape[0], w_mid.shape[1]
    for j in range(taps):
        part = dot_nt(win[:, j * width : (j + 1) * width], w_mid[taps - 1 - j])
        if j == 0:
            z[...] = part
        else:
            z[...] += part


def k_back1(
    place, vec_in, own, other, halo, w_mid, gw, gn,
    e1, e3, e2, edge, vec, win, pad, z, f1, *, near, step, rows_of, coming, keeping,
):
    vec[...] = vec_in[...]
    windows(place, near, own, other, halo, win, pad, step)
    flow_two(win, w_mid, z)
    n2, d2, r2, w_in = (coming.get(i) for i in range(4))
    back_narrow(z, n2, d2, r2, gn[1, 0:1], e1, vec, rows_of[0])
    f1[...] = dot_nt(e1[...], w_in[...])
    base = base_of(place, near, own.shape[0])
    (dx,) = keeping.held
    x, d1, stat1, dy = (coming.get(i) for i in range(4, 8))
    back_wide(f1, x, 0, stat1, d1, gw[1:2], dy, base, dx, 0, e3, vec, rows_of[1], rows_of[3])
    keeping.put(0)
    w_out, n3, d3, r3 = (coming.get(i) for i in range(8, 12))
    z[...] = dot_nt(e3[...], w_out[...])
    back_narrow(z, n3, d3, r3, gn[0, 1:2], e2, vec, rows_of[2])
    put_edge(edge, e2, place, near)


def k_back0(
    place, vec_in, own, other, halo, w_mid, gn, e1, vec, win, pad, z, *, near, step, row, coming
):
    vec[...] = vec_in[...]
    windows(place, near, own, other, halo, win, pad, step)
    flow_two(win, w_mid, z)
    n2, d2, r2 = (coming.get(i) for i in range(3))
    back_narrow(z, n2, d2, r2, gn[0, 0:1], e1, vec, row)


def k_dx(place, vec_in, gw, e1_n, e1_f, vec, f1, *, row, coming, keeping):
    vec[...] = vec_in[...]
    half = e1_n.shape[0]
    (out,) = keeping.held
    w_in, x = coming.get(0), coming.get(1)
    for near, e1 in ((True, e1_n), (False, e1_f)):
        f1[...] = dot_nt(e1[...], w_in[...])
        d, stat, dy = (coming.get(i + (0 if near else 3)) for i in (2, 3, 4))
        base = base_of(place, near, half)
        back_wide(f1, x, base, stat, d, gw[0:1], dy, 0, out, base, None, vec, row, None)
        keeping.put(0, at=pl.ds(pl.multiple_of(base, half), half))


def k_split(place, *refs, jobs, parts, side, coming=None):
    n_outs = sum(parts)
    outs, turned = list(refs[-1 - n_outs : -1]), refs[-1]
    refs = refs[: -1 - n_outs]
    _, shards, _, u, rows = turned.shape
    inner = outs[0].shape[-1]

    def ref(i):
        return refs[i] if i < len(refs) else coming.get(i - len(refs))

    def whole(places, at=slice(None)):
        if len(places) == 1:
            half = rows // 2
            bases = [base_of(place, near, half) for near in (True, False)]
            parts = [ref(places[0])[pl.ds(pl.multiple_of(b, half), half)] for b in bases]
        else:
            parts = [ref(i)[:, at] for i in places]
        return jnp.concatenate(parts, axis=0)

    core = place[CORE, 0] ^ side
    kept = {}
    halves = 0
    for n, (kind, left, right, j) in zip(parts, jobs):
        here, outs = outs[:n], outs[n:]

        def put(product):
            height = product.shape[0] // n
            for i, out in enumerate(here):
                out[...] = product[i * height : (i + 1) * height]

        if kind == "half":
            turned[halves] = whole(left).T.reshape(turned.shape[1:])
            part = turned[halves, :, core].reshape(shards * u, rows)
            put(dot(part, whole(right)).astype(BF16))
            halves += 1
            continue
        if left not in kept:
            kept[left] = whole(left).T
        if kind == "taps":
            at = pl.ds(pl.multiple_of((j + 2 * core) * inner, 128), inner)
            put(dot(kept[left], whole(right, at)).astype(BF16))
            continue
        tap, before = j

        @pl.when(core == 0)
        def _():
            put(ref(before)[...])

        @pl.when(core != 0)
        def _():
            at = slice(tap * inner, (tap + 1) * inner)
            put(dot(kept[left], whole(right, at)).astype(BF16))


def k_tap(e_n, e_f, win_n, win_f, out, *, tap):
    inner = out.shape[-1]
    at = slice(tap * inner, (tap + 1) * inner)
    left = jnp.concatenate([e_n[...], e_f[...]], axis=0).T
    right = jnp.concatenate([win_n[:, at], win_f[:, at]], axis=0)
    out[...] = dot(left, right).astype(BF16)


def added(*parts):
    first, *rest = [p.astype(F32) for p in parts]
    for p in rest:
        first = first + p
    return first


def k_first(place, *refs, pairs, singles):
    refs = list(refs)
    x, y = place[BIT_X, 0], place[NEAR, 0]

    def take(n):
        first = refs[:n]
        del refs[:n]
        return first

    ins = [(take(1)[0], take(n)) for two_units in pairs for n in two_units]
    ins += [(take(1)[0], take(n)) for n in singles]

    def add_rows(a, parts, out):
        height = a.shape[0] // len(parts)
        for i, b in enumerate(parts):

            def step(k, c):
                here = pl.ds(pl.multiple_of(k * 80, 80), 80)
                at = pl.ds(pl.multiple_of(i * height + k * 80, 80), 80)
                out[at] = added(a[at], b[here]).astype(BF16)
                return c

            lax.fori_loop(0, height // 80, step, 0)

    for i in range(len(pairs)):
        (a0, b0), (a1, b1) = ins[2 * i : 2 * i + 2]
        send, stay = take(2)

        @pl.when(x == 0)
        def _():
            add_rows(a1, b1, send)
            add_rows(a0, b0, stay)

        @pl.when(x != 0)
        def _():
            add_rows(a0, b0, send)
            add_rows(a1, b1, stay)

    for out, side in zip(refs, (1 - y, y)):
        at = 0
        for a, parts in ins[2 * len(pairs) :]:
            u = a.shape[2]
            each = a.shape[0] // len(parts)
            for k in range(a.shape[0]):
                b = parts[k // each]
                out[at : at + u] = added(a[k, side], b[k % each, side]).astype(BF16)
                at += u


def k_second(place, a, b, *refs, extra):
    if extra:
        *vec, more_a, more_b, send, stay, more = refs
        more[...] = added(more_a[...], more_b[...]).astype(BF16)
    else:
        vec, (send, stay) = (), refs
    mine = place[NEAR, 0]
    u = a.shape[2]
    for out, side in ((send, 1 - mine), (stay, mine)):

        def step(k, c):
            at = pl.ds(pl.multiple_of(k * u, u), u)
            out[at] = added(a[k, side], b[k, side]).astype(BF16)
            return c

        lax.fori_loop(0, 4, step, 0)
    if vec:
        pack(vec[0][...], send, stay, at=4 * u)


def pack(v, *outs, at):
    n = v.shape[0]
    upper = v.astype(BF16)
    lower = (v - upper.astype(F32)).astype(BF16)
    for out in outs:
        out[at : at + n], out[at + n : at + 2 * n] = upper, lower


def unpack(ref, at):
    n = (ref.shape[0] - at) // 2
    return ref[at : at + n].astype(F32) + ref[at + n : at + 2 * n].astype(F32)


def k_line(place, *refs, sums, wholes, packed, bit, u):
    mine = (place[LINE, 0] >> bit) & 1
    arrays = [refs[2 * i : 2 * i + 2] for i in range(sums)]
    arrays += [refs[2 * sums + i : 2 * sums + i + 1] for i in range(wholes)]
    send, stay = refs[2 * sums + wholes :]
    for out, side in ((send, 1 - mine), (stay, mine)):
        at = 0
        for i, parts in enumerate(arrays):
            rows = parts[0].shape[0] - (packed if i == 0 else 0)
            for j in range(rows // (2 * u)):
                part = pl.ds(pl.multiple_of((2 * j + side) * u, u), u)
                out[at : at + u] = added(*[p[part] for p in parts]).astype(BF16)
                at += u
    if packed:
        a, b = arrays[0]
        n = a.shape[0] - packed
        pack(unpack(a, n) + unpack(b, n), send, stay, at=send.shape[0] - packed)


def k_sum(place, *refs, rows):
    out = refs[-1]
    at = 0
    for i, n in enumerate(rows):
        a, b = refs[2 * i], refs[2 * i + 1]
        out[at : at + n] = added(a[0:n], b[0:n]).astype(BF16)
        at += n
    if refs[0].shape[0] > rows[0]:
        pack(unpack(refs[0], rows[0]) + unpack(refs[1], rows[0]), out, at=at)


def k_rows(place, *refs, splits, u):
    *refs, out = refs
    x = place[BIT_X, 0]
    at = 0
    refs = list(refs)
    for split in splits:
        if split is None:
            ready = refs.pop(0)
            out[at : at + ready.shape[0]] = ready[...]
            at += ready.shape[0]
            continue
        mine, got = refs.pop(0), refs.pop(0)
        for k, apart in enumerate(split):
            here = slice(k * u, (k + 1) * u)
            if apart:
                base = pl.multiple_of(at + x * u, u)
                other = pl.multiple_of(at + (1 - x) * u, u)
                out[pl.ds(base, u)], out[pl.ds(other, u)] = mine[here], got[here]
                at += 2 * u
            else:
                out[at : at + u] = added(mine[here], got[here]).astype(BF16)
                at += u
        if mine.shape[0] > len(split) * u:
            n = len(split) * u
            pack(unpack(mine, n) + unpack(got, n), out, at=out.shape[0] - (mine.shape[0] - n))


def k_results(place, mine, got, vec, *, keeping, u):
    core = place[CORE, 0]
    out_in, out_mid, out_out, gw, sw, gn, sn, bn, bw = keeping.held

    def unit(ref, i):
        return ref[i * u : (i + 1) * u].astype(F32)

    for ref, c in ((mine, core), (got, 1 - core)):
        for k in range(2):
            out_mid[1, 2 * c + k] = unit(ref, k)
            out_mid[0, 2 * c + k] = unit(ref, 3 + k)
        out_mid[1 - c, 4] = unit(ref, 5)
    keeping.put(1)
    for ref, c in ((mine, core), (got, 1 - core)):
        at = pl.ds(pl.multiple_of(c * u, u), u)
        out_out[1, at], out_in[0, at] = unit(ref, 2), unit(ref, 6)
        out_in[1, at], out_out[0, at] = unit(ref, 7), unit(ref, 8)
    keeping.put(0, 2)
    vec[...] = unpack(mine, 9 * u) + unpack(got, 9 * u)
    inner = vec.shape[1]
    two = gw.shape[1] // inner
    for block in range(2):
        for i in range(2):
            row = 3 * (2 * block + i)
            for j, ref in enumerate((gn, sn, bn)):
                ref[block, i : i + 1] = vec[row + j : row + j + 1]
        for j, ref in enumerate((gw, sw, bw)):
            for k in range(two):
                row = 12 + (3 * block + j) * two + k
                ref[block : block + 1, k * inner : (k + 1) * inner] = vec[row : row + 1]
    keeping.put(*range(3, 9))


def k_plus(a, b, out):
    out[...] = added(a[...], b[...]).astype(BF16)


def k_nothing(*refs, coming):
    pass


def swap(v, axis, bits):
    count = lax.axis_size(axis)
    return lax.ppermute(v, axis, [(i, i ^ bits) for i in range(count)])


def to_near(v):
    return swap(v, "seq", 1)


def to_far(v):
    count = lax.axis_size("seq")
    pairs = [(i, i + 1) for i in range(1, count - 1, 2)]
    return lax.ppermute(v, "seq", pairs + [(j, i) for i, j in pairs])


def dot_tn(a, b):
    return lax.dot_general(a, b, (((0,), (0,)), ((), ())), preferred_element_type=F32)


def plain_weights(a1, e1, win, e2, a3, e3):
    taps = win.shape[1] // e2.shape[1]
    grad_mid = dot_tn(win, e2).reshape(taps, e2.shape[1], e2.shape[1])
    shares = (
        lax.psum_scatter(dot_tn(a1, e1), "seq", scatter_dimension=0, tiled=True),
        lax.psum_scatter(grad_mid, "seq", scatter_dimension=2, tiled=True),
        lax.psum_scatter(dot_tn(a3, e3), "seq", scatter_dimension=1, tiled=True),
    )
    return [lax.psum(v.astype(BF16), "dp").astype(F32) for v in shares]


def body(
    tokens, bounds, w_in, w_mid, w_out, gain_wide, shift_wide, gain_narrow, shift_narrow,
    bias_narrow, bias_wide, cotangent,
):
    x0 = tokens[0]
    cot = cotangent[0]
    rows, width = x0.shape
    taps, inner = w_mid.shape[1], w_mid.shape[2]
    shards = lax.axis_size("seq")
    u = inner // shards
    two = width // inner
    half = rows // 2
    close, broad = DILATION_CLOSE, DILATION_BROAD

    wide_h, narrow_h, column = (half, width), (half, inner), ((half, 128), F32)
    win_h = ((half, taps * inner), BF16)
    act_wide = [(wide_h, BF16), (wide_h, BF16), ((2, half, 128), F32)]
    act_narrow = [(narrow_h, BF16), (narrow_h, BF16), (narrow_h, BF16), column]
    edge = ((16, inner), BF16)
    z = pltpu.VMEM(narrow_h, F32)
    f1 = pltpu.VMEM(wide_h, F32)
    win_scratch = pltpu.VMEM(*win_h)
    pad_0 = pltpu.VMEM((half + 32, inner), F32)
    pad_1 = pltpu.VMEM((half + 4 * broad, inner), BF16)
    n_narrow = 12
    vec_shape = ((n_narrow + 6 * two, inner), F32)

    def row_narrow(b, i):
        return 3 * (2 * b + i)

    def row_wide(b, i):
        return n_narrow + (3 * b + i) * two

    def brief(*arrays):
        return tuple((a, None, False) for a in arrays)

    place, a2_n, *p_n, edge_n, a1_n, d1_n, stat_n, x, gw, sw, gn, sn, bn, bw, w_mid_0 = call(
        k_in_near, [((8, 128), jnp.int32)] + act_narrow + [edge], (), [z], "k_in",
        loads=((x0, None, True), (gain_wide, None, True), (shift_wide, None, True), (w_in, 0, False),
               (gain_narrow, None, True), (shift_narrow, None, True), (bias_narrow, None, True),
               (bias_wide, None, True), (w_mid, 0, True), (bounds, None, False)),
        stores=act_wide, cost=4,
    )
    halo_n = to_near(edge_n)
    a2_f, *p_f, edge_f, a1_f, d1_f, stat_f, p1, p2, p3 = call(
        k_in_far, act_narrow + [edge], (place, x, gw, sw, gn, sn, bn), [z], "k_in", (edge_n,),
        loads=((w_in, 0, False),), stores=act_wide, offloads=p_n, cost=4,
    )
    p_n = (p1, p2, p3)
    halo_f = to_far(edge_f)

    def mid_call(near, own, other, halo, deps, loads, offloads):
        return call(
            functools.partial(k_mid, near=near, step=close),
            [(narrow_h, BF16), column] + act_narrow,
            (place, x, own, other, halo, w_mid_0, gw, sw, bw, gn, sn, bn),
            [pad_0, z], "k_mid", deps, ((w_out, 0, False), (w_in, 1, False)) + loads,
            [win_h, (narrow_h, BF16), (narrow_h, BF16), (wide_h, F32)] + act_wide, offloads, cost=8,
        )

    a3_n, r3_n, b2_n, *q_n = mid_call(True, a2_n, a2_f, halo_n, (), (), p_f)
    s_n, p_f = q_n[3:10], q_n[10:]
    halo_n = to_near(b2_n)
    a3_f, r3_f, b2_f, *q_f = mid_call(
        False, a2_f, a2_n, halo_f, (b2_n,), ((w_out, 1, True), (cot, None, True)),
        (a3_n, r3_n, *q_n[:3]),
    )
    s_f, (w_out_1, cot_v), q_n = q_f[3:10], q_f[10:12], q_f[12:]
    halo_f = to_far(b2_f)
    f3, vec, w_mid_1, *q_f = call(
        functools.partial(k_flow, row=row_wide(1, 2)),
        [((rows, inner), F32), vec_shape], (cot_v, w_out_1), (), "k_flow",
        loads=((w_mid, 1, True),), offloads=(a3_f, r3_f, *q_f[:3]), cost=3,
    )

    def conv_call(near, vec, own, other, halo):
        return call(
            functools.partial(k_conv, near=near, step=broad, row=row_narrow(1, 1)),
            [(narrow_h, BF16), (narrow_h, BF16), vec_shape, win_h],
            (place, vec, own, other, halo, w_mid_1, gn, sn, bn, f3),
            [pad_1, z], "k_conv", cost=3,
        )

    c3_n, e2_n, vec, win_n = conv_call(True, vec, b2_n, b2_f, halo_n)
    halo_n = to_near(e2_n)
    c3_f, e2_f, vec, win_f = conv_call(False, vec, b2_f, b2_n, halo_f)
    halo_f = to_far(e2_f)

    fast = shards == 8 and u % 16 == 0
    unit = (inner, inner)
    part = (u, inner)

    def split_call(jobs, args, loads, side, name, deps, cost=0, parts=None):
        parts = parts or (1,) * len(jobs)
        halves = sum(kind == "half" for kind, *_ in jobs)
        turned = pltpu.VMEM((halves, shards, 2, u, rows), BF16)
        return call(
            functools.partial(k_split, jobs=jobs, side=side, parts=parts),
            [((inner // n, inner), BF16) for n in parts for _ in range(n)],
            (place, *args), [turned], name, deps, loads, cost=cost,
        )

    def swap_cores(units, parts=None):
        got = [swap(v, "dp", 1) for v in units]
        parts = parts or (1,) * len(units)
        return [tuple(got.pop(0) for _ in range(n)) for n in parts]

    def first_sum(keep, got, pairs, singles, name, deps, cost=0):
        args = []
        for i in [j for pair in pairs for j in (pair, pair + 1)]:
            args += [keep[i], *got[i]]
        for i in singles:
            args += [v.reshape(-1, 2, u, inner) for v in (keep[i], *got[i])]
        outs = [(unit, BF16)] * (2 * len(pairs))
        outs += [((4 * u * len(singles), inner), BF16)] * (2 if singles else 0)
        kernel = functools.partial(
            k_first, pairs=tuple((len(got[i]), len(got[i + 1])) for i in pairs),
            singles=tuple(len(got[i]) for i in singles),
        )
        return call(kernel, outs, (place, *args), (), name, deps, cost=cost)

    n_packed = 2 * vec_shape[0][0]

    def second_sum(stay, got, name, deps, cost=0, extra=()):
        views = [v.reshape(4, 2, u, inner) for v in (stay, got)]
        n = 4 * u + (n_packed if extra else 0)
        outs = [((n, inner), BF16)] * 2 + ([((4 * u, inner), BF16)] if extra else [])
        kernel = functools.partial(k_second, extra=bool(extra))
        return call(kernel, outs, (place, *views, *extra), (), name, deps, cost=cost)

    def line_half(pairs, wholes, bit, name, deps, cost=0, packed=0):
        arrays = [pair[0] for pair in pairs] + list(wholes)
        n = sum(a.shape[0] for a in arrays) - packed
        n = n // 2 + packed
        kernel = functools.partial(k_line, sums=len(pairs), wholes=len(wholes), packed=packed, bit=bit, u=u)
        send, stay = call(
            kernel, [((n, inner), BF16)] * 2, (place, *[v for pair in pairs for v in pair], *wholes),
            (), name, deps, cost=cost,
        )
        return stay, swap(send, "seq", 2 << bit)

    def line_sums(pairs, rows, name, deps, cost=0):
        n = sum(rows) + pairs[0][0].shape[0] - rows[0]
        return call(
            functools.partial(k_sum, rows=rows), [((n, inner), BF16)],
            (place, *[v for pair in pairs for v in pair]), (), name, deps, cost=cost,
        )[0]

    def row_sums(pairs, splits, name, deps):
        n = sum(pair[0].shape[0] for pair in pairs) + u * sum(sum(split or ()) for split in splits)
        return call(
            functools.partial(k_rows, splits=splits, u=u), [((n, inner), BF16)],
            (place, *[v for pair in pairs for v in pair]), (), name, deps,
        )[0]

    def back1_call(near, vec, own, other, halo, q, s, deps, more=()):
        return call(
            functools.partial(
                k_back1, near=near, step=broad,
                rows_of=(row_narrow(1, 0), row_wide(1, 0), row_narrow(0, 1), row_wide(0, 2)),
            ),
            [(narrow_h, BF16), (wide_h, BF16), (narrow_h, BF16), edge, vec_shape],
            (place, vec, own, other, halo, w_mid_1, gw, gn),
            [win_scratch, pad_1, z, f1], "k_back1", deps, stores=[(wide_h, F32)], cost=5 if near else 2,
            loads=(*brief(*q[2:5]), (w_in, 1, False), *brief(s[3], s[5], s[6], cot),
                   (w_out, 0, False), *brief(s[1], s[2], q[1]), *more),
        )

    def back0_call(near, vec, own, other, halo, p, deps, loads, cost=0):
        return call(
            functools.partial(k_back0, near=near, step=close, row=row_narrow(0, 0)),
            [(narrow_h, BF16), vec_shape], (place, vec, own, other, halo, w_mid_0, gn),
            [win_scratch, pad_0, z], "k_back0", deps, loads=brief(*p) + loads, cost=cost,
        )

    def out_call(deps):
        return call(
            k_out, [], (place, c3_n, c3_f, bw), (), "k_out", deps,
            loads=((w_out, 1, False), *brief(s_n[3], s_f[3])), stores=[((rows, width), F32)], parts=2,
        )[0]

    def dx_call(vec, deps):
        return call(
            functools.partial(k_dx, row=row_wide(0, 0)), [vec_shape],
            (place, vec, gw, e1_n0, e1_f0), [f1], "k_dx", deps,
            loads=((w_in, 0, False), *brief(x0, d1_n, stat_n, dx_n, d1_f, stat_f, dx_f)),
            stores=[((rows, width), F32)], parts=2,
        )

    def rowed(v):
        return v.reshape(-1, inner)

    if fast:
        jobs = (("taps", (0, 1), (5, 6), 0), ("taps", (0, 1), (5, 6), 1), ("half", (2,), (3, 4), None))
        args = (e2_n, e2_f, cot_v, c3_n, c3_f, win_n, win_f)
        send_1 = split_call(jobs, args, (), 1, "k_weights1", (vec,))
        got_1 = swap_cores(send_1)
        keep_1 = split_call(jobs, args, (), 0, "k_weights1", (send_1[0],))
        (tap_1,) = call(
            functools.partial(k_tap, tap=4), [(unit, BF16)], (e2_n, e2_f, win_n, win_f), (), "k_tap",
            (keep_1[0],),
        )
        last = tap_1
    else:
        last = vec
    e1_n, e3_n, e2_n0, edge_n, vec, dx_n = back1_call(
        True, vec, e2_n, e2_f, halo_n, q_n, s_n, (last,)
    )
    halo_n = to_near(edge_n)
    if fast:
        xs, x1, ys, y1b = first_sum(keep_1, got_1, (0,), (2,), "k_first1", (vec, halo_f))
        x_got, y_got = swap(xs, "dp", 2), swap(ys, "seq", 1)
        last = x1
    more = tuple((v, None, True) for v in (s_n[0], s_f[0], s_n[4], s_f[4], q_n[0], q_f[0])) if fast else ()
    e1_f, e3_f, e2_f0, edge_f, vec, dx_f, *held = back1_call(
        False, vec, e2_f, e2_n, halo_f, q_f, s_f, (last,), more
    )
    halo_f = to_far(edge_f)

    if not fast:
        (w_mid_0,) = call(k_nothing, [], (place,), (), "k_load", (vec,), ((w_mid, 0, True),))
        e1_n0, vec = back0_call(True, vec, e2_n0, e2_f0, halo_n, p_n, (), ())
        e1_f0, vec = back0_call(False, vec, e2_f0, e2_n0, halo_f, p_f, (), ())
        y1 = out_call((vec,))
        vec, dx = dx_call(vec, (y1,))

        def both(n, f):
            return jnp.concatenate([n, f])

        at = half * (1 - (lax.axis_index("seq") & 1))
        e3_1 = jnp.roll(cot, -at, axis=0)
        w_1 = plain_weights(
            both(s_n[4], s_f[4]), both(e1_n, e1_f), both(win_n, win_f), both(e2_n, e2_f),
            both(c3_n, c3_f), e3_1,
        )
        w_0 = plain_weights(
            both(a1_n, a1_f), both(e1_n0, e1_f0), both(s_n[0], s_f[0]), both(e2_n0, e2_f0),
            both(q_n[0], q_f[0]), both(e3_n, e3_f),
        )
        grad_w_in, grad_w_mid, grad_w_out = (jnp.stack(pair) for pair in zip(w_0, w_1))
        vec = lax.psum(vec, ("dp", "seq"))
    else:
        jobs = (
            ("taps", (4, 5), (7, 8), 0), ("taps", (4, 5), (7, 8), 1), ("half", (9, 10), (0, 1), None),
            ("half", (2, 3), (11, 12), None), ("odd", (4, 5), (7, 8), (4, 6)),
        )
        args = (e1_n, e1_f, e3_n, e3_f, e2_n0, e2_f0, tap_1, *held)
        send_2 = split_call(jobs, args, (), 1, "k_weights2", (vec,))
        got_2 = swap_cores(send_2)
        *keep_2, w_mid_0 = split_call(jobs, args, ((w_mid, 0, True),), 0, "k_weights2", (send_2[0],))
        (y1b,) = call(
            k_plus, [((4 * u, inner), BF16)], (y1b, y_got), (), "k_plus",
            (keep_2[0], halo_n, halo_f), cost=3,
        )
        xys, xy = second_sum(x1, x_got, "k_second1", (y1b,), 1)
        xy_got = swap(xys, "seq", 1)
        as_, a1, bs, b1 = first_sum(
            keep_2, got_2, (0,), (4,), "k_first2", (xy, *got_2[2], *got_2[3])
        )
        a_got, b_got = swap(as_, "dp", 2), swap(bs, "seq", 1)
        e1_n0, vec = back0_call(True, vec, e2_n0, e2_f0, halo_n, p_n, (a1,), (), 7)
        e1_f0, vec, a1_n, a1_f = back0_call(
            False, vec, e2_f0, e2_n0, halo_f, p_f, (e1_n0,), ((a1_n, None, True), (a1_f, None, True)), 1
        )
        vec, dx = dx_call(vec, ())
        jobs = (("half", (0, 1), (2, 3), None),)
        args = (a1_n, a1_f, e1_n0, e1_f0)
        send_3 = split_call(jobs, args, (), 1, "k_weights3", (vec,), parts=(2,))
        got_3 = swap_cores(send_3, (2,))
        keep_3 = split_call(jobs, args, (), 0, "k_weights3", (send_3[0],))
        line_a = line_half([(xy, xy_got)], [y1b], 0, "k_line1", (keep_3[0],))
        ays, ay, b1 = second_sum(a1, a_got, "k_second2", (line_a[0],), 0.3, (vec, b1, b_got))
        ay_got = swap(ays, "seq", 1)
        ds, d1 = first_sum(keep_2, got_2, (2,), (), "k_first3", (ay,), 2)
        d_got = swap(ds, "dp", 2)
        cs, c1 = first_sum(keep_3, got_3, (), (0,), "k_first4", (d1,))
        c_got = swap(cs, "seq", 1)
        y1 = out_call((c1,))
        line_a = line_half([line_a], [], 1, "k_line2", (y1,))
        line_b = line_half([(ay, ay_got)], [b1], 0, "k_line3", (line_a[0],), 0, n_packed)
        line_e = line_half([(c1, c_got)], [], 0, "k_line4", (line_b[0],))
        dys, dy = second_sum(d1, d_got, "k_second3", (line_e[0],))
        dy_got = swap(dys, "seq", 1)
        sums_a = line_sums([line_a], (2 * u,), "k_sum1", (dy,), 2.5)
        a_rows = (sums_a, swap(sums_a, "dp", 2))
        line_b = line_half([line_b], [], 1, "k_line5", (sums_a,), 0, n_packed)
        line_e = line_half([line_e], [], 1, "k_line6", (line_b[0],), 2)
        line_c = line_half([(dy, dy_got)], [], 0, "k_line7", (line_e[0],))
        whole = row_sums([a_rows], ((1, 0),), "k_rows1", (line_c[0],))
        sums_b = line_sums([line_b, line_e], (2 * u, u), "k_sum2", (whole,), 1.5)
        b_rows = (sums_b, swap(sums_b, "dp", 2))
        line_c = line_half([line_c], [], 1, "k_line8", (sums_b,), 2)
        sums_c = line_sums([line_c], (u,), "k_sum3", (line_c[0],))
        c_rows = (sums_c, swap(sums_c, "dp", 2))
        whole = row_sums(
            [(whole,), b_rows, c_rows], (None, (1, 0, 0), (1,)), "k_rows2", (sums_c,)
        )
        _, grad_w_in, grad_w_mid, grad_w_out, *vectors = call(
            functools.partial(k_results, u=u), [vec_shape], (place, whole, swap(whole, "dp", 1)), (),
            "k_results", (),
            stores=[((2, 2 * u, inner), F32), ((2, taps, u, inner), F32), ((2, 2 * u, inner), F32),
                    ((2, width), F32), ((2, width), F32), ((2, 2, inner), F32),
                    ((2, 2, inner), F32), ((2, 2, inner), F32), ((2, width), F32)],
        )
        return (
            y1[None], dx[None], grad_w_in, grad_w_mid.swapaxes(2, 3), grad_w_out.swapaxes(1, 2),
            *vectors,
        )

    narrow = vec[:n_narrow].reshape(2, 2, 3, inner)
    wide = vec[n_narrow:].reshape(2, 3, width)
    return (
        y1[None],
        dx[None],
        grad_w_in,
        grad_w_mid,
        grad_w_out,
        wide[:, 0],
        wide[:, 1],
        narrow[:, :, 0],
        narrow[:, :, 1],
        narrow[:, :, 2],
        wide[:, 2],
    )


def solution(mesh):
    row = P("dp", "seq", None)
    return jax.shard_map(
        body,
        mesh=mesh,
        in_specs=(row, P(None, "dp", "seq")) + (P(),) * 9 + (row,),
        out_specs=(
            row,
            row,
            P(None, "seq", None),
            P(None, None, None, "seq"),
            P(None, None, "seq"),
        )
        + (P(),) * 6,
        check_vma=False,
    )
```

```python
import functools

import jax
import jax.numpy as jnp
from jax import lax
from jax.experimental import pallas as pl
from jax.experimental.pallas import tpu as pltpu
from jax.sharding import PartitionSpec as P

DILATION_CLOSE = 4
DILATION_BROAD = 128
EPS = 1e-05
F32 = jnp.float32
BF16 = jnp.bfloat16
VMEM_LIMIT = 18 * 1024 * 1024
EXP2 = -0.7213475204444817

C0 = 0.3275911 * 0.7071067811865476
POLY = tuple(0.5 * c for c in (0.254829592, -0.284496736, 1.421413741, -1.453152027, 1.061405429))
ROOT_2PI = 0.3989422804014327


def normal_parts(q):
    bell = jnp.exp2((q * EXP2) * q)
    t = pltpu.reciprocal(1.0 + C0 * jnp.abs(q), approx=True)
    h = POLY[4]
    for c in POLY[3::-1]:
        h = h * t + c
    tail = h * t * bell
    return jnp.where(q >= 0, 1.0 - tail, tail), q * bell * ROOT_2PI


def act_forward(v, gain, shift):
    c = v.shape[-1]
    mean = jnp.sum(v, axis=-1, keepdims=True) * (1.0 / c)
    centred = v - mean
    r = lax.rsqrt(jnp.sum(centred * centred, axis=-1, keepdims=True) * (1.0 / c) + EPS)
    n = centred * r
    q = n * gain + shift
    below, slope = normal_parts(q)
    return mean, r, n, q * below, below + slope


def act_backward(f, n, r, d, gain):
    c = f.shape[-1]
    p = f * d
    gp = gain * p
    first = jnp.sum(gp, axis=-1, keepdims=True) * (1.0 / c)
    second = jnp.sum(gp * n, axis=-1, keepdims=True) * (1.0 / c)
    return p, r * (gp - first - n * second)


def fold(v):
    return jnp.sum(v.reshape(v.shape[0] // 8, 8, v.shape[1]), axis=0)


def total(acc):
    return jnp.sum(acc, axis=0, keepdims=True)


def lanes(column):
    return jnp.broadcast_to(column, (column.shape[0], 128))


def strips(rows, height, step, carry=(), unroll=4):
    turns = rows // (height * unroll)

    def body(i, c):
        for j in range(unroll):
            c = step(pl.ds(pl.multiple_of((i * unroll + j) * height, height), height), c)
        return c

    return lax.fori_loop(0, turns, body, carry)


def at_base(at, base):
    return pl.ds(pl.multiple_of(at.start + base, at.size), at.size)


def dot(a, b):
    return jnp.dot(a, b, preferred_element_type=F32)


def dot_nt(a, b):
    return lax.dot_general(a, b, (((1,), (1,)), ((), ())), preferred_element_type=F32)


class Loads:
    def __init__(self, sources, targets, sems):
        self.targets = targets
        self.copies = [
            pltpu.make_async_copy(src if b is None else src.at[b], dst, sems.at[i])
            for i, ((src, b), dst) in enumerate(zip(sources, targets))
        ]
        self.waiting = set(range(len(targets)))
        for copy in self.copies:
            copy.start()

    def get(self, i):
        if i in self.waiting:
            self.waiting.remove(i)
            self.copies[i].wait()
        return self.targets[i]

    def finish(self):
        for i in sorted(self.waiting):
            self.get(i)


class Stores:
    def __init__(self, held, targets, sems):
        self.held, self.targets, self.sems = held, targets, sems
        self.copies = []

    def put(self, *which, at=None):
        for i in which:
            src, dst = self.held[i], self.targets[i]
            if at is not None:
                src, dst = src.at[at], dst.at[at]
            copy = pltpu.make_async_copy(src, dst, self.sems.at[len(self.copies)])
            copy.start()
            self.copies.append(copy)

    def finish(self):
        for copy in self.copies:
            copy.wait()


def call(
    kernel, outs, args, scratch=(), name=None, deps=(), loads=(), stores=(), offloads=(), parts=1,
    limit=VMEM_LIMIT, cost=0,
):
    n_args, n_loads, n_deps, n_off = len(args), len(loads), len(deps), len(offloads)
    n_outs, n_stores = len(outs), len(stores)
    loaded = [(a.shape if b is None else a.shape[1:], a.dtype) for a, b, _ in loads]
    kept = [i for i, (_, _, keep) in enumerate(loads) if keep]
    brief = [i for i in range(n_loads) if i not in kept]
    out_shape = [pltpu.VMEM(s, t) for s, t in outs] + [pltpu.HBM(s, t) for s, t in stores]
    out_shape += [pltpu.VMEM(*loaded[i]) for i in kept]
    out_shape += [pltpu.HBM(a.shape, a.dtype) for a in offloads]

    def run(*refs):
        def take(n):
            nonlocal refs
            first, refs = refs[:n], refs[n:]
            return first

        ins, going, sources, _ = take(n_args), take(n_off), take(n_loads), take(n_deps)
        results, stored, held, gone = take(n_outs), take(n_stores), take(len(kept)), take(n_off)
        targets = dict(zip(kept, held))
        scr = list(refs)
        more = {}
        if n_loads:
            sems = scr.pop()
            for i in reversed(brief):
                targets[i] = scr.pop()
            sources = [(r, b) for r, (_, b, _) in zip(sources, loads)]
            more["coming"] = Loads(sources, [targets[i] for i in range(n_loads)], sems)
        if n_off:
            leaving = Stores(going, gone, scr.pop())
            leaving.put(*range(n_off))
        if n_stores:
            sems = scr.pop()
            held = [scr.pop() for _ in stores][::-1]
            more["keeping"] = Stores(held, stored, sems)
        kernel(*ins, *results, *scr, **more)
        for part in more.values():
            part.finish()
        if n_off:
            leaving.finish()

    hbm, vmem = pl.BlockSpec(memory_space=pltpu.HBM), pl.BlockSpec(memory_space=pltpu.VMEM)
    specs = [vmem] * (n_args + n_off) + [hbm] * n_loads
    specs += [pl.BlockSpec(memory_space=pl.ANY)] * n_deps
    out_specs = [vmem] * n_outs + [hbm] * n_stores + [vmem] * len(kept) + [hbm] * n_off
    scratch = list(scratch)
    if n_stores:
        scratch += [pltpu.VMEM(s, t) for s, t in stores]
        scratch += [pltpu.SemaphoreType.DMA((n_stores * parts,))]
    if n_off:
        scratch += [pltpu.SemaphoreType.DMA((n_off,))]
    if n_loads:
        scratch += [pltpu.VMEM(*loaded[i]) for i in brief] + [pltpu.SemaphoreType.DMA((n_loads,))]
    return pl.pallas_call(
        run,
        out_shape=out_shape,
        in_specs=specs,
        out_specs=out_specs,
        scratch_shapes=scratch,
        compiler_params=pltpu.CompilerParams(vmem_limit_bytes=limit),
        cost_estimate=pl.CostEstimate(flops=1 + int(cost * 1.15e9), bytes_accessed=1, transcendentals=0),
        name=name,
    )(
        *[pltpu.with_memory_space_constraint(a, pltpu.VMEM) for a in (*args, *offloads)],
        *[pltpu.with_memory_space_constraint(a, pltpu.HBM) for a, _, _ in loads],
        *deps,
    )


NEAR, CUT, LOW_0, LOW_1, HIGH_1, CORE, BIT_X, LINE = range(8)


def find_marks(bounds, place):
    rows = bounds.shape[2]
    first = lax.axis_index("seq") * rows
    marks = (bounds[1, 0:1, 0:1], bounds[0, 0:1, 0:1], bounds[0, 0:1, rows - 1 :], bounds[1, 0:1, rows - 1 :])
    for row, v in zip((CUT, LOW_0, LOW_1, HIGH_1), marks):
        place[row : row + 1] = jnp.broadcast_to(v - first, (1, 128))


def find_place(place):
    seq, dp = lax.axis_index("seq"), lax.axis_index("dp")
    for row, v in ((NEAR, seq & 1), (CORE, dp & 1), (BIT_X, dp >> 1), (LINE, seq >> 1)):
        place[row : row + 1] = jnp.full((1, 128), v, jnp.int32)


def base_of(place, near, rows):
    odd = place[NEAR, 0]
    return rows * (1 - odd) if near else rows * odd


def wide_act(x, base, gain, shift, a1, d1, stat):
    def wide(at, c):
        mean, r, n, a, d = act_forward(x[at_base(at, base)].astype(F32), gain, shift)
        a1[at], d1[at] = a.astype(BF16), d.astype(BF16)
        stat[0, at], stat[1, at] = lanes(mean), lanes(r)
        return c

    strips(a1.shape[0], 32, wide)


def narrow_act(z, gain, shift, a, n, d, stat):
    def narrow(at, c):
        _, r, nn, aa, dd = act_forward(z[at], gain, shift)
        n[at], d[at], a[at] = nn.astype(BF16), dd.astype(BF16), aa.astype(BF16)
        stat[at] = lanes(r)
        return c

    strips(z.shape[0], 32, narrow)


def windows(place, near, own, other, halo, win, pad, step):
    rows, width = own.shape
    taps = win.shape[1] // width
    rim = (pad.shape[0] - rows) // 2
    pad[rim : rim + rows] = own[...].astype(pad.dtype)
    lower = place[NEAR, 0] == (1 if near else 0)

    @pl.when(lower)
    def _():
        pad[0:rim] = halo[halo.shape[0] - rim :].astype(pad.dtype)
        pad[rim + rows :] = other[0:rim].astype(pad.dtype)

    @pl.when(jnp.logical_not(lower))
    def _():
        pad[0:rim] = other[rows - rim :].astype(pad.dtype)
        pad[rim + rows :] = halo[0:rim].astype(pad.dtype)

    base = base_of(place, near, rows)
    cut, low_0, low_1, high_1 = (place[i : i + 1] for i in (CUT, LOW_0, LOW_1, HIGH_1))
    height = 64
    for i in range(0, rows, height):
        t = lax.broadcasted_iota(jnp.int32, (height, 128), 0) + (base + i)
        first = t < cut
        low = jnp.where(first, low_0, low_1)
        high = jnp.where(first, cut, high_1)
        for k in range(taps):
            offset = (k - taps // 2) * step
            m = jnp.where((t + offset >= low) & (t + offset < high), 1.0, 0.0).astype(pad.dtype)
            m = jnp.concatenate([m] * (width // 128), axis=1)
            start = rim + offset + i
            win[i : i + height, k * width : (k + 1) * width] = (
                pad[start : start + height] * m
            ).astype(BF16)


def put_edge(edge, v, place, near):
    n = edge.shape[0]
    lower = place[NEAR, 0] == (1 if near else 0)

    @pl.when(lower)
    def _():
        edge[...] = v[0:n]

    @pl.when(jnp.logical_not(lower))
    def _():
        edge[...] = v[v.shape[0] - n :]


def k_in_near(place, a2, n2, d2, r2, edge, z, *, coming, keeping):
    a1, d1, stat1 = keeping.held
    find_place(place)
    x, gw, sw = coming.get(0), coming.get(1), coming.get(2)
    wide_act(x, base_of(place, True, a1.shape[0]), gw[0:1], sw[0:1], a1, d1, stat1)
    keeping.put(0, 1, 2)
    w_in, gn, sn, bn = (coming.get(i) for i in (3, 4, 5, 6))
    z[...] = dot(a1[...], w_in[...]) + bn[0, 0:1]
    narrow_act(z, gn[0, 0:1], sn[0, 0:1], a2, n2, d2, r2)
    put_edge(edge, a2, place, True)
    find_marks(coming.get(9), place)


def k_in_far(place, x, gw, sw, gn, sn, bn, a2, n2, d2, r2, edge, z, *, coming, keeping):
    a1, d1, stat1 = keeping.held
    wide_act(x, base_of(place, False, a1.shape[0]), gw[0:1], sw[0:1], a1, d1, stat1)
    keeping.put(0, 1, 2)
    z[...] = dot(a1[...], coming.get(0)[...]) + bn[0, 0:1]
    narrow_act(z, gn[0, 0:1], sn[0, 0:1], a2, n2, d2, r2)
    put_edge(edge, a2, place, False)


def k_mid(
    place, x, own, other, halo, w_mid, gw, sw, bw, gn, sn, bn,
    a3, r3, a2, n2, d2, r2, pad, z, *, near, step, coming, keeping,
):
    rows, width = own.shape
    win, n3, d3, y, a1, d1, stat1 = keeping.held
    windows(place, near, own, other, halo, win, pad, step)
    keeping.put(0)
    z[...] = dot(win[...], w_mid[...].reshape(win.shape[1], width)) + bn[0, 1:2]
    narrow_act(z, gn[0, 1:2], sn[0, 1:2], a3, n3, d3, r3)
    keeping.put(1, 2)
    base = base_of(place, near, rows)
    old = x[pl.ds(pl.multiple_of(base, rows), rows)].astype(F32)
    y[...] = old + dot(a3[...], coming.get(0)[...]) + bw[0:1]
    keeping.put(3)
    wide_act(y, 0, gw[1:2], sw[1:2], a1, d1, stat1)
    keeping.put(4, 5, 6)
    z[...] = dot(a1[...], coming.get(1)[...]) + bn[1, 0:1]
    narrow_act(z, gn[1, 0:1], sn[1, 0:1], a2, n2, d2, r2)


def put_wide(vec, row, acc):
    inner = vec.shape[1]
    for i in range(acc.shape[1] // inner):
        vec[row + i : row + i + 1] += total(acc[:, i * inner : (i + 1) * inner])


def k_flow(e, w_out, f, vec, *, row, coming):
    f[...] = dot_nt(e[...], w_out[...])
    vec[...] = jnp.zeros_like(vec)

    def step(at, acc):
        return acc + fold(e[at].astype(F32))

    put_wide(vec, row, strips(e.shape[0], 32, step, jnp.zeros((8, e.shape[1]), F32)))


def k_conv(
    place, vec_in, own, other, halo, w_mid, gn, sn, bn, f, a3, e2, vec, win, pad, z, *, near, step, row
):
    rows, width = own.shape
    windows(place, near, own, other, halo, win, pad, step)
    z[...] = dot(win[...], w_mid[...].reshape(win.shape[1], width)) + bn[1, 1:2]
    gain = gn[1, 1:2]
    base = base_of(place, near, rows)

    def narrow(at, c):
        _, r, n, a, d = act_forward(z[at], gain, sn[1, 1:2])
        a3[at] = a.astype(BF16)
        p, v = act_backward(f[at_base(at, base)], n, r, d, gain)
        e = v.astype(BF16)
        e2[at] = e
        return c[0] + fold(p * n), c[1] + fold(p), c[2] + fold(e.astype(F32))

    vec[...] = vec_in[...]
    zero = jnp.zeros((8, width), F32)
    for i, acc in enumerate(strips(rows, 32, narrow, (zero,) * 3)):
        vec[row + i : row + i + 1] += total(acc)


def k_out(place, a_n, a_f, bw, *, coming, keeping):
    half = a_n.shape[0]
    (y,) = keeping.held
    w_out = coming.get(0)
    for near, a in ((True, a_n), (False, a_f)):
        at = pl.ds(pl.multiple_of(base_of(place, near, half), half), half)
        y[at] = dot(a[...], w_out[...]) + bw[1:2] + coming.get(1 if near else 2)[...]
        keeping.put(0, at=at)


def back_narrow(f, n, d, r, gain, e_out, vec, row):
    rows, width = f.shape

    def step(at, c):
        nn = n[at].astype(F32)
        p, v = act_backward(f[at], nn, r[at][:, 0:1], d[at].astype(F32), gain)
        e = v.astype(BF16)
        e_out[at] = e
        return c[0] + fold(p * nn), c[1] + fold(p), c[2] + fold(e.astype(F32))

    zero = jnp.zeros((8, width), F32)
    for i, acc in enumerate(strips(rows, 32, step, (zero,) * 3)):
        vec[row + i : row + i + 1] += total(acc)


def back_wide(f, x, x_base, stat, d, gain, dy, dy_base, out, out_base, cast, vec, row, cast_row):
    rows, width = f.shape

    def step(at, c):
        r = stat[1, at][:, 0:1]
        n = (x[at_base(at, x_base)].astype(F32) - stat[0, at][:, 0:1]) * r
        p, v = act_backward(f[at], n, r, d[at].astype(F32), gain)
        dx = dy[at_base(at, dy_base)].astype(F32) + v
        out[at_base(at, out_base)] = dx
        sums = (c[0] + fold(p * n), c[1] + fold(p))
        if cast is not None:
            e = dx.astype(BF16)
            cast[at] = e
            sums += (c[2] + fold(e.astype(F32)),)
        return sums

    zero = jnp.zeros((8, width), F32)
    sums = strips(rows, 32, step, (zero,) * (2 if cast is None else 3), 2)
    put_wide(vec, row, sums[0])
    put_wide(vec, row + width // vec.shape[1], sums[1])
    if cast is not None:
        put_wide(vec, cast_row, sums[2])


def flow_two(win, w_mid, z):
    taps, width = w_mid.shape[0], w_mid.shape[1]
    for j in range(taps):
        part = dot_nt(win[:, j * width : (j + 1) * width], w_mid[taps - 1 - j])
        if j == 0:
            z[...] = part
        else:
            z[...] += part


def k_back1(
    place, vec_in, own, other, halo, w_mid, gw, gn,
    e1, e3, e2, edge, vec, win, pad, z, f1, *, near, step, rows_of, coming, keeping,
):
    vec[...] = vec_in[...]
    windows(place, near, own, other, halo, win, pad, step)
    flow_two(win, w_mid, z)
    n2, d2, r2, w_in = (coming.get(i) for i in range(4))
    back_narrow(z, n2, d2, r2, gn[1, 0:1], e1, vec, rows_of[0])
    f1[...] = dot_nt(e1[...], w_in[...])
    base = base_of(place, near, own.shape[0])
    (dx,) = keeping.held
    x, d1, stat1, dy = (coming.get(i) for i in range(4, 8))
    back_wide(f1, x, 0, stat1, d1, gw[1:2], dy, base, dx, 0, e3, vec, rows_of[1], rows_of[3])
    keeping.put(0)
    w_out, n3, d3, r3 = (coming.get(i) for i in range(8, 12))
    z[...] = dot_nt(e3[...], w_out[...])
    back_narrow(z, n3, d3, r3, gn[0, 1:2], e2, vec, rows_of[2])
    put_edge(edge, e2, place, near)


def k_back0(
    place, vec_in, own, other, halo, w_mid, gn, e1, vec, win, pad, z, *, near, step, row, coming
):
    vec[...] = vec_in[...]
    halo = halo.at[pl.ds(halo.shape[0] - 16, 16)]
    windows(place, near, own, other, halo, win, pad, step)
    flow_two(win, w_mid, z)
    n2, d2, r2 = (coming.get(i) for i in range(3))
    back_narrow(z, n2, d2, r2, gn[0, 0:1], e1, vec, row)


def k_dx(place, vec_in, gw, e1_n, e1_f, vec, f1, *, row, coming, keeping):
    vec[...] = vec_in[...]
    half = e1_n.shape[0]
    (out,) = keeping.held
    w_in, x = coming.get(0), coming.get(1)
    for near, e1 in ((True, e1_n), (False, e1_f)):
        f1[...] = dot_nt(e1[...], w_in[...])
        d, stat, dy = (coming.get(i + (0 if near else 3)) for i in (2, 3, 4))
        base = base_of(place, near, half)
        back_wide(f1, x, base, stat, d, gw[0:1], dy, 0, out, base, None, vec, row, None)
        keeping.put(0, at=pl.ds(pl.multiple_of(base, half), half))


def k_split(place, *refs, jobs, parts, side, coming=None):
    n_outs = sum(parts)
    outs, turned = list(refs[-1 - n_outs : -1]), refs[-1]
    refs = refs[: -1 - n_outs]
    _, shards, _, u, rows = turned.shape
    inner = outs[0].shape[-1]

    def ref(i):
        return refs[i] if i < len(refs) else coming.get(i - len(refs))

    def whole(places, at=slice(None)):
        if len(places) == 1:
            half = rows // 2
            bases = [base_of(place, near, half) for near in (True, False)]
            parts = [ref(places[0])[pl.ds(pl.multiple_of(b, half), half)] for b in bases]
        else:
            parts = [ref(i)[:, at] for i in places]
        return jnp.concatenate(parts, axis=0)

    core = place[CORE, 0] ^ side
    kept = {}
    halves = 0
    for n, (kind, left, right, j) in zip(parts, jobs):
        here, outs = outs[:n], outs[n:]

        def put(product):
            height = product.shape[0] // n
            for i, out in enumerate(here):
                out[...] = product[i * height : (i + 1) * height]

        if kind == "half":
            turned[halves] = whole(left).T.reshape(turned.shape[1:])
            part = turned[halves, :, core].reshape(shards * u, rows)
            put(dot(part, whole(right)).astype(BF16))
            halves += 1
            continue
        if left not in kept:
            kept[left] = whole(left).T
        if kind == "taps":
            at = pl.ds(pl.multiple_of((j + 2 * core) * inner, 128), inner)
            put(dot(kept[left], whole(right, at)).astype(BF16))
            continue
        tap, before = j

        @pl.when(core == 0)
        def _():
            put(ref(before)[...])

        @pl.when(core != 0)
        def _():
            at = slice(tap * inner, (tap + 1) * inner)
            put(dot(kept[left], whole(right, at)).astype(BF16))


def k_tap(e_n, e_f, win_n, win_f, out, *, tap):
    inner = out.shape[-1]
    at = slice(tap * inner, (tap + 1) * inner)
    left = jnp.concatenate([e_n[...], e_f[...]], axis=0).T
    right = jnp.concatenate([win_n[:, at], win_f[:, at]], axis=0)
    out[...] = dot(left, right).astype(BF16)


def added(*parts):
    first, *rest = [p.astype(F32) for p in parts]
    for p in rest:
        first = first + p
    return first


def k_first(place, *refs, pairs, singles, edge):
    refs = list(refs)
    x, y = place[BIT_X, 0], place[NEAR, 0]

    def take(n):
        first = refs[:n]
        del refs[:n]
        return first

    ins = [(take(1)[0], take(n)) for two_units in pairs for n in two_units]
    ins += [(take(1)[0], take(n)) for n in singles]
    rim = take(1)[0] if edge else None

    def add_rows(a, parts, out):
        height = a.shape[0] // len(parts)
        for i, b in enumerate(parts):

            def step(k, c):
                here = pl.ds(pl.multiple_of(k * 80, 80), 80)
                at = pl.ds(pl.multiple_of(i * height + k * 80, 80), 80)
                out[at] = added(a[at], b[here]).astype(BF16)
                return c

            lax.fori_loop(0, height // 80, step, 0)

    for i in range(len(pairs)):
        (a0, b0), (a1, b1) = ins[2 * i : 2 * i + 2]
        send, stay = take(2)

        @pl.when(x == 0)
        def _():
            add_rows(a1, b1, send)
            add_rows(a0, b0, stay)

        @pl.when(x != 0)
        def _():
            add_rows(a0, b0, send)
            add_rows(a1, b1, stay)

    for out, side in zip(refs, (1 - y, y)):
        at = 0
        for a, parts in ins[2 * len(pairs) :]:
            u = a.shape[2]
            each = a.shape[0] // len(parts)
            for k in range(a.shape[0]):
                b = parts[k // each]
                out[at : at + u] = added(a[k, side], b[k % each, side]).astype(BF16)
                at += u
    if edge:
        refs[0][at:] = rim[...]


def k_second(place, a, b, *refs, extra):
    if extra:
        *vec, more_a, more_b, send, stay, more = refs
        more[...] = added(more_a[...], more_b[...]).astype(BF16)
    else:
        vec, (send, stay) = (), refs
    mine = place[NEAR, 0]
    u = a.shape[2]
    for out, side in ((send, 1 - mine), (stay, mine)):

        def step(k, c):
            at = pl.ds(pl.multiple_of(k * u, u), u)
            out[at] = added(a[k, side], b[k, side]).astype(BF16)
            return c

        lax.fori_loop(0, 4, step, 0)
    if vec:
        pack(vec[0][...], send, stay, at=4 * u)


def pack(v, *outs, at):
    n = v.shape[0]
    upper = v.astype(BF16)
    lower = (v - upper.astype(F32)).astype(BF16)
    for out in outs:
        out[at : at + n], out[at + n : at + 2 * n] = upper, lower


def unpack(ref, at):
    n = (ref.shape[0] - at) // 2
    return ref[at : at + n].astype(F32) + ref[at + n : at + 2 * n].astype(F32)


def k_line(place, *refs, sums, wholes, packed, bit, u):
    mine = (place[LINE, 0] >> bit) & 1
    arrays = [refs[2 * i : 2 * i + 2] for i in range(sums)]
    arrays += [refs[2 * sums + i : 2 * sums + i + 1] for i in range(wholes)]
    send, stay = refs[2 * sums + wholes :]
    for out, side in ((send, 1 - mine), (stay, mine)):
        at = 0
        for i, parts in enumerate(arrays):
            rows = parts[0].shape[0] - (packed if i == 0 else 0)
            for j in range(rows // (2 * u)):
                part = pl.ds(pl.multiple_of((2 * j + side) * u, u), u)
                out[at : at + u] = added(*[p[part] for p in parts]).astype(BF16)
                at += u
    if packed:
        a, b = arrays[0]
        n = a.shape[0] - packed
        pack(unpack(a, n) + unpack(b, n), send, stay, at=send.shape[0] - packed)


def k_sum(place, *refs, rows):
    out = refs[-1]
    at = 0
    for i, n in enumerate(rows):
        a, b = refs[2 * i], refs[2 * i + 1]
        out[at : at + n] = added(a[0:n], b[0:n]).astype(BF16)
        at += n
    if refs[0].shape[0] > rows[0]:
        pack(unpack(refs[0], rows[0]) + unpack(refs[1], rows[0]), out, at=at)


def k_rows(place, *refs, splits, u):
    *refs, out = refs
    x = place[BIT_X, 0]
    at = 0
    refs = list(refs)
    for split in splits:
        if split is None:
            ready = refs.pop(0)
            out[at : at + ready.shape[0]] = ready[...]
            at += ready.shape[0]
            continue
        mine, got = refs.pop(0), refs.pop(0)
        for k, apart in enumerate(split):
            here = slice(k * u, (k + 1) * u)
            if apart:
                base = pl.multiple_of(at + x * u, u)
                other = pl.multiple_of(at + (1 - x) * u, u)
                out[pl.ds(base, u)], out[pl.ds(other, u)] = mine[here], got[here]
                at += 2 * u
            else:
                out[at : at + u] = added(mine[here], got[here]).astype(BF16)
                at += u
        if mine.shape[0] > len(split) * u:
            n = len(split) * u
            pack(unpack(mine, n) + unpack(got, n), out, at=out.shape[0] - (mine.shape[0] - n))


def k_results(place, mine, got, vec, *, keeping, u):
    core = place[CORE, 0]
    out_in, out_mid, out_out, gw, sw, gn, sn, bn, bw = keeping.held

    def unit(ref, i):
        return ref[i * u : (i + 1) * u].astype(F32)

    for ref, c in ((mine, core), (got, 1 - core)):
        for k in range(2):
            out_mid[1, 2 * c + k] = unit(ref, k)
            out_mid[0, 2 * c + k] = unit(ref, 3 + k)
        out_mid[1 - c, 4] = unit(ref, 5)
    keeping.put(1)
    for ref, c in ((mine, core), (got, 1 - core)):
        at = pl.ds(pl.multiple_of(c * u, u), u)
        out_out[1, at], out_in[0, at] = unit(ref, 2), unit(ref, 6)
        out_in[1, at], out_out[0, at] = unit(ref, 7), unit(ref, 8)
    keeping.put(0, 2)
    vec[...] = unpack(mine, 9 * u) + unpack(got, 9 * u)
    inner = vec.shape[1]
    two = gw.shape[1] // inner
    for block in range(2):
        for i in range(2):
            row = 3 * (2 * block + i)
            for j, ref in enumerate((gn, sn, bn)):
                ref[block, i : i + 1] = vec[row + j : row + j + 1]
        for j, ref in enumerate((gw, sw, bw)):
            for k in range(two):
                row = 12 + (3 * block + j) * two + k
                ref[block : block + 1, k * inner : (k + 1) * inner] = vec[row : row + 1]
    keeping.put(*range(3, 9))


def k_plus(a, b, out):
    out[...] = added(a[...], b[0 : a.shape[0]]).astype(BF16)


def k_nothing(*refs, coming):
    pass


def swap(v, axis, bits):
    count = lax.axis_size(axis)
    return lax.ppermute(v, axis, [(i, i ^ bits) for i in range(count)])


def to_near(v):
    return swap(v, "seq", 1)


def to_far(v):
    count = lax.axis_size("seq")
    pairs = [(i, i + 1) for i in range(1, count - 1, 2)]
    return lax.ppermute(v, "seq", pairs + [(j, i) for i, j in pairs])


def dot_tn(a, b):
    return lax.dot_general(a, b, (((0,), (0,)), ((), ())), preferred_element_type=F32)


def plain_weights(a1, e1, win, e2, a3, e3):
    taps = win.shape[1] // e2.shape[1]
    grad_mid = dot_tn(win, e2).reshape(taps, e2.shape[1], e2.shape[1])
    shares = (
        lax.psum_scatter(dot_tn(a1, e1), "seq", scatter_dimension=0, tiled=True),
        lax.psum_scatter(grad_mid, "seq", scatter_dimension=2, tiled=True),
        lax.psum_scatter(dot_tn(a3, e3), "seq", scatter_dimension=1, tiled=True),
    )
    return [lax.psum(v.astype(BF16), "dp").astype(F32) for v in shares]


def body(
    tokens, bounds, w_in, w_mid, w_out, gain_wide, shift_wide, gain_narrow, shift_narrow,
    bias_narrow, bias_wide, cotangent,
):
    x0 = tokens[0]
    cot = cotangent[0]
    rows, width = x0.shape
    taps, inner = w_mid.shape[1], w_mid.shape[2]
    shards = lax.axis_size("seq")
    u = inner // shards
    two = width // inner
    half = rows // 2
    close, broad = DILATION_CLOSE, DILATION_BROAD

    wide_h, narrow_h, column = (half, width), (half, inner), ((half, 128), F32)
    win_h = ((half, taps * inner), BF16)
    act_wide = [(wide_h, BF16), (wide_h, BF16), ((2, half, 128), F32)]
    act_narrow = [(narrow_h, BF16), (narrow_h, BF16), (narrow_h, BF16), column]
    edge = ((16, inner), BF16)
    z = pltpu.VMEM(narrow_h, F32)
    f1 = pltpu.VMEM(wide_h, F32)
    win_scratch = pltpu.VMEM(*win_h)
    pad_0 = pltpu.VMEM((half + 32, inner), F32)
    pad_1 = pltpu.VMEM((half + 4 * broad, inner), BF16)
    n_narrow = 12
    vec_shape = ((n_narrow + 6 * two, inner), F32)

    def row_narrow(b, i):
        return 3 * (2 * b + i)

    def row_wide(b, i):
        return n_narrow + (3 * b + i) * two

    def brief(*arrays):
        return tuple((a, None, False) for a in arrays)

    place, a2_n, *p_n, edge_n, a1_n, d1_n, stat_n, x, gw, sw, gn, sn, bn, bw, w_mid_0 = call(
        k_in_near, [((8, 128), jnp.int32)] + act_narrow + [edge], (), [z], "k_in",
        loads=((x0, None, True), (gain_wide, None, True), (shift_wide, None, True), (w_in, 0, False),
               (gain_narrow, None, True), (shift_narrow, None, True), (bias_narrow, None, True),
               (bias_wide, None, True), (w_mid, 0, True), (bounds, None, False)),
        stores=act_wide, cost=4,
    )
    halo_n = to_near(edge_n)
    a2_f, *p_f, edge_f, a1_f, d1_f, stat_f, p1, p2, p3 = call(
        k_in_far, act_narrow + [edge], (place, x, gw, sw, gn, sn, bn), [z], "k_in", (edge_n,),
        loads=((w_in, 0, False),), stores=act_wide, offloads=p_n, cost=4,
    )
    p_n = (p1, p2, p3)
    halo_f = to_far(edge_f)

    def mid_call(near, own, other, halo, deps, loads, offloads):
        return call(
            functools.partial(k_mid, near=near, step=close),
            [(narrow_h, BF16), column] + act_narrow,
            (place, x, own, other, halo, w_mid_0, gw, sw, bw, gn, sn, bn),
            [pad_0, z], "k_mid", deps, ((w_out, 0, False), (w_in, 1, False)) + loads,
            [win_h, (narrow_h, BF16), (narrow_h, BF16), (wide_h, F32)] + act_wide, offloads, cost=8,
        )

    a3_n, r3_n, b2_n, *q_n = mid_call(True, a2_n, a2_f, halo_n, (), (), p_f)
    s_n, p_f = q_n[3:10], q_n[10:]
    halo_n = to_near(b2_n)
    a3_f, r3_f, b2_f, *q_f = mid_call(
        False, a2_f, a2_n, halo_f, (b2_n,), ((w_out, 1, True), (cot, None, True)),
        (a3_n, r3_n, *q_n[:3]),
    )
    s_f, (w_out_1, cot_v), q_n = q_f[3:10], q_f[10:12], q_f[12:]
    halo_f = to_far(b2_f)
    f3, vec, w_mid_1, *q_f = call(
        functools.partial(k_flow, row=row_wide(1, 2)),
        [((rows, inner), F32), vec_shape], (cot_v, w_out_1), (), "k_flow",
        loads=((w_mid, 1, True),), offloads=(a3_f, r3_f, *q_f[:3]), cost=3,
    )

    def conv_call(near, vec, own, other, halo):
        return call(
            functools.partial(k_conv, near=near, step=broad, row=row_narrow(1, 1)),
            [(narrow_h, BF16), (narrow_h, BF16), vec_shape, win_h],
            (place, vec, own, other, halo, w_mid_1, gn, sn, bn, f3),
            [pad_1, z], "k_conv", cost=3,
        )

    c3_n, e2_n, vec, win_n = conv_call(True, vec, b2_n, b2_f, halo_n)
    halo_n = to_near(e2_n)
    c3_f, e2_f, vec, win_f = conv_call(False, vec, b2_f, b2_n, halo_f)
    halo_f = to_far(e2_f)

    fast = shards == 8 and u % 16 == 0
    unit = (inner, inner)
    part = (u, inner)

    def split_call(jobs, args, loads, side, name, deps, cost=0, parts=None):
        parts = parts or (1,) * len(jobs)
        halves = sum(kind == "half" for kind, *_ in jobs)
        turned = pltpu.VMEM((halves, shards, 2, u, rows), BF16)
        return call(
            functools.partial(k_split, jobs=jobs, side=side, parts=parts),
            [((inner // n, inner), BF16) for n in parts for _ in range(n)],
            (place, *args), [turned], name, deps, loads, cost=cost,
        )

    def swap_cores(units, parts=None):
        got = [swap(v, "dp", 1) for v in units]
        parts = parts or (1,) * len(units)
        return [tuple(got.pop(0) for _ in range(n)) for n in parts]

    def first_sum(keep, got, pairs, singles, name, deps, cost=0, edge=()):
        args = []
        for i in [j for pair in pairs for j in (pair, pair + 1)]:
            args += [keep[i], *got[i]]
        for i in singles:
            args += [v.reshape(-1, 2, u, inner) for v in (keep[i], *got[i])]
        outs = [(unit, BF16)] * (2 * len(pairs))
        n = 4 * u * len(singles)
        if singles:
            outs += [((n + sum(v.shape[0] for v in edge), inner), BF16), ((n, inner), BF16)]
        kernel = functools.partial(
            k_first, pairs=tuple((len(got[i]), len(got[i + 1])) for i in pairs),
            singles=tuple(len(got[i]) for i in singles), edge=bool(edge),
        )
        return call(kernel, outs, (place, *args, *edge), (), name, deps, cost=cost)

    n_packed = 2 * vec_shape[0][0]

    def second_sum(stay, got, name, deps, cost=0, extra=()):
        views = [v.reshape(4, 2, u, inner) for v in (stay, got)]
        n = 4 * u + (n_packed if extra else 0)
        outs = [((n, inner), BF16)] * 2 + ([((4 * u, inner), BF16)] if extra else [])
        kernel = functools.partial(k_second, extra=bool(extra))
        return call(kernel, outs, (place, *views, *extra), (), name, deps, cost=cost)

    def line_half(pairs, wholes, bit, name, deps, cost=0, packed=0):
        arrays = [pair[0] for pair in pairs] + list(wholes)
        n = sum(a.shape[0] for a in arrays) - packed
        n = n // 2 + packed
        kernel = functools.partial(k_line, sums=len(pairs), wholes=len(wholes), packed=packed, bit=bit, u=u)
        send, stay = call(
            kernel, [((n, inner), BF16)] * 2, (place, *[v for pair in pairs for v in pair], *wholes),
            (), name, deps, cost=cost,
        )
        return stay, swap(send, "seq", 2 << bit)

    def line_sums(pairs, rows, name, deps, cost=0):
        n = sum(rows) + pairs[0][0].shape[0] - rows[0]
        return call(
            functools.partial(k_sum, rows=rows), [((n, inner), BF16)],
            (place, *[v for pair in pairs for v in pair]), (), name, deps, cost=cost,
        )[0]

    def row_sums(pairs, splits, name, deps):
        n = sum(pair[0].shape[0] for pair in pairs) + u * sum(sum(split or ()) for split in splits)
        return call(
            functools.partial(k_rows, splits=splits, u=u), [((n, inner), BF16)],
            (place, *[v for pair in pairs for v in pair]), (), name, deps,
        )[0]

    def back1_call(near, vec, own, other, halo, q, s, deps, more=()):
        return call(
            functools.partial(
                k_back1, near=near, step=broad,
                rows_of=(row_narrow(1, 0), row_wide(1, 0), row_narrow(0, 1), row_wide(0, 2)),
            ),
            [(narrow_h, BF16), (wide_h, BF16), (narrow_h, BF16), edge, vec_shape],
            (place, vec, own, other, halo, w_mid_1, gw, gn),
            [win_scratch, pad_1, z, f1], "k_back1", deps, stores=[(wide_h, F32)], cost=5 if near else 2,
            loads=(*brief(*q[2:5]), (w_in, 1, False), *brief(s[3], s[5], s[6], cot),
                   (w_out, 0, False), *brief(s[1], s[2], q[1]), *more),
        )

    def back0_call(near, vec, own, other, halo, p, deps, loads, cost=0):
        return call(
            functools.partial(k_back0, near=near, step=close, row=row_narrow(0, 0)),
            [(narrow_h, BF16), vec_shape], (place, vec, own, other, halo, w_mid_0, gn),
            [win_scratch, pad_0, z], "k_back0", deps, loads=brief(*p) + loads, cost=cost,
        )

    def out_call(deps):
        return call(
            k_out, [], (place, c3_n, c3_f, bw), (), "k_out", deps,
            loads=((w_out, 1, False), *brief(s_n[3], s_f[3])), stores=[((rows, width), F32)], parts=2,
        )[0]

    def dx_call(vec, deps):
        return call(
            functools.partial(k_dx, row=row_wide(0, 0)), [vec_shape],
            (place, vec, gw, e1_n0, e1_f0), [f1], "k_dx", deps,
            loads=((w_in, 0, False), *brief(x0, d1_n, stat_n, dx_n, d1_f, stat_f, dx_f)),
            stores=[((rows, width), F32)], parts=2,
        )

    def rowed(v):
        return v.reshape(-1, inner)

    if fast:
        jobs = (("taps", (0, 1), (5, 6), 0), ("taps", (0, 1), (5, 6), 1), ("half", (2,), (3, 4), None))
        args = (e2_n, e2_f, cot_v, c3_n, c3_f, win_n, win_f)
        send_1 = split_call(jobs, args, (), 1, "k_weights1", (vec,))
        got_1 = swap_cores(send_1)
        keep_1 = split_call(jobs, args, (), 0, "k_weights1", (send_1[0],))
        (tap_1,) = call(
            functools.partial(k_tap, tap=4), [(unit, BF16)], (e2_n, e2_f, win_n, win_f), (), "k_tap",
            (keep_1[0],),
        )
        last = tap_1
    else:
        last = vec
    e1_n, e3_n, e2_n0, edge_n, vec, dx_n = back1_call(
        True, vec, e2_n, e2_f, halo_n, q_n, s_n, (last,)
    )
    if fast:
        xs, x1, ys, y1b = first_sum(
            keep_1, got_1, (0,), (2,), "k_first1", (vec, halo_f), 0, (edge_n,)
        )
        x_got, y_got = swap(xs, "dp", 2), swap(ys, "seq", 1)
        halo_n, last = y_got, x1
    else:
        halo_n = to_near(edge_n)
    more = tuple((v, None, True) for v in (s_n[0], s_f[0], s_n[4], s_f[4], q_n[0], q_f[0])) if fast else ()
    e1_f, e3_f, e2_f0, edge_f, vec, dx_f, *held = back1_call(
        False, vec, e2_f, e2_n, halo_f, q_f, s_f, (last,), more
    )
    halo_f = to_far(edge_f)

    if not fast:
        (w_mid_0,) = call(k_nothing, [], (place,), (), "k_load", (vec,), ((w_mid, 0, True),))
        e1_n0, vec = back0_call(True, vec, e2_n0, e2_f0, halo_n, p_n, (), ())
        e1_f0, vec = back0_call(False, vec, e2_f0, e2_n0, halo_f, p_f, (), ())
        y1 = out_call((vec,))
        vec, dx = dx_call(vec, (y1,))

        def both(n, f):
            return jnp.concatenate([n, f])

        at = half * (1 - (lax.axis_index("seq") & 1))
        e3_1 = jnp.roll(cot, -at, axis=0)
        w_1 = plain_weights(
            both(s_n[4], s_f[4]), both(e1_n, e1_f), both(win_n, win_f), both(e2_n, e2_f),
            both(c3_n, c3_f), e3_1,
        )
        w_0 = plain_weights(
            both(a1_n, a1_f), both(e1_n0, e1_f0), both(s_n[0], s_f[0]), both(e2_n0, e2_f0),
            both(q_n[0], q_f[0]), both(e3_n, e3_f),
        )
        grad_w_in, grad_w_mid, grad_w_out = (jnp.stack(pair) for pair in zip(w_0, w_1))
        vec = lax.psum(vec, ("dp", "seq"))
    else:
        jobs = (
            ("taps", (4, 5), (7, 8), 0), ("taps", (4, 5), (7, 8), 1), ("half", (9, 10), (0, 1), None),
            ("half", (2, 3), (11, 12), None), ("odd", (4, 5), (7, 8), (4, 6)),
        )
        args = (e1_n, e1_f, e3_n, e3_f, e2_n0, e2_f0, tap_1, *held)
        parts = (1, 1)
        send_2 = split_call(jobs[:2], args, (), 1, "k_weights2", (vec,), parts=parts)
        got_2 = swap_cores(send_2, parts)
        *keep_2, w_mid_0 = split_call(jobs, args, ((w_mid, 0, True),), 0, "k_weights2", (send_2[0],))
        send_4 = split_call(jobs[2:], args, (), 1, "k_weights4", (keep_2[0],))
        got_2 = got_2 + swap_cores(send_4)
        (y1b,) = call(
            k_plus, [((4 * u, inner), BF16)], (y1b, y_got), (), "k_plus", (send_4[0], halo_f)
        )
        as_, a1 = first_sum(keep_2, got_2, (0,), (), "k_first2", (y1b, x_got))
        a_got = swap(as_, "dp", 2)
        xys, xy = second_sum(x1, x_got, "k_second1", (a1,))
        xy_got = swap(xys, "seq", 1)
        bs, b1 = first_sum(keep_2, got_2, (), (4,), "k_first5", (xy, *got_2[2], *got_2[3]))
        b_got = swap(bs, "seq", 1)
        e1_n0, vec = back0_call(True, vec, e2_n0, e2_f0, halo_n, p_n, (b1,), (), 7)
        e1_f0, vec, a1_n, a1_f = back0_call(
            False, vec, e2_f0, e2_n0, halo_f, p_f, (e1_n0,), ((a1_n, None, True), (a1_f, None, True)), 1
        )
        vec, dx = dx_call(vec, ())
        jobs = (("half", (0, 1), (2, 3), None),)
        args = (a1_n, a1_f, e1_n0, e1_f0)
        send_3 = split_call(jobs, args, (), 1, "k_weights3", (vec,), parts=(2,))
        got_3 = swap_cores(send_3, (2,))
        keep_3 = split_call(jobs, args, (), 0, "k_weights3", (send_3[0],))
        line_a = line_half([(xy, xy_got)], [y1b], 0, "k_line1", (keep_3[0],))
        ays, ay, b1 = second_sum(a1, a_got, "k_second2", (line_a[0],), 0.3, (vec, b1, b_got))
        ay_got = swap(ays, "seq", 1)
        ds, d1 = first_sum(keep_2, got_2, (2,), (), "k_first3", (ay,), 2)
        d_got = swap(ds, "dp", 2)
        cs, c1 = first_sum(keep_3, got_3, (), (0,), "k_first4", (d1,))
        c_got = swap(cs, "seq", 1)
        y1 = out_call((c1,))
        line_a = line_half([line_a], [], 1, "k_line2", (y1,))
        line_b = line_half([(ay, ay_got)], [b1], 0, "k_line3", (line_a[0],), 0, n_packed)
        line_e = line_half([(c1, c_got)], [], 0, "k_line4", (line_b[0],))
        dys, dy = second_sum(d1, d_got, "k_second3", (line_e[0],))
        dy_got = swap(dys, "seq", 1)
        sums_a = line_sums([line_a], (2 * u,), "k_sum1", (dy,), 2.5)
        a_rows = (sums_a, swap(sums_a, "dp", 2))
        line_b = line_half([line_b], [], 1, "k_line5", (sums_a,), 0, n_packed)
        line_e = line_half([line_e], [], 1, "k_line6", (line_b[0],), 2)
        line_c = line_half([(dy, dy_got)], [], 0, "k_line7", (line_e[0],))
        whole = row_sums([a_rows], ((1, 0),), "k_rows1", (line_c[0],))
        sums_b = line_sums([line_b, line_e], (2 * u, u), "k_sum2", (whole,), 1.5)
        b_rows = (sums_b, swap(sums_b, "dp", 2))
        line_c = line_half([line_c], [], 1, "k_line8", (sums_b,), 2)
        sums_c = line_sums([line_c], (u,), "k_sum3", (line_c[0],))
        c_rows = (sums_c, swap(sums_c, "dp", 2))
        whole = row_sums(
            [(whole,), b_rows, c_rows], (None, (1, 0, 0), (1,)), "k_rows2", (sums_c,)
        )
        _, grad_w_in, grad_w_mid, grad_w_out, *vectors = call(
            functools.partial(k_results, u=u), [vec_shape], (place, whole, swap(whole, "dp", 1)), (),
            "k_results", (),
            stores=[((2, 2 * u, inner), F32), ((2, taps, u, inner), F32), ((2, 2 * u, inner), F32),
                    ((2, width), F32), ((2, width), F32), ((2, 2, inner), F32),
                    ((2, 2, inner), F32), ((2, 2, inner), F32), ((2, width), F32)],
        )
        return (
            y1[None], dx[None], grad_w_in, grad_w_mid.swapaxes(2, 3), grad_w_out.swapaxes(1, 2),
            *vectors,
        )

    narrow = vec[:n_narrow].reshape(2, 2, 3, inner)
    wide = vec[n_narrow:].reshape(2, 3, width)
    return (
        y1[None],
        dx[None],
        grad_w_in,
        grad_w_mid,
        grad_w_out,
        wide[:, 0],
        wide[:, 1],
        narrow[:, :, 0],
        narrow[:, :, 1],
        narrow[:, :, 2],
        wide[:, 2],
    )


def solution(mesh):
    row = P("dp", "seq", None)
    return jax.shard_map(
        body,
        mesh=mesh,
        in_specs=(row, P(None, "dp", "seq")) + (P(),) * 9 + (row,),
        out_specs=(
            row,
            row,
            P(None, "seq", None),
            P(None, None, None, "seq"),
            P(None, None, "seq"),
        )
        + (P(),) * 6,
        check_vma=False,
    )
```

```python
import functools

import jax
import jax.numpy as jnp
from jax import lax
from jax.experimental import pallas as pl
from jax.experimental.pallas import tpu as pltpu
from jax.sharding import PartitionSpec as P

DILATION_CLOSE = 4
DILATION_BROAD = 128
EPS = 1e-05
F32 = jnp.float32
BF16 = jnp.bfloat16
VMEM_LIMIT = 18 * 1024 * 1024
HEIGHT = 128
EXP2 = -0.7213475204444817

C0 = 0.3275911 * 0.7071067811865476
POLY = tuple(0.5 * c for c in (0.254829592, -0.284496736, 1.421413741, -1.453152027, 1.061405429))
ROOT_2PI = 0.3989422804014327


def normal_parts(q):
    bell = jnp.exp2((q * EXP2) * q)
    t = pltpu.reciprocal(1.0 + C0 * jnp.abs(q), approx=True)
    h = POLY[4]
    for c in POLY[3::-1]:
        h = h * t + c
    tail = h * t * bell
    return jnp.where(q >= 0, 1.0 - tail, tail), q * bell * ROOT_2PI


def act_forward(v, gain, shift):
    c = v.shape[-1]
    mean = jnp.sum(v, axis=-1, keepdims=True) * (1.0 / c)
    centred = v - mean
    r = lax.rsqrt(jnp.sum(centred * centred, axis=-1, keepdims=True) * (1.0 / c) + EPS)
    n = centred * r
    q = n * gain + shift
    below, slope = normal_parts(q)
    return mean, r, n, q * below, below + slope


def act_backward(f, n, r, d, gain):
    c = f.shape[-1]
    p = f * d
    gp = gain * p
    first = jnp.sum(gp, axis=-1, keepdims=True) * (1.0 / c)
    second = jnp.sum(gp * n, axis=-1, keepdims=True) * (1.0 / c)
    return p, r * (gp - first - n * second)


def fold(v):
    return jnp.sum(v.reshape(v.shape[0] // 8, 8, v.shape[1]), axis=0)


def total(acc):
    return jnp.sum(acc, axis=0, keepdims=True)


def lanes(column):
    return jnp.broadcast_to(column, (column.shape[0], 128))


def strips(rows, height, step, carry=(), unroll=8, first=0):
    turns = rows // (height * unroll)
    if turns <= 1:
        for j in range(rows // height):
            carry = step(pl.ds(first + j * height, height), carry)
        return carry

    def body(i, c):
        for j in range(unroll):
            c = step(pl.ds(pl.multiple_of((i * unroll + j) * height, height), height), c)
        return c

    return lax.fori_loop(0, turns, body, carry)


def staggered(rows, height, *stages):
    parts = [slice(i, i + height) for i in range(0, rows, height)]
    for t in range(len(parts) + len(stages) - 1):
        for i in reversed(range(len(stages))):
            if 0 <= t - i < len(parts):
                stages[i](parts[t - i])


def at_base(at, base):
    if isinstance(base, int) and base == 0:
        return at
    return pl.ds(pl.multiple_of(at.start + base, at.size), at.size)


def dot(a, b):
    return jnp.dot(a, b, preferred_element_type=F32)


def dot_nt(a, b):
    return lax.dot_general(a, b, (((1,), (1,)), ((), ())), preferred_element_type=F32)


class Loads:
    def __init__(self, sources, targets, sems):
        self.targets = targets
        self.copies = [
            pltpu.make_async_copy(src if b is None else src.at[b], dst, sems.at[i])
            for i, ((src, b), dst) in enumerate(zip(sources, targets))
        ]
        self.waiting = set(range(len(targets)))
        for copy in self.copies:
            copy.start()

    def get(self, i):
        if i in self.waiting:
            self.waiting.remove(i)
            self.copies[i].wait()
        return self.targets[i]

    def finish(self):
        for i in sorted(self.waiting):
            self.get(i)


class Stores:
    def __init__(self, held, targets, sems):
        self.held, self.targets, self.sems = held, targets, sems
        self.copies = []

    def put(self, *which, at=None):
        for i in which:
            src, dst = self.held[i], self.targets[i]
            if at is not None:
                src, dst = src.at[at], dst.at[at]
            copy = pltpu.make_async_copy(src, dst, self.sems.at[len(self.copies)])
            copy.start()
            self.copies.append(copy)

    def finish(self):
        for copy in self.copies:
            copy.wait()


def call(
    kernel, outs, args, scratch=(), name=None, deps=(), loads=(), stores=(), offloads=(), parts=1,
    limit=VMEM_LIMIT, cost=0,
):
    n_args, n_loads, n_deps, n_off = len(args), len(loads), len(deps), len(offloads)
    n_outs, n_stores = len(outs), len(stores)
    loaded = [(a.shape if b is None else a.shape[1:], a.dtype) for a, b, _ in loads]
    kept = [i for i, (_, _, keep) in enumerate(loads) if keep]
    brief = [i for i in range(n_loads) if i not in kept]
    out_shape = [pltpu.VMEM(s, t) for s, t in outs] + [pltpu.HBM(s, t) for s, t in stores]
    out_shape += [pltpu.VMEM(*loaded[i]) for i in kept]
    out_shape += [pltpu.HBM(a.shape, a.dtype) for a in offloads]

    def run(*refs):
        def take(n):
            nonlocal refs
            first, refs = refs[:n], refs[n:]
            return first

        ins, going, sources, _ = take(n_args), take(n_off), take(n_loads), take(n_deps)
        results, stored, held, gone = take(n_outs), take(n_stores), take(len(kept)), take(n_off)
        targets = dict(zip(kept, held))
        scr = list(refs)
        more = {}
        if n_loads:
            sems = scr.pop()
            for i in reversed(brief):
                targets[i] = scr.pop()
            sources = [(r, b) for r, (_, b, _) in zip(sources, loads)]
            more["coming"] = Loads(sources, [targets[i] for i in range(n_loads)], sems)
        if n_off:
            leaving = Stores(going, gone, scr.pop())
            leaving.put(*range(n_off))
        if n_stores:
            sems = scr.pop()
            held = [scr.pop() for _ in stores][::-1]
            more["keeping"] = Stores(held, stored, sems)
        kernel(*ins, *results, *scr, **more)
        for part in more.values():
            part.finish()
        if n_off:
            leaving.finish()

    hbm, vmem = pl.BlockSpec(memory_space=pltpu.HBM), pl.BlockSpec(memory_space=pltpu.VMEM)
    specs = [vmem] * (n_args + n_off) + [hbm] * n_loads
    specs += [pl.BlockSpec(memory_space=pl.ANY)] * n_deps
    out_specs = [vmem] * n_outs + [hbm] * n_stores + [vmem] * len(kept) + [hbm] * n_off
    scratch = list(scratch)
    if n_stores:
        scratch += [pltpu.VMEM(s, t) for s, t in stores]
        scratch += [pltpu.SemaphoreType.DMA((n_stores * parts,))]
    if n_off:
        scratch += [pltpu.SemaphoreType.DMA((n_off,))]
    if n_loads:
        scratch += [pltpu.VMEM(*loaded[i]) for i in brief] + [pltpu.SemaphoreType.DMA((n_loads,))]
    return pl.pallas_call(
        run,
        out_shape=out_shape,
        in_specs=specs,
        out_specs=out_specs,
        scratch_shapes=scratch,
        compiler_params=pltpu.CompilerParams(vmem_limit_bytes=limit),
        cost_estimate=pl.CostEstimate(flops=1 + int(cost * 1.15e9), bytes_accessed=1, transcendentals=0),
        name=name,
    )(
        *[pltpu.with_memory_space_constraint(a, pltpu.VMEM) for a in (*args, *offloads)],
        *[pltpu.with_memory_space_constraint(a, pltpu.HBM) for a, _, _ in loads],
        *deps,
    )


NEAR, CUT, LOW_0, LOW_1, HIGH_1, CORE, BIT_X, LINE = range(8)


def find_marks(bounds, place):
    rows = bounds.shape[2]
    first = lax.axis_index("seq") * rows
    marks = (bounds[1, 0:1, 0:1], bounds[0, 0:1, 0:1], bounds[0, 0:1, rows - 1 :], bounds[1, 0:1, rows - 1 :])
    for row, v in zip((CUT, LOW_0, LOW_1, HIGH_1), marks):
        place[row : row + 1] = jnp.broadcast_to(v - first, (1, 128))


def find_place(place):
    seq, dp = lax.axis_index("seq"), lax.axis_index("dp")
    for row, v in ((NEAR, seq & 1), (CORE, dp & 1), (BIT_X, dp >> 1), (LINE, seq >> 1)):
        place[row : row + 1] = jnp.full((1, 128), v, jnp.int32)


def base_of(place, near, rows):
    odd = place[NEAR, 0]
    return rows * (1 - odd) if near else rows * odd


def wide_act(x, base, gain, shift, a1, d1, stat, part):
    def wide(at, c):
        mean, r, n, a, d = act_forward(x[at_base(at, base)].astype(F32), gain, shift)
        a1[at], d1[at] = a.astype(BF16), d.astype(BF16)
        stat[0, at], stat[1, at] = lanes(mean), lanes(r)
        return c

    strips(part.stop - part.start, 32, wide, first=part.start)


def narrow_act(z, gain, shift, a, n, d, stat, part):
    def narrow(at, c):
        _, r, nn, aa, dd = act_forward(z[at], gain, shift)
        n[at], d[at], a[at] = nn.astype(BF16), dd.astype(BF16), aa.astype(BF16)
        stat[at] = lanes(r)
        return c

    strips(part.stop - part.start, 32, narrow, first=part.start)


def windows(place, near, own, other, halo, win, pad, step):
    rows, width = own.shape
    taps = win.shape[1] // width
    rim = (pad.shape[0] - rows) // 2
    pad[rim : rim + rows] = own[...].astype(pad.dtype)
    lower = place[NEAR, 0] == (1 if near else 0)

    @pl.when(lower)
    def _():
        pad[0:rim] = halo[halo.shape[0] - rim :].astype(pad.dtype)
        pad[rim + rows :] = other[0:rim].astype(pad.dtype)

    @pl.when(jnp.logical_not(lower))
    def _():
        pad[0:rim] = other[rows - rim :].astype(pad.dtype)
        pad[rim + rows :] = halo[0:rim].astype(pad.dtype)

    base = base_of(place, near, rows)
    cut, low_0, low_1, high_1 = (place[i : i + 1] for i in (CUT, LOW_0, LOW_1, HIGH_1))
    height = 64

    def fill(part):
        for i in range(part.start, part.stop, height):
            rows_at(i)

    def rows_at(i):
        t = lax.broadcasted_iota(jnp.int32, (height, 128), 0) + (base + i)
        first = t < cut
        low = jnp.where(first, low_0, low_1)
        high = jnp.where(first, cut, high_1)
        for k in range(taps):
            offset = (k - taps // 2) * step
            m = jnp.where((t + offset >= low) & (t + offset < high), 1.0, 0.0).astype(pad.dtype)
            m = jnp.concatenate([m] * (width // 128), axis=1)
            start = rim + offset + i
            win[i : i + height, k * width : (k + 1) * width] = (
                pad[start : start + height] * m
            ).astype(BF16)

    return fill


def put_edge(edge, v, place, near):
    n = edge.shape[0]
    lower = place[NEAR, 0] == (1 if near else 0)

    @pl.when(lower)
    def _():
        edge[...] = v[0:n]

    @pl.when(jnp.logical_not(lower))
    def _():
        edge[...] = v[v.shape[0] - n :]


def first_half(x, base, gw, sw, w_in, bn, gn, sn, a1, d1, stat1, a2, n2, d2, r2, z, keeping):
    rows = a1.shape[0]

    def wide(p):
        wide_act(x, base, gw(), sw(), a1, d1, stat1, p)
        if p.stop == rows:
            keeping.put(*FIRST_STORES[len(keeping.held)])

    def inner(p):
        z[p] = dot(a1[p], w_in()[...]) + bn()

    def narrow(p):
        narrow_act(z, gn(), sn(), a2, n2, d2, r2, p)

    return wide, inner, narrow


FIRST_STORES = {3: (0, 1, 2), 7: (4, 5, 6)}


def k_in_near(place, a2, n2, d2, r2, edge, z, *, coming, keeping):
    a1, d1, stat1 = keeping.held
    find_place(place)
    x = coming.get(0)
    staggered(a1.shape[0], a1.shape[0], *first_half(
        x, base_of(place, True, a1.shape[0]), lambda: coming.get(1)[0:1], lambda: coming.get(2)[0:1],
        lambda: coming.get(3), lambda: coming.get(6)[0, 0:1], lambda: coming.get(4)[0, 0:1],
        lambda: coming.get(5)[0, 0:1], a1, d1, stat1, a2, n2, d2, r2, z, keeping,
    ))
    put_edge(edge, a2, place, True)
    find_marks(coming.get(9), place)


def k_in_far(place, x, gw, sw, gn, sn, bn, a2, n2, d2, r2, edge, z, *, coming, keeping):
    a1, d1, stat1 = keeping.held
    staggered(a1.shape[0], a1.shape[0], *first_half(
        x, base_of(place, False, a1.shape[0]), lambda: gw[0:1], lambda: sw[0:1],
        lambda: coming.get(0), lambda: bn[0, 0:1], lambda: gn[0, 0:1], lambda: sn[0, 0:1],
        a1, d1, stat1, a2, n2, d2, r2, z, keeping,
    ))
    put_edge(edge, a2, place, False)


def k_mid(
    place, x, own, other, halo, w_mid, gw, sw, bw, gn, sn, bn,
    a3, r3, a2, n2, d2, r2, pad, z, z1, *, near, step, coming, keeping,
):
    rows, width = own.shape
    win, n3, d3, y, a1, d1, stat1 = keeping.held
    fill = windows(place, near, own, other, halo, win, pad, step)
    base = base_of(place, near, rows)
    weights = w_mid[...].reshape(win.shape[1], width)

    def conv(p):
        fill(p)
        z[p] = dot(win[p], weights) + bn[0, 1:2]
        if p.stop == rows:
            keeping.put(0)

    def narrow(p):
        narrow_act(z, gn[0, 1:2], sn[0, 1:2], a3, n3, d3, r3, p)
        if p.stop == rows:
            keeping.put(1, 2)

    def outer(p):
        n = p.stop - p.start
        old = x[pl.ds(pl.multiple_of(base + p.start, n), n)].astype(F32)
        y[p] = old + dot(a3[p], coming.get(0)[...]) + bw[0:1]
        if p.stop == rows:
            keeping.put(3)

    staggered(rows, HEIGHT, conv, narrow, outer, *first_half(
        y, 0, lambda: gw[1:2], lambda: sw[1:2], lambda: coming.get(1), lambda: bn[1, 0:1],
        lambda: gn[1, 0:1], lambda: sn[1, 0:1], a1, d1, stat1, a2, n2, d2, r2, z1, keeping,
    ))


def put_wide(vec, row, acc):
    inner = vec.shape[1]
    for i in range(acc.shape[1] // inner):
        vec[row + i : row + i + 1] += total(acc[:, i * inner : (i + 1) * inner])


def k_flow(e, w_out, f, vec, *, row, coming):
    f[...] = dot_nt(e[...], w_out[...])
    vec[...] = jnp.zeros_like(vec)

    def step(at, acc):
        return acc + fold(e[at].astype(F32))

    put_wide(vec, row, strips(e.shape[0], 32, step, jnp.zeros((8, e.shape[1]), F32)))


def k_conv(
    place, vec_in, own, other, halo, w_mid, gn, sn, bn, f, a3, e2, vec, win, pad, z, *, near, step, row
):
    rows, width = own.shape
    windows(place, near, own, other, halo, win, pad, step)(slice(0, own.shape[0]))
    z[...] = dot(win[...], w_mid[...].reshape(win.shape[1], width)) + bn[1, 1:2]
    gain = gn[1, 1:2]
    base = base_of(place, near, rows)

    def narrow(at, c):
        _, r, n, a, d = act_forward(z[at], gain, sn[1, 1:2])
        a3[at] = a.astype(BF16)
        p, v = act_backward(f[at_base(at, base)], n, r, d, gain)
        e = v.astype(BF16)
        e2[at] = e
        return c[0] + fold(p * n), c[1] + fold(p), c[2] + fold(e.astype(F32))

    vec[...] = vec_in[...]
    zero = jnp.zeros((8, width), F32)
    for i, acc in enumerate(strips(rows, 32, narrow, (zero,) * 3)):
        vec[row + i : row + i + 1] += total(acc)


def k_out(place, a_n, a_f, bw, token, *, coming, keeping):
    half = a_n.shape[0]
    token[...] = jnp.zeros_like(token)
    (y,) = keeping.held
    w_out = coming.get(0)
    for near, a in ((True, a_n), (False, a_f)):
        at = pl.ds(pl.multiple_of(base_of(place, near, half), half), half)
        y[at] = dot(a[...], w_out[...]) + bw[1:2] + coming.get(1 if near else 2)[...]
        keeping.put(0, at=at)


def back_narrow(f, n, d, r, gain, e_out, vec, row):
    rows, width = f.shape

    def step(at, c):
        nn = n[at].astype(F32)
        p, v = act_backward(f[at], nn, r[at][:, 0:1], d[at].astype(F32), gain)
        e = v.astype(BF16)
        e_out[at] = e
        return c[0] + fold(p * nn), c[1] + fold(p), c[2] + fold(e.astype(F32))

    zero = jnp.zeros((8, width), F32)
    for i, acc in enumerate(strips(rows, 32, step, (zero,) * 3)):
        vec[row + i : row + i + 1] += total(acc)


def back_wide(f, x, x_base, stat, d, gain, dy, dy_base, out, out_base, cast, vec, row, cast_row):
    rows, width = f.shape

    def step(at, c):
        r = stat[1, at][:, 0:1]
        n = (x[at_base(at, x_base)].astype(F32) - stat[0, at][:, 0:1]) * r
        p, v = act_backward(f[at], n, r, d[at].astype(F32), gain)
        dx = dy[at_base(at, dy_base)].astype(F32) + v
        out[at_base(at, out_base)] = dx
        sums = (c[0] + fold(p * n), c[1] + fold(p))
        if cast is not None:
            e = dx.astype(BF16)
            cast[at] = e
            sums += (c[2] + fold(e.astype(F32)),)
        return sums

    zero = jnp.zeros((8, width), F32)
    sums = strips(rows, 32, step, (zero,) * (2 if cast is None else 3), 8)
    put_wide(vec, row, sums[0])
    put_wide(vec, row + width // vec.shape[1], sums[1])
    if cast is not None:
        put_wide(vec, cast_row, sums[2])


def flow_two(win, w_mid, z):
    taps, width = w_mid.shape[0], w_mid.shape[1]
    for j in range(taps):
        part = dot_nt(win[:, j * width : (j + 1) * width], w_mid[taps - 1 - j])
        if j == 0:
            z[...] = part
        else:
            z[...] += part


def k_back1(
    place, vec_in, own, other, halo, w_mid, gw, gn,
    e1, e3, e2, edge, vec, win, pad, z, f1, *, near, step, rows_of, coming, keeping,
):
    vec[...] = vec_in[...]
    windows(place, near, own, other, halo, win, pad, step)(slice(0, own.shape[0]))
    flow_two(win, w_mid, z)
    n2, d2, r2, w_in = (coming.get(i) for i in range(4))
    back_narrow(z, n2, d2, r2, gn[1, 0:1], e1, vec, rows_of[0])
    f1[...] = dot_nt(e1[...], w_in[...])
    base = base_of(place, near, own.shape[0])
    (dx,) = keeping.held
    x, d1, stat1, dy = (coming.get(i) for i in range(4, 8))
    back_wide(f1, x, 0, stat1, d1, gw[1:2], dy, base, dx, 0, e3, vec, rows_of[1], rows_of[3])
    keeping.put(0)
    w_out, n3, d3, r3 = (coming.get(i) for i in range(8, 12))
    z[...] = dot_nt(e3[...], w_out[...])
    back_narrow(z, n3, d3, r3, gn[0, 1:2], e2, vec, rows_of[2])
    put_edge(edge, e2, place, near)


def k_back0(
    place, vec_in, own, other, halo, w_mid, gn, e1, vec, win, pad, z, *, near, step, row, coming
):
    vec[...] = vec_in[...]
    halo = halo.at[pl.ds(halo.shape[0] - 16, 16)]
    windows(place, near, own, other, halo, win, pad, step)(slice(0, own.shape[0]))
    flow_two(win, w_mid, z)
    n2, d2, r2 = (coming.get(i) for i in range(3))
    back_narrow(z, n2, d2, r2, gn[0, 0:1], e1, vec, row)


def k_dx(place, vec_in, gw, e1_n, e1_f, vec, f1, *, row, coming, keeping):
    vec[...] = vec_in[...]
    half = e1_n.shape[0]
    (out,) = keeping.held
    w_in, x = coming.get(0), coming.get(1)
    for near, e1 in ((True, e1_n), (False, e1_f)):
        f1[...] = dot_nt(e1[...], w_in[...])
        d, stat, dy = (coming.get(i + (0 if near else 3)) for i in (2, 3, 4))
        base = base_of(place, near, half)
        back_wide(f1, x, base, stat, d, gw[0:1], dy, 0, out, base, None, vec, row, None)
        keeping.put(0, at=pl.ds(pl.multiple_of(base, half), half))


def k_split(place, *refs, jobs, parts, side, coming=None):
    n_outs = sum(parts)
    outs, turned = list(refs[-1 - n_outs : -1]), refs[-1]
    refs = refs[: -1 - n_outs]
    _, shards, _, u, rows = turned.shape
    inner = outs[0].shape[-1]

    def ref(i):
        return refs[i] if i < len(refs) else coming.get(i - len(refs))

    def whole(places, at=slice(None)):
        if len(places) == 1:
            half = rows // 2
            bases = [base_of(place, near, half) for near in (True, False)]
            parts = [ref(places[0])[pl.ds(pl.multiple_of(b, half), half)] for b in bases]
        else:
            parts = [ref(i)[:, at] for i in places]
        return jnp.concatenate(parts, axis=0)

    core = place[CORE, 0] ^ side
    kept = {}
    halves = 0
    for n, (kind, left, right, j) in zip(parts, jobs):
        here, outs = outs[:n], outs[n:]

        def put(product):
            height = product.shape[0] // n
            for i, out in enumerate(here):
                out[...] = product[i * height : (i + 1) * height]

        if kind == "half":
            turned[halves] = whole(left).T.reshape(turned.shape[1:])
            part = turned[halves, :, core].reshape(shards * u, rows)
            put(dot(part, whole(right)).astype(BF16))
            halves += 1
            continue
        if left not in kept:
            kept[left] = whole(left).T
        if kind == "taps":
            at = pl.ds(pl.multiple_of((j + 2 * core) * inner, 128), inner)
            put(dot(kept[left], whole(right, at)).astype(BF16))
            continue
        tap, before = j

        @pl.when(core == 0)
        def _():
            put(ref(before)[...])

        @pl.when(core != 0)
        def _():
            at = slice(tap * inner, (tap + 1) * inner)
            put(dot(kept[left], whole(right, at)).astype(BF16))


def k_tap(e_n, e_f, win_n, win_f, out, *, tap):
    inner = out.shape[-1]
    at = slice(tap * inner, (tap + 1) * inner)
    left = jnp.concatenate([e_n[...], e_f[...]], axis=0).T
    right = jnp.concatenate([win_n[:, at], win_f[:, at]], axis=0)
    out[...] = dot(left, right).astype(BF16)


def added(*parts):
    first, *rest = [p.astype(F32) for p in parts]
    for p in rest:
        first = first + p
    return first


def k_first(place, *refs, pairs, singles, edge):
    refs = list(refs)
    x, y = place[BIT_X, 0], place[NEAR, 0]

    def take(n):
        first = refs[:n]
        del refs[:n]
        return first

    ins = [(take(1)[0], take(n)) for two_units in pairs for n in two_units]
    ins += [(take(1)[0], take(n)) for n in singles]
    rim = take(1)[0] if edge else None

    def add_rows(a, parts, out):
        height = a.shape[0] // len(parts)
        for i, b in enumerate(parts):

            def step(k, c):
                here = pl.ds(pl.multiple_of(k * 80, 80), 80)
                at = pl.ds(pl.multiple_of(i * height + k * 80, 80), 80)
                out[at] = added(a[at], b[here]).astype(BF16)
                return c

            lax.fori_loop(0, height // 80, step, 0)

    for i in range(len(pairs)):
        (a0, b0), (a1, b1) = ins[2 * i : 2 * i + 2]
        send, stay = take(2)

        @pl.when(x == 0)
        def _():
            add_rows(a1, b1, send)
            add_rows(a0, b0, stay)

        @pl.when(x != 0)
        def _():
            add_rows(a0, b0, send)
            add_rows(a1, b1, stay)

    for out, side in zip(refs, (1 - y, y)):
        at = 0
        for a, parts in ins[2 * len(pairs) :]:
            u = a.shape[2]
            each = a.shape[0] // len(parts)
            for k in range(a.shape[0]):
                b = parts[k // each]
                out[at : at + u] = added(a[k, side], b[k % each, side]).astype(BF16)
                at += u
    if edge:
        refs[0][at:] = rim[...]


def k_second(place, a, b, *refs, extra):
    if extra:
        *vec, more_a, more_b, send, stay, more = refs
        more[...] = added(more_a[...], more_b[...]).astype(BF16)
    else:
        vec, (send, stay) = (), refs
    mine = place[NEAR, 0]
    u = a.shape[2]
    for out, side in ((send, 1 - mine), (stay, mine)):

        def step(k, c):
            at = pl.ds(pl.multiple_of(k * u, u), u)
            out[at] = added(a[k, side], b[k, side]).astype(BF16)
            return c

        lax.fori_loop(0, 4, step, 0)
    if vec:
        pack(vec[0][...], send, stay, at=4 * u)


def pack(v, *outs, at):
    n = v.shape[0]
    upper = v.astype(BF16)
    lower = (v - upper.astype(F32)).astype(BF16)
    for out in outs:
        out[at : at + n], out[at + n : at + 2 * n] = upper, lower


def unpack(ref, at):
    n = (ref.shape[0] - at) // 2
    return ref[at : at + n].astype(F32) + ref[at + n : at + 2 * n].astype(F32)


def k_line(place, *refs, sums, wholes, packed, bit, u):
    mine = (place[LINE, 0] >> bit) & 1
    arrays = [refs[2 * i : 2 * i + 2] for i in range(sums)]
    arrays += [refs[2 * sums + i : 2 * sums + i + 1] for i in range(wholes)]
    send, stay = refs[2 * sums + wholes :]
    for out, side in ((send, 1 - mine), (stay, mine)):
        at = 0
        for i, parts in enumerate(arrays):
            rows = parts[0].shape[0] - (packed if i == 0 else 0)
            for j in range(rows // (2 * u)):
                part = pl.ds(pl.multiple_of((2 * j + side) * u, u), u)
                out[at : at + u] = added(*[p[part] for p in parts]).astype(BF16)
                at += u
    if packed:
        a, b = arrays[0]
        n = a.shape[0] - packed
        pack(unpack(a, n) + unpack(b, n), send, stay, at=send.shape[0] - packed)


def k_sum(place, *refs, rows):
    out = refs[-1]
    at = 0
    for i, n in enumerate(rows):
        a, b = refs[2 * i], refs[2 * i + 1]
        out[at : at + n] = added(a[0:n], b[0:n]).astype(BF16)
        at += n
    if refs[0].shape[0] > rows[0]:
        pack(unpack(refs[0], rows[0]) + unpack(refs[1], rows[0]), out, at=at)


def k_rows(place, *refs, splits, u):
    *refs, out = refs
    x = place[BIT_X, 0]
    at = 0
    refs = list(refs)
    for split in splits:
        if split is None:
            ready = refs.pop(0)
            out[at : at + ready.shape[0]] = ready[...]
            at += ready.shape[0]
            continue
        mine, got = refs.pop(0), refs.pop(0)
        for k, apart in enumerate(split):
            here = slice(k * u, (k + 1) * u)
            if apart:
                base = pl.multiple_of(at + x * u, u)
                other = pl.multiple_of(at + (1 - x) * u, u)
                out[pl.ds(base, u)], out[pl.ds(other, u)] = mine[here], got[here]
                at += 2 * u
            else:
                out[at : at + u] = added(mine[here], got[here]).astype(BF16)
                at += u
        if mine.shape[0] > len(split) * u:
            n = len(split) * u
            pack(unpack(mine, n) + unpack(got, n), out, at=out.shape[0] - (mine.shape[0] - n))


def k_share(place, ref, *refs, side, u):
    vectors, n_vec = (), 0
    if side:
        mine, *refs = refs
        refs = refs[3:]
        n_vec = 6
    out_in, out_mid, out_out = refs[:3]
    vectors, refs = refs[3 : 3 + n_vec], refs[3 + n_vec :]
    stage, held, sems = refs[0], refs[1:-1], refs[-1]
    c = place[CORE, 0] ^ side
    rows = pl.ds(pl.multiple_of(c * u, u), u)
    copies = []

    def put(src, dst):
        copies.append(pltpu.make_async_copy(src, dst, sems.at[len(copies)]))
        copies[-1].start()

    def units(i, n=1):
        for k in range(i, i + n):
            stage[k] = ref[k * u : (k + 1) * u].astype(F32)
        return stage.at[i] if n == 1 else stage.at[i : i + n]

    put(units(0, 2), out_mid.at[1, pl.ds(2 * c, 2)])
    put(units(2), out_out.at[1, rows])
    put(units(3, 2), out_mid.at[0, pl.ds(2 * c, 2)])
    put(units(5), out_mid.at[1 - c, 4])
    put(units(6), out_in.at[0, rows])
    put(units(7), out_in.at[1, rows])
    put(units(8), out_out.at[0, rows])
    if side:
        vec, gw, sw, gn, sn, bn, bw = held
        vec[...] = unpack(mine, 9 * u) + unpack(ref, 9 * u)
        inner = vec.shape[1]
        two = gw.shape[1] // inner
        for block in range(2):
            for i in range(2):
                row = 3 * (2 * block + i)
                for j, out in enumerate((gn, sn, bn)):
                    out[block, i : i + 1] = vec[row + j : row + j + 1]
            for j, out in enumerate((gw, sw, bw)):
                for k in range(two):
                    row = 12 + (3 * block + j) * two + k
                    out[block : block + 1, k * inner : (k + 1) * inner] = vec[row : row + 1]
        for src, dst in zip((gw, sw, gn, sn, bn, bw), vectors):
            put(src, dst)
    for copy in copies:
        copy.wait()


def share(side, args, before, shapes, vector_shapes, vec_shape, u):
    inner = shapes[0][-1]
    vmem, hbm = pl.BlockSpec(memory_space=pltpu.VMEM), pl.BlockSpec(memory_space=pltpu.HBM)
    outs = list(shapes) + list(vector_shapes)
    held = [pltpu.VMEM(s, F32) for s in ([vec_shape] + list(vector_shapes) if side else [])]
    return pl.pallas_call(
        functools.partial(k_share, side=side, u=u),
        out_shape=[pltpu.HBM(s, F32) for s in outs],
        in_specs=[vmem] * len(args) + [hbm] * len(before),
        out_specs=[hbm] * len(outs),
        scratch_shapes=[pltpu.VMEM((9, u, inner), F32), *held, pltpu.SemaphoreType.DMA((7 + len(vector_shapes),))],
        input_output_aliases={len(args) + i: i for i in range(len(before))},
        compiler_params=pltpu.CompilerParams(vmem_limit_bytes=VMEM_LIMIT),
        cost_estimate=pl.CostEstimate(flops=1, bytes_accessed=1, transcendentals=0),
        name="k_share",
    )(
        *[pltpu.with_memory_space_constraint(a, pltpu.VMEM) for a in args],
        *[pltpu.with_memory_space_constraint(a, pltpu.HBM) for a in before],
    )


def k_plus(a, b, out):
    out[...] = added(a[...], b[0 : a.shape[0]]).astype(BF16)


def k_nothing(*refs, coming):
    pass


def swap(v, axis, bits):
    count = lax.axis_size(axis)
    return lax.ppermute(v, axis, [(i, i ^ bits) for i in range(count)])


def to_near(v):
    return swap(v, "seq", 1)


def to_far(v):
    count = lax.axis_size("seq")
    pairs = [(i, i + 1) for i in range(1, count - 1, 2)]
    return lax.ppermute(v, "seq", pairs + [(j, i) for i, j in pairs])


def dot_tn(a, b):
    return lax.dot_general(a, b, (((0,), (0,)), ((), ())), preferred_element_type=F32)


def plain_weights(a1, e1, win, e2, a3, e3):
    taps = win.shape[1] // e2.shape[1]
    grad_mid = dot_tn(win, e2).reshape(taps, e2.shape[1], e2.shape[1])
    shares = (
        lax.psum_scatter(dot_tn(a1, e1), "seq", scatter_dimension=0, tiled=True),
        lax.psum_scatter(grad_mid, "seq", scatter_dimension=2, tiled=True),
        lax.psum_scatter(dot_tn(a3, e3), "seq", scatter_dimension=1, tiled=True),
    )
    return [lax.psum(v.astype(BF16), "dp").astype(F32) for v in shares]


def body(
    tokens, bounds, w_in, w_mid, w_out, gain_wide, shift_wide, gain_narrow, shift_narrow,
    bias_narrow, bias_wide, cotangent,
):
    x0 = tokens[0]
    cot = cotangent[0]
    rows, width = x0.shape
    taps, inner = w_mid.shape[1], w_mid.shape[2]
    shards = lax.axis_size("seq")
    u = inner // shards
    two = width // inner
    half = rows // 2
    close, broad = DILATION_CLOSE, DILATION_BROAD

    wide_h, narrow_h, column = (half, width), (half, inner), ((half, 128), F32)
    win_h = ((half, taps * inner), BF16)
    act_wide = [(wide_h, BF16), (wide_h, BF16), ((2, half, 128), F32)]
    act_narrow = [(narrow_h, BF16), (narrow_h, BF16), (narrow_h, BF16), column]
    edge = ((16, inner), BF16)
    z = pltpu.VMEM(narrow_h, F32)
    f1 = pltpu.VMEM(wide_h, F32)
    win_scratch = pltpu.VMEM(*win_h)
    pad_0 = pltpu.VMEM((half + 32, inner), F32)
    pad_1 = pltpu.VMEM((half + 4 * broad, inner), BF16)
    n_narrow = 12
    vec_shape = ((n_narrow + 6 * two, inner), F32)

    def row_narrow(b, i):
        return 3 * (2 * b + i)

    def row_wide(b, i):
        return n_narrow + (3 * b + i) * two

    def brief(*arrays):
        return tuple((a, None, False) for a in arrays)

    place, a2_n, *p_n, edge_n, a1_n, d1_n, stat_n, x, gw, sw, gn, sn, bn, bw, w_mid_0 = call(
        k_in_near, [((8, 128), jnp.int32)] + act_narrow + [edge], (), [z], "k_in",
        loads=((x0, None, True), (gain_wide, None, True), (shift_wide, None, True), (w_in, 0, False),
               (gain_narrow, None, True), (shift_narrow, None, True), (bias_narrow, None, True),
               (bias_wide, None, True), (w_mid, 0, True), (bounds, None, False)),
        stores=act_wide, cost=4,
    )
    halo_n = to_near(edge_n)
    a2_f, *p_f, edge_f, a1_f, d1_f, stat_f, p1, p2, p3 = call(
        k_in_far, act_narrow + [edge], (place, x, gw, sw, gn, sn, bn), [z], "k_in", (edge_n,),
        loads=((w_in, 0, False),), stores=act_wide, offloads=p_n, cost=4,
    )
    p_n = (p1, p2, p3)
    halo_f = to_far(edge_f)

    def mid_call(near, own, other, halo, deps, loads, offloads):
        return call(
            functools.partial(k_mid, near=near, step=close),
            [(narrow_h, BF16), column] + act_narrow,
            (place, x, own, other, halo, w_mid_0, gw, sw, bw, gn, sn, bn),
            [pad_0, z, z], "k_mid", deps, ((w_out, 0, False), (w_in, 1, False)) + loads,
            [win_h, (narrow_h, BF16), (narrow_h, BF16), (wide_h, F32)] + act_wide, offloads, cost=8,
        )

    a3_n, r3_n, b2_n, *q_n = mid_call(True, a2_n, a2_f, halo_n, (), (), p_f)
    s_n, p_f = q_n[3:10], q_n[10:]
    halo_n = to_near(b2_n)
    a3_f, r3_f, b2_f, *q_f = mid_call(
        False, a2_f, a2_n, halo_f, (b2_n,), ((w_out, 1, True), (cot, None, True)),
        (a3_n, r3_n, *q_n[:3]),
    )
    s_f, (w_out_1, cot_v), q_n = q_f[3:10], q_f[10:12], q_f[12:]
    halo_f = to_far(b2_f)
    f3, vec, w_mid_1, *q_f = call(
        functools.partial(k_flow, row=row_wide(1, 2)),
        [((rows, inner), F32), vec_shape], (cot_v, w_out_1), (), "k_flow",
        loads=((w_mid, 1, True),), offloads=(a3_f, r3_f, *q_f[:3]), cost=3,
    )

    def conv_call(near, vec, own, other, halo):
        return call(
            functools.partial(k_conv, near=near, step=broad, row=row_narrow(1, 1)),
            [(narrow_h, BF16), (narrow_h, BF16), vec_shape, win_h],
            (place, vec, own, other, halo, w_mid_1, gn, sn, bn, f3),
            [pad_1, z], "k_conv", cost=3,
        )

    c3_n, e2_n, vec, win_n = conv_call(True, vec, b2_n, b2_f, halo_n)
    halo_n = to_near(e2_n)
    c3_f, e2_f, vec, win_f = conv_call(False, vec, b2_f, b2_n, halo_f)
    halo_f = to_far(e2_f)

    fast = shards == 8 and u % 16 == 0
    unit = (inner, inner)
    part = (u, inner)

    def split_call(jobs, args, loads, side, name, deps, cost=0, parts=None):
        parts = parts or (1,) * len(jobs)
        halves = sum(kind == "half" for kind, *_ in jobs)
        turned = pltpu.VMEM((halves, shards, 2, u, rows), BF16)
        return call(
            functools.partial(k_split, jobs=jobs, side=side, parts=parts),
            [((inner // n, inner), BF16) for n in parts for _ in range(n)],
            (place, *args), [turned], name, deps, loads, cost=cost,
        )

    def swap_cores(units, parts=None):
        got = [swap(v, "dp", 1) for v in units]
        parts = parts or (1,) * len(units)
        return [tuple(got.pop(0) for _ in range(n)) for n in parts]

    def first_sum(keep, got, pairs, singles, name, deps, cost=0, edge=()):
        args = []
        for i in [j for pair in pairs for j in (pair, pair + 1)]:
            args += [keep[i], *got[i]]
        for i in singles:
            args += [v.reshape(-1, 2, u, inner) for v in (keep[i], *got[i])]
        outs = [(unit, BF16)] * (2 * len(pairs))
        n = 4 * u * len(singles)
        if singles:
            outs += [((n + sum(v.shape[0] for v in edge), inner), BF16), ((n, inner), BF16)]
        kernel = functools.partial(
            k_first, pairs=tuple((len(got[i]), len(got[i + 1])) for i in pairs),
            singles=tuple(len(got[i]) for i in singles), edge=bool(edge),
        )
        return call(kernel, outs, (place, *args, *edge), (), name, deps, cost=cost)

    n_packed = 2 * vec_shape[0][0]

    def second_sum(stay, got, name, deps, cost=0, extra=()):
        views = [v.reshape(4, 2, u, inner) for v in (stay, got)]
        n = 4 * u + (n_packed if extra else 0)
        outs = [((n, inner), BF16)] * 2 + ([((4 * u, inner), BF16)] if extra else [])
        kernel = functools.partial(k_second, extra=bool(extra))
        return call(kernel, outs, (place, *views, *extra), (), name, deps, cost=cost)

    def line_half(pairs, wholes, bit, name, deps, cost=0, packed=0):
        arrays = [pair[0] for pair in pairs] + list(wholes)
        n = sum(a.shape[0] for a in arrays) - packed
        n = n // 2 + packed
        kernel = functools.partial(k_line, sums=len(pairs), wholes=len(wholes), packed=packed, bit=bit, u=u)
        send, stay = call(
            kernel, [((n, inner), BF16)] * 2, (place, *[v for pair in pairs for v in pair], *wholes),
            (), name, deps, cost=cost,
        )
        return stay, swap(send, "seq", 2 << bit)

    def line_sums(pairs, rows, name, deps, cost=0):
        n = sum(rows) + pairs[0][0].shape[0] - rows[0]
        return call(
            functools.partial(k_sum, rows=rows), [((n, inner), BF16)],
            (place, *[v for pair in pairs for v in pair]), (), name, deps, cost=cost,
        )[0]

    def row_sums(pairs, splits, name, deps):
        n = sum(pair[0].shape[0] for pair in pairs) + u * sum(sum(split or ()) for split in splits)
        return call(
            functools.partial(k_rows, splits=splits, u=u), [((n, inner), BF16)],
            (place, *[v for pair in pairs for v in pair]), (), name, deps,
        )[0]

    def back1_call(near, vec, own, other, halo, q, s, deps, more=()):
        return call(
            functools.partial(
                k_back1, near=near, step=broad,
                rows_of=(row_narrow(1, 0), row_wide(1, 0), row_narrow(0, 1), row_wide(0, 2)),
            ),
            [(narrow_h, BF16), (wide_h, BF16), (narrow_h, BF16), edge, vec_shape],
            (place, vec, own, other, halo, w_mid_1, gw, gn),
            [win_scratch, pad_1, z, f1], "k_back1", deps, stores=[(wide_h, F32)], cost=5 if near else 2,
            loads=(*brief(*q[2:5]), (w_in, 1, False), *brief(s[3], s[5], s[6], cot),
                   (w_out, 0, False), *brief(s[1], s[2], q[1]), *more),
        )

    def back0_call(near, vec, own, other, halo, p, deps, loads, cost=0):
        return call(
            functools.partial(k_back0, near=near, step=close, row=row_narrow(0, 0)),
            [(narrow_h, BF16), vec_shape], (place, vec, own, other, halo, w_mid_0, gn),
            [win_scratch, pad_0, z], "k_back0", deps, loads=brief(*p) + loads, cost=cost,
        )

    def out_call(deps):
        return call(
            k_out, [((8, 128), F32)], (place, c3_n, c3_f, bw), (), "k_out", deps,
            loads=((w_out, 1, False), *brief(s_n[3], s_f[3])), stores=[((rows, width), F32)], parts=2,
        )

    def dx_call(vec, deps):
        return call(
            functools.partial(k_dx, row=row_wide(0, 0)), [vec_shape],
            (place, vec, gw, e1_n0, e1_f0), [f1], "k_dx", deps,
            loads=((w_in, 0, False), *brief(x0, d1_n, stat_n, dx_n, d1_f, stat_f, dx_f)),
            stores=[((rows, width), F32)], parts=2,
        )

    def rowed(v):
        return v.reshape(-1, inner)

    if fast:
        jobs = (("taps", (0, 1), (5, 6), 0), ("taps", (0, 1), (5, 6), 1), ("half", (2,), (3, 4), None))
        args = (e2_n, e2_f, cot_v, c3_n, c3_f, win_n, win_f)
        send_1 = split_call(jobs, args, (), 1, "k_weights1", (vec,))
        got_1 = swap_cores(send_1)
        keep_1 = split_call(jobs, args, (), 0, "k_weights1", (send_1[0],))
        last = keep_1[0]
    else:
        last = vec
    e1_n, e3_n, e2_n0, edge_n, vec, dx_n = back1_call(
        True, vec, e2_n, e2_f, halo_n, q_n, s_n, (last,)
    )
    if fast:
        xs, x1, ys, y1b = first_sum(
            keep_1, got_1, (0,), (2,), "k_first1", (vec, halo_f), 0, (edge_n,)
        )
        x_got, y_got = swap(xs, "dp", 2), swap(ys, "seq", 1)
        (tap_1,) = call(
            functools.partial(k_tap, tap=4), [(unit, BF16)], (e2_n, e2_f, win_n, win_f), (), "k_tap",
            (x1,),
        )
        halo_n, last = y_got, tap_1
    else:
        halo_n = to_near(edge_n)
    more = tuple((v, None, True) for v in (s_n[0], s_f[0], s_n[4], s_f[4], q_n[0], q_f[0])) if fast else ()
    e1_f, e3_f, e2_f0, edge_f, vec, dx_f, *held = back1_call(
        False, vec, e2_f, e2_n, halo_f, q_f, s_f, (last,), more
    )
    halo_f = to_far(edge_f)

    if not fast:
        (w_mid_0,) = call(k_nothing, [], (place,), (), "k_load", (vec,), ((w_mid, 0, True),))
        e1_n0, vec = back0_call(True, vec, e2_n0, e2_f0, halo_n, p_n, (), ())
        e1_f0, vec = back0_call(False, vec, e2_f0, e2_n0, halo_f, p_f, (), ())
        token, y1 = out_call((vec,))
        vec, dx = dx_call(vec, (token,))

        def both(n, f):
            return jnp.concatenate([n, f])

        at = half * (1 - (lax.axis_index("seq") & 1))
        e3_1 = jnp.roll(cot, -at, axis=0)
        w_1 = plain_weights(
            both(s_n[4], s_f[4]), both(e1_n, e1_f), both(win_n, win_f), both(e2_n, e2_f),
            both(c3_n, c3_f), e3_1,
        )
        w_0 = plain_weights(
            both(a1_n, a1_f), both(e1_n0, e1_f0), both(s_n[0], s_f[0]), both(e2_n0, e2_f0),
            both(q_n[0], q_f[0]), both(e3_n, e3_f),
        )
        grad_w_in, grad_w_mid, grad_w_out = (jnp.stack(pair) for pair in zip(w_0, w_1))
        vec = lax.psum(vec, ("dp", "seq"))
    else:
        jobs = (
            ("taps", (4, 5), (7, 8), 0), ("taps", (4, 5), (7, 8), 1), ("half", (9, 10), (0, 1), None),
            ("half", (2, 3), (11, 12), None), ("odd", (4, 5), (7, 8), (4, 6)),
        )
        args = (e1_n, e1_f, e3_n, e3_f, e2_n0, e2_f0, tap_1, *held)
        parts = (1, 1)
        send_2 = split_call(jobs[:2], args, (), 1, "k_weights2", (vec,), parts=parts)
        got_2 = swap_cores(send_2, parts)
        *keep_2, w_mid_0 = split_call(jobs, args, ((w_mid, 0, True),), 0, "k_weights2", (send_2[0],))
        send_4 = split_call(jobs[2:], args, (), 1, "k_weights4", (keep_2[0],))
        got_2 = got_2 + swap_cores(send_4)
        (y1b,) = call(
            k_plus, [((4 * u, inner), BF16)], (y1b, y_got), (), "k_plus", (send_4[0], halo_f)
        )
        as_, a1 = first_sum(keep_2, got_2, (0,), (), "k_first2", (y1b, x_got))
        a_got = swap(as_, "dp", 2)
        xys, xy = second_sum(x1, x_got, "k_second1", (a1,))
        xy_got = swap(xys, "seq", 1)
        bs, b1 = first_sum(keep_2, got_2, (), (4,), "k_first5", (xy, *got_2[2], *got_2[3]))
        b_got = swap(bs, "seq", 1)
        e1_n0, vec = back0_call(True, vec, e2_n0, e2_f0, halo_n, p_n, (b1,), (), 7)
        e1_f0, vec, a1_n, a1_f = back0_call(
            False, vec, e2_f0, e2_n0, halo_f, p_f, (e1_n0,), ((a1_n, None, True), (a1_f, None, True)), 1
        )
        vec, dx = dx_call(vec, ())
        jobs = (("half", (0, 1), (2, 3), None),)
        args = (a1_n, a1_f, e1_n0, e1_f0)
        send_3 = split_call(jobs, args, (), 1, "k_weights3", (vec,), parts=(2,))
        got_3 = swap_cores(send_3, (2,))
        keep_3 = split_call(jobs, args, (), 0, "k_weights3", (send_3[0],))
        line_a = line_half([(xy, xy_got)], [y1b], 0, "k_line1", (keep_3[0],))
        ays, ay, b1 = second_sum(a1, a_got, "k_second2", (line_a[0],), 0.3, (vec, b1, b_got))
        ay_got = swap(ays, "seq", 1)
        ds, d1 = first_sum(keep_2, got_2, (2,), (), "k_first3", (ay,), 2)
        d_got = swap(ds, "dp", 2)
        cs, c1 = first_sum(keep_3, got_3, (), (0,), "k_first4", (d1,))
        c_got = swap(cs, "seq", 1)
        token, y1 = out_call((c1,))
        line_a = line_half([line_a], [], 1, "k_line2", (token,))
        line_b = line_half([(ay, ay_got)], [b1], 0, "k_line3", (line_a[0],), 0, n_packed)
        line_e = line_half([(c1, c_got)], [], 0, "k_line4", (line_b[0],))
        dys, dy = second_sum(d1, d_got, "k_second3", (line_e[0],))
        dy_got = swap(dys, "seq", 1)
        sums_a = line_sums([line_a], (2 * u,), "k_sum1", (dy,), 2.5)
        a_rows = (sums_a, swap(sums_a, "dp", 2))
        line_b = line_half([line_b], [], 1, "k_line5", (sums_a,), 0, n_packed)
        line_e = line_half([line_e], [], 1, "k_line6", (line_b[0],), 2)
        line_c = line_half([(dy, dy_got)], [], 0, "k_line7", (line_e[0],))
        whole = row_sums([a_rows], ((1, 0),), "k_rows1", (line_c[0],))
        sums_b = line_sums([line_b, line_e], (2 * u, u), "k_sum2", (whole,), 1.5)
        b_rows = (sums_b, swap(sums_b, "dp", 2))
        line_c = line_half([line_c], [], 1, "k_line8", (sums_b,), 2)
        sums_c = line_sums([line_c], (u,), "k_sum3", (line_c[0],))
        c_rows = (sums_c, swap(sums_c, "dp", 2))
        whole = row_sums(
            [(whole,), b_rows, c_rows], (None, (1, 0, 0), (1,)), "k_rows2", (sums_c,)
        )
        got = swap(whole, "dp", 1)
        shapes = ((2, 2 * u, inner), (2, taps, u, inner), (2, 2 * u, inner))
        vector_shapes = ((2, width), (2, width), (2, 2, inner), (2, 2, inner), (2, 2, inner), (2, width))
        grads = share(0, (place, whole), (), shapes, (), vec_shape[0], u)
        grad_w_in, grad_w_mid, grad_w_out, *vectors = share(
            1, (place, got, whole), grads, shapes, vector_shapes, vec_shape[0], u
        )
        return (
            y1[None], dx[None], grad_w_in, grad_w_mid.swapaxes(2, 3), grad_w_out.swapaxes(1, 2),
            *vectors,
        )

    narrow = vec[:n_narrow].reshape(2, 2, 3, inner)
    wide = vec[n_narrow:].reshape(2, 3, width)
    return (
        y1[None],
        dx[None],
        grad_w_in,
        grad_w_mid,
        grad_w_out,
        wide[:, 0],
        wide[:, 1],
        narrow[:, :, 0],
        narrow[:, :, 1],
        narrow[:, :, 2],
        wide[:, 2],
    )


def solution(mesh):
    row = P("dp", "seq", None)
    return jax.shard_map(
        body,
        mesh=mesh,
        in_specs=(row, P(None, "dp", "seq")) + (P(),) * 9 + (row,),
        out_specs=(
            row,
            row,
            P(None, "seq", None),
            P(None, None, None, "seq"),
            P(None, None, "seq"),
        )
        + (P(),) * 6,
        check_vma=False,
    )
```

```python
import functools

import jax
import jax.numpy as jnp
from jax import lax
from jax.experimental import pallas as pl
from jax.experimental.pallas import tpu as pltpu
from jax.sharding import PartitionSpec as P

DILATION_CLOSE = 4
DILATION_BROAD = 128
EPS = 1e-05
F32 = jnp.float32
BF16 = jnp.bfloat16
VMEM_LIMIT = 18 * 1024 * 1024
HEIGHT = 128
EXP2 = -0.7213475204444817

C0 = 0.3275911 * 0.7071067811865476
POLY = tuple(0.5 * c for c in (0.254829592, -0.284496736, 1.421413741, -1.453152027, 1.061405429))
ROOT_2PI = 0.3989422804014327


def normal_parts(q):
    bell = jnp.exp2((q * EXP2) * q)
    t = pltpu.reciprocal(1.0 + C0 * jnp.abs(q), approx=True)
    h = POLY[4]
    for c in POLY[3::-1]:
        h = h * t + c
    tail = h * t * bell
    return jnp.where(q >= 0, 1.0 - tail, tail), q * bell * ROOT_2PI


def act_forward(v, gain, shift):
    c = v.shape[-1]
    mean = jnp.sum(v, axis=-1, keepdims=True) * (1.0 / c)
    centred = v - mean
    r = lax.rsqrt(jnp.sum(centred * centred, axis=-1, keepdims=True) * (1.0 / c) + EPS)
    n = centred * r
    q = n * gain + shift
    below, slope = normal_parts(q)
    return mean, r, n, q * below, below + slope


def act_backward(f, n, r, d, gain):
    c = f.shape[-1]
    p = f * d
    gp = gain * p
    first = jnp.sum(gp, axis=-1, keepdims=True) * (1.0 / c)
    second = jnp.sum(gp * n, axis=-1, keepdims=True) * (1.0 / c)
    return p, r * (gp - first - n * second)


def fold(v):
    return jnp.sum(v.reshape(v.shape[0] // 8, 8, v.shape[1]), axis=0)


def total(acc):
    return jnp.sum(acc, axis=0, keepdims=True)


def lanes(column):
    return jnp.broadcast_to(column, (column.shape[0], 128))


def strips(rows, height, step, carry=(), unroll=8, first=0):
    turns = rows // (height * unroll)
    if turns <= 1:
        for j in range(rows // height):
            carry = step(pl.ds(first + j * height, height), carry)
        return carry

    def body(i, c):
        for j in range(unroll):
            c = step(pl.ds(pl.multiple_of((i * unroll + j) * height, height), height), c)
        return c

    return lax.fori_loop(0, turns, body, carry)


def staggered(rows, height, *stages):
    parts = [slice(i, i + height) for i in range(0, rows, height)]
    for t in range(len(parts) + len(stages) - 1):
        for i in reversed(range(len(stages))):
            if 0 <= t - i < len(parts):
                stages[i](parts[t - i])


def at_base(at, base):
    if isinstance(base, int) and base == 0:
        return at
    return pl.ds(pl.multiple_of(at.start + base, at.size), at.size)


def dot(a, b):
    return jnp.dot(a, b, preferred_element_type=F32)


def dot_nt(a, b):
    return lax.dot_general(a, b, (((1,), (1,)), ((), ())), preferred_element_type=F32)


class Loads:
    def __init__(self, sources, targets, sems):
        self.targets = targets
        self.copies = [
            pltpu.make_async_copy(src if b is None else src.at[b], dst, sems.at[i])
            for i, ((src, b), dst) in enumerate(zip(sources, targets))
        ]
        self.waiting = set(range(len(targets)))
        for copy in self.copies:
            copy.start()

    def get(self, i):
        if i in self.waiting:
            self.waiting.remove(i)
            self.copies[i].wait()
        return self.targets[i]

    def finish(self):
        for i in sorted(self.waiting):
            self.get(i)


class Stores:
    def __init__(self, held, targets, sems):
        self.held, self.targets, self.sems = held, targets, sems
        self.copies = []

    def put(self, *which, at=None):
        for i in which:
            src, dst = self.held[i], self.targets[i]
            if at is not None:
                src, dst = src.at[at], dst.at[at]
            copy = pltpu.make_async_copy(src, dst, self.sems.at[len(self.copies)])
            copy.start()
            self.copies.append(copy)

    def finish(self):
        for copy in self.copies:
            copy.wait()


def call(
    kernel, outs, args, scratch=(), name=None, deps=(), loads=(), stores=(), offloads=(), parts=1,
    limit=VMEM_LIMIT, cost=0,
):
    n_args, n_loads, n_deps, n_off = len(args), len(loads), len(deps), len(offloads)
    n_outs, n_stores = len(outs), len(stores)
    loaded = [(a.shape if b is None else a.shape[1:], a.dtype) for a, b, _ in loads]
    kept = [i for i, (_, _, keep) in enumerate(loads) if keep]
    brief = [i for i in range(n_loads) if i not in kept]
    out_shape = [pltpu.VMEM(s, t) for s, t in outs] + [pltpu.HBM(s, t) for s, t in stores]
    out_shape += [pltpu.VMEM(*loaded[i]) for i in kept]
    out_shape += [pltpu.HBM(a.shape, a.dtype) for a in offloads]

    def run(*refs):
        def take(n):
            nonlocal refs
            first, refs = refs[:n], refs[n:]
            return first

        ins, going, sources, _ = take(n_args), take(n_off), take(n_loads), take(n_deps)
        results, stored, held, gone = take(n_outs), take(n_stores), take(len(kept)), take(n_off)
        targets = dict(zip(kept, held))
        scr = list(refs)
        more = {}
        if n_loads:
            sems = scr.pop()
            for i in reversed(brief):
                targets[i] = scr.pop()
            sources = [(r, b) for r, (_, b, _) in zip(sources, loads)]
            more["coming"] = Loads(sources, [targets[i] for i in range(n_loads)], sems)
        if n_off:
            leaving = Stores(going, gone, scr.pop())
            leaving.put(*range(n_off))
        if n_stores:
            sems = scr.pop()
            held = [scr.pop() for _ in stores][::-1]
            more["keeping"] = Stores(held, stored, sems)
        kernel(*ins, *results, *scr, **more)
        for part in more.values():
            part.finish()
        if n_off:
            leaving.finish()

    hbm, vmem = pl.BlockSpec(memory_space=pltpu.HBM), pl.BlockSpec(memory_space=pltpu.VMEM)
    specs = [vmem] * (n_args + n_off) + [hbm] * n_loads
    specs += [pl.BlockSpec(memory_space=pl.ANY)] * n_deps
    out_specs = [vmem] * n_outs + [hbm] * n_stores + [vmem] * len(kept) + [hbm] * n_off
    scratch = list(scratch)
    if n_stores:
        scratch += [pltpu.VMEM(s, t) for s, t in stores]
        scratch += [pltpu.SemaphoreType.DMA((n_stores * parts,))]
    if n_off:
        scratch += [pltpu.SemaphoreType.DMA((n_off,))]
    if n_loads:
        scratch += [pltpu.VMEM(*loaded[i]) for i in brief] + [pltpu.SemaphoreType.DMA((n_loads,))]
    return pl.pallas_call(
        run,
        out_shape=out_shape,
        in_specs=specs,
        out_specs=out_specs,
        scratch_shapes=scratch,
        compiler_params=pltpu.CompilerParams(vmem_limit_bytes=limit),
        cost_estimate=pl.CostEstimate(flops=1 + int(cost * 1.15e9), bytes_accessed=1, transcendentals=0),
        name=name,
    )(
        *[pltpu.with_memory_space_constraint(a, pltpu.VMEM) for a in (*args, *offloads)],
        *[pltpu.with_memory_space_constraint(a, pltpu.HBM) for a, _, _ in loads],
        *deps,
    )


NEAR, CUT, LOW_0, LOW_1, HIGH_1, CORE, BIT_X, LINE = range(8)


def find_marks(bounds, place):
    rows = bounds.shape[2]
    first = lax.axis_index("seq") * rows
    marks = (bounds[1, 0:1, 0:1], bounds[0, 0:1, 0:1], bounds[0, 0:1, rows - 1 :], bounds[1, 0:1, rows - 1 :])
    for row, v in zip((CUT, LOW_0, LOW_1, HIGH_1), marks):
        place[row : row + 1] = jnp.broadcast_to(v - first, (1, 128))


def find_place(place):
    seq, dp = lax.axis_index("seq"), lax.axis_index("dp")
    for row, v in ((NEAR, seq & 1), (CORE, dp & 1), (BIT_X, dp >> 1), (LINE, seq >> 1)):
        place[row : row + 1] = jnp.full((1, 128), v, jnp.int32)


def base_of(place, near, rows):
    odd = place[NEAR, 0]
    return rows * (1 - odd) if near else rows * odd


def wide_act(x, base, gain, shift, a1, d1, stat, part):
    def wide(at, c):
        mean, r, n, a, d = act_forward(x[at_base(at, base)].astype(F32), gain, shift)
        a1[at], d1[at] = a.astype(BF16), d.astype(BF16)
        stat[0, at], stat[1, at] = lanes(mean), lanes(r)
        return c

    strips(part.stop - part.start, 32, wide, first=part.start)


def narrow_act(z, gain, shift, a, n, d, stat, part):
    def narrow(at, c):
        _, r, nn, aa, dd = act_forward(z[at], gain, shift)
        n[at], d[at], a[at] = nn.astype(BF16), dd.astype(BF16), aa.astype(BF16)
        stat[at] = lanes(r)
        return c

    strips(part.stop - part.start, 32, narrow, first=part.start)


def windows(place, near, own, other, halo, win, pad, step):
    rows, width = own.shape
    taps = win.shape[1] // width
    rim = (pad.shape[0] - rows) // 2
    pad[rim : rim + rows] = own[...].astype(pad.dtype)
    lower = place[NEAR, 0] == (1 if near else 0)

    @pl.when(lower)
    def _():
        pad[0:rim] = halo[halo.shape[0] - rim :].astype(pad.dtype)
        pad[rim + rows :] = other[0:rim].astype(pad.dtype)

    @pl.when(jnp.logical_not(lower))
    def _():
        pad[0:rim] = other[rows - rim :].astype(pad.dtype)
        pad[rim + rows :] = halo[0:rim].astype(pad.dtype)

    base = base_of(place, near, rows)
    cut, low_0, low_1, high_1 = (place[i : i + 1] for i in (CUT, LOW_0, LOW_1, HIGH_1))
    height = 64

    def fill(part):
        for i in range(part.start, part.stop, height):
            rows_at(i)

    def rows_at(i):
        t = lax.broadcasted_iota(jnp.int32, (height, 128), 0) + (base + i)
        first = t < cut
        low = jnp.where(first, low_0, low_1)
        high = jnp.where(first, cut, high_1)
        for k in range(taps):
            offset = (k - taps // 2) * step
            m = jnp.where((t + offset >= low) & (t + offset < high), 1.0, 0.0).astype(pad.dtype)
            m = jnp.concatenate([m] * (width // 128), axis=1)
            start = rim + offset + i
            win[i : i + height, k * width : (k + 1) * width] = (
                pad[start : start + height] * m
            ).astype(BF16)

    return fill


def put_edge(edge, v, place, near):
    n = edge.shape[0]
    lower = place[NEAR, 0] == (1 if near else 0)

    @pl.when(lower)
    def _():
        edge[...] = v[0:n]

    @pl.when(jnp.logical_not(lower))
    def _():
        edge[...] = v[v.shape[0] - n :]


def first_half(x, base, gw, sw, w_in, bn, gn, sn, a1, d1, stat1, a2, n2, d2, r2, z, keeping):
    rows = a1.shape[0]

    def wide(p):
        wide_act(x, base, gw(), sw(), a1, d1, stat1, p)
        if p.stop == rows:
            keeping.put(*FIRST_STORES[len(keeping.held)])

    def inner(p):
        z[p] = dot(a1[p], w_in()[...]) + bn()

    def narrow(p):
        narrow_act(z, gn(), sn(), a2, n2, d2, r2, p)

    return wide, inner, narrow


FIRST_STORES = {3: (0, 1, 2), 7: (4, 5, 6)}


def k_in_near(place, a2, n2, d2, r2, edge, z, *, coming, keeping):
    a1, d1, stat1 = keeping.held
    find_place(place)
    x = coming.get(0)
    staggered(a1.shape[0], a1.shape[0], *first_half(
        x, base_of(place, True, a1.shape[0]), lambda: coming.get(1)[0:1], lambda: coming.get(2)[0:1],
        lambda: coming.get(3), lambda: coming.get(6)[0, 0:1], lambda: coming.get(4)[0, 0:1],
        lambda: coming.get(5)[0, 0:1], a1, d1, stat1, a2, n2, d2, r2, z, keeping,
    ))
    put_edge(edge, a2, place, True)
    find_marks(coming.get(9), place)


def k_in_far(place, x, gw, sw, gn, sn, bn, a2, n2, d2, r2, edge, z, *, coming, keeping):
    a1, d1, stat1 = keeping.held
    staggered(a1.shape[0], a1.shape[0], *first_half(
        x, base_of(place, False, a1.shape[0]), lambda: gw[0:1], lambda: sw[0:1],
        lambda: coming.get(0), lambda: bn[0, 0:1], lambda: gn[0, 0:1], lambda: sn[0, 0:1],
        a1, d1, stat1, a2, n2, d2, r2, z, keeping,
    ))
    put_edge(edge, a2, place, False)


def k_mid(
    place, x, own, other, halo, w_mid, gw, sw, bw, gn, sn, bn,
    a3, r3, a2, n2, d2, r2, pad, z, z1, *, near, step, coming, keeping,
):
    rows, width = own.shape
    win, n3, d3, y, a1, d1, stat1 = keeping.held
    fill = windows(place, near, own, other, halo, win, pad, step)
    base = base_of(place, near, rows)
    weights = w_mid[...].reshape(win.shape[1], width)

    def conv(p):
        fill(p)
        z[p] = dot(win[p], weights) + bn[0, 1:2]
        if p.stop == rows:
            keeping.put(0)

    def narrow(p):
        narrow_act(z, gn[0, 1:2], sn[0, 1:2], a3, n3, d3, r3, p)
        if p.stop == rows:
            keeping.put(1, 2)

    def outer(p):
        n = p.stop - p.start
        old = x[pl.ds(pl.multiple_of(base + p.start, n), n)].astype(F32)
        y[p] = old + dot(a3[p], coming.get(0)[...]) + bw[0:1]
        if p.stop == rows:
            keeping.put(3)

    staggered(rows, HEIGHT, conv, narrow, outer, *first_half(
        y, 0, lambda: gw[1:2], lambda: sw[1:2], lambda: coming.get(1), lambda: bn[1, 0:1],
        lambda: gn[1, 0:1], lambda: sn[1, 0:1], a1, d1, stat1, a2, n2, d2, r2, z1, keeping,
    ))


def put_wide(vec, row, acc):
    inner = vec.shape[1]
    for i in range(acc.shape[1] // inner):
        vec[row + i : row + i + 1] += total(acc[:, i * inner : (i + 1) * inner])


def k_flow(e, w_out, f, vec, *, row, coming):
    f[...] = dot_nt(e[...], w_out[...])
    vec[...] = jnp.zeros_like(vec)

    def step(at, acc):
        return acc + fold(e[at].astype(F32))

    put_wide(vec, row, strips(e.shape[0], 32, step, jnp.zeros((8, e.shape[1]), F32)))


def k_conv(
    place, vec_in, own, other, halo, w_mid, gn, sn, bn, f, a3, e2, vec, win, pad, z, *, near, step, row
):
    rows, width = own.shape
    windows(place, near, own, other, halo, win, pad, step)(slice(0, own.shape[0]))
    z[...] = dot(win[...], w_mid[...].reshape(win.shape[1], width)) + bn[1, 1:2]
    gain = gn[1, 1:2]
    base = base_of(place, near, rows)

    def narrow(at, c):
        _, r, n, a, d = act_forward(z[at], gain, sn[1, 1:2])
        a3[at] = a.astype(BF16)
        p, v = act_backward(f[at_base(at, base)], n, r, d, gain)
        e = v.astype(BF16)
        e2[at] = e
        return c[0] + fold(p * n), c[1] + fold(p), c[2] + fold(e.astype(F32))

    vec[...] = vec_in[...]
    zero = jnp.zeros((8, width), F32)
    for i, acc in enumerate(strips(rows, 32, narrow, (zero,) * 3)):
        vec[row + i : row + i + 1] += total(acc)


def k_out(place, a_n, a_f, bw, token, *, coming, keeping):
    half = a_n.shape[0]
    token[...] = jnp.zeros_like(token)
    (y,) = keeping.held
    w_out = coming.get(0)
    for near, a in ((True, a_n), (False, a_f)):
        at = pl.ds(pl.multiple_of(base_of(place, near, half), half), half)
        y[at] = dot(a[...], w_out[...]) + bw[1:2] + coming.get(1 if near else 2)[...]
        keeping.put(0, at=at)


def back_narrow(f, n, d, r, gain, e_out, vec, row):
    rows, width = f.shape

    def step(at, c):
        nn = n[at].astype(F32)
        p, v = act_backward(f[at], nn, r[at][:, 0:1], d[at].astype(F32), gain)
        e = v.astype(BF16)
        e_out[at] = e
        return c[0] + fold(p * nn), c[1] + fold(p), c[2] + fold(e.astype(F32))

    zero = jnp.zeros((8, width), F32)
    for i, acc in enumerate(strips(rows, 32, step, (zero,) * 3)):
        vec[row + i : row + i + 1] += total(acc)


def back_wide(f, x, x_base, stat, d, gain, dy, dy_base, out, out_base, cast, vec, row, cast_row):
    rows, width = f.shape

    def step(at, c):
        r = stat[1, at][:, 0:1]
        n = (x[at_base(at, x_base)].astype(F32) - stat[0, at][:, 0:1]) * r
        p, v = act_backward(f[at], n, r, d[at].astype(F32), gain)
        dx = dy[at_base(at, dy_base)].astype(F32) + v
        out[at_base(at, out_base)] = dx
        sums = (c[0] + fold(p * n), c[1] + fold(p))
        if cast is not None:
            e = dx.astype(BF16)
            cast[at] = e
            sums += (c[2] + fold(e.astype(F32)),)
        return sums

    zero = jnp.zeros((8, width), F32)
    sums = strips(rows, 32, step, (zero,) * (2 if cast is None else 3), 8)
    put_wide(vec, row, sums[0])
    put_wide(vec, row + width // vec.shape[1], sums[1])
    if cast is not None:
        put_wide(vec, cast_row, sums[2])


def flow_two(win, w_mid, z):
    taps, width = w_mid.shape[0], w_mid.shape[1]
    for j in range(taps):
        part = dot_nt(win[:, j * width : (j + 1) * width], w_mid[taps - 1 - j])
        if j == 0:
            z[...] = part
        else:
            z[...] += part


def k_back1(
    place, vec_in, own, other, halo, w_mid, gw, gn,
    e1, e3, e2, edge, vec, win, pad, z, f1, *, near, step, rows_of, coming, keeping,
):
    vec[...] = vec_in[...]
    windows(place, near, own, other, halo, win, pad, step)(slice(0, own.shape[0]))
    flow_two(win, w_mid, z)
    n2, d2, r2, w_in = (coming.get(i) for i in range(4))
    back_narrow(z, n2, d2, r2, gn[1, 0:1], e1, vec, rows_of[0])
    f1[...] = dot_nt(e1[...], w_in[...])
    base = base_of(place, near, own.shape[0])
    (dx,) = keeping.held
    x, d1, stat1, dy = (coming.get(i) for i in range(4, 8))
    back_wide(f1, x, 0, stat1, d1, gw[1:2], dy, base, dx, 0, e3, vec, rows_of[1], rows_of[3])
    keeping.put(0)
    w_out, n3, d3, r3 = (coming.get(i) for i in range(8, 12))
    z[...] = dot_nt(e3[...], w_out[...])
    back_narrow(z, n3, d3, r3, gn[0, 1:2], e2, vec, rows_of[2])
    put_edge(edge, e2, place, near)


def k_back0(
    place, vec_in, own, other, halo, w_mid, gn, e1, vec, win, pad, z, *, near, step, row, coming
):
    vec[...] = vec_in[...]
    halo = halo.at[pl.ds(halo.shape[0] - 16, 16)]
    windows(place, near, own, other, halo, win, pad, step)(slice(0, own.shape[0]))
    flow_two(win, w_mid, z)
    n2, d2, r2 = (coming.get(i) for i in range(3))
    back_narrow(z, n2, d2, r2, gn[0, 0:1], e1, vec, row)


def k_dx(place, vec_in, gw, e1_n, e1_f, vec, f1, *, row, coming, keeping):
    vec[...] = vec_in[...]
    half = e1_n.shape[0]
    (out,) = keeping.held
    w_in, x = coming.get(0), coming.get(1)
    for near, e1 in ((True, e1_n), (False, e1_f)):
        f1[...] = dot_nt(e1[...], w_in[...])
        d, stat, dy = (coming.get(i + (0 if near else 3)) for i in (2, 3, 4))
        base = base_of(place, near, half)
        back_wide(f1, x, base, stat, d, gw[0:1], dy, 0, out, base, None, vec, row, None)
        keeping.put(0, at=pl.ds(pl.multiple_of(base, half), half))


def k_split(place, *refs, jobs, parts, side, coming=None):
    n_outs = sum(parts)
    outs, turned = list(refs[-1 - n_outs : -1]), refs[-1]
    refs = refs[: -1 - n_outs]
    _, shards, _, u, rows = turned.shape
    inner = outs[0].shape[-1]

    def ref(i):
        return refs[i] if i < len(refs) else coming.get(i - len(refs))

    def whole(places, at=slice(None)):
        if len(places) == 1:
            half = rows // 2
            bases = [base_of(place, near, half) for near in (True, False)]
            parts = [ref(places[0])[pl.ds(pl.multiple_of(b, half), half)] for b in bases]
        else:
            parts = [ref(i)[:, at] for i in places]
        return jnp.concatenate(parts, axis=0)

    core = place[CORE, 0] ^ side
    kept = {}
    halves = 0
    for n, (kind, left, right, j) in zip(parts, jobs):
        here, outs = outs[:n], outs[n:]

        def put(product):
            height = product.shape[0] // n
            for i, out in enumerate(here):
                out[...] = product[i * height : (i + 1) * height]

        if kind == "half":
            turned[halves] = whole(left).T.reshape(turned.shape[1:])
            part = turned[halves, :, core].reshape(shards * u, rows)
            put(dot(part, whole(right)).astype(BF16))
            halves += 1
            continue
        if left not in kept:
            kept[left] = whole(left).T
        if kind == "taps":
            at = pl.ds(pl.multiple_of((j + 2 * core) * inner, 128), inner)
            put(dot(kept[left], whole(right, at)).astype(BF16))
            continue
        tap, before = j

        @pl.when(core == 0)
        def _():
            put(ref(before)[...])

        @pl.when(core != 0)
        def _():
            at = slice(tap * inner, (tap + 1) * inner)
            put(dot(kept[left], whole(right, at)).astype(BF16))


def k_tap(e_n, e_f, win_n, win_f, out, *, tap):
    inner = out.shape[-1]
    at = slice(tap * inner, (tap + 1) * inner)
    left = jnp.concatenate([e_n[...], e_f[...]], axis=0).T
    right = jnp.concatenate([win_n[:, at], win_f[:, at]], axis=0)
    out[...] = dot(left, right).astype(BF16)


def added(*parts):
    first, *rest = [p.astype(F32) for p in parts]
    for p in rest:
        first = first + p
    return first


def k_first(place, *refs, pairs, singles, edge):
    refs = list(refs)
    x, y = place[BIT_X, 0], place[NEAR, 0]

    def take(n):
        first = refs[:n]
        del refs[:n]
        return first

    ins = [(take(1)[0], take(n)) for two_units in pairs for n in two_units]
    ins += [(take(1)[0], take(n)) for n in singles]
    rim = take(1)[0] if edge else None

    def add_rows(a, parts, out):
        height = a.shape[0] // len(parts)
        for i, b in enumerate(parts):

            def step(k, c):
                here = pl.ds(pl.multiple_of(k * 80, 80), 80)
                at = pl.ds(pl.multiple_of(i * height + k * 80, 80), 80)
                out[at] = added(a[at], b[here]).astype(BF16)
                return c

            lax.fori_loop(0, height // 80, step, 0)

    for i in range(len(pairs)):
        (a0, b0), (a1, b1) = ins[2 * i : 2 * i + 2]
        send, stay = take(2)

        @pl.when(x == 0)
        def _():
            add_rows(a1, b1, send)
            add_rows(a0, b0, stay)

        @pl.when(x != 0)
        def _():
            add_rows(a0, b0, send)
            add_rows(a1, b1, stay)

    for out, side in zip(refs, (1 - y, y)):
        at = 0
        for a, parts in ins[2 * len(pairs) :]:
            u = a.shape[2]
            each = a.shape[0] // len(parts)
            for k in range(a.shape[0]):
                b = parts[k // each]
                out[at : at + u] = added(a[k, side], b[k % each, side]).astype(BF16)
                at += u
    if edge:
        refs[0][at:] = rim[...]


def k_second(place, a, b, *refs):
    *vec, send, stay = refs
    mine = place[NEAR, 0]
    u = a.shape[2]
    for out, side in ((send, 1 - mine), (stay, mine)):

        def step(k, c):
            at = pl.ds(pl.multiple_of(k * u, u), u)
            out[at] = added(a[k, side], b[k, side]).astype(BF16)
            return c

        lax.fori_loop(0, 4, step, 0)
    if vec:
        pack(vec[0][...], send, stay, at=4 * u)


def pack(v, *outs, at):
    n = v.shape[0]
    upper = v.astype(BF16)
    lower = (v - upper.astype(F32)).astype(BF16)
    for out in outs:
        out[at : at + n], out[at + n : at + 2 * n] = upper, lower


def unpack(ref, at):
    n = (ref.shape[0] - at) // 2
    return ref[at : at + n].astype(F32) + ref[at + n : at + 2 * n].astype(F32)


def k_line(place, *refs, sums, wholes, packed, bit, u):
    mine = (place[LINE, 0] >> bit) & 1
    arrays = [refs[2 * i : 2 * i + 2] for i in range(sums)]
    arrays += [refs[2 * sums + i : 2 * sums + i + 1] for i in range(wholes)]
    send, stay = refs[2 * sums + wholes :]
    for out, side in ((send, 1 - mine), (stay, mine)):
        at = 0
        for i, parts in enumerate(arrays):
            rows = parts[0].shape[0] - (packed if i == 0 else 0)
            for j in range(rows // (2 * u)):
                part = pl.ds(pl.multiple_of((2 * j + side) * u, u), u)
                out[at : at + u] = added(*[p[part] for p in parts]).astype(BF16)
                at += u
    if packed:
        a, b = arrays[0]
        n = a.shape[0] - packed
        pack(unpack(a, n) + unpack(b, n), send, stay, at=send.shape[0] - packed)


def k_sum(place, *refs, rows):
    out = refs[-1]
    at = 0
    for i, n in enumerate(rows):
        a, b = refs[2 * i], refs[2 * i + 1]
        out[at : at + n] = added(a[0:n], b[0:n]).astype(BF16)
        at += n
    if refs[0].shape[0] > rows[0]:
        pack(unpack(refs[0], rows[0]) + unpack(refs[1], rows[0]), out, at=at)


def k_rows(place, *refs, splits, u):
    *refs, out = refs
    x = place[BIT_X, 0]
    at = 0
    refs = list(refs)
    for split in splits:
        if split is None:
            ready = refs.pop(0)
            out[at : at + ready.shape[0]] = ready[...]
            at += ready.shape[0]
            continue
        mine, got = refs.pop(0), refs.pop(0)
        for k, apart in enumerate(split):
            here = slice(k * u, (k + 1) * u)
            if apart:
                base = pl.multiple_of(at + x * u, u)
                other = pl.multiple_of(at + (1 - x) * u, u)
                out[pl.ds(base, u)], out[pl.ds(other, u)] = mine[here], got[here]
                at += 2 * u
            else:
                out[at : at + u] = added(mine[here], got[here]).astype(BF16)
                at += u
        if mine.shape[0] > len(split) * u:
            n = len(split) * u
            pack(unpack(mine, n) + unpack(got, n), out, at=out.shape[0] - (mine.shape[0] - n))


def k_share(place, ref, *refs, side, u):
    vectors, n_vec = (), 0
    if side:
        mine, *refs = refs
        refs = refs[3:]
        n_vec = 6
    out_in, out_mid, out_out = refs[:3]
    vectors, refs = refs[3 : 3 + n_vec], refs[3 + n_vec :]
    stage, held, sems = refs[0], refs[1:-1], refs[-1]
    c = place[CORE, 0] ^ side
    rows = pl.ds(pl.multiple_of(c * u, u), u)
    copies = []

    def put(src, dst):
        copies.append(pltpu.make_async_copy(src, dst, sems.at[len(copies)]))
        copies[-1].start()

    def units(i, n=1):
        for k in range(i, i + n):
            stage[k] = ref[k * u : (k + 1) * u].astype(F32)
        return stage.at[i] if n == 1 else stage.at[i : i + n]

    put(units(0, 2), out_mid.at[1, pl.ds(2 * c, 2)])
    put(units(2), out_mid.at[1 - c, 4])
    put(units(3), out_out.at[1, rows])
    put(units(4, 2), out_mid.at[0, pl.ds(2 * c, 2)])
    put(units(6), out_in.at[0, rows])
    put(units(7), out_in.at[1, rows])
    put(units(8), out_out.at[0, rows])
    if side:
        vec, gw, sw, gn, sn, bn, bw = held
        vec[...] = unpack(mine, 9 * u) + unpack(ref, 9 * u)
        inner = vec.shape[1]
        two = gw.shape[1] // inner
        for block in range(2):
            for i in range(2):
                row = 3 * (2 * block + i)
                for j, out in enumerate((gn, sn, bn)):
                    out[block, i : i + 1] = vec[row + j : row + j + 1]
            for j, out in enumerate((gw, sw, bw)):
                for k in range(two):
                    row = 12 + (3 * block + j) * two + k
                    out[block : block + 1, k * inner : (k + 1) * inner] = vec[row : row + 1]
        for src, dst in zip((gw, sw, gn, sn, bn, bw), vectors):
            put(src, dst)
    for copy in copies:
        copy.wait()


def share(side, args, before, shapes, vector_shapes, vec_shape, u):
    inner = shapes[0][-1]
    vmem, hbm = pl.BlockSpec(memory_space=pltpu.VMEM), pl.BlockSpec(memory_space=pltpu.HBM)
    outs = list(shapes) + list(vector_shapes)
    held = [pltpu.VMEM(s, F32) for s in ([vec_shape] + list(vector_shapes) if side else [])]
    return pl.pallas_call(
        functools.partial(k_share, side=side, u=u),
        out_shape=[pltpu.HBM(s, F32) for s in outs],
        in_specs=[vmem] * len(args) + [hbm] * len(before),
        out_specs=[hbm] * len(outs),
        scratch_shapes=[pltpu.VMEM((9, u, inner), F32), *held, pltpu.SemaphoreType.DMA((7 + len(vector_shapes),))],
        input_output_aliases={len(args) + i: i for i in range(len(before))},
        compiler_params=pltpu.CompilerParams(vmem_limit_bytes=VMEM_LIMIT),
        cost_estimate=pl.CostEstimate(flops=1, bytes_accessed=1, transcendentals=0),
        name="k_share",
    )(
        *[pltpu.with_memory_space_constraint(a, pltpu.VMEM) for a in args],
        *[pltpu.with_memory_space_constraint(a, pltpu.HBM) for a in before],
    )


def k_plus(a, b, out):
    out[...] = added(a[...], b[0 : a.shape[0]]).astype(BF16)


def k_nothing(*refs, coming):
    pass


def swap(v, axis, bits):
    count = lax.axis_size(axis)
    return lax.ppermute(v, axis, [(i, i ^ bits) for i in range(count)])


def to_near(v):
    return swap(v, "seq", 1)


def to_far(v):
    count = lax.axis_size("seq")
    pairs = [(i, i + 1) for i in range(1, count - 1, 2)]
    return lax.ppermute(v, "seq", pairs + [(j, i) for i, j in pairs])


def dot_tn(a, b):
    return lax.dot_general(a, b, (((0,), (0,)), ((), ())), preferred_element_type=F32)


def plain_weights(a1, e1, win, e2, a3, e3):
    taps = win.shape[1] // e2.shape[1]
    grad_mid = dot_tn(win, e2).reshape(taps, e2.shape[1], e2.shape[1])
    shares = (
        lax.psum_scatter(dot_tn(a1, e1), "seq", scatter_dimension=0, tiled=True),
        lax.psum_scatter(grad_mid, "seq", scatter_dimension=2, tiled=True),
        lax.psum_scatter(dot_tn(a3, e3), "seq", scatter_dimension=1, tiled=True),
    )
    return [lax.psum(v.astype(BF16), "dp").astype(F32) for v in shares]


def body(
    tokens, bounds, w_in, w_mid, w_out, gain_wide, shift_wide, gain_narrow, shift_narrow,
    bias_narrow, bias_wide, cotangent,
):
    x0 = tokens[0]
    cot = cotangent[0]
    rows, width = x0.shape
    taps, inner = w_mid.shape[1], w_mid.shape[2]
    shards = lax.axis_size("seq")
    u = inner // shards
    two = width // inner
    half = rows // 2
    close, broad = DILATION_CLOSE, DILATION_BROAD

    wide_h, narrow_h, column = (half, width), (half, inner), ((half, 128), F32)
    win_h = ((half, taps * inner), BF16)
    act_wide = [(wide_h, BF16), (wide_h, BF16), ((2, half, 128), F32)]
    act_narrow = [(narrow_h, BF16), (narrow_h, BF16), (narrow_h, BF16), column]
    edge = ((16, inner), BF16)
    z = pltpu.VMEM(narrow_h, F32)
    f1 = pltpu.VMEM(wide_h, F32)
    win_scratch = pltpu.VMEM(*win_h)
    pad_0 = pltpu.VMEM((half + 32, inner), F32)
    pad_1 = pltpu.VMEM((half + 4 * broad, inner), BF16)
    n_narrow = 12
    vec_shape = ((n_narrow + 6 * two, inner), F32)

    def row_narrow(b, i):
        return 3 * (2 * b + i)

    def row_wide(b, i):
        return n_narrow + (3 * b + i) * two

    def brief(*arrays):
        return tuple((a, None, False) for a in arrays)

    place, a2_n, *p_n, edge_n, a1_n, d1_n, stat_n, x, gw, sw, gn, sn, bn, bw, w_mid_0 = call(
        k_in_near, [((8, 128), jnp.int32)] + act_narrow + [edge], (), [z], "k_in",
        loads=((x0, None, True), (gain_wide, None, True), (shift_wide, None, True), (w_in, 0, False),
               (gain_narrow, None, True), (shift_narrow, None, True), (bias_narrow, None, True),
               (bias_wide, None, True), (w_mid, 0, True), (bounds, None, False)),
        stores=act_wide, cost=4,
    )
    halo_n = to_near(edge_n)
    a2_f, *p_f, edge_f, a1_f, d1_f, stat_f, p1, p2, p3 = call(
        k_in_far, act_narrow + [edge], (place, x, gw, sw, gn, sn, bn), [z], "k_in", (edge_n,),
        loads=((w_in, 0, False),), stores=act_wide, offloads=p_n, cost=4,
    )
    p_n = (p1, p2, p3)
    halo_f = to_far(edge_f)

    def mid_call(near, own, other, halo, deps, loads, offloads):
        return call(
            functools.partial(k_mid, near=near, step=close),
            [(narrow_h, BF16), column] + act_narrow,
            (place, x, own, other, halo, w_mid_0, gw, sw, bw, gn, sn, bn),
            [pad_0, z, z], "k_mid", deps, ((w_out, 0, False), (w_in, 1, False)) + loads,
            [win_h, (narrow_h, BF16), (narrow_h, BF16), (wide_h, F32)] + act_wide, offloads, cost=8,
        )

    a3_n, r3_n, b2_n, *q_n = mid_call(True, a2_n, a2_f, halo_n, (), (), p_f)
    s_n, p_f = q_n[3:10], q_n[10:]
    halo_n = to_near(b2_n)
    a3_f, r3_f, b2_f, *q_f = mid_call(
        False, a2_f, a2_n, halo_f, (b2_n,), ((w_out, 1, True), (cot, None, True)),
        (a3_n, r3_n, *q_n[:3]),
    )
    s_f, (w_out_1, cot_v), q_n = q_f[3:10], q_f[10:12], q_f[12:]
    halo_f = to_far(b2_f)
    f3, vec, w_mid_1, *q_f = call(
        functools.partial(k_flow, row=row_wide(1, 2)),
        [((rows, inner), F32), vec_shape], (cot_v, w_out_1), (), "k_flow",
        loads=((w_mid, 1, True),), offloads=(a3_f, r3_f, *q_f[:3]), cost=3,
    )

    def conv_call(near, vec, own, other, halo):
        return call(
            functools.partial(k_conv, near=near, step=broad, row=row_narrow(1, 1)),
            [(narrow_h, BF16), (narrow_h, BF16), vec_shape, win_h],
            (place, vec, own, other, halo, w_mid_1, gn, sn, bn, f3),
            [pad_1, z], "k_conv", cost=3,
        )

    c3_n, e2_n, vec, win_n = conv_call(True, vec, b2_n, b2_f, halo_n)
    halo_n = to_near(e2_n)
    c3_f, e2_f, vec, win_f = conv_call(False, vec, b2_f, b2_n, halo_f)
    halo_f = to_far(e2_f)

    fast = shards == 8 and u % 16 == 0
    unit = (inner, inner)
    part = (u, inner)

    def split_call(jobs, args, loads, side, name, deps, cost=0, parts=None):
        parts = parts or (1,) * len(jobs)
        halves = sum(kind == "half" for kind, *_ in jobs)
        turned = pltpu.VMEM((halves, shards, 2, u, rows), BF16)
        return call(
            functools.partial(k_split, jobs=jobs, side=side, parts=parts),
            [((inner // n, inner), BF16) for n in parts for _ in range(n)],
            (place, *args), [turned], name, deps, loads, cost=cost,
        )

    def swap_cores(units, parts=None):
        got = [swap(v, "dp", 1) for v in units]
        parts = parts or (1,) * len(units)
        return [tuple(got.pop(0) for _ in range(n)) for n in parts]

    def first_sum(keep, got, pairs, singles, name, deps, cost=0, edge=()):
        args = []
        for i in [j for pair in pairs for j in (pair, pair + 1)]:
            args += [keep[i], *got[i]]
        for i in singles:
            args += [v.reshape(-1, 2, u, inner) for v in (keep[i], *got[i])]
        outs = [(unit, BF16)] * (2 * len(pairs))
        n = 4 * u * len(singles)
        if singles:
            outs += [((n + sum(v.shape[0] for v in edge), inner), BF16), ((n, inner), BF16)]
        kernel = functools.partial(
            k_first, pairs=tuple((len(got[i]), len(got[i + 1])) for i in pairs),
            singles=tuple(len(got[i]) for i in singles), edge=bool(edge),
        )
        return call(kernel, outs, (place, *args, *edge), (), name, deps, cost=cost)

    n_packed = 2 * vec_shape[0][0]

    def second_sum(stay, got, name, deps, cost=0, vec=()):
        views = [v.reshape(4, 2, u, inner) for v in (stay, got)]
        n = 4 * u + (n_packed if vec else 0)
        return call(
            k_second, [((n, inner), BF16)] * 2, (place, *views, *vec), (), name, deps, cost=cost
        )

    def line_half(pairs, wholes, bit, name, deps, cost=0, packed=0):
        arrays = [pair[0] for pair in pairs] + list(wholes)
        n = sum(a.shape[0] for a in arrays) - packed
        n = n // 2 + packed
        kernel = functools.partial(k_line, sums=len(pairs), wholes=len(wholes), packed=packed, bit=bit, u=u)
        send, stay = call(
            kernel, [((n, inner), BF16)] * 2, (place, *[v for pair in pairs for v in pair], *wholes),
            (), name, deps, cost=cost,
        )
        return stay, swap(send, "seq", 2 << bit)

    def line_sums(pairs, rows, name, deps, cost=0):
        n = sum(rows) + pairs[0][0].shape[0] - rows[0]
        return call(
            functools.partial(k_sum, rows=rows), [((n, inner), BF16)],
            (place, *[v for pair in pairs for v in pair]), (), name, deps, cost=cost,
        )[0]

    def row_sums(pairs, splits, name, deps):
        n = sum(pair[0].shape[0] for pair in pairs) + u * sum(sum(split or ()) for split in splits)
        return call(
            functools.partial(k_rows, splits=splits, u=u), [((n, inner), BF16)],
            (place, *[v for pair in pairs for v in pair]), (), name, deps,
        )[0]

    def back1_call(near, vec, own, other, halo, q, s, deps, more=()):
        return call(
            functools.partial(
                k_back1, near=near, step=broad,
                rows_of=(row_narrow(1, 0), row_wide(1, 0), row_narrow(0, 1), row_wide(0, 2)),
            ),
            [(narrow_h, BF16), (wide_h, BF16), (narrow_h, BF16), edge, vec_shape],
            (place, vec, own, other, halo, w_mid_1, gw, gn),
            [win_scratch, pad_1, z, f1], "k_back1", deps, stores=[(wide_h, F32)], cost=5 if near else 2,
            loads=(*brief(*q[2:5]), (w_in, 1, False), *brief(s[3], s[5], s[6], cot),
                   (w_out, 0, False), *brief(s[1], s[2], q[1]), *more),
        )

    def back0_call(near, vec, own, other, halo, p, deps, loads, cost=0):
        return call(
            functools.partial(k_back0, near=near, step=close, row=row_narrow(0, 0)),
            [(narrow_h, BF16), vec_shape], (place, vec, own, other, halo, w_mid_0, gn),
            [win_scratch, pad_0, z], "k_back0", deps, loads=brief(*p) + loads, cost=cost,
        )

    def out_call(deps):
        return call(
            k_out, [((8, 128), F32)], (place, c3_n, c3_f, bw), (), "k_out", deps,
            loads=((w_out, 1, False), *brief(s_n[3], s_f[3])), stores=[((rows, width), F32)], parts=2,
        )

    def dx_call(vec, deps):
        return call(
            functools.partial(k_dx, row=row_wide(0, 0)), [vec_shape],
            (place, vec, gw, e1_n0, e1_f0), [f1], "k_dx", deps,
            loads=((w_in, 0, False), *brief(x0, d1_n, stat_n, dx_n, d1_f, stat_f, dx_f)),
            stores=[((rows, width), F32)], parts=2,
        )

    def rowed(v):
        return v.reshape(-1, inner)

    if fast:
        jobs = (("taps", (0, 1), (5, 6), 0), ("taps", (0, 1), (5, 6), 1), ("half", (2,), (3, 4), None))
        args = (e2_n, e2_f, cot_v, c3_n, c3_f, win_n, win_f)
        send_1 = split_call(jobs, args, (), 1, "k_weights1", (vec,))
        got_1 = swap_cores(send_1)
        keep_1 = split_call(jobs, args, (), 0, "k_weights1", (send_1[0],))
        last = keep_1[0]
    else:
        last = vec
    e1_n, e3_n, e2_n0, edge_n, vec, dx_n = back1_call(
        True, vec, e2_n, e2_f, halo_n, q_n, s_n, (last,)
    )
    if fast:
        xs, x1, ys, y1b = first_sum(
            keep_1, got_1, (0,), (2,), "k_first1", (vec, halo_f), 0, (edge_n,)
        )
        x_got, y_got = swap(xs, "dp", 2), swap(ys, "seq", 1)
        (tap_1,) = call(
            functools.partial(k_tap, tap=4), [(unit, BF16)], (e2_n, e2_f, win_n, win_f), (), "k_tap",
            (x1,),
        )
        halo_n, last = y_got, tap_1
    else:
        halo_n = to_near(edge_n)
    more = tuple((v, None, True) for v in (s_n[0], s_f[0], s_n[4], s_f[4], q_n[0], q_f[0])) if fast else ()
    e1_f, e3_f, e2_f0, edge_f, vec, dx_f, *held = back1_call(
        False, vec, e2_f, e2_n, halo_f, q_f, s_f, (last,), more
    )
    halo_f = to_far(edge_f)

    if not fast:
        (w_mid_0,) = call(k_nothing, [], (place,), (), "k_load", (vec,), ((w_mid, 0, True),))
        e1_n0, vec = back0_call(True, vec, e2_n0, e2_f0, halo_n, p_n, (), ())
        e1_f0, vec = back0_call(False, vec, e2_f0, e2_n0, halo_f, p_f, (), ())
        token, y1 = out_call((vec,))
        vec, dx = dx_call(vec, (token,))

        def both(n, f):
            return jnp.concatenate([n, f])

        at = half * (1 - (lax.axis_index("seq") & 1))
        e3_1 = jnp.roll(cot, -at, axis=0)
        w_1 = plain_weights(
            both(s_n[4], s_f[4]), both(e1_n, e1_f), both(win_n, win_f), both(e2_n, e2_f),
            both(c3_n, c3_f), e3_1,
        )
        w_0 = plain_weights(
            both(a1_n, a1_f), both(e1_n0, e1_f0), both(s_n[0], s_f[0]), both(e2_n0, e2_f0),
            both(q_n[0], q_f[0]), both(e3_n, e3_f),
        )
        grad_w_in, grad_w_mid, grad_w_out = (jnp.stack(pair) for pair in zip(w_0, w_1))
        vec = lax.psum(vec, ("dp", "seq"))
    else:
        jobs = (
            ("taps", (4, 5), (7, 8), 0), ("taps", (4, 5), (7, 8), 1), ("half", (9, 10), (0, 1), None),
            ("half", (2, 3), (11, 12), None), ("odd", (4, 5), (7, 8), (4, 6)),
        )
        args = (e1_n, e1_f, e3_n, e3_f, e2_n0, e2_f0, tap_1, *held)
        parts = (1, 1)
        send_2 = split_call(jobs[:2], args, (), 1, "k_weights2", (vec,), parts=parts)
        got_2 = swap_cores(send_2, parts)
        *keep_2, w_mid_0 = split_call(jobs, args, ((w_mid, 0, True),), 0, "k_weights2", (send_2[0],))
        send_4 = split_call(jobs[2:], args, (), 1, "k_weights4", (keep_2[0],))
        got_2 = got_2 + swap_cores(send_4)
        (y1b,) = call(
            k_plus, [((4 * u, inner), BF16)], (y1b, y_got), (), "k_plus", (send_4[0], halo_f)
        )
        as_, a1 = first_sum(keep_2, got_2, (0,), (), "k_first2", (y1b, x_got))
        a_got = swap(as_, "dp", 2)
        xys, xy = second_sum(x1, x_got, "k_second1", (a1,))
        xy_got = swap(xys, "seq", 1)
        bs, b1 = first_sum(keep_2, got_2, (), (4,), "k_first5", (xy, *got_2[2], *got_2[3]))
        b_got = swap(bs, "seq", 1)
        line_y = line_half([], [y1b], 0, "k_line0", (b1,))
        e1_n0, vec = back0_call(True, vec, e2_n0, e2_f0, halo_n, p_n, (line_y[0],), (), 7)
        e1_f0, vec, a1_n, a1_f = back0_call(
            False, vec, e2_f0, e2_n0, halo_f, p_f, (e1_n0,), ((a1_n, None, True), (a1_f, None, True)), 1
        )
        vec, dx = dx_call(vec, ())
        jobs = (("half", (0, 1), (2, 3), None),)
        args = (a1_n, a1_f, e1_n0, e1_f0)
        send_3 = split_call(jobs, args, (), 1, "k_weights3", (vec,), parts=(2,))
        got_3 = swap_cores(send_3, (2,))
        keep_3 = split_call(jobs, args, (), 0, "k_weights3", (send_3[0],))
        (sums_y,) = call(k_plus, [((2 * u, inner), BF16)], line_y, (), "k_plus", (keep_3[0],))
        line_a = line_half([(xy, xy_got), (b1, b_got)], [], 0, "k_line1", (sums_y,))
        ays, ay = second_sum(a1, a_got, "k_second2", (line_a[0],), 0.3, (vec,))
        ay_got = swap(ays, "seq", 1)
        ds, d1 = first_sum(keep_2, got_2, (2,), (), "k_first3", (ay,), 2)
        d_got = swap(ds, "dp", 2)
        cs, c1 = first_sum(keep_3, got_3, (), (0,), "k_first4", (d1,))
        c_got = swap(cs, "seq", 1)
        token, y1 = out_call((c1,))
        line_a = line_half([line_a], [sums_y], 1, "k_line2", (token,))
        line_b = line_half([(ay, ay_got)], [], 0, "k_line3", (line_a[0],), 0, n_packed)
        line_e = line_half([(c1, c_got)], [], 0, "k_line4", (line_b[0],))
        dys, dy = second_sum(d1, d_got, "k_second3", (line_e[0],))
        dy_got = swap(dys, "seq", 1)
        sums_a = line_sums([line_a], (3 * u,), "k_sum1", (dy,), 0.7)
        a_rows = (sums_a, swap(sums_a, "dp", 2))
        line_b = line_half([line_b], [], 1, "k_line5", (sums_a,), 0, n_packed)
        line_e = line_half([line_e], [], 1, "k_line6", (line_b[0],), 2)
        line_c = line_half([(dy, dy_got)], [], 0, "k_line7", (line_e[0],))
        whole = row_sums([a_rows], ((1, 0, 0),), "k_rows1", (line_c[0],))
        sums_b = line_sums([line_b, line_e], (u, u), "k_sum2", (whole,), 1.5)
        b_rows = (sums_b, swap(sums_b, "dp", 2))
        line_c = line_half([line_c], [], 1, "k_line8", (sums_b,), 2)
        sums_c = line_sums([line_c], (u,), "k_sum3", (line_c[0],))
        c_rows = (sums_c, swap(sums_c, "dp", 2))
        whole = row_sums(
            [(whole,), b_rows, c_rows], (None, (1, 0), (1,)), "k_rows2", (sums_c,)
        )
        got = swap(whole, "dp", 1)
        shapes = ((2, 2 * u, inner), (2, taps, u, inner), (2, 2 * u, inner))
        vector_shapes = ((2, width), (2, width), (2, 2, inner), (2, 2, inner), (2, 2, inner), (2, width))
        grads = share(0, (place, whole), (), shapes, (), vec_shape[0], u)
        grad_w_in, grad_w_mid, grad_w_out, *vectors = share(
            1, (place, got, whole), grads, shapes, vector_shapes, vec_shape[0], u
        )
        return (
            y1[None], dx[None], grad_w_in, grad_w_mid.swapaxes(2, 3), grad_w_out.swapaxes(1, 2),
            *vectors,
        )

    narrow = vec[:n_narrow].reshape(2, 2, 3, inner)
    wide = vec[n_narrow:].reshape(2, 3, width)
    return (
        y1[None],
        dx[None],
        grad_w_in,
        grad_w_mid,
        grad_w_out,
        wide[:, 0],
        wide[:, 1],
        narrow[:, :, 0],
        narrow[:, :, 1],
        narrow[:, :, 2],
        wide[:, 2],
    )


def solution(mesh):
    row = P("dp", "seq", None)
    return jax.shard_map(
        body,
        mesh=mesh,
        in_specs=(row, P(None, "dp", "seq")) + (P(),) * 9 + (row,),
        out_specs=(
            row,
            row,
            P(None, "seq", None),
            P(None, None, None, "seq"),
            P(None, None, "seq"),
        )
        + (P(),) * 6,
        check_vma=False,
    )
```

```python
import functools

import jax
import jax.numpy as jnp
from jax import lax
from jax.experimental import pallas as pl
from jax.experimental.pallas import tpu as pltpu
from jax.sharding import PartitionSpec as P

DILATION_CLOSE = 4
DILATION_BROAD = 128
EPS = 1e-05
F32 = jnp.float32
BF16 = jnp.bfloat16
VMEM_LIMIT = 18 * 1024 * 1024
HEIGHT = 128
EXP2 = -0.7213475204444817

C0 = 0.3275911 * 0.7071067811865476
POLY = tuple(0.5 * c for c in (0.254829592, -0.284496736, 1.421413741, -1.453152027, 1.061405429))
ROOT_2PI = 0.3989422804014327


def normal_parts(q):
    bell = jnp.exp2((q * EXP2) * q)
    t = pltpu.reciprocal(1.0 + C0 * jnp.abs(q), approx=True)
    h = POLY[4]
    for c in POLY[3::-1]:
        h = h * t + c
    tail = h * t * bell
    return jnp.where(q >= 0, 1.0 - tail, tail), q * bell * ROOT_2PI


def act_forward(v, gain, shift):
    c = v.shape[-1]
    mean = jnp.sum(v, axis=-1, keepdims=True) * (1.0 / c)
    centred = v - mean
    r = lax.rsqrt(jnp.sum(centred * centred, axis=-1, keepdims=True) * (1.0 / c) + EPS)
    n = centred * r
    q = n * gain + shift
    below, slope = normal_parts(q)
    return mean, r, n, q * below, below + slope


def act_backward(f, n, r, d, gain):
    c = f.shape[-1]
    p = f * d
    gp = gain * p
    first = jnp.sum(gp, axis=-1, keepdims=True) * (1.0 / c)
    second = jnp.sum(gp * n, axis=-1, keepdims=True) * (1.0 / c)
    return p, r * (gp - first - n * second)


def fold(v):
    return jnp.sum(v.reshape(v.shape[0] // 8, 8, v.shape[1]), axis=0)


def total(acc):
    return jnp.sum(acc, axis=0, keepdims=True)


def lanes(column):
    return jnp.broadcast_to(column, (column.shape[0], 128))


def strips(rows, height, step, carry=(), unroll=8, first=0):
    turns = rows // (height * unroll)
    if turns <= 1:
        for j in range(rows // height):
            carry = step(pl.ds(first + j * height, height), carry)
        return carry

    def body(i, c):
        for j in range(unroll):
            c = step(pl.ds(pl.multiple_of((i * unroll + j) * height, height), height), c)
        return c

    return lax.fori_loop(0, turns, body, carry)


def staggered(rows, height, *stages):
    parts = [slice(i, i + height) for i in range(0, rows, height)]
    for t in range(len(parts) + len(stages) - 1):
        for i in reversed(range(len(stages))):
            if 0 <= t - i < len(parts):
                stages[i](parts[t - i])


def at_base(at, base):
    if isinstance(base, int) and base == 0:
        return at
    return pl.ds(pl.multiple_of(at.start + base, at.size), at.size)


def dot(a, b):
    return jnp.dot(a, b, preferred_element_type=F32)


def dot_nt(a, b):
    return lax.dot_general(a, b, (((1,), (1,)), ((), ())), preferred_element_type=F32)


class Loads:
    def __init__(self, sources, targets, sems):
        self.targets = targets
        self.copies = [
            pltpu.make_async_copy(src if b is None else src.at[b], dst, sems.at[i])
            for i, ((src, b), dst) in enumerate(zip(sources, targets))
        ]
        self.waiting = set(range(len(targets)))
        for copy in self.copies:
            copy.start()

    def get(self, i):
        if i in self.waiting:
            self.waiting.remove(i)
            self.copies[i].wait()
        return self.targets[i]

    def finish(self):
        for i in sorted(self.waiting):
            self.get(i)


class Stores:
    def __init__(self, held, targets, sems):
        self.held, self.targets, self.sems = held, targets, sems
        self.copies = []

    def put(self, *which, at=None):
        for i in which:
            src, dst = self.held[i], self.targets[i]
            if at is not None:
                src, dst = src.at[at], dst.at[at]
            copy = pltpu.make_async_copy(src, dst, self.sems.at[len(self.copies)])
            copy.start()
            self.copies.append(copy)

    def finish(self):
        for copy in self.copies:
            copy.wait()


def call(
    kernel, outs, args, scratch=(), name=None, deps=(), loads=(), stores=(), offloads=(), parts=1,
    limit=VMEM_LIMIT, cost=0,
):
    n_args, n_loads, n_deps, n_off = len(args), len(loads), len(deps), len(offloads)
    n_outs, n_stores = len(outs), len(stores)
    loaded = [(a.shape if b is None else a.shape[1:], a.dtype) for a, b, _ in loads]
    kept = [i for i, (_, _, keep) in enumerate(loads) if keep]
    brief = [i for i in range(n_loads) if i not in kept]
    out_shape = [pltpu.VMEM(s, t) for s, t in outs] + [pltpu.HBM(s, t) for s, t in stores]
    out_shape += [pltpu.VMEM(*loaded[i]) for i in kept]
    out_shape += [pltpu.HBM(a.shape, a.dtype) for a in offloads]

    def run(*refs):
        def take(n):
            nonlocal refs
            first, refs = refs[:n], refs[n:]
            return first

        ins, going, sources, _ = take(n_args), take(n_off), take(n_loads), take(n_deps)
        results, stored, held, gone = take(n_outs), take(n_stores), take(len(kept)), take(n_off)
        targets = dict(zip(kept, held))
        scr = list(refs)
        more = {}
        if n_loads:
            sems = scr.pop()
            for i in reversed(brief):
                targets[i] = scr.pop()
            sources = [(r, b) for r, (_, b, _) in zip(sources, loads)]
            more["coming"] = Loads(sources, [targets[i] for i in range(n_loads)], sems)
        if n_off:
            leaving = Stores(going, gone, scr.pop())
            leaving.put(*range(n_off))
        if n_stores:
            sems = scr.pop()
            held = [scr.pop() for _ in stores][::-1]
            more["keeping"] = Stores(held, stored, sems)
        kernel(*ins, *results, *scr, **more)
        for part in more.values():
            part.finish()
        if n_off:
            leaving.finish()

    hbm, vmem = pl.BlockSpec(memory_space=pltpu.HBM), pl.BlockSpec(memory_space=pltpu.VMEM)
    specs = [vmem] * (n_args + n_off) + [hbm] * n_loads
    specs += [pl.BlockSpec(memory_space=pl.ANY)] * n_deps
    out_specs = [vmem] * n_outs + [hbm] * n_stores + [vmem] * len(kept) + [hbm] * n_off
    scratch = list(scratch)
    if n_stores:
        scratch += [pltpu.VMEM(s, t) for s, t in stores]
        scratch += [pltpu.SemaphoreType.DMA((n_stores * parts,))]
    if n_off:
        scratch += [pltpu.SemaphoreType.DMA((n_off,))]
    if n_loads:
        scratch += [pltpu.VMEM(*loaded[i]) for i in brief] + [pltpu.SemaphoreType.DMA((n_loads,))]
    return pl.pallas_call(
        run,
        out_shape=out_shape,
        in_specs=specs,
        out_specs=out_specs,
        scratch_shapes=scratch,
        compiler_params=pltpu.CompilerParams(vmem_limit_bytes=limit),
        cost_estimate=pl.CostEstimate(flops=1 + int(cost * 1.15e9), bytes_accessed=1, transcendentals=0),
        name=name,
    )(
        *[pltpu.with_memory_space_constraint(a, pltpu.VMEM) for a in (*args, *offloads)],
        *[pltpu.with_memory_space_constraint(a, pltpu.HBM) for a, _, _ in loads],
        *deps,
    )


NEAR, CUT, LOW_0, LOW_1, HIGH_1, CORE, BIT_X, LINE = range(8)


def find_marks(bounds, place):
    rows = bounds.shape[2]
    first = lax.axis_index("seq") * rows
    marks = (bounds[1, 0:1, 0:1], bounds[0, 0:1, 0:1], bounds[0, 0:1, rows - 1 :], bounds[1, 0:1, rows - 1 :])
    for row, v in zip((CUT, LOW_0, LOW_1, HIGH_1), marks):
        place[row : row + 1] = jnp.broadcast_to(v - first, (1, 128))


def find_place(place):
    seq, dp = lax.axis_index("seq"), lax.axis_index("dp")
    for row, v in ((NEAR, seq & 1), (CORE, dp & 1), (BIT_X, dp >> 1), (LINE, seq >> 1)):
        place[row : row + 1] = jnp.full((1, 128), v, jnp.int32)


def base_of(place, near, rows):
    odd = place[NEAR, 0]
    return rows * (1 - odd) if near else rows * odd


def wide_act(x, base, gain, shift, a1, d1, stat, part):
    def wide(at, c):
        mean, r, n, a, d = act_forward(x[at_base(at, base)].astype(F32), gain, shift)
        a1[at], d1[at] = a.astype(BF16), d.astype(BF16)
        stat[0, at], stat[1, at] = lanes(mean), lanes(r)
        return c

    strips(part.stop - part.start, 32, wide, first=part.start)


def narrow_act(z, gain, shift, a, n, d, stat, part):
    def narrow(at, c):
        _, r, nn, aa, dd = act_forward(z[at], gain, shift)
        n[at], d[at], a[at] = nn.astype(BF16), dd.astype(BF16), aa.astype(BF16)
        stat[at] = lanes(r)
        return c

    strips(part.stop - part.start, 32, narrow, first=part.start)


def windows(place, near, own, other, halo, win, pad, step):
    rows, width = own.shape
    taps = win.shape[1] // width
    rim = (pad.shape[0] - rows) // 2
    pad[rim : rim + rows] = own[...].astype(pad.dtype)
    lower = place[NEAR, 0] == (1 if near else 0)

    @pl.when(lower)
    def _():
        pad[0:rim] = halo[halo.shape[0] - rim :].astype(pad.dtype)
        pad[rim + rows :] = other[0:rim].astype(pad.dtype)

    @pl.when(jnp.logical_not(lower))
    def _():
        pad[0:rim] = other[rows - rim :].astype(pad.dtype)
        pad[rim + rows :] = halo[0:rim].astype(pad.dtype)

    base = base_of(place, near, rows)
    cut, low_0, low_1, high_1 = (place[i : i + 1] for i in (CUT, LOW_0, LOW_1, HIGH_1))
    height = 64

    def fill(part):
        for i in range(part.start, part.stop, height):
            rows_at(i)

    def rows_at(i):
        t = lax.broadcasted_iota(jnp.int32, (height, 128), 0) + (base + i)
        first = t < cut
        low = jnp.where(first, low_0, low_1)
        high = jnp.where(first, cut, high_1)
        for k in range(taps):
            offset = (k - taps // 2) * step
            m = jnp.where((t + offset >= low) & (t + offset < high), 1.0, 0.0).astype(pad.dtype)
            m = jnp.concatenate([m] * (width // 128), axis=1)
            start = rim + offset + i
            win[i : i + height, k * width : (k + 1) * width] = (
                pad[start : start + height] * m
            ).astype(BF16)

    return fill


def put_edge(edge, v, place, near):
    n = edge.shape[0]
    lower = place[NEAR, 0] == (1 if near else 0)

    @pl.when(lower)
    def _():
        edge[...] = v[0:n]

    @pl.when(jnp.logical_not(lower))
    def _():
        edge[...] = v[v.shape[0] - n :]


def first_half(x, base, gw, sw, w_in, bn, gn, sn, a1, d1, stat1, a2, n2, d2, r2, z, keeping):
    rows = a1.shape[0]

    def wide(p):
        wide_act(x, base, gw(), sw(), a1, d1, stat1, p)
        if p.stop == rows:
            keeping.put(*FIRST_STORES[len(keeping.held)])

    def inner(p):
        z[p] = dot(a1[p], w_in()[...]) + bn()

    def narrow(p):
        narrow_act(z, gn(), sn(), a2, n2, d2, r2, p)

    return wide, inner, narrow


FIRST_STORES = {3: (0, 1, 2), 7: (4, 5, 6)}


def k_in_near(place, a2, n2, d2, r2, edge, z, *, coming, keeping):
    a1, d1, stat1 = keeping.held
    find_place(place)
    x = coming.get(0)
    staggered(a1.shape[0], a1.shape[0], *first_half(
        x, base_of(place, True, a1.shape[0]), lambda: coming.get(1)[0:1], lambda: coming.get(2)[0:1],
        lambda: coming.get(3), lambda: coming.get(6)[0, 0:1], lambda: coming.get(4)[0, 0:1],
        lambda: coming.get(5)[0, 0:1], a1, d1, stat1, a2, n2, d2, r2, z, keeping,
    ))
    put_edge(edge, a2, place, True)
    find_marks(coming.get(9), place)


def k_in_far(place, x, gw, sw, gn, sn, bn, a2, n2, d2, r2, edge, z, *, coming, keeping):
    a1, d1, stat1 = keeping.held
    staggered(a1.shape[0], a1.shape[0], *first_half(
        x, base_of(place, False, a1.shape[0]), lambda: gw[0:1], lambda: sw[0:1],
        lambda: coming.get(0), lambda: bn[0, 0:1], lambda: gn[0, 0:1], lambda: sn[0, 0:1],
        a1, d1, stat1, a2, n2, d2, r2, z, keeping,
    ))
    put_edge(edge, a2, place, False)


def k_mid(
    place, x, own, other, halo, w_mid, gw, sw, bw, gn, sn, bn,
    a3, r3, a2, n2, d2, r2, pad, z, z1, *, near, step, coming, keeping,
):
    rows, width = own.shape
    win, n3, d3, y, a1, d1, stat1 = keeping.held
    fill = windows(place, near, own, other, halo, win, pad, step)
    base = base_of(place, near, rows)
    weights = w_mid[...].reshape(win.shape[1], width)

    def conv(p):
        fill(p)
        z[p] = dot(win[p], weights) + bn[0, 1:2]
        if p.stop == rows:
            keeping.put(0)

    def narrow(p):
        narrow_act(z, gn[0, 1:2], sn[0, 1:2], a3, n3, d3, r3, p)
        if p.stop == rows:
            keeping.put(1, 2)

    def outer(p):
        n = p.stop - p.start
        old = x[pl.ds(pl.multiple_of(base + p.start, n), n)].astype(F32)
        y[p] = old + dot(a3[p], coming.get(0)[...]) + bw[0:1]
        if p.stop == rows:
            keeping.put(3)

    staggered(rows, HEIGHT, conv, narrow, outer, *first_half(
        y, 0, lambda: gw[1:2], lambda: sw[1:2], lambda: coming.get(1), lambda: bn[1, 0:1],
        lambda: gn[1, 0:1], lambda: sn[1, 0:1], a1, d1, stat1, a2, n2, d2, r2, z1, keeping,
    ))


def put_wide(vec, row, acc):
    inner = vec.shape[1]
    for i in range(acc.shape[1] // inner):
        vec[row + i : row + i + 1] += total(acc[:, i * inner : (i + 1) * inner])


def k_flow(e, w_out, f, vec, *, row, coming):
    f[...] = dot_nt(e[...], w_out[...])
    vec[...] = jnp.zeros_like(vec)

    def step(at, acc):
        return acc + fold(e[at].astype(F32))

    put_wide(vec, row, strips(e.shape[0], 32, step, jnp.zeros((8, e.shape[1]), F32)))


def k_conv(
    place, vec_in, own, other, halo, w_mid, gn, sn, bn, f, a3, e2, vec, win, pad, z, *, near, step, row
):
    rows, width = own.shape
    windows(place, near, own, other, halo, win, pad, step)(slice(0, own.shape[0]))
    z[...] = dot(win[...], w_mid[...].reshape(win.shape[1], width)) + bn[1, 1:2]
    gain = gn[1, 1:2]
    base = base_of(place, near, rows)

    def narrow(at, c):
        _, r, n, a, d = act_forward(z[at], gain, sn[1, 1:2])
        a3[at] = a.astype(BF16)
        p, v = act_backward(f[at_base(at, base)], n, r, d, gain)
        e = v.astype(BF16)
        e2[at] = e
        return c[0] + fold(p * n), c[1] + fold(p), c[2] + fold(e.astype(F32))

    vec[...] = vec_in[...]
    zero = jnp.zeros((8, width), F32)
    for i, acc in enumerate(strips(rows, 32, narrow, (zero,) * 3)):
        vec[row + i : row + i + 1] += total(acc)


def k_out(place, a_n, a_f, bw, token, *, coming, keeping):
    half = a_n.shape[0]
    token[...] = jnp.zeros_like(token)
    (y,) = keeping.held
    w_out = coming.get(0)
    for near, a in ((True, a_n), (False, a_f)):
        at = pl.ds(pl.multiple_of(base_of(place, near, half), half), half)
        y[at] = dot(a[...], w_out[...]) + bw[1:2] + coming.get(1 if near else 2)[...]
        keeping.put(0, at=at)


def back_narrow(f, n, d, r, gain, e_out, vec, row):
    rows, width = f.shape

    def step(at, c):
        nn = n[at].astype(F32)
        p, v = act_backward(f[at], nn, r[at][:, 0:1], d[at].astype(F32), gain)
        e = v.astype(BF16)
        e_out[at] = e
        return c[0] + fold(p * nn), c[1] + fold(p), c[2] + fold(e.astype(F32))

    zero = jnp.zeros((8, width), F32)
    for i, acc in enumerate(strips(rows, 32, step, (zero,) * 3)):
        vec[row + i : row + i + 1] += total(acc)


def back_wide(f, x, x_base, stat, d, gain, dy, dy_base, out, out_base, cast, vec, row, cast_row):
    rows, width = f.shape

    def step(at, c):
        r = stat[1, at][:, 0:1]
        n = (x[at_base(at, x_base)].astype(F32) - stat[0, at][:, 0:1]) * r
        p, v = act_backward(f[at], n, r, d[at].astype(F32), gain)
        dx = dy[at_base(at, dy_base)].astype(F32) + v
        out[at_base(at, out_base)] = dx
        sums = (c[0] + fold(p * n), c[1] + fold(p))
        if cast is not None:
            e = dx.astype(BF16)
            cast[at] = e
            sums += (c[2] + fold(e.astype(F32)),)
        return sums

    zero = jnp.zeros((8, width), F32)
    sums = strips(rows, 32, step, (zero,) * (2 if cast is None else 3), 8)
    put_wide(vec, row, sums[0])
    put_wide(vec, row + width // vec.shape[1], sums[1])
    if cast is not None:
        put_wide(vec, cast_row, sums[2])


def flow_two(win, w_mid, z):
    taps, width = w_mid.shape[0], w_mid.shape[1]
    for j in range(taps):
        part = dot_nt(win[:, j * width : (j + 1) * width], w_mid[taps - 1 - j])
        if j == 0:
            z[...] = part
        else:
            z[...] += part


def k_back1(
    place, vec_in, own, other, halo, w_mid, gw, gn,
    e1, e3, e2, edge, vec, win, pad, z, f1, *, near, step, rows_of, coming, keeping,
):
    vec[...] = vec_in[...]
    windows(place, near, own, other, halo, win, pad, step)(slice(0, own.shape[0]))
    flow_two(win, w_mid, z)
    n2, d2, r2, w_in = (coming.get(i) for i in range(4))
    back_narrow(z, n2, d2, r2, gn[1, 0:1], e1, vec, rows_of[0])
    f1[...] = dot_nt(e1[...], w_in[...])
    base = base_of(place, near, own.shape[0])
    (dx,) = keeping.held
    x, d1, stat1, dy = (coming.get(i) for i in range(4, 8))
    back_wide(f1, x, 0, stat1, d1, gw[1:2], dy, base, dx, 0, e3, vec, rows_of[1], rows_of[3])
    keeping.put(0)
    w_out, n3, d3, r3 = (coming.get(i) for i in range(8, 12))
    z[...] = dot_nt(e3[...], w_out[...])
    back_narrow(z, n3, d3, r3, gn[0, 1:2], e2, vec, rows_of[2])
    put_edge(edge, e2, place, near)


def k_back0(
    place, vec_in, own, other, halo, w_mid, gn, e1, vec, win, pad, z, *, near, step, row, coming
):
    vec[...] = vec_in[...]
    halo = halo.at[pl.ds(halo.shape[0] - 16, 16)]
    windows(place, near, own, other, halo, win, pad, step)(slice(0, own.shape[0]))
    flow_two(win, w_mid, z)
    n2, d2, r2 = (coming.get(i) for i in range(3))
    back_narrow(z, n2, d2, r2, gn[0, 0:1], e1, vec, row)


def k_dx(place, vec_in, gw, e1_n, e1_f, vec, f1, *, row, coming, keeping):
    vec[...] = vec_in[...]
    half = e1_n.shape[0]
    (out,) = keeping.held
    w_in, x = coming.get(0), coming.get(1)
    for near, e1 in ((True, e1_n), (False, e1_f)):
        f1[...] = dot_nt(e1[...], w_in[...])
        d, stat, dy = (coming.get(i + (0 if near else 3)) for i in (2, 3, 4))
        base = base_of(place, near, half)
        back_wide(f1, x, base, stat, d, gw[0:1], dy, 0, out, base, None, vec, row, None)
        keeping.put(0, at=pl.ds(pl.multiple_of(base, half), half))


def k_split(place, *refs, jobs, parts, side, coming=None):
    n_outs = sum(parts)
    outs, turned = list(refs[-1 - n_outs : -1]), refs[-1]
    refs = refs[: -1 - n_outs]
    _, shards, _, u, rows = turned.shape
    inner = outs[0].shape[-1]

    def ref(i):
        return refs[i] if i < len(refs) else coming.get(i - len(refs))

    def whole(places, at=slice(None)):
        if len(places) == 1:
            half = rows // 2
            bases = [base_of(place, near, half) for near in (True, False)]
            parts = [ref(places[0])[pl.ds(pl.multiple_of(b, half), half)] for b in bases]
        else:
            parts = [ref(i)[:, at] for i in places]
        return jnp.concatenate(parts, axis=0)

    core = place[CORE, 0] ^ side
    kept = {}
    halves = 0
    for n, (kind, left, right, j) in zip(parts, jobs):
        here, outs = outs[:n], outs[n:]

        def put(product):
            height = product.shape[0] // n
            for i, out in enumerate(here):
                out[...] = product[i * height : (i + 1) * height]

        if kind == "half":
            turned[halves] = whole(left).T.reshape(turned.shape[1:])
            part = turned[halves, :, core].reshape(shards * u, rows)
            put(dot(part, whole(right)).astype(BF16))
            halves += 1
            continue
        if left not in kept:
            kept[left] = whole(left).T
        if kind == "taps":
            at = pl.ds(pl.multiple_of((j + 2 * core) * inner, 128), inner)
            put(dot(kept[left], whole(right, at)).astype(BF16))
            continue
        tap, before = j

        @pl.when(core == 0)
        def _():
            put(ref(before)[...])

        @pl.when(core != 0)
        def _():
            at = slice(tap * inner, (tap + 1) * inner)
            put(dot(kept[left], whole(right, at)).astype(BF16))


def k_tap(e_n, e_f, win_n, win_f, out, *, tap):
    inner = out.shape[-1]
    at = slice(tap * inner, (tap + 1) * inner)
    left = jnp.concatenate([e_n[...], e_f[...]], axis=0).T
    right = jnp.concatenate([win_n[:, at], win_f[:, at]], axis=0)
    out[...] = dot(left, right).astype(BF16)


def added(*parts):
    first, *rest = [p.astype(F32) for p in parts]
    for p in rest:
        first = first + p
    return first


def k_first(place, *refs, pairs, singles, edge):
    refs = list(refs)
    x, y = place[BIT_X, 0], place[NEAR, 0]

    def take(n):
        first = refs[:n]
        del refs[:n]
        return first

    ins = [(take(1)[0], take(n)) for two_units in pairs for n in two_units]
    ins += [(take(1)[0], take(n)) for n in singles]
    rim = take(1)[0] if edge else None

    def add_rows(a, parts, out):
        height = a.shape[0] // len(parts)
        for i, b in enumerate(parts):

            def step(k, c):
                here = pl.ds(pl.multiple_of(k * 80, 80), 80)
                at = pl.ds(pl.multiple_of(i * height + k * 80, 80), 80)
                out[at] = added(a[at], b[here]).astype(BF16)
                return c

            lax.fori_loop(0, height // 80, step, 0)

    for i in range(len(pairs)):
        (a0, b0), (a1, b1) = ins[2 * i : 2 * i + 2]
        send, stay = take(2)

        @pl.when(x == 0)
        def _():
            add_rows(a1, b1, send)
            add_rows(a0, b0, stay)

        @pl.when(x != 0)
        def _():
            add_rows(a0, b0, send)
            add_rows(a1, b1, stay)

    for out, side in zip(refs, (1 - y, y)):
        at = 0
        for a, parts in ins[2 * len(pairs) :]:
            u = a.shape[2]
            each = a.shape[0] // len(parts)
            for k in range(a.shape[0]):
                b = parts[k // each]
                out[at : at + u] = added(a[k, side], b[k % each, side]).astype(BF16)
                at += u
    if edge:
        refs[0][at:] = rim[...]


def k_second(place, a, b, *refs):
    *vec, send, stay = refs
    mine = place[NEAR, 0]
    u = a.shape[2]
    for out, side in ((send, 1 - mine), (stay, mine)):

        def step(k, c):
            at = pl.ds(pl.multiple_of(k * u, u), u)
            out[at] = added(a[k, side], b[k, side]).astype(BF16)
            return c

        lax.fori_loop(0, 4, step, 0)
    if vec:
        pack(vec[0][...], send, stay, at=4 * u)


def pack(v, *outs, at):
    upper = v.astype(BF16).astype(F32)
    parts = jnp.concatenate([upper, v - upper], axis=0).astype(BF16)
    for out in outs:
        out[at : at + parts.shape[0]] = parts


def unpack(ref, at):
    parts = ref[at:].astype(F32)
    n = parts.shape[0] // 2
    return parts[:n] + parts[n:]


def k_line(place, *refs, sums, wholes, packed, bit, u):
    mine = (place[LINE, 0] >> bit) & 1
    arrays = [refs[2 * i : 2 * i + 2] for i in range(sums)]
    arrays += [refs[2 * sums + i : 2 * sums + i + 1] for i in range(wholes)]
    send, stay = refs[2 * sums + wholes :]
    for out, side in ((send, 1 - mine), (stay, mine)):
        at = 0
        for i, parts in enumerate(arrays):
            rows = parts[0].shape[0] - (packed if i == 0 else 0)
            for j in range(rows // (2 * u)):
                part = pl.ds(pl.multiple_of((2 * j + side) * u, u), u)
                out[at : at + u] = added(*[p[part] for p in parts]).astype(BF16)
                at += u
    if packed:
        a, b = arrays[0]
        n = a.shape[0] - packed
        pack(unpack(a, n) + unpack(b, n), send, stay, at=send.shape[0] - packed)


def k_sum(place, *refs, rows):
    out = refs[-1]
    at = 0
    for i, n in enumerate(rows):
        a, b = refs[2 * i], refs[2 * i + 1]
        out[at : at + n] = added(a[0:n], b[0:n]).astype(BF16)
        at += n
    if refs[0].shape[0] > rows[0]:
        pack(unpack(refs[0], rows[0]) + unpack(refs[1], rows[0]), out, at=at)


def k_rows(place, *refs, splits, u):
    *refs, out = refs
    x = place[BIT_X, 0]
    at = 0
    refs = list(refs)
    for split in splits:
        if split is None:
            ready = refs.pop(0)
            out[at : at + ready.shape[0]] = ready[...]
            at += ready.shape[0]
            continue
        mine, got = refs.pop(0), refs.pop(0)
        for k, apart in enumerate(split):
            here = slice(k * u, (k + 1) * u)
            if apart:
                base = pl.multiple_of(at + x * u, u)
                other = pl.multiple_of(at + (1 - x) * u, u)
                out[pl.ds(base, u)], out[pl.ds(other, u)] = mine[here], got[here]
                at += 2 * u
            else:
                out[at : at + u] = added(mine[here], got[here]).astype(BF16)
                at += u
        if mine.shape[0] > len(split) * u:
            n = len(split) * u
            pack(unpack(mine, n) + unpack(got, n), out, at=out.shape[0] - (mine.shape[0] - n))


def k_share(place, ref, *refs, side, u):
    vectors, n_vec = (), 0
    if side:
        mine, *refs = refs
        refs = refs[3:]
        n_vec = 6
    out_in, out_mid, out_out = refs[:3]
    vectors, refs = refs[3 : 3 + n_vec], refs[3 + n_vec :]
    stage, held, sems = refs[0], refs[1:-1], refs[-1]
    c = place[CORE, 0] ^ side
    rows = pl.ds(pl.multiple_of(c * u, u), u)
    copies = []

    def put(src, dst):
        copies.append(pltpu.make_async_copy(src, dst, sems.at[len(copies)]))
        copies[-1].start()

    def units(i, n=1):
        for k in range(i, i + n):
            stage[k] = ref[k * u : (k + 1) * u].astype(F32)
        return stage.at[i] if n == 1 else stage.at[i : i + n]

    put(units(0, 2), out_mid.at[1, pl.ds(2 * c, 2)])
    put(units(2), out_mid.at[1 - c, 4])
    put(units(3), out_out.at[1, rows])
    put(units(4, 2), out_mid.at[0, pl.ds(2 * c, 2)])
    put(units(6), out_in.at[0, rows])
    put(units(7), out_in.at[1, rows])
    put(units(8), out_out.at[0, rows])
    if side:
        vec, gw, sw, gn, sn, bn, bw = held
        vec[...] = unpack(mine, 9 * u) + unpack(ref, 9 * u)
        inner = vec.shape[1]
        two = gw.shape[1] // inner
        for block in range(2):
            for i in range(2):
                row = 3 * (2 * block + i)
                for j, out in enumerate((gn, sn, bn)):
                    out[block, i : i + 1] = vec[row + j : row + j + 1]
            for j, out in enumerate((gw, sw, bw)):
                for k in range(two):
                    row = 12 + (3 * block + j) * two + k
                    out[block : block + 1, k * inner : (k + 1) * inner] = vec[row : row + 1]
        for src, dst in zip((gw, sw, gn, sn, bn, bw), vectors):
            put(src, dst)
    for copy in copies:
        copy.wait()


def share(side, args, before, shapes, vector_shapes, vec_shape, u):
    inner = shapes[0][-1]
    vmem, hbm = pl.BlockSpec(memory_space=pltpu.VMEM), pl.BlockSpec(memory_space=pltpu.HBM)
    outs = list(shapes) + list(vector_shapes)
    held = [pltpu.VMEM(s, F32) for s in ([vec_shape] + list(vector_shapes) if side else [])]
    return pl.pallas_call(
        functools.partial(k_share, side=side, u=u),
        out_shape=[pltpu.HBM(s, F32) for s in outs],
        in_specs=[vmem] * len(args) + [hbm] * len(before),
        out_specs=[hbm] * len(outs),
        scratch_shapes=[pltpu.VMEM((9, u, inner), F32), *held, pltpu.SemaphoreType.DMA((7 + len(vector_shapes),))],
        input_output_aliases={len(args) + i: i for i in range(len(before))},
        compiler_params=pltpu.CompilerParams(vmem_limit_bytes=VMEM_LIMIT),
        cost_estimate=pl.CostEstimate(flops=1, bytes_accessed=1, transcendentals=0),
        name="k_share",
    )(
        *[pltpu.with_memory_space_constraint(a, pltpu.VMEM) for a in args],
        *[pltpu.with_memory_space_constraint(a, pltpu.HBM) for a in before],
    )


def k_plus(a, b, out):
    out[...] = added(a[...], b[0 : a.shape[0]]).astype(BF16)


def k_nothing(*refs, coming):
    pass


def swap(v, axis, bits):
    count = lax.axis_size(axis)
    return lax.ppermute(v, axis, [(i, i ^ bits) for i in range(count)])


def to_near(v):
    return swap(v, "seq", 1)


def to_far(v):
    count = lax.axis_size("seq")
    pairs = [(i, i + 1) for i in range(1, count - 1, 2)]
    return lax.ppermute(v, "seq", pairs + [(j, i) for i, j in pairs])


def dot_tn(a, b):
    return lax.dot_general(a, b, (((0,), (0,)), ((), ())), preferred_element_type=F32)


def plain_weights(a1, e1, win, e2, a3, e3):
    taps = win.shape[1] // e2.shape[1]
    grad_mid = dot_tn(win, e2).reshape(taps, e2.shape[1], e2.shape[1])
    shares = (
        lax.psum_scatter(dot_tn(a1, e1), "seq", scatter_dimension=0, tiled=True),
        lax.psum_scatter(grad_mid, "seq", scatter_dimension=2, tiled=True),
        lax.psum_scatter(dot_tn(a3, e3), "seq", scatter_dimension=1, tiled=True),
    )
    return [lax.psum(v.astype(BF16), "dp").astype(F32) for v in shares]


def body(
    tokens, bounds, w_in, w_mid, w_out, gain_wide, shift_wide, gain_narrow, shift_narrow,
    bias_narrow, bias_wide, cotangent,
):
    x0 = tokens[0]
    cot = cotangent[0]
    rows, width = x0.shape
    taps, inner = w_mid.shape[1], w_mid.shape[2]
    shards = lax.axis_size("seq")
    u = inner // shards
    two = width // inner
    half = rows // 2
    close, broad = DILATION_CLOSE, DILATION_BROAD

    wide_h, narrow_h, column = (half, width), (half, inner), ((half, 128), F32)
    win_h = ((half, taps * inner), BF16)
    act_wide = [(wide_h, BF16), (wide_h, BF16), ((2, half, 128), F32)]
    act_narrow = [(narrow_h, BF16), (narrow_h, BF16), (narrow_h, BF16), column]
    edge = ((16, inner), BF16)
    z = pltpu.VMEM(narrow_h, F32)
    f1 = pltpu.VMEM(wide_h, F32)
    win_scratch = pltpu.VMEM(*win_h)
    pad_0 = pltpu.VMEM((half + 32, inner), F32)
    pad_1 = pltpu.VMEM((half + 4 * broad, inner), BF16)
    n_narrow = 12
    vec_shape = ((n_narrow + 6 * two, inner), F32)

    def row_narrow(b, i):
        return 3 * (2 * b + i)

    def row_wide(b, i):
        return n_narrow + (3 * b + i) * two

    def brief(*arrays):
        return tuple((a, None, False) for a in arrays)

    place, a2_n, *p_n, edge_n, a1_n, d1_n, stat_n, x, gw, sw, gn, sn, bn, bw, w_mid_0 = call(
        k_in_near, [((8, 128), jnp.int32)] + act_narrow + [edge], (), [z], "k_in",
        loads=((x0, None, True), (gain_wide, None, True), (shift_wide, None, True), (w_in, 0, False),
               (gain_narrow, None, True), (shift_narrow, None, True), (bias_narrow, None, True),
               (bias_wide, None, True), (w_mid, 0, True), (bounds, None, False)),
        stores=act_wide, cost=4,
    )
    halo_n = to_near(edge_n)
    a2_f, *p_f, edge_f, a1_f, d1_f, stat_f, p1, p2, p3 = call(
        k_in_far, act_narrow + [edge], (place, x, gw, sw, gn, sn, bn), [z], "k_in", (edge_n,),
        loads=((w_in, 0, False),), stores=act_wide, offloads=p_n, cost=4,
    )
    p_n = (p1, p2, p3)
    halo_f = to_far(edge_f)

    def mid_call(near, own, other, halo, deps, loads, offloads):
        return call(
            functools.partial(k_mid, near=near, step=close),
            [(narrow_h, BF16), column] + act_narrow,
            (place, x, own, other, halo, w_mid_0, gw, sw, bw, gn, sn, bn),
            [pad_0, z, z], "k_mid", deps, ((w_out, 0, False), (w_in, 1, False)) + loads,
            [win_h, (narrow_h, BF16), (narrow_h, BF16), (wide_h, F32)] + act_wide, offloads, cost=8,
        )

    a3_n, r3_n, b2_n, *q_n = mid_call(True, a2_n, a2_f, halo_n, (), (), p_f)
    s_n, p_f = q_n[3:10], q_n[10:]
    halo_n = to_near(b2_n)
    a3_f, r3_f, b2_f, *q_f = mid_call(
        False, a2_f, a2_n, halo_f, (b2_n,), ((w_out, 1, True), (cot, None, True)),
        (a3_n, r3_n, *q_n[:3]),
    )
    s_f, (w_out_1, cot_v), q_n = q_f[3:10], q_f[10:12], q_f[12:]
    halo_f = to_far(b2_f)
    f3, vec, w_mid_1, *q_f = call(
        functools.partial(k_flow, row=row_wide(1, 2)),
        [((rows, inner), F32), vec_shape], (cot_v, w_out_1), (), "k_flow",
        loads=((w_mid, 1, True),), offloads=(a3_f, r3_f, *q_f[:3]), cost=3,
    )

    def conv_call(near, vec, own, other, halo):
        return call(
            functools.partial(k_conv, near=near, step=broad, row=row_narrow(1, 1)),
            [(narrow_h, BF16), (narrow_h, BF16), vec_shape, win_h],
            (place, vec, own, other, halo, w_mid_1, gn, sn, bn, f3),
            [pad_1, z], "k_conv", cost=3,
        )

    c3_n, e2_n, vec, win_n = conv_call(True, vec, b2_n, b2_f, halo_n)
    halo_n = to_near(e2_n)
    c3_f, e2_f, vec, win_f = conv_call(False, vec, b2_f, b2_n, halo_f)
    halo_f = to_far(e2_f)

    fast = shards == 8 and u % 16 == 0
    unit = (inner, inner)
    part = (u, inner)

    def split_call(jobs, args, loads, side, name, deps, cost=0, parts=None):
        parts = parts or (1,) * len(jobs)
        halves = sum(kind == "half" for kind, *_ in jobs)
        turned = pltpu.VMEM((halves, shards, 2, u, rows), BF16)
        return call(
            functools.partial(k_split, jobs=jobs, side=side, parts=parts),
            [((inner // n, inner), BF16) for n in parts for _ in range(n)],
            (place, *args), [turned], name, deps, loads, cost=cost,
        )

    def swap_cores(units, parts=None):
        got = [swap(v, "dp", 1) for v in units]
        parts = parts or (1,) * len(units)
        return [tuple(got.pop(0) for _ in range(n)) for n in parts]

    def first_sum(keep, got, pairs, singles, name, deps, cost=0, edge=()):
        args = []
        for i in [j for pair in pairs for j in (pair, pair + 1)]:
            args += [keep[i], *got[i]]
        for i in singles:
            args += [v.reshape(-1, 2, u, inner) for v in (keep[i], *got[i])]
        outs = [(unit, BF16)] * (2 * len(pairs))
        n = 4 * u * len(singles)
        if singles:
            outs += [((n + sum(v.shape[0] for v in edge), inner), BF16), ((n, inner), BF16)]
        kernel = functools.partial(
            k_first, pairs=tuple((len(got[i]), len(got[i + 1])) for i in pairs),
            singles=tuple(len(got[i]) for i in singles), edge=bool(edge),
        )
        return call(kernel, outs, (place, *args, *edge), (), name, deps, cost=cost)

    n_packed = 2 * vec_shape[0][0]

    def second_sum(stay, got, name, deps, cost=0, vec=()):
        views = [v.reshape(4, 2, u, inner) for v in (stay, got)]
        n = 4 * u + (n_packed if vec else 0)
        return call(
            k_second, [((n, inner), BF16)] * 2, (place, *views, *vec), (), name, deps, cost=cost
        )

    def line_half(pairs, wholes, bit, name, deps, cost=0, packed=0):
        arrays = [pair[0] for pair in pairs] + list(wholes)
        n = sum(a.shape[0] for a in arrays) - packed
        n = n // 2 + packed
        kernel = functools.partial(k_line, sums=len(pairs), wholes=len(wholes), packed=packed, bit=bit, u=u)
        send, stay = call(
            kernel, [((n, inner), BF16)] * 2, (place, *[v for pair in pairs for v in pair], *wholes),
            (), name, deps, cost=cost,
        )
        return stay, swap(send, "seq", 2 << bit)

    def line_sums(pairs, rows, name, deps, cost=0):
        n = sum(rows) + pairs[0][0].shape[0] - rows[0]
        return call(
            functools.partial(k_sum, rows=rows), [((n, inner), BF16)],
            (place, *[v for pair in pairs for v in pair]), (), name, deps, cost=cost,
        )[0]

    def row_sums(pairs, splits, name, deps):
        n = sum(pair[0].shape[0] for pair in pairs) + u * sum(sum(split or ()) for split in splits)
        return call(
            functools.partial(k_rows, splits=splits, u=u), [((n, inner), BF16)],
            (place, *[v for pair in pairs for v in pair]), (), name, deps,
        )[0]

    def back1_call(near, vec, own, other, halo, q, s, deps, more=()):
        return call(
            functools.partial(
                k_back1, near=near, step=broad,
                rows_of=(row_narrow(1, 0), row_wide(1, 0), row_narrow(0, 1), row_wide(0, 2)),
            ),
            [(narrow_h, BF16), (wide_h, BF16), (narrow_h, BF16), edge, vec_shape],
            (place, vec, own, other, halo, w_mid_1, gw, gn),
            [win_scratch, pad_1, z, f1], "k_back1", deps, stores=[(wide_h, F32)], cost=5 if near else 2,
            loads=(*brief(*q[2:5]), (w_in, 1, False), *brief(s[3], s[5], s[6], cot),
                   (w_out, 0, False), *brief(s[1], s[2], q[1]), *more),
        )

    def back0_call(near, vec, own, other, halo, p, deps, loads, cost=0):
        return call(
            functools.partial(k_back0, near=near, step=close, row=row_narrow(0, 0)),
            [(narrow_h, BF16), vec_shape], (place, vec, own, other, halo, w_mid_0, gn),
            [win_scratch, pad_0, z], "k_back0", deps, loads=brief(*p) + loads, cost=cost,
        )

    def out_call(deps):
        return call(
            k_out, [((8, 128), F32)], (place, c3_n, c3_f, bw), (), "k_out", deps,
            loads=((w_out, 1, False), *brief(s_n[3], s_f[3])), stores=[((rows, width), F32)], parts=2,
        )

    def dx_call(vec, deps):
        return call(
            functools.partial(k_dx, row=row_wide(0, 0)), [vec_shape],
            (place, vec, gw, e1_n0, e1_f0), [f1], "k_dx", deps,
            loads=((w_in, 0, False), *brief(x0, d1_n, stat_n, dx_n, d1_f, stat_f, dx_f)),
            stores=[((rows, width), F32)], parts=2,
        )

    def rowed(v):
        return v.reshape(-1, inner)

    if fast:
        jobs = (("taps", (0, 1), (5, 6), 0), ("taps", (0, 1), (5, 6), 1), ("half", (2,), (3, 4), None))
        args = (e2_n, e2_f, cot_v, c3_n, c3_f, win_n, win_f)
        send_1 = split_call(jobs, args, (), 1, "k_weights1", (vec,))
        got_1 = swap_cores(send_1)
        keep_1 = split_call(jobs, args, (), 0, "k_weights1", (send_1[0],))
        last = keep_1[0]
    else:
        last = vec
    e1_n, e3_n, e2_n0, edge_n, vec, dx_n = back1_call(
        True, vec, e2_n, e2_f, halo_n, q_n, s_n, (last,)
    )
    if fast:
        xs, x1, ys, y1b = first_sum(
            keep_1, got_1, (0,), (2,), "k_first1", (vec, halo_f), 0, (edge_n,)
        )
        x_got, y_got = swap(xs, "dp", 2), swap(ys, "seq", 1)
        (tap_1,) = call(
            functools.partial(k_tap, tap=4), [(unit, BF16)], (e2_n, e2_f, win_n, win_f), (), "k_tap",
            (x1,),
        )
        halo_n, last = y_got, tap_1
    else:
        halo_n = to_near(edge_n)
    more = tuple((v, None, True) for v in (s_n[0], s_f[0], s_n[4], s_f[4], q_n[0], q_f[0])) if fast else ()
    e1_f, e3_f, e2_f0, edge_f, vec, dx_f, *held = back1_call(
        False, vec, e2_f, e2_n, halo_f, q_f, s_f, (last,), more
    )
    halo_f = to_far(edge_f)

    if not fast:
        (w_mid_0,) = call(k_nothing, [], (place,), (), "k_load", (vec,), ((w_mid, 0, True),))
        e1_n0, vec = back0_call(True, vec, e2_n0, e2_f0, halo_n, p_n, (), ())
        e1_f0, vec = back0_call(False, vec, e2_f0, e2_n0, halo_f, p_f, (), ())
        token, y1 = out_call((vec,))
        vec, dx = dx_call(vec, (token,))

        def both(n, f):
            return jnp.concatenate([n, f])

        at = half * (1 - (lax.axis_index("seq") & 1))
        e3_1 = jnp.roll(cot, -at, axis=0)
        w_1 = plain_weights(
            both(s_n[4], s_f[4]), both(e1_n, e1_f), both(win_n, win_f), both(e2_n, e2_f),
            both(c3_n, c3_f), e3_1,
        )
        w_0 = plain_weights(
            both(a1_n, a1_f), both(e1_n0, e1_f0), both(s_n[0], s_f[0]), both(e2_n0, e2_f0),
            both(q_n[0], q_f[0]), both(e3_n, e3_f),
        )
        grad_w_in, grad_w_mid, grad_w_out = (jnp.stack(pair) for pair in zip(w_0, w_1))
        vec = lax.psum(vec, ("dp", "seq"))
    else:
        jobs = (
            ("taps", (4, 5), (7, 8), 0), ("taps", (4, 5), (7, 8), 1), ("half", (9, 10), (0, 1), None),
            ("half", (2, 3), (11, 12), None), ("odd", (4, 5), (7, 8), (4, 6)),
        )
        args = (e1_n, e1_f, e3_n, e3_f, e2_n0, e2_f0, tap_1, *held)
        parts = (1, 1)
        send_2 = split_call(jobs[:2], args, (), 1, "k_weights2", (vec,), parts=parts)
        got_2 = swap_cores(send_2, parts)
        *keep_2, w_mid_0 = split_call(jobs, args, ((w_mid, 0, True),), 0, "k_weights2", (send_2[0],))
        send_4 = split_call(jobs[2:], args, (), 1, "k_weights4", (keep_2[0],))
        got_2 = got_2 + swap_cores(send_4)
        (y1b,) = call(
            k_plus, [((4 * u, inner), BF16)], (y1b, y_got), (), "k_plus", (send_4[0], halo_f)
        )
        as_, a1 = first_sum(keep_2, got_2, (0,), (), "k_first2", (y1b, x_got))
        a_got = swap(as_, "dp", 2)
        xys, xy = second_sum(x1, x_got, "k_second1", (a1,))
        xy_got = swap(xys, "seq", 1)
        bs, b1 = first_sum(keep_2, got_2, (), (4,), "k_first5", (xy, *got_2[2], *got_2[3]))
        b_got = swap(bs, "seq", 1)
        line_y = line_half([], [y1b], 0, "k_line0", (b1,))
        e1_n0, vec = back0_call(True, vec, e2_n0, e2_f0, halo_n, p_n, (line_y[0],), (), 7)
        e1_f0, vec, a1_n, a1_f = back0_call(
            False, vec, e2_f0, e2_n0, halo_f, p_f, (e1_n0,), ((a1_n, None, True), (a1_f, None, True)), 1
        )
        vec, dx = dx_call(vec, ())
        jobs = (("half", (0, 1), (2, 3), None),)
        args = (a1_n, a1_f, e1_n0, e1_f0)
        send_3 = split_call(jobs, args, (), 1, "k_weights3", (vec,), parts=(2,))
        got_3 = swap_cores(send_3, (2,))
        keep_3 = split_call(jobs, args, (), 0, "k_weights3", (send_3[0],))
        (sums_y,) = call(k_plus, [((2 * u, inner), BF16)], line_y, (), "k_plus", (keep_3[0],))
        line_a = line_half([(xy, xy_got), (b1, b_got)], [], 0, "k_line1", (sums_y,))
        ays, ay = second_sum(a1, a_got, "k_second2", (line_a[0],), 0.3, (vec,))
        ay_got = swap(ays, "seq", 1)
        ds, d1 = first_sum(keep_2, got_2, (2,), (), "k_first3", (ay,), 2)
        d_got = swap(ds, "dp", 2)
        cs, c1 = first_sum(keep_3, got_3, (), (0,), "k_first4", (d1,))
        c_got = swap(cs, "seq", 1)
        token, y1 = out_call((c1,))
        line_a = line_half([line_a], [sums_y], 1, "k_line2", (token,))
        line_b = line_half([(ay, ay_got)], [], 0, "k_line3", (line_a[0],), 0, n_packed)
        line_e = line_half([(c1, c_got)], [], 0, "k_line4", (line_b[0],))
        dys, dy = second_sum(d1, d_got, "k_second3", (line_e[0],))
        dy_got = swap(dys, "seq", 1)
        sums_a = line_sums([line_a], (3 * u,), "k_sum1", (dy,), 0.7)
        a_rows = (sums_a, swap(sums_a, "dp", 2))
        line_b = line_half([line_b], [], 1, "k_line5", (sums_a,), 0, n_packed)
        line_e = line_half([line_e], [], 1, "k_line6", (line_b[0],), 2)
        line_c = line_half([(dy, dy_got)], [], 0, "k_line7", (line_e[0],))
        whole = row_sums([a_rows], ((1, 0, 0),), "k_rows1", (line_c[0],))
        sums_b = line_sums([line_b, line_e], (u, u), "k_sum2", (whole,), 1.5)
        b_rows = (sums_b, swap(sums_b, "dp", 2))
        line_c = line_half([line_c], [], 1, "k_line8", (sums_b,), 2)
        sums_c = line_sums([line_c], (u,), "k_sum3", (line_c[0],))
        c_rows = (sums_c, swap(sums_c, "dp", 2))
        whole = row_sums(
            [(whole,), b_rows, c_rows], (None, (1, 0), (1,)), "k_rows2", (sums_c,)
        )
        got = swap(whole, "dp", 1)
        shapes = ((2, 2 * u, inner), (2, taps, u, inner), (2, 2 * u, inner))
        vector_shapes = ((2, width), (2, width), (2, 2, inner), (2, 2, inner), (2, 2, inner), (2, width))
        grads = share(0, (place, whole), (), shapes, (), vec_shape[0], u)
        grad_w_in, grad_w_mid, grad_w_out, *vectors = share(
            1, (place, got, whole), grads, shapes, vector_shapes, vec_shape[0], u
        )
        return (
            y1[None], dx[None], grad_w_in, grad_w_mid.swapaxes(2, 3), grad_w_out.swapaxes(1, 2),
            *vectors,
        )

    narrow = vec[:n_narrow].reshape(2, 2, 3, inner)
    wide = vec[n_narrow:].reshape(2, 3, width)
    return (
        y1[None],
        dx[None],
        grad_w_in,
        grad_w_mid,
        grad_w_out,
        wide[:, 0],
        wide[:, 1],
        narrow[:, :, 0],
        narrow[:, :, 1],
        narrow[:, :, 2],
        wide[:, 2],
    )


def solution(mesh):
    row = P("dp", "seq", None)
    return jax.shard_map(
        body,
        mesh=mesh,
        in_specs=(row, P(None, "dp", "seq")) + (P(),) * 9 + (row,),
        out_specs=(
            row,
            row,
            P(None, "seq", None),
            P(None, None, None, "seq"),
            P(None, None, "seq"),
        )
        + (P(),) * 6,
        check_vma=False,
    )
```

```python
import functools

import jax
import jax.numpy as jnp
from jax import lax
from jax.experimental import pallas as pl
from jax.experimental.pallas import tpu as pltpu
from jax.sharding import PartitionSpec as P

DILATION_CLOSE = 4
DILATION_BROAD = 128
EPS = 1e-05
F32 = jnp.float32
BF16 = jnp.bfloat16
VMEM_LIMIT = 18 * 1024 * 1024
HEIGHT = 128
EXP2 = -0.7213475204444817

C0 = 0.3275911 * 0.7071067811865476
POLY = tuple(0.5 * c for c in (0.254829592, -0.284496736, 1.421413741, -1.453152027, 1.061405429))
ROOT_2PI = 0.3989422804014327


def normal_parts(q):
    bell = jnp.exp2((q * EXP2) * q)
    t = pltpu.reciprocal(1.0 + C0 * jnp.abs(q), approx=True)
    h = POLY[4]
    for c in POLY[3::-1]:
        h = h * t + c
    tail = h * t * bell
    return jnp.where(q >= 0, 1.0 - tail, tail), q * bell * ROOT_2PI


def act_forward(v, gain, shift):
    c = v.shape[-1]
    mean = jnp.sum(v, axis=-1, keepdims=True) * (1.0 / c)
    centred = v - mean
    r = lax.rsqrt(jnp.sum(centred * centred, axis=-1, keepdims=True) * (1.0 / c) + EPS)
    n = centred * r
    q = n * gain + shift
    below, slope = normal_parts(q)
    return mean, r, n, q * below, below + slope


def act_backward(f, n, r, d, gain):
    c = f.shape[-1]
    p = f * d
    gp = gain * p
    first = jnp.sum(gp, axis=-1, keepdims=True) * (1.0 / c)
    second = jnp.sum(gp * n, axis=-1, keepdims=True) * (1.0 / c)
    return p, r * (gp - first - n * second)


def fold(v):
    return jnp.sum(v.reshape(v.shape[0] // 8, 8, v.shape[1]), axis=0)


def total(acc):
    return jnp.sum(acc, axis=0, keepdims=True)


def lanes(column):
    return jnp.broadcast_to(column, (column.shape[0], 128))


def strips(rows, height, step, carry=(), unroll=8, first=0):
    turns = rows // (height * unroll)
    if turns <= 1:
        for j in range(rows // height):
            carry = step(pl.ds(first + j * height, height), carry)
        return carry

    def body(i, c):
        for j in range(unroll):
            c = step(pl.ds(pl.multiple_of((i * unroll + j) * height, height), height), c)
        return c

    return lax.fori_loop(0, turns, body, carry)


def staggered(rows, height, *stages):
    parts = [slice(i, i + height) for i in range(0, rows, height)]
    for t in range(len(parts) + len(stages) - 1):
        for i in reversed(range(len(stages))):
            if 0 <= t - i < len(parts):
                stages[i](parts[t - i])


def at_base(at, base):
    if isinstance(base, int) and base == 0:
        return at
    return pl.ds(pl.multiple_of(at.start + base, at.size), at.size)


def dot(a, b):
    return jnp.dot(a, b, preferred_element_type=F32)


def dot_nt(a, b):
    return lax.dot_general(a, b, (((1,), (1,)), ((), ())), preferred_element_type=F32)


class Loads:
    def __init__(self, sources, targets, sems):
        self.targets = targets
        self.copies = [
            pltpu.make_async_copy(src if b is None else src.at[b], dst, sems.at[i])
            for i, ((src, b), dst) in enumerate(zip(sources, targets))
        ]
        self.waiting = set(range(len(targets)))
        for copy in self.copies:
            copy.start()

    def get(self, i):
        if i in self.waiting:
            self.waiting.remove(i)
            self.copies[i].wait()
        return self.targets[i]

    def finish(self):
        for i in sorted(self.waiting):
            self.get(i)


class Stores:
    def __init__(self, held, targets, sems):
        self.held, self.targets, self.sems = held, targets, sems
        self.copies = []

    def put(self, *which, at=None):
        for i in which:
            src, dst = self.held[i], self.targets[i]
            if at is not None:
                src, dst = src.at[at], dst.at[at]
            copy = pltpu.make_async_copy(src, dst, self.sems.at[len(self.copies)])
            copy.start()
            self.copies.append(copy)

    def finish(self):
        for copy in self.copies:
            copy.wait()


def call(
    kernel, outs, args, scratch=(), name=None, deps=(), loads=(), stores=(), offloads=(), parts=1,
    limit=VMEM_LIMIT, cost=0,
):
    n_args, n_loads, n_deps, n_off = len(args), len(loads), len(deps), len(offloads)
    n_outs, n_stores = len(outs), len(stores)
    loaded = [(a.shape if b is None else a.shape[1:], a.dtype) for a, b, _ in loads]
    kept = [i for i, (_, _, keep) in enumerate(loads) if keep]
    brief = [i for i in range(n_loads) if i not in kept]
    out_shape = [pltpu.VMEM(s, t) for s, t in outs] + [pltpu.HBM(s, t) for s, t in stores]
    out_shape += [pltpu.VMEM(*loaded[i]) for i in kept]
    out_shape += [pltpu.HBM(a.shape, a.dtype) for a in offloads]

    def run(*refs):
        def take(n):
            nonlocal refs
            first, refs = refs[:n], refs[n:]
            return first

        ins, going, sources, _ = take(n_args), take(n_off), take(n_loads), take(n_deps)
        results, stored, held, gone = take(n_outs), take(n_stores), take(len(kept)), take(n_off)
        targets = dict(zip(kept, held))
        scr = list(refs)
        more = {}
        if n_loads:
            sems = scr.pop()
            for i in reversed(brief):
                targets[i] = scr.pop()
            sources = [(r, b) for r, (_, b, _) in zip(sources, loads)]
            more["coming"] = Loads(sources, [targets[i] for i in range(n_loads)], sems)
        if n_off:
            leaving = Stores(going, gone, scr.pop())
            leaving.put(*range(n_off))
        if n_stores:
            sems = scr.pop()
            held = [scr.pop() for _ in stores][::-1]
            more["keeping"] = Stores(held, stored, sems)
        kernel(*ins, *results, *scr, **more)
        for part in more.values():
            part.finish()
        if n_off:
            leaving.finish()

    hbm, vmem = pl.BlockSpec(memory_space=pltpu.HBM), pl.BlockSpec(memory_space=pltpu.VMEM)
    specs = [vmem] * (n_args + n_off) + [hbm] * n_loads
    specs += [pl.BlockSpec(memory_space=pl.ANY)] * n_deps
    out_specs = [vmem] * n_outs + [hbm] * n_stores + [vmem] * len(kept) + [hbm] * n_off
    scratch = list(scratch)
    if n_stores:
        scratch += [pltpu.VMEM(s, t) for s, t in stores]
        scratch += [pltpu.SemaphoreType.DMA((n_stores * parts,))]
    if n_off:
        scratch += [pltpu.SemaphoreType.DMA((n_off,))]
    if n_loads:
        scratch += [pltpu.VMEM(*loaded[i]) for i in brief] + [pltpu.SemaphoreType.DMA((n_loads,))]
    return pl.pallas_call(
        run,
        out_shape=out_shape,
        in_specs=specs,
        out_specs=out_specs,
        scratch_shapes=scratch,
        compiler_params=pltpu.CompilerParams(vmem_limit_bytes=limit),
        cost_estimate=pl.CostEstimate(flops=1 + int(cost * 1.15e9), bytes_accessed=1, transcendentals=0),
        name=name,
    )(
        *[pltpu.with_memory_space_constraint(a, pltpu.VMEM) for a in (*args, *offloads)],
        *[pltpu.with_memory_space_constraint(a, pltpu.HBM) for a, _, _ in loads],
        *deps,
    )


NEAR, CUT, LOW_0, LOW_1, HIGH_1, CORE, BIT_X, LINE = range(8)


def find_marks(bounds, place):
    rows = bounds.shape[2]
    first = lax.axis_index("seq") * rows
    marks = (bounds[1, 0:1, 0:1], bounds[0, 0:1, 0:1], bounds[0, 0:1, rows - 1 :], bounds[1, 0:1, rows - 1 :])
    for row, v in zip((CUT, LOW_0, LOW_1, HIGH_1), marks):
        place[row : row + 1] = jnp.broadcast_to(v - first, (1, 128))


def find_place(place):
    seq, dp = lax.axis_index("seq"), lax.axis_index("dp")
    for row, v in ((NEAR, seq & 1), (CORE, dp & 1), (BIT_X, dp >> 1), (LINE, seq >> 1)):
        place[row : row + 1] = jnp.full((1, 128), v, jnp.int32)


def base_of(place, near, rows):
    odd = place[NEAR, 0]
    return rows * (1 - odd) if near else rows * odd


def wide_act(x, base, gain, shift, a1, d1, stat, part):
    def wide(at, c):
        mean, r, n, a, d = act_forward(x[at_base(at, base)].astype(F32), gain, shift)
        a1[at], d1[at] = a.astype(BF16), d.astype(BF16)
        stat[0, at], stat[1, at] = lanes(mean), lanes(r)
        return c

    strips(part.stop - part.start, 32, wide, first=part.start)


def narrow_act(z, gain, shift, a, n, d, stat, part):
    def narrow(at, c):
        _, r, nn, aa, dd = act_forward(z[at], gain, shift)
        n[at], d[at], a[at] = nn.astype(BF16), dd.astype(BF16), aa.astype(BF16)
        stat[at] = lanes(r)
        return c

    strips(part.stop - part.start, 32, narrow, first=part.start)


def windows(place, near, own, other, halo, win, pad, step):
    rows, width = own.shape
    taps = win.shape[1] // width
    rim = (pad.shape[0] - rows) // 2
    pad[rim : rim + rows] = own[...].astype(pad.dtype)
    lower = place[NEAR, 0] == (1 if near else 0)

    @pl.when(lower)
    def _():
        pad[0:rim] = halo[halo.shape[0] - rim :].astype(pad.dtype)
        pad[rim + rows :] = other[0:rim].astype(pad.dtype)

    @pl.when(jnp.logical_not(lower))
    def _():
        pad[0:rim] = other[rows - rim :].astype(pad.dtype)
        pad[rim + rows :] = halo[0:rim].astype(pad.dtype)

    base = base_of(place, near, rows)
    cut, low_0, low_1, high_1 = (place[i : i + 1] for i in (CUT, LOW_0, LOW_1, HIGH_1))
    height = 64

    def fill(part):
        for i in range(part.start, part.stop, height):
            rows_at(i)

    def rows_at(i):
        t = lax.broadcasted_iota(jnp.int32, (height, 128), 0) + (base + i)
        first = t < cut
        low = jnp.where(first, low_0, low_1)
        high = jnp.where(first, cut, high_1)
        for k in range(taps):
            offset = (k - taps // 2) * step
            m = jnp.where((t + offset >= low) & (t + offset < high), 1.0, 0.0).astype(pad.dtype)
            m = jnp.concatenate([m] * (width // 128), axis=1)
            start = rim + offset + i
            win[i : i + height, k * width : (k + 1) * width] = (
                pad[start : start + height] * m
            ).astype(BF16)

    return fill


def put_edge(edge, v, place, near):
    n = edge.shape[0]
    lower = place[NEAR, 0] == (1 if near else 0)

    @pl.when(lower)
    def _():
        edge[...] = v[0:n]

    @pl.when(jnp.logical_not(lower))
    def _():
        edge[...] = v[v.shape[0] - n :]


def first_half(x, base, gw, sw, w_in, bn, gn, sn, a1, d1, stat1, a2, n2, d2, r2, z, keeping):
    rows = a1.shape[0]

    def wide(p):
        wide_act(x, base, gw(), sw(), a1, d1, stat1, p)
        if p.stop == rows:
            keeping.put(*FIRST_STORES[len(keeping.held)])

    def inner(p):
        z[p] = dot(a1[p], w_in()[...]) + bn()

    def narrow(p):
        narrow_act(z, gn(), sn(), a2, n2, d2, r2, p)

    return wide, inner, narrow


FIRST_STORES = {3: (0, 1, 2), 7: (4, 5, 6)}


def k_in_near(place, a2, n2, d2, r2, edge, z, *, coming, keeping):
    a1, d1, stat1 = keeping.held
    find_place(place)
    x = coming.get(0)
    staggered(a1.shape[0], a1.shape[0], *first_half(
        x, base_of(place, True, a1.shape[0]), lambda: coming.get(1)[0:1], lambda: coming.get(2)[0:1],
        lambda: coming.get(3), lambda: coming.get(6)[0, 0:1], lambda: coming.get(4)[0, 0:1],
        lambda: coming.get(5)[0, 0:1], a1, d1, stat1, a2, n2, d2, r2, z, keeping,
    ))
    put_edge(edge, a2, place, True)
    find_marks(coming.get(9), place)


def k_in_far(place, x, gw, sw, gn, sn, bn, a2, n2, d2, r2, edge, z, *, coming, keeping):
    a1, d1, stat1 = keeping.held
    staggered(a1.shape[0], a1.shape[0], *first_half(
        x, base_of(place, False, a1.shape[0]), lambda: gw[0:1], lambda: sw[0:1],
        lambda: coming.get(0), lambda: bn[0, 0:1], lambda: gn[0, 0:1], lambda: sn[0, 0:1],
        a1, d1, stat1, a2, n2, d2, r2, z, keeping,
    ))
    put_edge(edge, a2, place, False)


def k_mid(
    place, x, own, other, halo, w_mid, gw, sw, bw, gn, sn, bn,
    a3, r3, a2, n2, d2, r2, pad, z, z1, *, near, step, coming, keeping,
):
    rows, width = own.shape
    win, n3, d3, y, a1, d1, stat1 = keeping.held
    fill = windows(place, near, own, other, halo, win, pad, step)
    base = base_of(place, near, rows)
    weights = w_mid[...].reshape(win.shape[1], width)

    def conv(p):
        fill(p)
        z[p] = dot(win[p], weights) + bn[0, 1:2]
        if p.stop == rows:
            keeping.put(0)

    def narrow(p):
        narrow_act(z, gn[0, 1:2], sn[0, 1:2], a3, n3, d3, r3, p)
        if p.stop == rows:
            keeping.put(1, 2)

    def outer(p):
        n = p.stop - p.start
        old = x[pl.ds(pl.multiple_of(base + p.start, n), n)].astype(F32)
        y[p] = old + dot(a3[p], coming.get(0)[...]) + bw[0:1]
        if p.stop == rows:
            keeping.put(3)

    staggered(rows, HEIGHT, conv, narrow, outer, *first_half(
        y, 0, lambda: gw[1:2], lambda: sw[1:2], lambda: coming.get(1), lambda: bn[1, 0:1],
        lambda: gn[1, 0:1], lambda: sn[1, 0:1], a1, d1, stat1, a2, n2, d2, r2, z1, keeping,
    ))


def put_wide(vec, row, acc):
    inner = vec.shape[1]
    for i in range(acc.shape[1] // inner):
        vec[row + i : row + i + 1] += total(acc[:, i * inner : (i + 1) * inner])


def k_flow(e, w_out, f, vec, *, row, coming):
    f[...] = dot_nt(e[...], w_out[...])
    vec[...] = jnp.zeros_like(vec)

    def step(at, acc):
        return acc + fold(e[at].astype(F32))

    put_wide(vec, row, strips(e.shape[0], 32, step, jnp.zeros((8, e.shape[1]), F32)))


def k_conv(
    place, vec_in, own, other, halo, w_mid, gn, sn, bn, f, a3, e2, vec, win, pad, z, *, near, step, row
):
    rows, width = own.shape
    windows(place, near, own, other, halo, win, pad, step)(slice(0, own.shape[0]))
    z[...] = dot(win[...], w_mid[...].reshape(win.shape[1], width)) + bn[1, 1:2]
    gain = gn[1, 1:2]
    base = base_of(place, near, rows)

    def narrow(at, c):
        _, r, n, a, d = act_forward(z[at], gain, sn[1, 1:2])
        a3[at] = a.astype(BF16)
        p, v = act_backward(f[at_base(at, base)], n, r, d, gain)
        e = v.astype(BF16)
        e2[at] = e
        return c[0] + fold(p * n), c[1] + fold(p), c[2] + fold(e.astype(F32))

    vec[...] = vec_in[...]
    zero = jnp.zeros((8, width), F32)
    for i, acc in enumerate(strips(rows, 32, narrow, (zero,) * 3)):
        vec[row + i : row + i + 1] += total(acc)


def k_out(place, a_n, a_f, bw, token, *, coming, keeping):
    half = a_n.shape[0]
    token[...] = jnp.zeros_like(token)
    (y,) = keeping.held
    w_out = coming.get(0)
    for near, a in ((True, a_n), (False, a_f)):
        at = pl.ds(pl.multiple_of(base_of(place, near, half), half), half)
        y[at] = dot(a[...], w_out[...]) + bw[1:2] + coming.get(1 if near else 2)[...]
        keeping.put(0, at=at)


def back_narrow(f, n, d, r, gain, e_out, vec, row):
    rows, width = f.shape

    def step(at, c):
        nn = n[at].astype(F32)
        p, v = act_backward(f[at], nn, r[at][:, 0:1], d[at].astype(F32), gain)
        e = v.astype(BF16)
        e_out[at] = e
        return c[0] + fold(p * nn), c[1] + fold(p), c[2] + fold(e.astype(F32))

    zero = jnp.zeros((8, width), F32)
    for i, acc in enumerate(strips(rows, 32, step, (zero,) * 3)):
        vec[row + i : row + i + 1] += total(acc)


def back_wide(f, x, x_base, stat, d, gain, dy, dy_base, out, out_base, cast, vec, row, cast_row):
    rows, width = f.shape

    def step(at, c):
        r = stat[1, at][:, 0:1]
        n = (x[at_base(at, x_base)].astype(F32) - stat[0, at][:, 0:1]) * r
        p, v = act_backward(f[at], n, r, d[at].astype(F32), gain)
        dx = dy[at_base(at, dy_base)].astype(F32) + v
        out[at_base(at, out_base)] = dx
        sums = (c[0] + fold(p * n), c[1] + fold(p))
        if cast is not None:
            e = dx.astype(BF16)
            cast[at] = e
            sums += (c[2] + fold(e.astype(F32)),)
        return sums

    zero = jnp.zeros((8, width), F32)
    sums = strips(rows, 32, step, (zero,) * (2 if cast is None else 3), 8)
    put_wide(vec, row, sums[0])
    put_wide(vec, row + width // vec.shape[1], sums[1])
    if cast is not None:
        put_wide(vec, cast_row, sums[2])


def flow_two(win, w_mid, z):
    taps, width = w_mid.shape[0], w_mid.shape[1]
    for j in range(taps):
        part = dot_nt(win[:, j * width : (j + 1) * width], w_mid[taps - 1 - j])
        if j == 0:
            z[...] = part
        else:
            z[...] += part


def k_back1(
    place, vec_in, own, other, halo, w_mid, gw, gn,
    e1, e3, e2, edge, vec, win, pad, z, f1, *, near, step, rows_of, coming, keeping,
):
    vec[...] = vec_in[...]
    windows(place, near, own, other, halo, win, pad, step)(slice(0, own.shape[0]))
    flow_two(win, w_mid, z)
    n2, d2, r2, w_in = (coming.get(i) for i in range(4))
    back_narrow(z, n2, d2, r2, gn[1, 0:1], e1, vec, rows_of[0])
    f1[...] = dot_nt(e1[...], w_in[...])
    base = base_of(place, near, own.shape[0])
    (dx,) = keeping.held
    x, d1, stat1, dy = (coming.get(i) for i in range(4, 8))
    back_wide(f1, x, 0, stat1, d1, gw[1:2], dy, base, dx, 0, e3, vec, rows_of[1], rows_of[3])
    keeping.put(0)
    w_out, n3, d3, r3 = (coming.get(i) for i in range(8, 12))
    z[...] = dot_nt(e3[...], w_out[...])
    back_narrow(z, n3, d3, r3, gn[0, 1:2], e2, vec, rows_of[2])
    put_edge(edge, e2, place, near)


def k_back0(
    place, vec_in, own, other, halo, w_mid, gn, e1, vec, win, pad, z, *, near, step, row, coming
):
    vec[...] = vec_in[...]
    halo = halo.at[pl.ds(halo.shape[0] - 16, 16)]
    windows(place, near, own, other, halo, win, pad, step)(slice(0, own.shape[0]))
    flow_two(win, w_mid, z)
    n2, d2, r2 = (coming.get(i) for i in range(3))
    back_narrow(z, n2, d2, r2, gn[0, 0:1], e1, vec, row)


def k_dx(place, vec_in, gw, e1_n, e1_f, vec, f1, *, row, coming, keeping):
    vec[...] = vec_in[...]
    half = e1_n.shape[0]
    (out,) = keeping.held
    w_in, x = coming.get(0), coming.get(1)
    for near, e1 in ((True, e1_n), (False, e1_f)):
        f1[...] = dot_nt(e1[...], w_in[...])
        d, stat, dy = (coming.get(i + (0 if near else 3)) for i in (2, 3, 4))
        base = base_of(place, near, half)
        back_wide(f1, x, base, stat, d, gw[0:1], dy, 0, out, base, None, vec, row, None)
        keeping.put(0, at=pl.ds(pl.multiple_of(base, half), half))


def k_split(place, *refs, jobs, parts, side, coming=None):
    n_outs = sum(parts)
    outs, turned = list(refs[-1 - n_outs : -1]), refs[-1]
    refs = refs[: -1 - n_outs]
    _, shards, _, u, rows = turned.shape
    inner = outs[0].shape[-1]

    def ref(i):
        return refs[i] if i < len(refs) else coming.get(i - len(refs))

    def whole(places, at=slice(None)):
        if len(places) == 1:
            half = rows // 2
            bases = [base_of(place, near, half) for near in (True, False)]
            parts = [ref(places[0])[pl.ds(pl.multiple_of(b, half), half)] for b in bases]
        else:
            parts = [ref(i)[:, at] for i in places]
        return jnp.concatenate(parts, axis=0)

    core = place[CORE, 0] ^ side
    kept = {}
    halves = 0
    for n, (kind, left, right, j) in zip(parts, jobs):
        here, outs = outs[:n], outs[n:]

        def put(product):
            height = product.shape[0] // n
            for i, out in enumerate(here):
                out[...] = product[i * height : (i + 1) * height]

        if kind == "half":
            turned[halves] = whole(left).T.reshape(turned.shape[1:])
            part = turned[halves, :, core].reshape(shards * u, rows)
            put(dot(part, whole(right)).astype(BF16))
            halves += 1
            continue
        if left not in kept:
            kept[left] = whole(left).T
        if kind == "taps":
            at = pl.ds(pl.multiple_of((j + 2 * core) * inner, 128), inner)
            put(dot(kept[left], whole(right, at)).astype(BF16))
            continue
        tap, before = j

        @pl.when(core == 0)
        def _():
            put(ref(before)[...])

        @pl.when(core != 0)
        def _():
            at = slice(tap * inner, (tap + 1) * inner)
            put(dot(kept[left], whole(right, at)).astype(BF16))


def k_tap(e_n, e_f, win_n, win_f, out, *, tap):
    inner = out.shape[-1]
    at = slice(tap * inner, (tap + 1) * inner)
    left = jnp.concatenate([e_n[...], e_f[...]], axis=0).T
    right = jnp.concatenate([win_n[:, at], win_f[:, at]], axis=0)
    out[...] = dot(left, right).astype(BF16)


def added(*parts):
    first, *rest = [p.astype(F32) for p in parts]
    for p in rest:
        first = first + p
    return first


def k_first(place, *refs, pairs, singles, edge):
    refs = list(refs)
    x, y = place[BIT_X, 0], place[NEAR, 0]

    def take(n):
        first = refs[:n]
        del refs[:n]
        return first

    ins = [(take(1)[0], take(n)) for two_units in pairs for n in two_units]
    ins += [(take(1)[0], take(n)) for n in singles]
    rim = take(1)[0] if edge else None

    def add_rows(a, parts, out):
        height = a.shape[0] // len(parts)
        for i, b in enumerate(parts):

            def step(k, c):
                here = pl.ds(pl.multiple_of(k * 80, 80), 80)
                at = pl.ds(pl.multiple_of(i * height + k * 80, 80), 80)
                out[at] = added(a[at], b[here]).astype(BF16)
                return c

            lax.fori_loop(0, height // 80, step, 0)

    for i in range(len(pairs)):
        (a0, b0), (a1, b1) = ins[2 * i : 2 * i + 2]
        send, stay = take(2)

        @pl.when(x == 0)
        def _():
            add_rows(a1, b1, send)
            add_rows(a0, b0, stay)

        @pl.when(x != 0)
        def _():
            add_rows(a0, b0, send)
            add_rows(a1, b1, stay)

    for out, side in zip(refs, (1 - y, y)):
        at = 0
        for a, parts in ins[2 * len(pairs) :]:
            u = a.shape[2]
            each = a.shape[0] // len(parts)
            for k in range(a.shape[0]):
                b = parts[k // each]
                out[at : at + u] = added(a[k, side], b[k % each, side]).astype(BF16)
                at += u
    if edge:
        refs[0][at:] = rim[...]


def k_second(place, a, b, *refs):
    *vec, send, stay = refs
    mine = place[NEAR, 0]
    u = a.shape[2]
    for out, side in ((send, 1 - mine), (stay, mine)):

        def step(k, c):
            at = pl.ds(pl.multiple_of(k * u, u), u)
            out[at] = added(a[k, side], b[k, side]).astype(BF16)
            return c

        lax.fori_loop(0, 4, step, 0)
    if vec:
        pack(vec[0][...], send, stay, at=4 * u)


def pack(v, *outs, at):
    upper = v.astype(BF16).astype(F32)
    parts = jnp.concatenate([upper, v - upper], axis=0).astype(BF16)
    for out in outs:
        out[at : at + parts.shape[0]] = parts


def unpack(ref, at):
    parts = ref[at:].astype(F32)
    n = parts.shape[0] // 2
    return parts[:n] + parts[n:]


def k_line(place, *refs, sums, wholes, packed, bit, u):
    mine = (place[LINE, 0] >> bit) & 1
    arrays = [refs[2 * i : 2 * i + 2] for i in range(sums)]
    arrays += [refs[2 * sums + i : 2 * sums + i + 1] for i in range(wholes)]
    send, stay = refs[2 * sums + wholes :]
    for out, side in ((send, 1 - mine), (stay, mine)):
        at = 0
        for i, parts in enumerate(arrays):
            rows = parts[0].shape[0] - (packed if i == 0 else 0)
            for j in range(rows // (2 * u)):
                part = pl.ds(pl.multiple_of((2 * j + side) * u, u), u)
                out[at : at + u] = added(*[p[part] for p in parts]).astype(BF16)
                at += u
    if packed:
        a, b = arrays[0]
        n = a.shape[0] - packed
        pack(unpack(a, n) + unpack(b, n), send, stay, at=send.shape[0] - packed)


def k_sum(place, *refs, rows):
    out = refs[-1]
    at = 0
    for i, n in enumerate(rows):
        a, b = refs[2 * i], refs[2 * i + 1]
        out[at : at + n] = added(a[0:n], b[0:n]).astype(BF16)
        at += n
    if refs[0].shape[0] > rows[0]:
        pack(unpack(refs[0], rows[0]) + unpack(refs[1], rows[0]), out, at=at)


def k_rows(place, *refs, splits, u):
    *refs, out = refs
    x = place[BIT_X, 0]
    at = 0
    refs = list(refs)
    for split in splits:
        if split is None:
            ready = refs.pop(0)
            out[at : at + ready.shape[0]] = ready[...]
            at += ready.shape[0]
            continue
        mine, got = refs.pop(0), refs.pop(0)
        for k, apart in enumerate(split):
            here = slice(k * u, (k + 1) * u)
            if apart:
                base = pl.multiple_of(at + x * u, u)
                other = pl.multiple_of(at + (1 - x) * u, u)
                out[pl.ds(base, u)], out[pl.ds(other, u)] = mine[here], got[here]
                at += 2 * u
            else:
                out[at : at + u] = added(mine[here], got[here]).astype(BF16)
                at += u
        if mine.shape[0] > len(split) * u:
            n = len(split) * u
            pack(unpack(mine, n) + unpack(got, n), out, at=out.shape[0] - (mine.shape[0] - n))


def k_share(place, ref, *refs, side, u):
    vectors, n_vec = (), 0
    if side:
        mine, *refs = refs
        refs = refs[3:]
        n_vec = 6
    out_in, out_mid, out_out = refs[:3]
    vectors, refs = refs[3 : 3 + n_vec], refs[3 + n_vec :]
    stage, held, sems = refs[0], refs[1:-1], refs[-1]
    c = place[CORE, 0] ^ side
    rows = pl.ds(pl.multiple_of(c * u, u), u)
    copies = []

    def put(src, dst):
        copies.append(pltpu.make_async_copy(src, dst, sems.at[len(copies)]))
        copies[-1].start()

    def units(i, n=1):
        for k in range(i, i + n):
            stage[k] = ref[k * u : (k + 1) * u].astype(F32)
        return stage.at[i] if n == 1 else stage.at[i : i + n]

    put(units(0, 2), out_mid.at[1, pl.ds(2 * c, 2)])
    put(units(2), out_mid.at[1 - c, 4])
    put(units(3), out_out.at[1, rows])
    put(units(4, 2), out_mid.at[0, pl.ds(2 * c, 2)])
    put(units(6), out_in.at[0, rows])
    put(units(7), out_in.at[1, rows])
    put(units(8), out_out.at[0, rows])
    if side:
        vec, gw, sw, gn, sn, bn, bw = held
        vec[...] = unpack(mine, 9 * u) + unpack(ref, 9 * u)
        inner = vec.shape[1]
        two = gw.shape[1] // inner
        for block in range(2):
            for i in range(2):
                row = 3 * (2 * block + i)
                for j, out in enumerate((gn, sn, bn)):
                    out[block, i : i + 1] = vec[row + j : row + j + 1]
            for j, out in enumerate((gw, sw, bw)):
                for k in range(two):
                    row = 12 + (3 * block + j) * two + k
                    out[block : block + 1, k * inner : (k + 1) * inner] = vec[row : row + 1]
        for src, dst in zip((gw, sw, gn, sn, bn, bw), vectors):
            put(src, dst)
    for copy in copies:
        copy.wait()


def share(side, args, before, shapes, vector_shapes, vec_shape, u):
    inner = shapes[0][-1]
    vmem, hbm = pl.BlockSpec(memory_space=pltpu.VMEM), pl.BlockSpec(memory_space=pltpu.HBM)
    outs = list(shapes) + list(vector_shapes)
    held = [pltpu.VMEM(s, F32) for s in ([vec_shape] + list(vector_shapes) if side else [])]
    return pl.pallas_call(
        functools.partial(k_share, side=side, u=u),
        out_shape=[pltpu.HBM(s, F32) for s in outs],
        in_specs=[vmem] * len(args) + [hbm] * len(before),
        out_specs=[hbm] * len(outs),
        scratch_shapes=[pltpu.VMEM((9, u, inner), F32), *held, pltpu.SemaphoreType.DMA((7 + len(vector_shapes),))],
        input_output_aliases={len(args) + i: i for i in range(len(before))},
        compiler_params=pltpu.CompilerParams(vmem_limit_bytes=VMEM_LIMIT),
        cost_estimate=pl.CostEstimate(flops=1, bytes_accessed=1, transcendentals=0),
        name="k_share",
    )(
        *[pltpu.with_memory_space_constraint(a, pltpu.VMEM) for a in args],
        *[pltpu.with_memory_space_constraint(a, pltpu.HBM) for a in before],
    )


def k_plus(a, b, out):
    out[...] = added(a[...], b[0 : a.shape[0]]).astype(BF16)


def k_nothing(*refs, coming):
    pass


def swap(v, axis, bits):
    count = lax.axis_size(axis)
    return lax.ppermute(v, axis, [(i, i ^ bits) for i in range(count)])


def to_near(v):
    return swap(v, "seq", 1)


def to_far(v):
    count = lax.axis_size("seq")
    pairs = [(i, i + 1) for i in range(1, count - 1, 2)]
    return lax.ppermute(v, "seq", pairs + [(j, i) for i, j in pairs])


def dot_tn(a, b):
    return lax.dot_general(a, b, (((0,), (0,)), ((), ())), preferred_element_type=F32)


def plain_weights(a1, e1, win, e2, a3, e3):
    taps = win.shape[1] // e2.shape[1]
    grad_mid = dot_tn(win, e2).reshape(taps, e2.shape[1], e2.shape[1])
    shares = (
        lax.psum_scatter(dot_tn(a1, e1), "seq", scatter_dimension=0, tiled=True),
        lax.psum_scatter(grad_mid, "seq", scatter_dimension=2, tiled=True),
        lax.psum_scatter(dot_tn(a3, e3), "seq", scatter_dimension=1, tiled=True),
    )
    return [lax.psum(v.astype(BF16), "dp").astype(F32) for v in shares]


def body(
    tokens, bounds, w_in, w_mid, w_out, gain_wide, shift_wide, gain_narrow, shift_narrow,
    bias_narrow, bias_wide, cotangent,
):
    x0 = tokens[0]
    cot = cotangent[0]
    rows, width = x0.shape
    taps, inner = w_mid.shape[1], w_mid.shape[2]
    shards = lax.axis_size("seq")
    u = inner // shards
    two = width // inner
    half = rows // 2
    close, broad = DILATION_CLOSE, DILATION_BROAD

    wide_h, narrow_h, column = (half, width), (half, inner), ((half, 128), F32)
    win_h = ((half, taps * inner), BF16)
    act_wide = [(wide_h, BF16), (wide_h, BF16), ((2, half, 128), F32)]
    act_narrow = [(narrow_h, BF16), (narrow_h, BF16), (narrow_h, BF16), column]
    edge = ((16, inner), BF16)
    z = pltpu.VMEM(narrow_h, F32)
    f1 = pltpu.VMEM(wide_h, F32)
    win_scratch = pltpu.VMEM(*win_h)
    pad_0 = pltpu.VMEM((half + 32, inner), F32)
    pad_1 = pltpu.VMEM((half + 4 * broad, inner), BF16)
    n_narrow = 12
    vec_shape = ((n_narrow + 6 * two, inner), F32)

    def row_narrow(b, i):
        return 3 * (2 * b + i)

    def row_wide(b, i):
        return n_narrow + (3 * b + i) * two

    def brief(*arrays):
        return tuple((a, None, False) for a in arrays)

    place, a2_n, *p_n, edge_n, a1_n, d1_n, stat_n, x, gw, sw, gn, sn, bn, bw, w_mid_0 = call(
        k_in_near, [((8, 128), jnp.int32)] + act_narrow + [edge], (), [z], "k_in",
        loads=((x0, None, True), (gain_wide, None, True), (shift_wide, None, True), (w_in, 0, False),
               (gain_narrow, None, True), (shift_narrow, None, True), (bias_narrow, None, True),
               (bias_wide, None, True), (w_mid, 0, True), (bounds, None, False)),
        stores=act_wide, cost=4,
    )
    halo_n = to_near(edge_n)
    a2_f, *p_f, edge_f, a1_f, d1_f, stat_f, p1, p2, p3 = call(
        k_in_far, act_narrow + [edge], (place, x, gw, sw, gn, sn, bn), [z], "k_in", (edge_n,),
        loads=((w_in, 0, False),), stores=act_wide, offloads=p_n, cost=4,
    )
    p_n = (p1, p2, p3)
    halo_f = to_far(edge_f)

    def mid_call(near, own, other, halo, deps, loads, offloads):
        return call(
            functools.partial(k_mid, near=near, step=close),
            [(narrow_h, BF16), column] + act_narrow,
            (place, x, own, other, halo, w_mid_0, gw, sw, bw, gn, sn, bn),
            [pad_0, z, z], "k_mid", deps, ((w_out, 0, False), (w_in, 1, False)) + loads,
            [win_h, (narrow_h, BF16), (narrow_h, BF16), (wide_h, F32)] + act_wide, offloads, cost=8,
        )

    a3_n, r3_n, b2_n, *q_n = mid_call(True, a2_n, a2_f, halo_n, (), (), p_f)
    s_n, p_f = q_n[3:10], q_n[10:]
    halo_n = to_near(b2_n)
    a3_f, r3_f, b2_f, *q_f = mid_call(
        False, a2_f, a2_n, halo_f, (b2_n,), ((w_out, 1, True), (cot, None, True)),
        (a3_n, r3_n, *q_n[:3]),
    )
    s_f, (w_out_1, cot_v), q_n = q_f[3:10], q_f[10:12], q_f[12:]
    halo_f = to_far(b2_f)
    f3, vec, w_mid_1, *q_f = call(
        functools.partial(k_flow, row=row_wide(1, 2)),
        [((rows, inner), F32), vec_shape], (cot_v, w_out_1), (), "k_flow",
        loads=((w_mid, 1, True),), offloads=(a3_f, r3_f, *q_f[:3]), cost=3,
    )

    def conv_call(near, vec, own, other, halo):
        return call(
            functools.partial(k_conv, near=near, step=broad, row=row_narrow(1, 1)),
            [(narrow_h, BF16), (narrow_h, BF16), vec_shape, win_h],
            (place, vec, own, other, halo, w_mid_1, gn, sn, bn, f3),
            [pad_1, z], "k_conv", cost=3,
        )

    c3_n, e2_n, vec, win_n = conv_call(True, vec, b2_n, b2_f, halo_n)
    halo_n = to_near(e2_n)
    c3_f, e2_f, vec, win_f = conv_call(False, vec, b2_f, b2_n, halo_f)
    halo_f = to_far(e2_f)

    fast = shards == 8 and u % 16 == 0
    unit = (inner, inner)
    part = (u, inner)

    def split_call(jobs, args, loads, side, name, deps, cost=0, parts=None):
        parts = parts or (1,) * len(jobs)
        halves = sum(kind == "half" for kind, *_ in jobs)
        turned = pltpu.VMEM((halves, shards, 2, u, rows), BF16)
        return call(
            functools.partial(k_split, jobs=jobs, side=side, parts=parts),
            [((inner // n, inner), BF16) for n in parts for _ in range(n)],
            (place, *args), [turned], name, deps, loads, cost=cost,
        )

    def swap_cores(units, parts=None):
        got = [swap(v, "dp", 1) for v in units]
        parts = parts or (1,) * len(units)
        return [tuple(got.pop(0) for _ in range(n)) for n in parts]

    def first_sum(keep, got, pairs, singles, name, deps, cost=0, edge=()):
        args = []
        for i in [j for pair in pairs for j in (pair, pair + 1)]:
            args += [keep[i], *got[i]]
        for i in singles:
            args += [v.reshape(-1, 2, u, inner) for v in (keep[i], *got[i])]
        outs = [(unit, BF16)] * (2 * len(pairs))
        n = 4 * u * len(singles)
        if singles:
            outs += [((n + sum(v.shape[0] for v in edge), inner), BF16), ((n, inner), BF16)]
        kernel = functools.partial(
            k_first, pairs=tuple((len(got[i]), len(got[i + 1])) for i in pairs),
            singles=tuple(len(got[i]) for i in singles), edge=bool(edge),
        )
        return call(kernel, outs, (place, *args, *edge), (), name, deps, cost=cost)

    n_packed = 2 * vec_shape[0][0]

    def second_sum(stay, got, name, deps, cost=0, vec=()):
        views = [v.reshape(4, 2, u, inner) for v in (stay, got)]
        n = 4 * u + (n_packed if vec else 0)
        return call(
            k_second, [((n, inner), BF16)] * 2, (place, *views, *vec), (), name, deps, cost=cost
        )

    def line_half(pairs, wholes, bit, name, deps, cost=0, packed=0):
        arrays = [pair[0] for pair in pairs] + list(wholes)
        n = sum(a.shape[0] for a in arrays) - packed
        n = n // 2 + packed
        kernel = functools.partial(k_line, sums=len(pairs), wholes=len(wholes), packed=packed, bit=bit, u=u)
        send, stay = call(
            kernel, [((n, inner), BF16)] * 2, (place, *[v for pair in pairs for v in pair], *wholes),
            (), name, deps, cost=cost,
        )
        return stay, swap(send, "seq", 2 << bit)

    def line_sums(pairs, rows, name, deps, cost=0):
        n = sum(rows) + pairs[0][0].shape[0] - rows[0]
        return call(
            functools.partial(k_sum, rows=rows), [((n, inner), BF16)],
            (place, *[v for pair in pairs for v in pair]), (), name, deps, cost=cost,
        )[0]

    def row_sums(pairs, splits, name, deps):
        n = sum(pair[0].shape[0] for pair in pairs) + u * sum(sum(split or ()) for split in splits)
        return call(
            functools.partial(k_rows, splits=splits, u=u), [((n, inner), BF16)],
            (place, *[v for pair in pairs for v in pair]), (), name, deps,
        )[0]

    def back1_call(near, vec, own, other, halo, q, s, deps, more=()):
        return call(
            functools.partial(
                k_back1, near=near, step=broad,
                rows_of=(row_narrow(1, 0), row_wide(1, 0), row_narrow(0, 1), row_wide(0, 2)),
            ),
            [(narrow_h, BF16), (wide_h, BF16), (narrow_h, BF16), edge, vec_shape],
            (place, vec, own, other, halo, w_mid_1, gw, gn),
            [win_scratch, pad_1, z, f1], "k_back1", deps, stores=[(wide_h, F32)], cost=5 if near else 2,
            loads=(*brief(*q[2:5]), (w_in, 1, False), *brief(s[3], s[5], s[6], cot),
                   (w_out, 0, False), *brief(s[1], s[2], q[1]), *more),
        )

    def back0_call(near, vec, own, other, halo, p, deps, loads, cost=0):
        return call(
            functools.partial(k_back0, near=near, step=close, row=row_narrow(0, 0)),
            [(narrow_h, BF16), vec_shape], (place, vec, own, other, halo, w_mid_0, gn),
            [win_scratch, pad_0, z], "k_back0", deps, loads=brief(*p) + loads, cost=cost,
        )

    def out_call(deps):
        return call(
            k_out, [((8, 128), F32)], (place, c3_n, c3_f, bw), (), "k_out", deps,
            loads=((w_out, 1, False), *brief(s_n[3], s_f[3])), stores=[((rows, width), F32)], parts=2,
        )

    def dx_call(vec, deps):
        return call(
            functools.partial(k_dx, row=row_wide(0, 0)), [vec_shape],
            (place, vec, gw, e1_n0, e1_f0), [f1], "k_dx", deps,
            loads=((w_in, 0, False), *brief(x0, d1_n, stat_n, dx_n, d1_f, stat_f, dx_f)),
            stores=[((rows, width), F32)], parts=2,
        )

    def rowed(v):
        return v.reshape(-1, inner)

    if fast:
        jobs = (("taps", (0, 1), (5, 6), 0), ("taps", (0, 1), (5, 6), 1), ("half", (2,), (3, 4), None))
        args = (e2_n, e2_f, cot_v, c3_n, c3_f, win_n, win_f)
        send_1 = split_call(jobs, args, (), 1, "k_weights1", (vec,))
        got_1 = swap_cores(send_1)
        keep_1 = split_call(jobs, args, (), 0, "k_weights1", (send_1[0],))
        last = keep_1[0]
    else:
        last = vec
    e1_n, e3_n, e2_n0, edge_n, vec, dx_n = back1_call(
        True, vec, e2_n, e2_f, halo_n, q_n, s_n, (last,)
    )
    if fast:
        xs, x1, ys, y1b = first_sum(
            keep_1, got_1, (0,), (2,), "k_first1", (vec, halo_f), 0, (edge_n,)
        )
        x_got, y_got = swap(xs, "dp", 2), swap(ys, "seq", 1)
        (tap_1,) = call(
            functools.partial(k_tap, tap=4), [(unit, BF16)], (e2_n, e2_f, win_n, win_f), (), "k_tap",
            (x1,),
        )
        halo_n, last = y_got, tap_1
    else:
        halo_n = to_near(edge_n)
    more = tuple((v, None, True) for v in (s_n[0], s_f[0], s_n[4], s_f[4], q_n[0], q_f[0])) if fast else ()
    e1_f, e3_f, e2_f0, edge_f, vec, dx_f, *held = back1_call(
        False, vec, e2_f, e2_n, halo_f, q_f, s_f, (last,), more
    )
    halo_f = to_far(edge_f)

    if not fast:
        (w_mid_0,) = call(k_nothing, [], (place,), (), "k_load", (vec,), ((w_mid, 0, True),))
        e1_n0, vec = back0_call(True, vec, e2_n0, e2_f0, halo_n, p_n, (), ())
        e1_f0, vec = back0_call(False, vec, e2_f0, e2_n0, halo_f, p_f, (), ())
        token, y1 = out_call((vec,))
        vec, dx = dx_call(vec, (token,))

        def both(n, f):
            return jnp.concatenate([n, f])

        at = half * (1 - (lax.axis_index("seq") & 1))
        e3_1 = jnp.roll(cot, -at, axis=0)
        w_1 = plain_weights(
            both(s_n[4], s_f[4]), both(e1_n, e1_f), both(win_n, win_f), both(e2_n, e2_f),
            both(c3_n, c3_f), e3_1,
        )
        w_0 = plain_weights(
            both(a1_n, a1_f), both(e1_n0, e1_f0), both(s_n[0], s_f[0]), both(e2_n0, e2_f0),
            both(q_n[0], q_f[0]), both(e3_n, e3_f),
        )
        grad_w_in, grad_w_mid, grad_w_out = (jnp.stack(pair) for pair in zip(w_0, w_1))
        vec = lax.psum(vec, ("dp", "seq"))
    else:
        jobs = (
            ("taps", (4, 5), (7, 8), 0), ("taps", (4, 5), (7, 8), 1), ("half", (9, 10), (0, 1), None),
            ("half", (2, 3), (11, 12), None), ("odd", (4, 5), (7, 8), (4, 6)),
        )
        args = (e1_n, e1_f, e3_n, e3_f, e2_n0, e2_f0, tap_1, *held)
        parts = (1, 1)
        send_2 = split_call(jobs[:2], args, (), 1, "k_weights2", (vec,), parts=parts)
        got_2 = swap_cores(send_2, parts)
        *keep_2, w_mid_0 = split_call(jobs, args, ((w_mid, 0, True),), 0, "k_weights2", (send_2[0],))
        send_4 = split_call(jobs[2:], args, (), 1, "k_weights4", (keep_2[0],))
        got_2 = got_2 + swap_cores(send_4)
        (y1b,) = call(
            k_plus, [((4 * u, inner), BF16)], (y1b, y_got), (), "k_plus", (send_4[0], halo_f)
        )
        as_, a1 = first_sum(keep_2, got_2, (0,), (), "k_first2", (y1b, x_got))
        a_got = swap(as_, "dp", 2)
        xys, xy = second_sum(x1, x_got, "k_second1", (a1,))
        xy_got = swap(xys, "seq", 1)
        bs, b1 = first_sum(keep_2, got_2, (), (4,), "k_first5", (xy, *got_2[2], *got_2[3]))
        b_got = swap(bs, "seq", 1)
        line_y = line_half([], [y1b], 0, "k_line0", (b1,))
        e1_n0, vec = back0_call(True, vec, e2_n0, e2_f0, halo_n, p_n, (line_y[0],), (), 7)
        e1_f0, vec, a1_n, a1_f = back0_call(
            False, vec, e2_f0, e2_n0, halo_f, p_f, (e1_n0,), ((a1_n, None, True), (a1_f, None, True)), 1
        )
        vec, dx = dx_call(vec, ())
        jobs = (("half", (0, 1), (2, 3), None),)
        args = (a1_n, a1_f, e1_n0, e1_f0)
        send_3 = split_call(jobs, args, (), 1, "k_weights3", (vec,), parts=(2,))
        got_3 = swap_cores(send_3, (2,))
        keep_3 = split_call(jobs, args, (), 0, "k_weights3", (send_3[0],))
        (sums_y,) = call(k_plus, [((2 * u, inner), BF16)], line_y, (), "k_plus", (keep_3[0],))
        line_a = line_half([(xy, xy_got), (b1, b_got)], [], 0, "k_line1", (sums_y,))
        ds, d1 = first_sum(keep_2, got_2, (2,), (), "k_first3", (line_a[0],), 0.3)
        d_got = swap(ds, "dp", 2)
        ays, ay = second_sum(a1, a_got, "k_second2", (d1,), 2, (vec,))
        ay_got = swap(ays, "seq", 1)
        cs, c1 = first_sum(keep_3, got_3, (), (0,), "k_first4", (ay,))
        c_got = swap(cs, "seq", 1)
        token, y1 = out_call((c1,))
        line_a = line_half([line_a], [sums_y], 1, "k_line2", (token,))
        line_b = line_half([(ay, ay_got)], [], 0, "k_line3", (line_a[0],), 0, n_packed)
        line_e = line_half([(c1, c_got)], [], 0, "k_line4", (line_b[0],))
        dys, dy = second_sum(d1, d_got, "k_second3", (line_e[0],))
        dy_got = swap(dys, "seq", 1)
        sums_a = line_sums([line_a], (3 * u,), "k_sum1", (dy,), 0.7)
        a_rows = (sums_a, swap(sums_a, "dp", 2))
        line_b = line_half([line_b], [], 1, "k_line5", (sums_a,), 0, n_packed)
        line_e = line_half([line_e], [], 1, "k_line6", (line_b[0],), 2)
        line_c = line_half([(dy, dy_got)], [], 0, "k_line7", (line_e[0],))
        whole = row_sums([a_rows], ((1, 0, 0),), "k_rows1", (line_c[0],))
        sums_b = line_sums([line_b, line_e], (u, u), "k_sum2", (whole,), 1.5)
        b_rows = (sums_b, swap(sums_b, "dp", 2))
        line_c = line_half([line_c], [], 1, "k_line8", (sums_b,), 2)
        sums_c = line_sums([line_c], (u,), "k_sum3", (line_c[0],))
        c_rows = (sums_c, swap(sums_c, "dp", 2))
        whole = row_sums(
            [(whole,), b_rows, c_rows], (None, (1, 0), (1,)), "k_rows2", (sums_c,)
        )
        got = swap(whole, "dp", 1)
        shapes = ((2, 2 * u, inner), (2, taps, u, inner), (2, 2 * u, inner))
        vector_shapes = ((2, width), (2, width), (2, 2, inner), (2, 2, inner), (2, 2, inner), (2, width))
        grads = share(0, (place, whole), (), shapes, (), vec_shape[0], u)
        grad_w_in, grad_w_mid, grad_w_out, *vectors = share(
            1, (place, got, whole), grads, shapes, vector_shapes, vec_shape[0], u
        )
        return (
            y1[None], dx[None], grad_w_in, grad_w_mid.swapaxes(2, 3), grad_w_out.swapaxes(1, 2),
            *vectors,
        )

    narrow = vec[:n_narrow].reshape(2, 2, 3, inner)
    wide = vec[n_narrow:].reshape(2, 3, width)
    return (
        y1[None],
        dx[None],
        grad_w_in,
        grad_w_mid,
        grad_w_out,
        wide[:, 0],
        wide[:, 1],
        narrow[:, :, 0],
        narrow[:, :, 1],
        narrow[:, :, 2],
        wide[:, 2],
    )


def solution(mesh):
    row = P("dp", "seq", None)
    return jax.shard_map(
        body,
        mesh=mesh,
        in_specs=(row, P(None, "dp", "seq")) + (P(),) * 9 + (row,),
        out_specs=(
            row,
            row,
            P(None, "seq", None),
            P(None, None, None, "seq"),
            P(None, None, "seq"),
        )
        + (P(),) * 6,
        check_vma=False,
    )
```

```python
import functools

import jax
import jax.numpy as jnp
from jax import lax
from jax.experimental import pallas as pl
from jax.experimental.pallas import tpu as pltpu
from jax.sharding import PartitionSpec as P

DILATION_CLOSE = 4
DILATION_BROAD = 128
EPS = 1e-05
F32 = jnp.float32
BF16 = jnp.bfloat16
VMEM_LIMIT = 18 * 1024 * 1024
HEIGHT = 128
VEC_ROWS = 24
EXP2 = -0.7213475204444817

C0 = 0.3275911 * 0.7071067811865476
POLY = tuple(0.5 * c for c in (0.254829592, -0.284496736, 1.421413741, -1.453152027, 1.061405429))
ROOT_2PI = 0.3989422804014327


def normal_parts(q):
    bell = jnp.exp2((q * EXP2) * q)
    t = pltpu.reciprocal(1.0 + C0 * jnp.abs(q), approx=True)
    h = POLY[4]
    for c in POLY[3::-1]:
        h = h * t + c
    tail = h * t * bell
    return jnp.where(q >= 0, 1.0 - tail, tail), q * bell * ROOT_2PI


def act_forward(v, gain, shift):
    c = v.shape[-1]
    mean = jnp.sum(v, axis=-1, keepdims=True) * (1.0 / c)
    centred = v - mean
    r = lax.rsqrt(jnp.sum(centred * centred, axis=-1, keepdims=True) * (1.0 / c) + EPS)
    n = centred * r
    q = n * gain + shift
    below, slope = normal_parts(q)
    return mean, r, n, q * below, below + slope


def act_backward(f, n, r, d, gain):
    c = f.shape[-1]
    p = f * d
    gp = gain * p
    first = jnp.sum(gp, axis=-1, keepdims=True) * (1.0 / c)
    second = jnp.sum(gp * n, axis=-1, keepdims=True) * (1.0 / c)
    return p, r * (gp - first - n * second)


def fold(v):
    return jnp.sum(v.reshape(v.shape[0] // 8, 8, v.shape[1]), axis=0)


def total(acc):
    return jnp.sum(acc, axis=0, keepdims=True)


def lanes(column):
    return jnp.broadcast_to(column, (column.shape[0], 128))


def strips(rows, height, step, carry=(), unroll=8, first=0):
    turns = rows // (height * unroll)
    if turns <= 1:
        for j in range(rows // height):
            carry = step(pl.ds(first + j * height, height), carry)
        return carry

    def body(i, c):
        for j in range(unroll):
            c = step(pl.ds(pl.multiple_of((i * unroll + j) * height, height), height), c)
        return c

    return lax.fori_loop(0, turns, body, carry)


def staggered(rows, height, *stages):
    parts = [slice(i, i + height) for i in range(0, rows, height)]
    for t in range(len(parts) + len(stages) - 1):
        for i in reversed(range(len(stages))):
            if 0 <= t - i < len(parts):
                stages[i](parts[t - i])


def at_base(at, base):
    if isinstance(base, int) and base == 0:
        return at
    return pl.ds(pl.multiple_of(at.start + base, at.size), at.size)


def dot(a, b):
    return jnp.dot(a, b, preferred_element_type=F32)


def dot_nt(a, b):
    return lax.dot_general(a, b, (((1,), (1,)), ((), ())), preferred_element_type=F32)


class Loads:
    def __init__(self, sources, targets, sems):
        self.targets = targets
        self.copies = [
            pltpu.make_async_copy(src if b is None else src.at[b], dst, sems.at[i])
            for i, ((src, b), dst) in enumerate(zip(sources, targets))
        ]
        self.waiting = set(range(len(targets)))
        for copy in self.copies:
            copy.start()

    def get(self, i):
        if i in self.waiting:
            self.waiting.remove(i)
            self.copies[i].wait()
        return self.targets[i]

    def finish(self):
        for i in sorted(self.waiting):
            self.get(i)


class Stores:
    def __init__(self, held, targets, sems):
        self.held, self.targets, self.sems = held, targets, sems
        self.copies = []

    def put(self, *which, at=None):
        for i in which:
            src, dst = self.held[i], self.targets[i]
            if at is not None:
                src, dst = src.at[at], dst.at[at]
            copy = pltpu.make_async_copy(src, dst, self.sems.at[len(self.copies)])
            copy.start()
            self.copies.append(copy)

    def finish(self):
        for copy in self.copies:
            copy.wait()


def call(
    kernel, outs, args, scratch=(), name=None, deps=(), loads=(), stores=(), offloads=(), parts=1,
    limit=VMEM_LIMIT, cost=0,
):
    n_args, n_loads, n_deps, n_off = len(args), len(loads), len(deps), len(offloads)
    n_outs, n_stores = len(outs), len(stores)
    loaded = [(a.shape if b is None else a.shape[1:], a.dtype) for a, b, _ in loads]
    kept = [i for i, (_, _, keep) in enumerate(loads) if keep]
    brief = [i for i in range(n_loads) if i not in kept]
    out_shape = [pltpu.VMEM(s, t) for s, t in outs] + [pltpu.HBM(s, t) for s, t in stores]
    out_shape += [pltpu.VMEM(*loaded[i]) for i in kept]
    out_shape += [pltpu.HBM(a.shape, a.dtype) for a in offloads]

    def run(*refs):
        def take(n):
            nonlocal refs
            first, refs = refs[:n], refs[n:]
            return first

        ins, going, sources, _ = take(n_args), take(n_off), take(n_loads), take(n_deps)
        results, stored, held, gone = take(n_outs), take(n_stores), take(len(kept)), take(n_off)
        targets = dict(zip(kept, held))
        scr = list(refs)
        more = {}
        if n_loads:
            sems = scr.pop()
            for i in reversed(brief):
                targets[i] = scr.pop()
            sources = [(r, b) for r, (_, b, _) in zip(sources, loads)]
            more["coming"] = Loads(sources, [targets[i] for i in range(n_loads)], sems)
        if n_off:
            leaving = Stores(going, gone, scr.pop())
            leaving.put(*range(n_off))
        if n_stores:
            sems = scr.pop()
            held = [scr.pop() for _ in stores][::-1]
            more["keeping"] = Stores(held, stored, sems)
        kernel(*ins, *results, *scr, **more)
        for part in more.values():
            part.finish()
        if n_off:
            leaving.finish()

    hbm, vmem = pl.BlockSpec(memory_space=pltpu.HBM), pl.BlockSpec(memory_space=pltpu.VMEM)
    specs = [vmem] * (n_args + n_off) + [hbm] * n_loads
    specs += [pl.BlockSpec(memory_space=pl.ANY)] * n_deps
    out_specs = [vmem] * n_outs + [hbm] * n_stores + [vmem] * len(kept) + [hbm] * n_off
    scratch = list(scratch)
    if n_stores:
        scratch += [pltpu.VMEM(s, t) for s, t in stores]
        scratch += [pltpu.SemaphoreType.DMA((n_stores * parts,))]
    if n_off:
        scratch += [pltpu.SemaphoreType.DMA((n_off,))]
    if n_loads:
        scratch += [pltpu.VMEM(*loaded[i]) for i in brief] + [pltpu.SemaphoreType.DMA((n_loads,))]
    return pl.pallas_call(
        run,
        out_shape=out_shape,
        in_specs=specs,
        out_specs=out_specs,
        scratch_shapes=scratch,
        compiler_params=pltpu.CompilerParams(vmem_limit_bytes=limit),
        cost_estimate=pl.CostEstimate(flops=1 + int(cost * 1.15e9), bytes_accessed=1, transcendentals=0),
        name=name,
    )(
        *[pltpu.with_memory_space_constraint(a, pltpu.VMEM) for a in (*args, *offloads)],
        *[pltpu.with_memory_space_constraint(a, pltpu.HBM) for a, _, _ in loads],
        *deps,
    )


NEAR, CUT, LOW_0, LOW_1, HIGH_1, CORE, BIT_X, LINE = range(8)


def find_marks(bounds, place):
    rows = bounds.shape[2]
    first = lax.axis_index("seq") * rows
    marks = (bounds[1, 0:1, 0:1], bounds[0, 0:1, 0:1], bounds[0, 0:1, rows - 1 :], bounds[1, 0:1, rows - 1 :])
    for row, v in zip((CUT, LOW_0, LOW_1, HIGH_1), marks):
        place[row : row + 1] = jnp.broadcast_to(v - first, (1, 128))


def find_place(place):
    seq, dp = lax.axis_index("seq"), lax.axis_index("dp")
    for row, v in ((NEAR, seq & 1), (CORE, dp & 1), (BIT_X, dp >> 1), (LINE, seq >> 1)):
        place[row : row + 1] = jnp.full((1, 128), v, jnp.int32)


def base_of(place, near, rows):
    odd = place[NEAR, 0]
    return rows * (1 - odd) if near else rows * odd


def wide_act(x, base, gain, shift, a1, d1, stat, part):
    def wide(at, c):
        mean, r, n, a, d = act_forward(x[at_base(at, base)].astype(F32), gain, shift)
        a1[at], d1[at] = a.astype(BF16), d.astype(BF16)
        stat[0, at], stat[1, at] = lanes(mean), lanes(r)
        return c

    strips(part.stop - part.start, 32, wide, first=part.start)


def narrow_act(z, gain, shift, a, n, d, stat, part):
    def narrow(at, c):
        _, r, nn, aa, dd = act_forward(z[at], gain, shift)
        n[at], d[at], a[at] = nn.astype(BF16), dd.astype(BF16), aa.astype(BF16)
        stat[at] = lanes(r)
        return c

    strips(part.stop - part.start, 32, narrow, first=part.start)


def windows(place, near, own, other, halo, win, pad, step):
    rows, width = own.shape
    taps = win.shape[1] // width
    rim = (pad.shape[0] - rows) // 2
    pad[rim : rim + rows] = own[...].astype(pad.dtype)
    lower = place[NEAR, 0] == (1 if near else 0)

    @pl.when(lower)
    def _():
        pad[0:rim] = halo[halo.shape[0] - rim :].astype(pad.dtype)
        pad[rim + rows :] = other[0:rim].astype(pad.dtype)

    @pl.when(jnp.logical_not(lower))
    def _():
        pad[0:rim] = other[rows - rim :].astype(pad.dtype)
        pad[rim + rows :] = halo[0:rim].astype(pad.dtype)

    base = base_of(place, near, rows)
    cut, low_0, low_1, high_1 = (place[i : i + 1] for i in (CUT, LOW_0, LOW_1, HIGH_1))
    height = 64

    def fill(part):
        for i in range(part.start, part.stop, height):
            rows_at(i)

    def rows_at(i):
        t = lax.broadcasted_iota(jnp.int32, (height, 128), 0) + (base + i)
        first = t < cut
        low = jnp.where(first, low_0, low_1)
        high = jnp.where(first, cut, high_1)
        for k in range(taps):
            offset = (k - taps // 2) * step
            m = jnp.where((t + offset >= low) & (t + offset < high), 1.0, 0.0).astype(pad.dtype)
            m = jnp.concatenate([m] * (width // 128), axis=1)
            start = rim + offset + i
            win[i : i + height, k * width : (k + 1) * width] = (
                pad[start : start + height] * m
            ).astype(BF16)

    return fill


def put_edge(edge, v, place, near):
    n = edge.shape[0]
    lower = place[NEAR, 0] == (1 if near else 0)

    @pl.when(lower)
    def _():
        edge[...] = v[0:n]

    @pl.when(jnp.logical_not(lower))
    def _():
        edge[...] = v[v.shape[0] - n :]


def first_half(x, base, gw, sw, w_in, bn, gn, sn, a1, d1, stat1, a2, n2, d2, r2, z, keeping):
    rows = a1.shape[0]

    def wide(p):
        wide_act(x, base, gw(), sw(), a1, d1, stat1, p)
        if p.stop == rows:
            keeping.put(*FIRST_STORES[len(keeping.held)])

    def inner(p):
        z[p] = dot(a1[p], w_in()[...]) + bn()

    def narrow(p):
        narrow_act(z, gn(), sn(), a2, n2, d2, r2, p)

    return wide, inner, narrow


FIRST_STORES = {3: (0, 1, 2), 7: (4, 5, 6)}


def k_in_near(place, a2, n2, d2, r2, edge, z, *, coming, keeping):
    a1, d1, stat1 = keeping.held
    find_place(place)
    x = coming.get(0)
    staggered(a1.shape[0], a1.shape[0], *first_half(
        x, base_of(place, True, a1.shape[0]), lambda: coming.get(1)[0:1], lambda: coming.get(2)[0:1],
        lambda: coming.get(3), lambda: coming.get(6)[0, 0:1], lambda: coming.get(4)[0, 0:1],
        lambda: coming.get(5)[0, 0:1], a1, d1, stat1, a2, n2, d2, r2, z, keeping,
    ))
    put_edge(edge, a2, place, True)
    find_marks(coming.get(9), place)


def k_in_far(place, x, gw, sw, gn, sn, bn, a2, n2, d2, r2, edge, z, *, coming, keeping):
    a1, d1, stat1 = keeping.held
    staggered(a1.shape[0], a1.shape[0], *first_half(
        x, base_of(place, False, a1.shape[0]), lambda: gw[0:1], lambda: sw[0:1],
        lambda: coming.get(0), lambda: bn[0, 0:1], lambda: gn[0, 0:1], lambda: sn[0, 0:1],
        a1, d1, stat1, a2, n2, d2, r2, z, keeping,
    ))
    put_edge(edge, a2, place, False)


def k_mid(
    place, x, own, other, halo, w_mid, gw, sw, bw, gn, sn, bn,
    a3, r3, a2, n2, d2, r2, pad, z, z1, *, near, step, coming, keeping,
):
    rows, width = own.shape
    win, n3, d3, y, a1, d1, stat1 = keeping.held
    fill = windows(place, near, own, other, halo, win, pad, step)
    base = base_of(place, near, rows)
    weights = w_mid[...].reshape(win.shape[1], width)

    def conv(p):
        fill(p)
        z[p] = dot(win[p], weights) + bn[0, 1:2]
        if p.stop == rows:
            keeping.put(0)

    def narrow(p):
        narrow_act(z, gn[0, 1:2], sn[0, 1:2], a3, n3, d3, r3, p)
        if p.stop == rows:
            keeping.put(1, 2)

    def outer(p):
        n = p.stop - p.start
        old = x[pl.ds(pl.multiple_of(base + p.start, n), n)].astype(F32)
        y[p] = old + dot(a3[p], coming.get(0)[...]) + bw[0:1]
        if p.stop == rows:
            keeping.put(3)

    staggered(rows, HEIGHT, conv, narrow, outer, *first_half(
        y, 0, lambda: gw[1:2], lambda: sw[1:2], lambda: coming.get(1), lambda: bn[1, 0:1],
        lambda: gn[1, 0:1], lambda: sn[1, 0:1], a1, d1, stat1, a2, n2, d2, r2, z1, keeping,
    ))


def put_wide(vec, row, acc):
    inner = vec.shape[1]
    for i in range(acc.shape[1] // inner):
        vec[row + i : row + i + 1] += total(acc[:, i * inner : (i + 1) * inner])


def k_flow(e, w_out, f, vec, *, row, coming):
    f[...] = dot_nt(e[...], w_out[...])
    vec[...] = jnp.zeros_like(vec)

    def step(at, acc):
        return acc + fold(e[at].astype(F32))

    put_wide(vec, row, strips(e.shape[0], 32, step, jnp.zeros((8, e.shape[1]), F32)))


def k_conv(
    place, vec_in, own, other, halo, w_mid, gn, sn, bn, f, a3, e2, vec, win, pad, z, *, near, step, row
):
    rows, width = own.shape
    windows(place, near, own, other, halo, win, pad, step)(slice(0, own.shape[0]))
    z[...] = dot(win[...], w_mid[...].reshape(win.shape[1], width)) + bn[1, 1:2]
    gain = gn[1, 1:2]
    base = base_of(place, near, rows)

    def narrow(at, c):
        _, r, n, a, d = act_forward(z[at], gain, sn[1, 1:2])
        a3[at] = a.astype(BF16)
        p, v = act_backward(f[at_base(at, base)], n, r, d, gain)
        e = v.astype(BF16)
        e2[at] = e
        return c[0] + fold(p * n), c[1] + fold(p), c[2] + fold(e.astype(F32))

    vec[...] = vec_in[...]
    zero = jnp.zeros((8, width), F32)
    for i, acc in enumerate(strips(rows, 32, narrow, (zero,) * 3)):
        vec[row + i : row + i + 1] += total(acc)


def k_out(place, a_n, a_f, bw, token, *, coming, keeping):
    half = a_n.shape[0]
    token[...] = jnp.zeros_like(token)
    (y,) = keeping.held
    w_out = coming.get(0)
    for near, a in ((True, a_n), (False, a_f)):
        at = pl.ds(pl.multiple_of(base_of(place, near, half), half), half)
        y[at] = dot(a[...], w_out[...]) + bw[1:2] + coming.get(1 if near else 2)[...]
        keeping.put(0, at=at)


def back_narrow(f, n, d, r, gain, e_out, vec, row):
    rows, width = f.shape

    def step(at, c):
        nn = n[at].astype(F32)
        p, v = act_backward(f[at], nn, r[at][:, 0:1], d[at].astype(F32), gain)
        e = v.astype(BF16)
        e_out[at] = e
        return c[0] + fold(p * nn), c[1] + fold(p), c[2] + fold(e.astype(F32))

    zero = jnp.zeros((8, width), F32)
    for i, acc in enumerate(strips(rows, 32, step, (zero,) * 3)):
        vec[row + i : row + i + 1] += total(acc)


def back_wide(f, x, x_base, stat, d, gain, dy, dy_base, out, out_base, cast, vec, row, cast_row):
    rows, width = f.shape

    def step(at, c):
        r = stat[1, at][:, 0:1]
        n = (x[at_base(at, x_base)].astype(F32) - stat[0, at][:, 0:1]) * r
        p, v = act_backward(f[at], n, r, d[at].astype(F32), gain)
        dx = dy[at_base(at, dy_base)].astype(F32) + v
        out[at_base(at, out_base)] = dx
        sums = (c[0] + fold(p * n), c[1] + fold(p))
        if cast is not None:
            e = dx.astype(BF16)
            cast[at] = e
            sums += (c[2] + fold(e.astype(F32)),)
        return sums

    zero = jnp.zeros((8, width), F32)
    sums = strips(rows, 32, step, (zero,) * (2 if cast is None else 3), 8)
    put_wide(vec, row, sums[0])
    put_wide(vec, row + width // vec.shape[1], sums[1])
    if cast is not None:
        put_wide(vec, cast_row, sums[2])


def flow_two(win, w_mid, z):
    taps, width = w_mid.shape[0], w_mid.shape[1]
    for j in range(taps):
        part = dot_nt(win[:, j * width : (j + 1) * width], w_mid[taps - 1 - j])
        if j == 0:
            z[...] = part
        else:
            z[...] += part


def k_back1(
    place, vec_in, own, other, halo, w_mid, gw, gn,
    e1, e3, e2, edge, vec, win, pad, z, f1, *, near, step, rows_of, coming, keeping,
):
    vec[...] = vec_in[...]
    windows(place, near, own, other, halo, win, pad, step)(slice(0, own.shape[0]))
    flow_two(win, w_mid, z)
    n2, d2, r2, w_in = (coming.get(i) for i in range(4))
    back_narrow(z, n2, d2, r2, gn[1, 0:1], e1, vec, rows_of[0])
    f1[...] = dot_nt(e1[...], w_in[...])
    base = base_of(place, near, own.shape[0])
    (dx,) = keeping.held
    x, d1, stat1, dy = (coming.get(i) for i in range(4, 8))
    back_wide(f1, x, 0, stat1, d1, gw[1:2], dy, base, dx, 0, e3, vec, rows_of[1], rows_of[3])
    keeping.put(0)
    w_out, n3, d3, r3 = (coming.get(i) for i in range(8, 12))
    z[...] = dot_nt(e3[...], w_out[...])
    back_narrow(z, n3, d3, r3, gn[0, 1:2], e2, vec, rows_of[2])
    put_edge(edge, e2, place, near)


def k_back0(
    place, vec_in, own, other, halo, w_mid, gn, e1, vec, win, pad, z, *, near, step, row, coming
):
    vec[...] = vec_in[...]
    halo = halo.at[pl.ds(halo.shape[0] - 16, 16)]
    windows(place, near, own, other, halo, win, pad, step)(slice(0, own.shape[0]))
    flow_two(win, w_mid, z)
    n2, d2, r2 = (coming.get(i) for i in range(3))
    back_narrow(z, n2, d2, r2, gn[0, 0:1], e1, vec, row)


def k_dx(place, vec_in, gw, e1_n, e1_f, vec, f1, *, row, coming, keeping):
    vec[...] = vec_in[...]
    half = e1_n.shape[0]
    (out,) = keeping.held
    w_in, x = coming.get(0), coming.get(1)
    for near, e1 in ((True, e1_n), (False, e1_f)):
        f1[...] = dot_nt(e1[...], w_in[...])
        d, stat, dy = (coming.get(i + (0 if near else 3)) for i in (2, 3, 4))
        base = base_of(place, near, half)
        back_wide(f1, x, base, stat, d, gw[0:1], dy, 0, out, base, None, vec, row, None)
        keeping.put(0, at=pl.ds(pl.multiple_of(base, half), half))


def k_split(place, *refs, jobs, parts, side, coming=None):
    n_outs = sum(parts)
    outs, turned = list(refs[-1 - n_outs : -1]), refs[-1]
    refs = refs[: -1 - n_outs]
    _, shards, _, u, rows = turned.shape
    inner = outs[0].shape[-1]

    def ref(i):
        return refs[i] if i < len(refs) else coming.get(i - len(refs))

    def whole(places, at=slice(None)):
        if len(places) == 1:
            half = rows // 2
            bases = [base_of(place, near, half) for near in (True, False)]
            parts = [ref(places[0])[pl.ds(pl.multiple_of(b, half), half)] for b in bases]
        else:
            parts = [ref(i)[:, at] for i in places]
        return jnp.concatenate(parts, axis=0)

    core = place[CORE, 0] ^ side
    kept = {}
    halves = 0
    for n, (kind, left, right, j) in zip(parts, jobs):
        here, outs = outs[:n], outs[n:]

        def put(product):
            height = product.shape[0] // n
            for i, out in enumerate(here):
                out[...] = product[i * height : (i + 1) * height]

        if kind == "half":
            turned[halves] = whole(left).T.reshape(turned.shape[1:])
            part = turned[halves, :, core].reshape(shards * u, rows)
            put(dot(part, whole(right)).astype(BF16))
            halves += 1
            continue
        if left not in kept:
            kept[left] = whole(left).T
        if kind == "taps":
            at = pl.ds(pl.multiple_of((j + 2 * core) * inner, 128), inner)
            put(dot(kept[left], whole(right, at)).astype(BF16))
            continue
        tap, before = j

        @pl.when(core == 0)
        def _():
            put(ref(before)[...])

        @pl.when(core != 0)
        def _():
            at = slice(tap * inner, (tap + 1) * inner)
            put(dot(kept[left], whole(right, at)).astype(BF16))


def k_tap(e_n, e_f, win_n, win_f, out, *, tap):
    inner = out.shape[-1]
    at = slice(tap * inner, (tap + 1) * inner)
    left = jnp.concatenate([e_n[...], e_f[...]], axis=0).T
    right = jnp.concatenate([win_n[:, at], win_f[:, at]], axis=0)
    out[...] = dot(left, right).astype(BF16)


def added(*parts):
    first, *rest = [p.astype(F32) for p in parts]
    for p in rest:
        first = first + p
    return first


def k_first(place, *refs, pairs, singles, edge):
    refs = list(refs)
    x, y = place[BIT_X, 0], place[NEAR, 0]

    def take(n):
        first = refs[:n]
        del refs[:n]
        return first

    ins = [(take(1)[0], take(n)) for two_units in pairs for n in two_units]
    ins += [(take(1)[0], take(n)) for n in singles]
    rim = take(1)[0] if edge else None

    def add_rows(a, parts, out):
        height = a.shape[0] // len(parts)
        for i, b in enumerate(parts):

            def step(k, c):
                here = pl.ds(pl.multiple_of(k * 80, 80), 80)
                at = pl.ds(pl.multiple_of(i * height + k * 80, 80), 80)
                out[at] = added(a[at], b[here]).astype(BF16)
                return c

            lax.fori_loop(0, height // 80, step, 0)

    for i in range(len(pairs)):
        (a0, b0), (a1, b1) = ins[2 * i : 2 * i + 2]
        send, stay = take(2)

        @pl.when(x == 0)
        def _():
            add_rows(a1, b1, send)
            add_rows(a0, b0, stay)

        @pl.when(x != 0)
        def _():
            add_rows(a0, b0, send)
            add_rows(a1, b1, stay)

    for out, side in zip(refs, (1 - y, y)):
        at = 0
        for a, parts in ins[2 * len(pairs) :]:
            u = a.shape[2]
            each = a.shape[0] // len(parts)
            for k in range(a.shape[0]):
                b = parts[k // each]
                out[at : at + u] = added(a[k, side], b[k % each, side]).astype(BF16)
                at += u
    if edge:
        refs[0][at:] = rim[...]


def k_second(place, a, b, *refs):
    *vec, send, stay = refs
    mine = place[NEAR, 0]
    u = a.shape[2]
    for out, side in ((send, 1 - mine), (stay, mine)):

        def step(k, c):
            at = pl.ds(pl.multiple_of(k * u, u), u)
            out[at] = added(a[k, side], b[k, side]).astype(BF16)
            return c

        lax.fori_loop(0, 4, step, 0)
    if vec:
        pack(vec[0][...], send, stay, at=4 * u)


def pack(v, *outs, at):
    more = jnp.zeros((-v.shape[0] % 16, v.shape[1]), F32)
    parts = jnp.concatenate([v, more], axis=0).astype(BF16)
    for out in outs:
        out[at : at + parts.shape[0]] = parts


def unpack(ref, at):
    return ref[at:].astype(F32)[:VEC_ROWS]


def k_line(place, *refs, sums, wholes, packed, bit, u):
    mine = (place[LINE, 0] >> bit) & 1
    arrays = [refs[2 * i : 2 * i + 2] for i in range(sums)]
    arrays += [refs[2 * sums + i : 2 * sums + i + 1] for i in range(wholes)]
    send, stay = refs[2 * sums + wholes :]
    for out, side in ((send, 1 - mine), (stay, mine)):
        at = 0
        for i, parts in enumerate(arrays):
            rows = parts[0].shape[0] - (packed if i == 0 else 0)
            for j in range(rows // (2 * u)):
                part = pl.ds(pl.multiple_of((2 * j + side) * u, u), u)
                out[at : at + u] = added(*[p[part] for p in parts]).astype(BF16)
                at += u
    if packed:
        a, b = arrays[0]
        n = a.shape[0] - packed
        pack(unpack(a, n) + unpack(b, n), send, stay, at=send.shape[0] - packed)


def k_sum(place, *refs, rows):
    out = refs[-1]
    at = 0
    for i, n in enumerate(rows):
        a, b = refs[2 * i], refs[2 * i + 1]
        out[at : at + n] = added(a[0:n], b[0:n]).astype(BF16)
        at += n
    if refs[0].shape[0] > rows[0]:
        pack(unpack(refs[0], rows[0]) + unpack(refs[1], rows[0]), out, at=at)


def k_rows(place, *refs, splits, u):
    *refs, out = refs
    x = place[BIT_X, 0]
    at = 0
    refs = list(refs)
    for split in splits:
        if split is None:
            ready = refs.pop(0)
            out[at : at + ready.shape[0]] = ready[...]
            at += ready.shape[0]
            continue
        mine, got = refs.pop(0), refs.pop(0)
        for k, apart in enumerate(split):
            here = slice(k * u, (k + 1) * u)
            if apart:
                base = pl.multiple_of(at + x * u, u)
                other = pl.multiple_of(at + (1 - x) * u, u)
                out[pl.ds(base, u)], out[pl.ds(other, u)] = mine[here], got[here]
                at += 2 * u
            else:
                out[at : at + u] = added(mine[here], got[here]).astype(BF16)
                at += u
        if mine.shape[0] > len(split) * u:
            n = len(split) * u
            pack(unpack(mine, n) + unpack(got, n), out, at=out.shape[0] - (mine.shape[0] - n))


def k_share(place, ref, *refs, side, u):
    vectors, n_vec = (), 0
    if side:
        mine, *refs = refs
        refs = refs[3:]
        n_vec = 6
    out_in, out_mid, out_out = refs[:3]
    vectors, refs = refs[3 : 3 + n_vec], refs[3 + n_vec :]
    stage, held, sems = refs[0], refs[1:-1], refs[-1]
    c = place[CORE, 0] ^ side
    rows = pl.ds(pl.multiple_of(c * u, u), u)
    copies = []

    def put(src, dst):
        copies.append(pltpu.make_async_copy(src, dst, sems.at[len(copies)]))
        copies[-1].start()

    def units(i, n=1):
        for k in range(i, i + n):
            stage[k] = ref[k * u : (k + 1) * u].astype(F32)
        return stage.at[i] if n == 1 else stage.at[i : i + n]

    put(units(0, 2), out_mid.at[1, pl.ds(2 * c, 2)])
    put(units(2), out_mid.at[1 - c, 4])
    put(units(3), out_out.at[1, rows])
    put(units(4, 2), out_mid.at[0, pl.ds(2 * c, 2)])
    put(units(6), out_in.at[0, rows])
    put(units(7), out_in.at[1, rows])
    put(units(8), out_out.at[0, rows])
    if side:
        vec, gw, sw, gn, sn, bn, bw = held
        vec[...] = unpack(mine, 9 * u) + unpack(ref, 9 * u)
        inner = vec.shape[1]
        two = gw.shape[1] // inner
        for block in range(2):
            for i in range(2):
                row = 3 * (2 * block + i)
                for j, out in enumerate((gn, sn, bn)):
                    out[block, i : i + 1] = vec[row + j : row + j + 1]
            for j, out in enumerate((gw, sw, bw)):
                for k in range(two):
                    row = 12 + (3 * block + j) * two + k
                    out[block : block + 1, k * inner : (k + 1) * inner] = vec[row : row + 1]
        for src, dst in zip((gw, sw, gn, sn, bn, bw), vectors):
            put(src, dst)
    for copy in copies:
        copy.wait()


def share(side, args, before, shapes, vector_shapes, vec_shape, u):
    inner = shapes[0][-1]
    vmem, hbm = pl.BlockSpec(memory_space=pltpu.VMEM), pl.BlockSpec(memory_space=pltpu.HBM)
    outs = list(shapes) + list(vector_shapes)
    held = [pltpu.VMEM(s, F32) for s in ([vec_shape] + list(vector_shapes) if side else [])]
    return pl.pallas_call(
        functools.partial(k_share, side=side, u=u),
        out_shape=[pltpu.HBM(s, F32) for s in outs],
        in_specs=[vmem] * len(args) + [hbm] * len(before),
        out_specs=[hbm] * len(outs),
        scratch_shapes=[pltpu.VMEM((9, u, inner), F32), *held, pltpu.SemaphoreType.DMA((7 + len(vector_shapes),))],
        input_output_aliases={len(args) + i: i for i in range(len(before))},
        compiler_params=pltpu.CompilerParams(vmem_limit_bytes=VMEM_LIMIT),
        cost_estimate=pl.CostEstimate(flops=1, bytes_accessed=1, transcendentals=0),
        name="k_share",
    )(
        *[pltpu.with_memory_space_constraint(a, pltpu.VMEM) for a in args],
        *[pltpu.with_memory_space_constraint(a, pltpu.HBM) for a in before],
    )


def k_plus(a, b, out):
    out[...] = added(a[...], b[0 : a.shape[0]]).astype(BF16)


def k_nothing(*refs, coming):
    pass


def swap(v, axis, bits):
    count = lax.axis_size(axis)
    return lax.ppermute(v, axis, [(i, i ^ bits) for i in range(count)])


def to_near(v):
    return swap(v, "seq", 1)


def to_far(v):
    count = lax.axis_size("seq")
    pairs = [(i, i + 1) for i in range(1, count - 1, 2)]
    return lax.ppermute(v, "seq", pairs + [(j, i) for i, j in pairs])


def dot_tn(a, b):
    return lax.dot_general(a, b, (((0,), (0,)), ((), ())), preferred_element_type=F32)


def plain_weights(a1, e1, win, e2, a3, e3):
    taps = win.shape[1] // e2.shape[1]
    grad_mid = dot_tn(win, e2).reshape(taps, e2.shape[1], e2.shape[1])
    shares = (
        lax.psum_scatter(dot_tn(a1, e1), "seq", scatter_dimension=0, tiled=True),
        lax.psum_scatter(grad_mid, "seq", scatter_dimension=2, tiled=True),
        lax.psum_scatter(dot_tn(a3, e3), "seq", scatter_dimension=1, tiled=True),
    )
    return [lax.psum(v.astype(BF16), "dp").astype(F32) for v in shares]


def body(
    tokens, bounds, w_in, w_mid, w_out, gain_wide, shift_wide, gain_narrow, shift_narrow,
    bias_narrow, bias_wide, cotangent,
):
    x0 = tokens[0]
    cot = cotangent[0]
    rows, width = x0.shape
    taps, inner = w_mid.shape[1], w_mid.shape[2]
    shards = lax.axis_size("seq")
    u = inner // shards
    two = width // inner
    half = rows // 2
    close, broad = DILATION_CLOSE, DILATION_BROAD

    wide_h, narrow_h, column = (half, width), (half, inner), ((half, 128), F32)
    win_h = ((half, taps * inner), BF16)
    act_wide = [(wide_h, BF16), (wide_h, BF16), ((2, half, 128), F32)]
    act_narrow = [(narrow_h, BF16), (narrow_h, BF16), (narrow_h, BF16), column]
    edge = ((16, inner), BF16)
    z = pltpu.VMEM(narrow_h, F32)
    f1 = pltpu.VMEM(wide_h, F32)
    win_scratch = pltpu.VMEM(*win_h)
    pad_0 = pltpu.VMEM((half + 32, inner), F32)
    pad_1 = pltpu.VMEM((half + 4 * broad, inner), BF16)
    n_narrow = 12
    vec_shape = ((n_narrow + 6 * two, inner), F32)

    def row_narrow(b, i):
        return 3 * (2 * b + i)

    def row_wide(b, i):
        return n_narrow + (3 * b + i) * two

    def brief(*arrays):
        return tuple((a, None, False) for a in arrays)

    place, a2_n, *p_n, edge_n, a1_n, d1_n, stat_n, x, gw, sw, gn, sn, bn, bw, w_mid_0 = call(
        k_in_near, [((8, 128), jnp.int32)] + act_narrow + [edge], (), [z], "k_in",
        loads=((x0, None, True), (gain_wide, None, True), (shift_wide, None, True), (w_in, 0, False),
               (gain_narrow, None, True), (shift_narrow, None, True), (bias_narrow, None, True),
               (bias_wide, None, True), (w_mid, 0, True), (bounds, None, False)),
        stores=act_wide, cost=4,
    )
    halo_n = to_near(edge_n)
    a2_f, *p_f, edge_f, a1_f, d1_f, stat_f, p1, p2, p3 = call(
        k_in_far, act_narrow + [edge], (place, x, gw, sw, gn, sn, bn), [z], "k_in", (edge_n,),
        loads=((w_in, 0, False),), stores=act_wide, offloads=p_n, cost=4,
    )
    p_n = (p1, p2, p3)
    halo_f = to_far(edge_f)

    def mid_call(near, own, other, halo, deps, loads, offloads):
        return call(
            functools.partial(k_mid, near=near, step=close),
            [(narrow_h, BF16), column] + act_narrow,
            (place, x, own, other, halo, w_mid_0, gw, sw, bw, gn, sn, bn),
            [pad_0, z, z], "k_mid", deps, ((w_out, 0, False), (w_in, 1, False)) + loads,
            [win_h, (narrow_h, BF16), (narrow_h, BF16), (wide_h, F32)] + act_wide, offloads, cost=8,
        )

    a3_n, r3_n, b2_n, *q_n = mid_call(True, a2_n, a2_f, halo_n, (), (), p_f)
    s_n, p_f = q_n[3:10], q_n[10:]
    halo_n = to_near(b2_n)
    a3_f, r3_f, b2_f, *q_f = mid_call(
        False, a2_f, a2_n, halo_f, (b2_n,), ((w_out, 1, True), (cot, None, True)),
        (a3_n, r3_n, *q_n[:3]),
    )
    s_f, (w_out_1, cot_v), q_n = q_f[3:10], q_f[10:12], q_f[12:]
    halo_f = to_far(b2_f)
    f3, vec, w_mid_1, *q_f = call(
        functools.partial(k_flow, row=row_wide(1, 2)),
        [((rows, inner), F32), vec_shape], (cot_v, w_out_1), (), "k_flow",
        loads=((w_mid, 1, True),), offloads=(a3_f, r3_f, *q_f[:3]), cost=3,
    )

    def conv_call(near, vec, own, other, halo):
        return call(
            functools.partial(k_conv, near=near, step=broad, row=row_narrow(1, 1)),
            [(narrow_h, BF16), (narrow_h, BF16), vec_shape, win_h],
            (place, vec, own, other, halo, w_mid_1, gn, sn, bn, f3),
            [pad_1, z], "k_conv", cost=3,
        )

    c3_n, e2_n, vec, win_n = conv_call(True, vec, b2_n, b2_f, halo_n)
    halo_n = to_near(e2_n)
    c3_f, e2_f, vec, win_f = conv_call(False, vec, b2_f, b2_n, halo_f)
    halo_f = to_far(e2_f)

    fast = shards == 8 and u % 16 == 0
    unit = (inner, inner)
    part = (u, inner)

    def split_call(jobs, args, loads, side, name, deps, cost=0, parts=None):
        parts = parts or (1,) * len(jobs)
        halves = sum(kind == "half" for kind, *_ in jobs)
        turned = pltpu.VMEM((halves, shards, 2, u, rows), BF16)
        return call(
            functools.partial(k_split, jobs=jobs, side=side, parts=parts),
            [((inner // n, inner), BF16) for n in parts for _ in range(n)],
            (place, *args), [turned], name, deps, loads, cost=cost,
        )

    def swap_cores(units, parts=None):
        got = [swap(v, "dp", 1) for v in units]
        parts = parts or (1,) * len(units)
        return [tuple(got.pop(0) for _ in range(n)) for n in parts]

    def first_sum(keep, got, pairs, singles, name, deps, cost=0, edge=()):
        args = []
        for i in [j for pair in pairs for j in (pair, pair + 1)]:
            args += [keep[i], *got[i]]
        for i in singles:
            args += [v.reshape(-1, 2, u, inner) for v in (keep[i], *got[i])]
        outs = [(unit, BF16)] * (2 * len(pairs))
        n = 4 * u * len(singles)
        if singles:
            outs += [((n + sum(v.shape[0] for v in edge), inner), BF16), ((n, inner), BF16)]
        kernel = functools.partial(
            k_first, pairs=tuple((len(got[i]), len(got[i + 1])) for i in pairs),
            singles=tuple(len(got[i]) for i in singles), edge=bool(edge),
        )
        return call(kernel, outs, (place, *args, *edge), (), name, deps, cost=cost)

    n_packed = -(-vec_shape[0][0] // 16) * 16
    assert vec_shape[0][0] == VEC_ROWS

    def second_sum(stay, got, name, deps, cost=0, vec=()):
        views = [v.reshape(4, 2, u, inner) for v in (stay, got)]
        n = 4 * u + (n_packed if vec else 0)
        return call(
            k_second, [((n, inner), BF16)] * 2, (place, *views, *vec), (), name, deps, cost=cost
        )

    def line_half(pairs, wholes, bit, name, deps, cost=0, packed=0):
        arrays = [pair[0] for pair in pairs] + list(wholes)
        n = sum(a.shape[0] for a in arrays) - packed
        n = n // 2 + packed
        kernel = functools.partial(k_line, sums=len(pairs), wholes=len(wholes), packed=packed, bit=bit, u=u)
        send, stay = call(
            kernel, [((n, inner), BF16)] * 2, (place, *[v for pair in pairs for v in pair], *wholes),
            (), name, deps, cost=cost,
        )
        return stay, swap(send, "seq", 2 << bit)

    def line_sums(pairs, rows, name, deps, cost=0):
        n = sum(rows) + pairs[0][0].shape[0] - rows[0]
        return call(
            functools.partial(k_sum, rows=rows), [((n, inner), BF16)],
            (place, *[v for pair in pairs for v in pair]), (), name, deps, cost=cost,
        )[0]

    def row_sums(pairs, splits, name, deps):
        n = sum(pair[0].shape[0] for pair in pairs) + u * sum(sum(split or ()) for split in splits)
        return call(
            functools.partial(k_rows, splits=splits, u=u), [((n, inner), BF16)],
            (place, *[v for pair in pairs for v in pair]), (), name, deps,
        )[0]

    def back1_call(near, vec, own, other, halo, q, s, deps, more=()):
        return call(
            functools.partial(
                k_back1, near=near, step=broad,
                rows_of=(row_narrow(1, 0), row_wide(1, 0), row_narrow(0, 1), row_wide(0, 2)),
            ),
            [(narrow_h, BF16), (wide_h, BF16), (narrow_h, BF16), edge, vec_shape],
            (place, vec, own, other, halo, w_mid_1, gw, gn),
            [win_scratch, pad_1, z, f1], "k_back1", deps, stores=[(wide_h, F32)], cost=5 if near else 2,
            loads=(*brief(*q[2:5]), (w_in, 1, False), *brief(s[3], s[5], s[6], cot),
                   (w_out, 0, False), *brief(s[1], s[2], q[1]), *more),
        )

    def back0_call(near, vec, own, other, halo, p, deps, loads, cost=0):
        return call(
            functools.partial(k_back0, near=near, step=close, row=row_narrow(0, 0)),
            [(narrow_h, BF16), vec_shape], (place, vec, own, other, halo, w_mid_0, gn),
            [win_scratch, pad_0, z], "k_back0", deps, loads=brief(*p) + loads, cost=cost,
        )

    def out_call(deps):
        return call(
            k_out, [((8, 128), F32)], (place, c3_n, c3_f, bw), (), "k_out", deps,
            loads=((w_out, 1, False), *brief(s_n[3], s_f[3])), stores=[((rows, width), F32)], parts=2,
        )

    def dx_call(vec, deps):
        return call(
            functools.partial(k_dx, row=row_wide(0, 0)), [vec_shape],
            (place, vec, gw, e1_n0, e1_f0), [f1], "k_dx", deps,
            loads=((w_in, 0, False), *brief(x0, d1_n, stat_n, dx_n, d1_f, stat_f, dx_f)),
            stores=[((rows, width), F32)], parts=2,
        )

    def rowed(v):
        return v.reshape(-1, inner)

    if fast:
        jobs = (("taps", (0, 1), (5, 6), 0), ("taps", (0, 1), (5, 6), 1), ("half", (2,), (3, 4), None))
        args = (e2_n, e2_f, cot_v, c3_n, c3_f, win_n, win_f)
        send_1 = split_call(jobs, args, (), 1, "k_weights1", (vec,))
        got_1 = swap_cores(send_1)
        keep_1 = split_call(jobs, args, (), 0, "k_weights1", (send_1[0],))
        last = keep_1[0]
    else:
        last = vec
    e1_n, e3_n, e2_n0, edge_n, vec, dx_n = back1_call(
        True, vec, e2_n, e2_f, halo_n, q_n, s_n, (last,)
    )
    if fast:
        xs, x1, ys, y1b = first_sum(
            keep_1, got_1, (0,), (2,), "k_first1", (vec, halo_f), 0, (edge_n,)
        )
        x_got, y_got = swap(xs, "dp", 2), swap(ys, "seq", 1)
        (tap_1,) = call(
            functools.partial(k_tap, tap=4), [(unit, BF16)], (e2_n, e2_f, win_n, win_f), (), "k_tap",
            (x1,),
        )
        halo_n, last = y_got, tap_1
    else:
        halo_n = to_near(edge_n)
    more = tuple((v, None, True) for v in (s_n[0], s_f[0], s_n[4], s_f[4], q_n[0], q_f[0])) if fast else ()
    e1_f, e3_f, e2_f0, edge_f, vec, dx_f, *held = back1_call(
        False, vec, e2_f, e2_n, halo_f, q_f, s_f, (last,), more
    )
    halo_f = to_far(edge_f)

    if not fast:
        (w_mid_0,) = call(k_nothing, [], (place,), (), "k_load", (vec,), ((w_mid, 0, True),))
        e1_n0, vec = back0_call(True, vec, e2_n0, e2_f0, halo_n, p_n, (), ())
        e1_f0, vec = back0_call(False, vec, e2_f0, e2_n0, halo_f, p_f, (), ())
        token, y1 = out_call((vec,))
        vec, dx = dx_call(vec, (token,))

        def both(n, f):
            return jnp.concatenate([n, f])

        at = half * (1 - (lax.axis_index("seq") & 1))
        e3_1 = jnp.roll(cot, -at, axis=0)
        w_1 = plain_weights(
            both(s_n[4], s_f[4]), both(e1_n, e1_f), both(win_n, win_f), both(e2_n, e2_f),
            both(c3_n, c3_f), e3_1,
        )
        w_0 = plain_weights(
            both(a1_n, a1_f), both(e1_n0, e1_f0), both(s_n[0], s_f[0]), both(e2_n0, e2_f0),
            both(q_n[0], q_f[0]), both(e3_n, e3_f),
        )
        grad_w_in, grad_w_mid, grad_w_out = (jnp.stack(pair) for pair in zip(w_0, w_1))
        vec = lax.psum(vec, ("dp", "seq"))
    else:
        jobs = (
            ("taps", (4, 5), (7, 8), 0), ("taps", (4, 5), (7, 8), 1), ("half", (9, 10), (0, 1), None),
            ("half", (2, 3), (11, 12), None), ("odd", (4, 5), (7, 8), (4, 6)),
        )
        args = (e1_n, e1_f, e3_n, e3_f, e2_n0, e2_f0, tap_1, *held)
        parts = (1, 1)
        send_2 = split_call(jobs[:2], args, (), 1, "k_weights2", (vec,), parts=parts)
        got_2 = swap_cores(send_2, parts)
        *keep_2, w_mid_0 = split_call(jobs, args, ((w_mid, 0, True),), 0, "k_weights2", (send_2[0],))
        send_4 = split_call(jobs[2:], args, (), 1, "k_weights4", (keep_2[0],))
        got_2 = got_2 + swap_cores(send_4)
        (y1b,) = call(
            k_plus, [((4 * u, inner), BF16)], (y1b, y_got), (), "k_plus", (send_4[0], halo_f)
        )
        as_, a1 = first_sum(keep_2, got_2, (0,), (), "k_first2", (y1b, x_got))
        a_got = swap(as_, "dp", 2)
        xys, xy = second_sum(x1, x_got, "k_second1", (a1,))
        xy_got = swap(xys, "seq", 1)
        bs, b1 = first_sum(keep_2, got_2, (), (4,), "k_first5", (xy, *got_2[2], *got_2[3]))
        b_got = swap(bs, "seq", 1)
        line_y = line_half([], [y1b], 0, "k_line0", (b1,))
        e1_n0, vec = back0_call(True, vec, e2_n0, e2_f0, halo_n, p_n, (line_y[0],), (), 7)
        e1_f0, vec, a1_n, a1_f = back0_call(
            False, vec, e2_f0, e2_n0, halo_f, p_f, (e1_n0,), ((a1_n, None, True), (a1_f, None, True)), 1
        )
        vec, dx = dx_call(vec, ())
        jobs = (("half", (0, 1), (2, 3), None),)
        args = (a1_n, a1_f, e1_n0, e1_f0)
        send_3 = split_call(jobs, args, (), 1, "k_weights3", (vec,), parts=(2,))
        got_3 = swap_cores(send_3, (2,))
        keep_3 = split_call(jobs, args, (), 0, "k_weights3", (send_3[0],))
        (sums_y,) = call(k_plus, [((2 * u, inner), BF16)], line_y, (), "k_plus", (keep_3[0],))
        line_a = line_half([(xy, xy_got), (b1, b_got)], [], 0, "k_line1", (sums_y,))
        ds, d1 = first_sum(keep_2, got_2, (2,), (), "k_first3", (line_a[0],), 0.3)
        d_got = swap(ds, "dp", 2)
        ays, ay = second_sum(a1, a_got, "k_second2", (d1,), 2, (vec,))
        ay_got = swap(ays, "seq", 1)
        cs, c1 = first_sum(keep_3, got_3, (), (0,), "k_first4", (ay,))
        c_got = swap(cs, "seq", 1)
        token, y1 = out_call((c1,))
        line_a = line_half([line_a], [sums_y], 1, "k_line2", (token,))
        line_b = line_half([(ay, ay_got)], [], 0, "k_line3", (line_a[0],), 0, n_packed)
        line_e = line_half([(c1, c_got)], [], 0, "k_line4", (line_b[0],))
        dys, dy = second_sum(d1, d_got, "k_second3", (line_e[0],))
        dy_got = swap(dys, "seq", 1)
        sums_a = line_sums([line_a], (3 * u,), "k_sum1", (dy,), 0.7)
        a_rows = (sums_a, swap(sums_a, "dp", 2))
        line_b = line_half([line_b], [], 1, "k_line5", (sums_a,), 0, n_packed)
        line_e = line_half([line_e], [], 1, "k_line6", (line_b[0],), 2)
        line_c = line_half([(dy, dy_got)], [], 0, "k_line7", (line_e[0],))
        whole = row_sums([a_rows], ((1, 0, 0),), "k_rows1", (line_c[0],))
        sums_b = line_sums([line_b, line_e], (u, u), "k_sum2", (whole,), 1.5)
        b_rows = (sums_b, swap(sums_b, "dp", 2))
        line_c = line_half([line_c], [], 1, "k_line8", (sums_b,), 2)
        sums_c = line_sums([line_c], (u,), "k_sum3", (line_c[0],))
        c_rows = (sums_c, swap(sums_c, "dp", 2))
        whole = row_sums(
            [(whole,), b_rows, c_rows], (None, (1, 0), (1,)), "k_rows2", (sums_c,)
        )
        got = swap(whole, "dp", 1)
        shapes = ((2, 2 * u, inner), (2, taps, u, inner), (2, 2 * u, inner))
        vector_shapes = ((2, width), (2, width), (2, 2, inner), (2, 2, inner), (2, 2, inner), (2, width))
        grads = share(0, (place, whole), (), shapes, (), vec_shape[0], u)
        grad_w_in, grad_w_mid, grad_w_out, *vectors = share(
            1, (place, got, whole), grads, shapes, vector_shapes, vec_shape[0], u
        )
        return (
            y1[None], dx[None], grad_w_in, grad_w_mid.swapaxes(2, 3), grad_w_out.swapaxes(1, 2),
            *vectors,
        )

    narrow = vec[:n_narrow].reshape(2, 2, 3, inner)
    wide = vec[n_narrow:].reshape(2, 3, width)
    return (
        y1[None],
        dx[None],
        grad_w_in,
        grad_w_mid,
        grad_w_out,
        wide[:, 0],
        wide[:, 1],
        narrow[:, :, 0],
        narrow[:, :, 1],
        narrow[:, :, 2],
        wide[:, 2],
    )


def solution(mesh):
    row = P("dp", "seq", None)
    return jax.shard_map(
        body,
        mesh=mesh,
        in_specs=(row, P(None, "dp", "seq")) + (P(),) * 9 + (row,),
        out_specs=(
            row,
            row,
            P(None, "seq", None),
            P(None, None, None, "seq"),
            P(None, None, "seq"),
        )
        + (P(),) * 6,
        check_vma=False,
    )
```
